32 devices in a mesh: mode: 4 (over y, core), dom: 8 (over z, x).
Axes of the slice: x: 2, y: 2, z: 4, core: 2. Of those that a mesh axis runs over, the one named last changes fastest.
Arguments:
- velocity_prev: float32 [256, 8192], P('mode', 'dom'), may hold values from -2 to 2
- elem_ops: float32 [128, 81, 81], P('dom'), as said below
- lumped_mass: float32 [8192], P('dom'), may hold values from 0.5 to 1.5
- span_slope: float32 [256], replicated, may hold values from -0.15 to 0.15
- local_to_global: int32 [128, 81], P('dom'), may hold values from 0 to 1023, as said below
- iface_nodes: int32 [8, 2, 128], P('dom'), may hold values from 0 to 1023, as said below
- live_elems: int32 [8], replicated, may hold values from 1 to 16, 96 in all
Outputs:
- velocity: float32 [256, 8192], P('mode', 'dom')
The draws below stay inside these ranges and needn't reach their ends.
Inputs may be any that keep to these rules, and one draw needn't show every extreme that they name: `elem_ops`: each element's operator is symmetric, with a positive diagonal and non-positive entries off it whose absolute sum in each row stays below 0.96 times that row's diagonal entry. `local_to_global`: the 81 entries of one element are distinct nodes of its partition, and every one of a partition's 1024 nodes belongs to some element slot. `iface_nodes`: within a partition the 256 entries are distinct. Entry s of partition q's list 1 and entry s of the next partition's list 0 (cyclically over the 8 partitions) are copies of one mesh node. `live_elems`: element slots at or beyond a partition's count are padding and take no part.
All inputs are finite; a program needn't handle non-finite values.
Results may differ from the reference program's by a relative error of at most 0.0003.
Values sent between devices are 32-bit elements; how exact they have to be, the bound alone decides.
No kernel may reach another device: no remote copies, remote signals or barrier semaphores. Data moves between devices by JAX's collectives and lax.ppermute only.
A program may use at most 128 MiB of HBM per device.

```python
import math
import jax
import jax.numpy as jnp
import numpy as np
from jax import lax

MODES = 256
NODE_ELEM = 81
ELEM_DEV = 16
IFACE = 128
ITERS = 3
SWEEPS = 6
NODES_DEV = 1024
ELEMS = 128
NODES = 8192
N_DOM = 8


def draw_elem_ops(key, part):
    key = jax.random.fold_in(key, 11)
    key_weak, key_pick, key_strong, key_ratio, key_scale = jax.random.split(key, 5)
    shape = (ELEMS, NODE_ELEM, NODE_ELEM)
    weak_top = 0.02
    strong_chance = 0.05
    ratio_low = 0.85
    ratio_high = 0.93
    scale_low = 2.0
    scale_high = 8.0
    weak = jax.random.uniform(key_weak, shape, jnp.float32, 0.0, weak_top)
    picked = (jax.random.uniform(key_pick, shape, jnp.float32) < strong_chance).astype(jnp.float32)
    strong = jax.random.uniform(key_strong, shape, jnp.float32, 0.1, 0.3) * picked
    raw_coupling = weak + strong
    eye_mask = jnp.eye(NODE_ELEM, dtype=jnp.float32)[None, :, :]
    coupled = 0.5 * (raw_coupling + jnp.transpose(raw_coupling, (0, 2, 1))) * (1.0 - eye_mask)
    row_total = jnp.sum(coupled, axis=2, keepdims=True)
    share = jax.random.uniform(key_ratio, (ELEMS, NODE_ELEM, 1), jnp.float32, ratio_low, ratio_high)
    diagonal = row_total / share
    scale = jnp.exp(jax.random.uniform(key_scale, (ELEMS, 1, 1), jnp.float32, jnp.log(scale_low), jnp.log(scale_high)))
    return scale * (eye_mask * diagonal - coupled)


def draw_local_to_global(key, part):
    key = jax.random.fold_in(key, 23)
    extra_count = NODE_ELEM - 64

    def one_partition(partition):
        part_key = jax.random.fold_in(key, partition)
        order = jax.random.permutation(jax.random.fold_in(part_key, 0), NODES_DEV).astype(jnp.int32)

        def one_slot(slot):
            slot_key = jax.random.fold_in(part_key, slot + 1)
            key_extra, key_mix = jax.random.split(slot_key)
            core = order[slot * 64 + jnp.arange(64, dtype=jnp.int32)]
            offsets = jax.random.permutation(key_extra, NODES_DEV - 64).astype(jnp.int32)[:extra_count]
            extras = order[(slot * 64 + 64 + offsets) % NODES_DEV]
            members = jnp.concatenate([core, extras])
            mixing = jax.random.permutation(key_mix, NODE_ELEM).astype(jnp.int32)
            return members[mixing]
        return jax.vmap(one_slot)(jnp.arange(ELEM_DEV, dtype=jnp.int32))
    return jax.vmap(one_partition)(jnp.arange(N_DOM, dtype=jnp.int32)).reshape(ELEMS, NODE_ELEM)


def draw_iface_nodes(key, part):
    key = jax.random.fold_in(key, 37)

    def one_partition(partition):
        part_key = jax.random.fold_in(key, partition)
        key_rest, key_pick = jax.random.split(part_key)
        remaining = 1 + jax.random.permutation(key_rest, NODES_DEV - 2).astype(jnp.int32)
        everything = jnp.concatenate([jnp.array([0, NODES_DEV - 1], jnp.int32), remaining])
        chosen = everything[:2 * IFACE]
        shuffled = chosen[jax.random.permutation(key_pick, 2 * IFACE)]
        return shuffled.reshape(2, IFACE)
    return jax.vmap(one_partition)(jnp.arange(N_DOM, dtype=jnp.int32))


def levels(key, dims, pieces, smallest, high):
    level, own = 1.0, jax.random.fold_in(key, 6)
    for axis_at, shards_of in pieces:
        steps = jnp.exp(jax.random.uniform(jax.random.fold_in(own, axis_at), (shards_of,), jnp.float32, smallest / len(pieces), high / len(pieces)))
        level = level * jnp.repeat(steps, dims[axis_at] // shards_of).reshape([-1 if axis == axis_at else 1 for axis in range(len(dims))])
    return level


def profile(number_of, total, limit, slope):
    portions = [(1 << 20) // math.isqrt(standing ** slope) + 1 for standing in range(2, number_of + 1)]
    spare, given = total - limit - (number_of - 1), [1] * (number_of - 1)
    while spare > 0:
        movable = [i for i in range(number_of - 1) if given[i] < limit]
        mass, left = sum([portions[i] for i in movable]), spare
        for i in movable:
            extra = min(limit - given[i], max(1, left * portions[i] // mass), spare)
            given[i] = given[i] + extra
            spare = spare - extra
    return np.array([limit] + given)


def uneven(key, amount, total, bound, lean):
    if amount == 2:
        one = jax.random.randint(key, (), max(1, total - bound), min(bound, total - 1) + 1)
        return jnp.stack([one, total - one])
    tallies = jnp.asarray(profile(amount, total, bound, lean), jnp.int32)
    pairs = (amount - 1) // 2
    giver, receiver = tallies[1:1 + 2 * pairs:2], tallies[2:2 + 2 * pairs:2]
    margin = jnp.minimum(giver - 1, bound - receiver)
    moved = jax.random.randint(jax.random.fold_in(key, 1), (pairs,), 0, 1 << 20) % (margin + 1)
    tallies = tallies.at[1:1 + 2 * pairs:2].set(giver - moved).at[2:2 + 2 * pairs:2].set(receiver + moved)
    return tallies[jax.random.permutation(jax.random.fold_in(key, 2), amount)]


def gaussian(rng, dims, width, limit, shards=(), held_as=jnp.bfloat16):
    loudness = levels(rng, dims, shards, -0.22, 0.18) if shards else 1.0
    entries = jax.random.normal(rng, dims, jnp.float32) * width * loudness
    return jnp.minimum(jnp.maximum(entries, -limit), limit).astype(held_as)


def setup_inputs(seed: int = 0) -> dict:
    streams_of = jax.random.split(jax.random.key(seed), 8)
    return {
        "velocity_prev": gaussian(streams_of[0], (MODES, NODES), 0.25, 2.0, ((0, 4), (1, 8)), jnp.float32),
        "elem_ops": draw_elem_ops(jax.random.fold_in(streams_of[7], 71), 0),
        "lumped_mass": jnp.clip(0.5 + 1.0 * jax.random.uniform(streams_of[2], (NODES,), jnp.float32) ** levels(streams_of[2], (NODES,), ((0, 8),), -0.2, 0.2), 0.5, 1.5),
        "span_slope": jnp.clip(jax.random.uniform(streams_of[3], (MODES,), jnp.float32, -0.15, 0.15), -0.15, 0.15),
        "local_to_global": draw_local_to_global(jax.random.fold_in(streams_of[7], 71), 0),
        "iface_nodes": draw_iface_nodes(jax.random.fold_in(streams_of[7], 71), 0),
        "live_elems": uneven(streams_of[6], N_DOM, N_DOM * ELEM_DEV * 3 // 4, ELEM_DEV, 2).astype(jnp.int32),
    }


mass_weight = 4.0
bound_low = 0.1
bound_high = 2.0


def wave_tables(mode_count):
    column = jnp.arange(mode_count, dtype=jnp.int32)
    number = jnp.where(column == 1, mode_count // 2, column // 2).astype(jnp.int32)
    is_sine = (column % 2 == 1) & (column > 1)
    planes = jnp.arange(mode_count, dtype=jnp.int32)
    phase_index = (planes[:, None] * number[None, :]) % mode_count
    angles = phase_index.astype(jnp.float32) * (2.0 * jnp.pi / mode_count)
    cosine = jnp.cos(angles)
    sine_part = jnp.sin(angles)
    synthesis = jnp.where(is_sine[None, :], sine_part, cosine)
    factor = number.astype(jnp.float32) / (mode_count // 2)
    derivative = jnp.where(is_sine[None, :], cosine, -sine_part) * factor[None, :]
    derivative = jnp.where(column[None, :] > 1, derivative, 0.0)
    weights = jnp.where(column < 2, 1.0 / mode_count, 2.0 / mode_count)
    analysis = synthesis.T * weights[:, None]
    helmholtz = mass_weight + (8.0 * number.astype(jnp.float32) / mode_count) ** 2
    return synthesis, derivative, analysis, helmholtz


def reference(velocity_prev, elem_ops, lumped_mass, span_slope, local_to_global, iface_nodes, live_elems):
    highest = lax.Precision.HIGHEST
    synthesis, derivative, analysis, helmholtz = wave_tables(MODES)
    slot_index = jnp.arange(ELEM_DEV, dtype=jnp.int32)
    live_mask = (slot_index[None, :] < live_elems[:, None]).astype(jnp.float32)
    ops_parts = elem_ops.reshape(N_DOM, ELEM_DEV, NODE_ELEM, NODE_ELEM)
    map_parts = local_to_global.reshape(N_DOM, ELEM_DEV, NODE_ELEM)
    mass_parts = lumped_mass.reshape(N_DOM, NODES_DEV)
    left_ids = iface_nodes[:, 0, :]
    right_ids = iface_nodes[:, 1, :]

    def element_part(packed):
        field, operator, mapping, mask = packed
        gathered = field[:, mapping]
        result = jnp.einsum("eij,mej->mei", operator, gathered, precision=highest) * mask[None, :, None]
        return jnp.zeros_like(field).at[:, mapping].add(result)

    def element_apply(fields):
        return lax.map(element_part, (fields, ops_parts, map_parts, live_mask))

    def take_nodes(field, nodes):
        return field[:, nodes]

    def add_nodes(field, left_nodes, right_nodes, from_prev, from_next):
        return field.at[:, left_nodes].add(from_prev).at[:, right_nodes].add(from_next)

    def assemble(fields):
        left_vals = jax.vmap(take_nodes)(fields, left_ids)
        right_vals = jax.vmap(take_nodes)(fields, right_ids)
        from_prev = jnp.roll(right_vals, 1, axis=0)
        from_next = jnp.roll(left_vals, -1, axis=0)
        return jax.vmap(add_nodes)(fields, left_ids, right_ids, from_prev, from_next)

    def stiff_part(operator, mapping, mask):
        values = jnp.diagonal(operator, axis1=1, axis2=2) * mask[:, None]
        return jnp.zeros((NODES_DEV,), jnp.float32).at[mapping].add(values)

    stiff_local = jax.vmap(stiff_part)(ops_parts, map_parts, live_mask)
    diagonals = assemble(jnp.stack([stiff_local, mass_parts], axis=1))
    inverse = 1.0 / (diagonals[:, 0][:, None, :] + helmholtz[None, :, None] * diagonals[:, 1][:, None, :])

    def local_operator(fields):
        return element_apply(fields) + helmholtz[None, :, None] * mass_parts[:, None, :] * fields

    centre = (bound_high + bound_low) / 2.0
    half_width = (bound_high - bound_low) / 2.0
    ratio = centre / half_width
    previous = jnp.transpose(velocity_prev.reshape(MODES, N_DOM, NODES_DEV), (1, 0, 2))
    current = previous
    for iteration in range(ITERS):
        flat = jnp.transpose(current, (1, 0, 2)).reshape(MODES, NODES)
        physical = jnp.dot(synthesis, flat, precision=highest)
        gradient = jnp.dot(derivative, flat, precision=highest)
        cross = span_slope[:, None] * physical * gradient
        convect = jnp.dot(analysis, cross, precision=highest)
        convect = jnp.transpose(convect.reshape(MODES, N_DOM, NODES_DEV), (1, 0, 2))
        source = mass_weight * mass_parts[:, None, :] * (previous + convect)
        solution = current
        residual = inverse * assemble(source - local_operator(solution))
        direction = residual / centre
        rho_now = 1.0 / ratio
        for sweep_index in range(SWEEPS):
            solution = solution + direction
            if sweep_index < SWEEPS - 1:
                residual = residual - inverse * assemble(local_operator(direction))
                rho_next = 1.0 / (2.0 * ratio - rho_now)
                direction = rho_next * rho_now * direction + (2.0 * rho_next / half_width) * residual
                rho_now = rho_next
        current = solution
    return jnp.transpose(current, (1, 0, 2)).reshape(MODES, NODES)
```

```python
import functools

import jax
import jax.numpy as jnp
import numpy as np
from jax import lax
from jax.experimental import pallas as pl
from jax.experimental.pallas import tpu as pltpu
from jax.sharding import PartitionSpec as P

ITERS = 3
SWEEPS = 6

mass_weight = 4.0
bound_low = 0.1
bound_high = 2.0
centre = (bound_high + bound_low) / 2.0
half_width = (bound_high - bound_low) / 2.0

F32 = jnp.float32
BF16 = jnp.bfloat16
ROW = 96


def chebyshev():
    ratio = centre / half_width
    rho = 1.0 / ratio
    coefs = [(0.0, 1.0 / centre)]
    for _ in range(SWEEPS - 1):
        rho_next = 1.0 / (2.0 * ratio - rho)
        coefs.append((rho_next * rho, 2.0 * rho_next / half_width))
        rho = rho_next
    return coefs


def wave_tables(mode_count):
    column = np.arange(mode_count)
    number = np.where(column == 1, mode_count // 2, column // 2)
    is_sine = (column % 2 == 1) & (column > 1)
    planes = np.arange(mode_count)
    angles = (planes[:, None] * number[None, :] % mode_count) * (2.0 * np.pi / mode_count)
    cosine, sine = np.cos(angles), np.sin(angles)
    synthesis = np.where(is_sine[None, :], sine, cosine)
    factor = number / (mode_count // 2)
    derivative = np.where(is_sine[None, :], cosine, -sine) * factor[None, :]
    derivative = np.where(column[None, :] > 1, derivative, 0.0)
    weights = np.where(column < 2, 1.0 / mode_count, 2.0 / mode_count)
    return synthesis, derivative, synthesis.T * weights[:, None]


def halves(table):
    high = table.astype(np.float32).astype(BF16)
    low = (table - high.astype(np.float64)).astype(np.float32).astype(BF16)
    return jnp.asarray(high), jnp.asarray(low)


def split(value):
    high = value.astype(BF16)
    return high, (value - high.astype(F32)).astype(BF16)


def dot(a, b):
    return lax.dot_general(a, b, (((1,), (0,)), ((), ())), preferred_element_type=F32)


def rows_times(value, high, low):
    count = value.shape[0]
    h, l = split(value)
    both = dot(jnp.concatenate([h, l], axis=0), high)
    return both[:count] + both[count:] + dot(h, low)


def table_times(high, low, value):
    count = value.shape[1]
    h, l = split(value)
    both = dot(high, jnp.concatenate([h, l], axis=1))
    return both[:, :count] + both[:, count:] + dot(low, h)


def iota(shape, dim):
    return lax.broadcasted_iota(jnp.int32, shape, dim)


def call(kernel, outs, smem, vmem, limit, scratch=(), flops=0, moved=1 << 20):
    in_specs = [pl.BlockSpec(memory_space=pltpu.SMEM)] * len(smem)
    in_specs += [pl.BlockSpec(memory_space=pltpu.VMEM)] * len(vmem)
    return pl.pallas_call(
        kernel,
        out_shape=[jax.ShapeDtypeStruct(s, t) for s, t in outs],
        in_specs=in_specs,
        out_specs=[pl.BlockSpec(memory_space=pltpu.VMEM)] * len(outs),
        scratch_shapes=list(scratch),
        compiler_params=pltpu.CompilerParams(vmem_limit_bytes=limit << 20),
        cost_estimate=pl.CostEstimate(flops=flops, bytes_accessed=moved, transcendentals=0),
    )(*smem, *vmem)


def order_kernel(face, nodes, sc, iface, l2g, vel, mass, keep, send, chunks, place_out):
    x = sc[0]
    count = mass.shape[1]
    lists = iface[...]
    hit = (lists == iota((2 * face, count), 1)).astype(F32)
    at = jnp.sum(hit * iota((2 * face, count), 0).astype(F32), axis=0, keepdims=True)
    shared = jnp.sum(hit, axis=0, keepdims=True)
    rest = jnp.broadcast_to(1.0 - shared, (8, count))
    lane = iota((8, count), 1)
    run = rest
    step = 1
    while step < count:
        run = run + jnp.where(lane >= step, pltpu.roll(run, step, 1), 0.0)
        step *= 2
    place = jnp.where(rest > 0.5, run - 1.0 + 2.0 * face, jnp.broadcast_to(at, (8, count)))
    place_out[...] = place
    column = jnp.transpose(place)[:, 0:1]
    slots = l2g.shape[1]
    width = 512
    pieces = []
    for first in range(0, slots, width):
        row = l2g[0:1, first : first + width]
        found = jnp.where(iota((count, width), 0) == row, column, 0.0)
        index = jnp.sum(found, axis=0, keepdims=True)
        pieces.append(jnp.where(row < 0, -1.0, index))
    index = jnp.concatenate(pieces, axis=1)
    unit = jnp.where(iota((count, count), 1).astype(F32) == column, 1.0, 0.0).astype(BF16)
    value = vel[...]
    high = value.astype(BF16)
    left = value - high.astype(F32)
    middle, low = split(left)
    parts = dot(jnp.concatenate([high, middle, low], axis=0), unit)
    modes = value.shape[0]
    moved = parts[:modes] + parts[modes : 2 * modes] + parts[2 * modes :]
    mass_high = jnp.broadcast_to(mass[...], (8, count))
    mh = mass_high.astype(BF16)
    mm, ml = split(mass_high - mh.astype(F32))
    weights = dot(mh, unit) + dot(mm, unit) + dot(ml, unit)
    half = modes // 2
    a, b = moved[:half], moved[half:]
    for ref, rows in ((keep, jnp.where(x == 0, a, b)), (send, jnp.where(x == 0, b, a))):
        ref[0:half, :] = rows
        ref[half : half + 8, :] = weights
        ref[half + 8 : half + 16, :] = jnp.broadcast_to(index[:, :count], (8, count))
        ref[half + 16 : half + 24, 0 : slots - count] = jnp.broadcast_to(
            index[:, count:], (8, slots - count)
        )
        ref[half + 16 : half + 24, slots - count :] = jnp.zeros((8, 2 * count - slots), F32)
    quarter = count // chunks.shape[0]
    for part in range(chunks.shape[0]):
        chunks[part] = moved[:, part * quarter : (part + 1) * quarter]


def build_kernel(slot, half, sc, ops, pack, high, low, diag, flat, tall, qh, ql, pad):
    live = sc[slot]
    elems, side = ops.shape[0], ops.shape[1]
    count = high.shape[0]
    slots = elems * ROW
    index = jnp.concatenate(
        [pack[half + 8 : half + 16, :], pack[half + 16 : half + 24, 0 : slots - count]], axis=1
    )
    column = jnp.transpose(index)[:, 0:1]
    for first in range(0, slots, 256):
        block = jnp.where(iota((256, count), 1).astype(F32) == column[first : first + 256], 1.0, 0.0)
        tall[first : first + 256, :] = block.astype(BF16)
    tall[slots:, :] = jnp.zeros((tall.shape[0] - slots, count), BF16)
    for first in range(0, count, 256):
        block = jnp.where((iota((256, slots), 0) + first).astype(F32) == index[0:1], 1.0, 0.0)
        flat[first : first + 256, :] = block.astype(BF16)
    pad[...] = jnp.zeros(pad.shape, F32)
    for e in range(elems):
        pad[0:side, 0:side] = ops[e] * jnp.where(e < live, 1.0, 0.0)
        oh, ol = split(pad[...])
        nodes = tall[e * ROW : e * ROW + 128, :]
        qh[e * ROW : (e + 1) * ROW, :] = dot(oh, nodes).astype(BF16)
        ql[e * ROW : (e + 1) * ROW, :] = dot(ol, nodes).astype(BF16)
    tile = 256
    diag[...] = jnp.zeros(diag.shape, F32)
    for j in range(0, count, tile):

        def rows(i, carry):
            at = pl.multiple_of(i * tile, tile)
            left = flat[pl.ds(at, tile), :]
            block = dot(left, qh[:, j : j + tile]) + dot(left, ql[:, j : j + tile])
            h, l = split(block)
            high[pl.ds(at, tile), j : j + tile] = h
            low[pl.ds(at, tile), j : j + tile] = l
            own = iota((tile, tile), 0) + at == iota((tile, tile), 1) + j
            diag[:, j : j + tile] += jnp.broadcast_to(
                jnp.sum(jnp.where(own, block, 0.0), axis=0, keepdims=True), (8, tile)
            )
            return carry

        lax.fori_loop(0, count // tile, rows, 0)


def apply(value, mats, columns, half):
    oh, ol, ph, pl_ = mats
    return jnp.concatenate(
        [
            rows_times(value[:half], oh[:, columns], ol[:, columns]),
            rows_times(value[half:], ph[:, columns], pl_[:, columns]),
        ],
        axis=0,
    )


def helmholtz(first, half, mode_count):
    mode = first + iota((half, 1), 0)
    number = jnp.where(mode == 1, mode_count // 2, lax.shift_right_arithmetic(mode, 1))
    return mass_weight + (8.0 * number.astype(F32) / mode_count) ** 2


def start_kernel(half, face, mode_count, sc, own, oth, do, dp, oh, ol, ph, plo, cm_out, v_out, g_out, ma, mb):
    c = helmholtz(sc[1], half, mode_count)
    mass = [own[half : half + 1, :], oth[half : half + 1, :]]
    v = jnp.concatenate([own[0:half, :], oth[0:half, :]], axis=0)
    cm = jnp.concatenate([c * mass[0], c * mass[1]], axis=0)
    m4 = mass_weight * jnp.concatenate([jnp.broadcast_to(m, (half, m.shape[1])) for m in mass], axis=0)
    g = apply(v, (oh, ol, ph, plo), slice(None), half) + (cm - m4) * v
    cm_out[...] = cm
    v_out[...] = v
    g_out[...] = g
    for message, h, l, d, m, at in ((ma, oh, ol, do, own, 0), (mb, ph, plo, dp, oth, half)):
        message[0:face, :] = h[0:face, 0:face].astype(F32) + l[0:face, 0:face].astype(F32)
        message[face : face + 8, :] = d[:, 0:face]
        message[face + 8 : face + 16, :] = m[half : half + 8, 0:face]
        message[face + 16 :, :] = g[at : at + half, 0:face]


def assembled(y, outer, half, face):
    inner = y[:half, face : 2 * face] + y[half:, face : 2 * face]
    first = y[:, :face] if outer is None else y[:, :face] + outer
    return jnp.concatenate([first, jnp.concatenate([inner, inner], axis=0), y[:, 2 * face :]], axis=1)


def inverse_kernel(half, face, mode_count, sc, own, oth, do, dp, g, ra, rb, inv_out, cmn_out, r_out):
    c = helmholtz(sc[1], half, mode_count)
    stiff = [do[0:1, :], dp[0:1, :]]
    mass = [own[half : half + 1, :], oth[half : half + 1, :]]

    def summed(pair, row):
        inner = pair[0][:, face : 2 * face] + pair[1][:, face : 2 * face]
        return [
            jnp.concatenate([t[:, :face] + n[row : row + 1, :], inner, t[:, 2 * face :]], axis=1)
            for t, n in zip(pair, (rb, ra))
        ]

    stiff_sum, mass_sum = summed(stiff, face), summed(mass, face + 8)
    inv = jnp.concatenate([1.0 / (s + c * m) for s, m in zip(stiff_sum, mass_sum)], axis=0)
    inv_out[...] = inv
    cmn_out[...] = jnp.concatenate([c * n[face + 8 : face + 9, :] for n in (rb, ra)], axis=0)
    outer = jnp.concatenate([rb[face + 16 :, :], ra[face + 16 :, :]], axis=0)
    r_out[...] = -inv * assembled(g[...], outer, half, face)


def planes_kernel(u, wh, wl, fh, fl, slope, out):
    count = wh.shape[0] // 2
    both = table_times(wh[...], wl[...], u[...])
    cross = slope[...] * both[:count] * both[count:]
    out[...] = table_times(fh[...], fl[...], cross)


def provisional(r, d, g, inv, cm, mats, alpha, beta, half, face):
    r = r - inv * assembled(g, None, half, face)
    d = alpha * d + beta * r if alpha else beta * r
    y = apply(d, mats, slice(0, face), half) + cm[:, :face] * d[:, :face]
    return r, d, y


def put(message, g, y, at, half, face):
    message[0:half, :] = g[at : at + half, :face]
    message[half:, :] = y[at : at + half, :]


def source_kernel(half, face, sc, conv, old, own, oth, r, inv, cm, oh, ol, ph, plo, r_out, d_out, conv_out, ma, mb):
    x = sc[0]
    parts = conv.shape[0]
    new = jnp.concatenate(
        [
            jnp.concatenate([conv[m, x] for m in range(parts)], axis=1),
            jnp.concatenate([conv[m, 1 - x] for m in range(parts)], axis=1),
        ],
        axis=0,
    )
    conv_out[...] = new
    if old is not None:
        new = new - old[...]
    g = jnp.concatenate(
        [
            (-mass_weight * own[half : half + 1, :]) * new[:half],
            (-mass_weight * oth[half : half + 1, :]) * new[half:],
        ],
        axis=0,
    )
    beta = 1.0 / centre
    cmv = cm[...]
    rv, dv, y = provisional(r[...], None, g, inv[...], cmv, (oh, ol, ph, plo), 0.0, beta, half, face)
    r_out[...] = rv
    d_out[...] = dv
    put(ma, g, y, 0, half, face)
    put(mb, g, y, half, half, face)


def first_source_kernel(half, face, sc, conv, own, oth, r, inv, cm, *refs):
    source_kernel(half, face, sc, conv, None, own, oth, r, inv, cm, *refs)


def rest_kernel(half, face, d, cm, oh, ol, ph, plo, out):
    dv = d[...]
    out[...] = apply(dv, (oh, ol, ph, plo), slice(face, None), half) + cm[:, face:] * dv[:, face:]


def exact(half, face, beta, alpha_next, beta_next, r, d, y_rest, ma, mb, ra, rb, na, nb, inv, cm, cmn, mats):
    oh, ol, ph, plo = mats
    inv_face = inv[:, :face]
    forced = jnp.concatenate([rb[0:half, :], ra[0:half, :]], axis=0)
    other = jnp.concatenate([rb[half:, :], ra[half:, :]], axis=0)
    mine = jnp.concatenate([ma[0:half, :], mb[0:half, :]], axis=0)
    mine_y = jnp.concatenate([ma[half:, :], mb[half:, :]], axis=0)
    dr = -(inv_face * forced)
    dd = beta * dr
    theirs = -beta * (inv_face * mine)
    change = jnp.concatenate(
        [
            rows_times(dd[:half], oh[0:face, :], ol[0:face, :]),
            rows_times(dd[half:], ph[0:face, :], plo[0:face, :]),
        ],
        axis=0,
    )
    their_change = jnp.concatenate(
        [
            rows_times(theirs[:half], *split(nb[0:face, :])),
            rows_times(theirs[half:], *split(na[0:face, :])),
        ],
        axis=0,
    )
    y = jnp.concatenate([mine_y + cm[:, :face] * dd, y_rest], axis=1) + change
    outer = other + their_change + cmn * theirs
    r = jnp.concatenate([r[:, :face] + dr, r[:, face:]], axis=1)
    d = jnp.concatenate([d[:, :face] + dd, d[:, face:]], axis=1)
    r = r - inv * assembled(y, outer, half, face)
    return r, d, alpha_next * d + beta_next * r


def sweep_kernel(
    half, face, before, now, then,
    r, d, y_rest, sol, ma, mb, ra, rb, na, nb, inv, cm, cmn, oh, ol, ph, plo,
    r_out, d_out, sol_out, ma_out, mb_out,
):
    mats = (oh, ol, ph, plo)
    inv_v, cm_v = inv[...], cm[...]
    rv, dv, dn = exact(
        half, face, before[1], now[0], now[1], r[...], d[...], y_rest[...], ma, mb, ra, rb, na, nb,
        inv_v, cm_v, cmn[...], mats,
    )
    sol_out[...] = sol[...] + dv + dn
    g = apply(dn, mats, slice(None), half) + cm_v * dn
    rv, dv, y = provisional(rv, dn, g, inv_v, cm_v, mats, then[0], then[1], half, face)
    r_out[...] = rv
    d_out[...] = dv
    put(ma_out, g, y, 0, half, face)
    put(mb_out, g, y, half, half, face)


def last_kernel(
    half, face, before, now,
    sc, r, d, y_rest, sol, ma, mb, ra, rb, na, nb, inv, cm, cmn, oh, ol, ph, plo,
    r_out, d_out, sol_out, chunks,
):
    rv, dv, dn = exact(
        half, face, before[1], now[0], now[1], r[...], d[...], y_rest[...], ma, mb, ra, rb, na, nb,
        inv[...], cm[...], cmn[...], (oh, ol, ph, plo),
    )
    new = sol[...] + dv + dn
    r_out[...] = rv
    d_out[...] = dn
    sol_out[...] = new
    x = sc[0]
    parts, width = chunks.shape[0], chunks.shape[3]
    for m in range(parts):
        chunks[m, x] = new[:half, m * width : (m + 1) * width]
        chunks[m, 1 - x] = new[half:, m * width : (m + 1) * width]


def tail_kernel(half, face, d, cm, oh, ol, ph, plo, y_out, ma, mb):
    dv = d[...]
    y = apply(dv, (oh, ol, ph, plo), slice(None), half) + cm[...] * dv
    y_out[...] = y
    ma[...] = y[:half, :face]
    mb[...] = y[half:, :face]


def carry_kernel(half, face, r, y, inv, ra, rb, r_out):
    outer = jnp.concatenate([rb[...], ra[...]], axis=0)
    r_out[...] = r[...] - inv[...] * assembled(y[...], outer, half, face)


def finish_kernel(half, sc, own, other, place, out):
    x = sc[0]
    a, b = own[...], other[...]
    count = a.shape[1]
    value = jnp.concatenate([jnp.where(x == 0, a, b), jnp.where(x == 0, b, a)], axis=0)
    unit = jnp.where(iota((count, count), 0).astype(F32) == place[0:1, :], 1.0, 0.0).astype(BF16)
    high = value.astype(BF16)
    middle, low = split(value - high.astype(F32))
    parts = dot(jnp.concatenate([high, middle, low], axis=0), unit)
    modes = 2 * half
    out[...] = parts[:modes] + parts[modes : 2 * modes] + parts[2 * modes :]


def body(n_mode, n_dom, velocity_prev, elem_ops, lumped_mass, span_slope, local_to_global, iface_nodes, live_elems):
    modes, count = velocity_prev.shape
    half = modes // 2
    elems, side = local_to_global.shape
    face = iface_nodes.shape[2]
    mode_count = span_slope.shape[0]
    quarter = count // n_mode
    pairs = n_dom // 2
    slots = elems * ROW
    q = lax.axis_index("dom")
    x = q % 2
    swap = [(i, i ^ 1) for i in range(n_dom)]
    out_way = [(2 * z + s, 2 * ((z + (1 if s else -1)) % pairs) + s) for z in range(pairs) for s in (0, 1)]
    back_way = [(j, i) for i, j in out_way]
    groups = [[m * n_dom + 2 * z + s for m in range(n_mode) for s in (0, 1)] for z in range(pairs)]

    def to_neighbours(ma, mb):
        return lax.ppermute(ma, "dom", out_way), lax.ppermute(mb, "dom", back_way)

    first_mode = lax.axis_index("mode") * modes + x * half
    live = lax.dynamic_slice_in_dim(live_elems, q, 1)
    live_other = lax.dynamic_slice_in_dim(live_elems, q ^ 1, 1)
    sc = jnp.concatenate([jnp.stack([x, first_mode]).astype(jnp.int32), live, live_other])

    ops_other = lax.ppermute(elem_ops, "dom", swap)
    lists = jnp.where(x == 0, iface_nodes[0], iface_nodes[0, ::-1]).reshape(2 * face, 1)
    l2g = jnp.pad(local_to_global, ((0, 0), (0, ROW - side)), constant_values=-1).reshape(1, slots)
    pack = (half + 24, count)
    wide = (2 * half, count)
    keep, send, chunks, place = call(
        functools.partial(order_kernel, face, None),
        [(pack, F32), (pack, F32), ((n_mode, modes, quarter), F32), ((8, count), F32)],
        [sc], [lists, l2g, velocity_prev, lumped_mass.reshape(1, count)], 40,
    )
    planes_in = lax.all_to_all(chunks, "mode", 0, 0, tiled=True)
    oth = lax.ppermute(send, "dom", swap)

    def build(slot, ops, packed):
        return call(
            functools.partial(build_kernel, slot, half),
            [((count, count), BF16), ((count, count), BF16), ((8, count), F32)],
            [sc], [ops, packed], 40,
            scratch=[
                pltpu.VMEM((count, slots), BF16),
                pltpu.VMEM((slots + 32, count), BF16),
                pltpu.VMEM((slots, count), BF16),
                pltpu.VMEM((slots, count), BF16),
                pltpu.VMEM((ROW, 128), F32),
            ],
            flops=6 << 30,
        )

    oh, ol, do = build(2, elem_ops, keep)
    synthesis, derivative, analysis = wave_tables(mode_count)
    tables = (*halves(np.concatenate([synthesis, derivative])), *halves(analysis))
    slope = span_slope.reshape(mode_count, 1)

    def convect(value):
        (out,) = call(
            planes_kernel, [((mode_count, quarter), F32)], [],
            [value.reshape(mode_count, quarter), *tables, slope], 24, flops=600 << 20,
        )
        got = lax.all_to_all(
            out.reshape(2 * n_mode, half, quarter), ("mode", "dom"), 0, 0, axis_index_groups=groups, tiled=True
        )
        return got.reshape(n_mode, 2, half, quarter)

    conv = convect(planes_in)
    ph, plo, dp = build(3, ops_other, oth)
    mats = [oh, ol, ph, plo]
    note = (face + 16 + half, face)
    cm, sol, g, na, nb = call(
        functools.partial(start_kernel, half, face, mode_count),
        [(wide, F32), (wide, F32), (wide, F32), (note, F32), (note, F32)],
        [sc], [keep, oth, do, dp, *mats], 32, flops=400 << 20,
    )
    na, nb = to_neighbours(na, nb)
    inv, cmn, r = call(
        functools.partial(inverse_kernel, half, face, mode_count),
        [(wide, F32), ((2 * half, face), F32), (wide, F32)],
        [sc], [keep, oth, do, dp, g, na, nb], 16,
    )
    coefs = chebyshev()
    message = (2 * half, face)
    exchange_outs = [(message, F32), (message, F32)]
    old = None
    for iteration in range(ITERS):
        if old is None:
            kernel, given = first_source_kernel, [conv]
        else:
            kernel, given = source_kernel, [conv, old]
        r, d, old, ma, mb = call(
            functools.partial(kernel, half, face),
            [(wide, F32), (wide, F32), (wide, F32), *exchange_outs],
            [sc], [*given, keep, oth, r, inv, cm, *mats], 32, flops=50 << 20,
        )
        for k in (0, 2, 4):
            ra, rb = to_neighbours(ma, mb)
            (rest,) = call(
                functools.partial(rest_kernel, half, face), [((2 * half, count - face), F32)],
                [], [d, cm, *mats], 32, flops=400 << 20,
            )
            given = [r, d, rest, sol, ma, mb, ra, rb, na, nb, inv, cm, cmn, *mats]
            if k < 4:
                r, d, sol, ma, mb = call(
                    functools.partial(sweep_kernel, half, face, coefs[k], coefs[k + 1], coefs[k + 2]),
                    [(wide, F32), (wide, F32), (wide, F32), *exchange_outs], [], given, 32, flops=500 << 20,
                )
            else:
                r, d, sol, chunks = call(
                    functools.partial(last_kernel, half, face, coefs[k], coefs[k + 1]),
                    [(wide, F32), (wide, F32), (wide, F32), ((n_mode, 2, half, quarter), F32)],
                    [sc], given, 32, flops=100 << 20,
                )
        if iteration == ITERS - 1:
            break
        planes_in = lax.all_to_all(
            chunks.reshape(2 * n_mode, half, quarter), ("mode", "dom"), 0, 0, axis_index_groups=groups, tiled=True
        )
        y, ma, mb = call(
            functools.partial(tail_kernel, half, face),
            [(wide, F32), ((half, face), F32), ((half, face), F32)], [], [d, cm, *mats], 32, flops=400 << 20,
        )
        ra, rb = to_neighbours(ma, mb)
        conv = convect(planes_in)
        (r,) = call(functools.partial(carry_kernel, half, face), [(wide, F32)], [], [r, y, inv, ra, rb], 16)
    other = lax.ppermute(sol[half:], "dom", swap)
    (out,) = call(
        functools.partial(finish_kernel, half), [((modes, count), F32)], [sc], [sol[:half], other, place], 16
    )
    return out


def solution(mesh):
    placed = (
        P("mode", "dom"),
        P("dom", None, None),
        P("dom"),
        P(),
        P("dom", None),
        P("dom", None, None),
        P(),
    )
    return jax.shard_map(
        functools.partial(body, mesh.shape["mode"], mesh.shape["dom"]),
        mesh=mesh, in_specs=placed, out_specs=P("mode", "dom"), check_vma=False,
    )
```

```python
import functools

import jax
import jax.numpy as jnp
import numpy as np
from jax import lax
from jax.experimental import pallas as pl
from jax.experimental.pallas import tpu as pltpu
from jax.sharding import PartitionSpec as P

ITERS = 3
SWEEPS = 6

mass_weight = 4.0
bound_low = 0.1
bound_high = 2.0
centre = (bound_high + bound_low) / 2.0
half_width = (bound_high - bound_low) / 2.0

F32 = jnp.float32
BF16 = jnp.bfloat16
ROW = 96


def chebyshev():
    ratio = centre / half_width
    rho = 1.0 / ratio
    coefs = [(0.0, 1.0 / centre)]
    for _ in range(SWEEPS - 1):
        rho_next = 1.0 / (2.0 * ratio - rho)
        coefs.append((rho_next * rho, 2.0 * rho_next / half_width))
        rho = rho_next
    return coefs


def wave_tables(mode_count):
    column = np.arange(mode_count)
    number = np.where(column == 1, mode_count // 2, column // 2)
    is_sine = (column % 2 == 1) & (column > 1)
    planes = np.arange(mode_count)
    angles = (planes[:, None] * number[None, :] % mode_count) * (2.0 * np.pi / mode_count)
    cosine, sine = np.cos(angles), np.sin(angles)
    synthesis = np.where(is_sine[None, :], sine, cosine)
    factor = number / (mode_count // 2)
    derivative = np.where(is_sine[None, :], cosine, -sine) * factor[None, :]
    derivative = np.where(column[None, :] > 1, derivative, 0.0)
    weights = np.where(column < 2, 1.0 / mode_count, 2.0 / mode_count)
    return synthesis, derivative, synthesis.T * weights[:, None]


def halves(table):
    high = table.astype(np.float32).astype(BF16)
    return [high, (table - high.astype(np.float64)).astype(np.float32).astype(BF16)]


def split(value):
    high = value.astype(BF16)
    return high, (value - high.astype(F32)).astype(BF16)


def dot(a, b):
    return lax.dot_general(a, b, (((1,), (0,)), ((), ())), preferred_element_type=F32)


def rows_times(value, high, low):
    count = value.shape[0]
    h, l = split(value)
    both = dot(jnp.concatenate([h, l], axis=0), high)
    return both[:count] + both[count:] + dot(h, low)


def table_times(high, low, value):
    count = value.shape[1]
    h, l = split(value)
    both = dot(high, jnp.concatenate([h, l], axis=1))
    return both[:, :count] + both[:, count:] + dot(low, h)


def iota(shape, dim):
    return lax.broadcasted_iota(jnp.int32, shape, dim)


def call(kernel, outs, smem, vmem, limit, scratch=(), flops=0, moved=1 << 20):
    in_specs = [pl.BlockSpec(memory_space=pltpu.SMEM)] * len(smem)
    in_specs += [pl.BlockSpec(memory_space=pltpu.VMEM)] * len(vmem)
    return pl.pallas_call(
        kernel,
        out_shape=[jax.ShapeDtypeStruct(s, t) for s, t in outs],
        in_specs=in_specs,
        out_specs=[pl.BlockSpec(memory_space=pltpu.VMEM)] * len(outs),
        scratch_shapes=list(scratch),
        compiler_params=pltpu.CompilerParams(vmem_limit_bytes=limit << 20),
        cost_estimate=pl.CostEstimate(flops=flops, bytes_accessed=moved, transcendentals=0),
    )(*smem, *vmem)


def position():
    q = lax.axis_index("dom")
    z = lax.shift_right_arithmetic(q, 1)
    return q, z, q - 2 * z


def picked(first, a, b):
    return jnp.where(first, a, b)


def order_kernel(iface, l2g, vel, mass, keep, send, chunks, place_out):
    _, _, x = position()
    count = mass.shape[1]
    face = iface.shape[1]
    lists = jnp.concatenate(
        [picked(x == 0, iface[0:1, :], iface[1:2, :]), picked(x == 0, iface[1:2, :], iface[0:1, :])], axis=1
    ).astype(F32)
    lists = jnp.transpose(jnp.broadcast_to(lists, (8, 2 * face)))[:, 0:1]
    hit = jnp.where(lists == iota((2 * face, count), 1).astype(F32), 1.0, 0.0)
    at = jnp.sum(hit * iota((2 * face, count), 0).astype(F32), axis=0, keepdims=True)
    shared = jnp.sum(hit, axis=0, keepdims=True)
    rest = jnp.broadcast_to(1.0 - shared, (8, count))
    lane = iota((8, count), 1)
    run = rest
    step = 1
    while step < count:
        run = run + jnp.where(lane >= step, pltpu.roll(run, step, 1), 0.0)
        step *= 2
    place = jnp.where(rest > 0.5, run - 1.0 + 2.0 * face, jnp.broadcast_to(at, (8, count)))
    place_out[...] = place
    column = jnp.transpose(place)[:, 0:1]
    elems, side = l2g.shape
    slots = elems * ROW
    blank = jnp.full((1, ROW - side), -1, jnp.int32)
    row = jnp.concatenate([piece for e in range(elems) for piece in (l2g[e : e + 1, :], blank)], axis=1)
    pieces = []
    for first in range(0, slots, 512):
        part = row[:, first : first + 512]
        found = jnp.where(iota((count, 512), 0) == part, column, 0.0)
        pieces.append(jnp.where(part < 0, -1.0, jnp.sum(found, axis=0, keepdims=True)))
    index = jnp.concatenate(pieces, axis=1)
    unit = jnp.where(iota((count, count), 1).astype(F32) == column, 1.0, 0.0).astype(BF16)
    modes = vel.shape[0]
    half = modes // 2
    value = jnp.concatenate([vel[...], jnp.broadcast_to(mass[...], (16, count))], axis=0)
    high = value.astype(BF16)
    middle, low = split(value - high.astype(F32))
    total = modes + 16
    parts = dot(jnp.concatenate([high, middle, low], axis=0), unit)
    moved = parts[:total] + parts[total : 2 * total] + parts[2 * total :]
    a, b = moved[:half], moved[half:modes]
    for ref, rows in ((keep, picked(x == 0, a, b)), (send, picked(x == 0, b, a))):
        ref[0:half, :] = rows
        ref[half : half + 8, :] = moved[modes : modes + 8]
        ref[half + 8 : half + 16, :] = jnp.broadcast_to(index[:, :count], (8, count))
        ref[half + 16 : half + 24, 0 : slots - count] = jnp.broadcast_to(
            index[:, count:], (8, slots - count)
        )
        ref[half + 16 : half + 24, slots - count :] = jnp.zeros((8, 2 * count - slots), F32)
    quarter = count // chunks.shape[0]
    for part in range(chunks.shape[0]):
        chunks[part] = moved[:modes, part * quarter : (part + 1) * quarter]


def build_kernel(own, half, live_elems, ops, pack, high, low, diag, note, flat, tall, qh, ql, pad):
    q, z, x = position()
    live = live_elems[q if own else 2 * z + 1 - x]
    side, elems = ops.shape[0], ops.shape[1]
    count = high.shape[0]
    slots = elems * ROW
    index = jnp.concatenate(
        [pack[half + 8 : half + 16, :], pack[half + 16 : half + 24, 0 : slots - count]], axis=1
    )
    column = jnp.transpose(index)[:, 0:1]
    for first in range(0, slots, 256):
        block = jnp.where(iota((256, count), 1).astype(F32) == column[first : first + 256], 1.0, 0.0)
        tall[first : first + 256, :] = block.astype(BF16)
    tall[slots:, :] = jnp.zeros((tall.shape[0] - slots, count), BF16)
    for first in range(0, count, 256):
        block = jnp.where((iota((256, slots), 0) + first).astype(F32) == index[0:1], 1.0, 0.0)
        flat[first : first + 256, :] = block.astype(BF16)
    pad[...] = jnp.zeros(pad.shape, F32)
    for e in range(elems):
        pad[0:side, 0:side] = ops[:, e, :] * jnp.where(e < live, 1.0, 0.0)
        oh, ol = split(pad[...])
        spread = dot(jnp.concatenate([oh, ol], axis=0), tall[e * ROW : e * ROW + 128, :])
        qh[e * ROW : (e + 1) * ROW, :] = spread[:ROW].astype(BF16)
        ql[e * ROW : (e + 1) * ROW, :] = spread[ROW:].astype(BF16)
    tile = 256
    for j in range(0, count, tile):
        top = j + tile
        block = dot(flat[0:top, :], qh[:, j:top]) + dot(flat[0:top, :], ql[:, j:top])
        h, l = split(block)
        high[0:top, j:top] = h
        low[0:top, j:top] = l
        if j:
            mirror = jnp.transpose(block[:j])
            h, l = split(mirror)
            high[j:top, 0:j] = h
            low[j:top, 0:j] = l
        own_node = iota((tile, tile), 0) == iota((tile, tile), 1)
        line = jnp.sum(jnp.where(own_node, block[j:top], 0.0), axis=0, keepdims=True)
        diag[:, j:top] = jnp.broadcast_to(line, (8, tile))
        if note is not None and not j:
            face = note.shape[1]
            note[0:face, :] = block[0:face, 0:face]
            note[face : face + 8, :] = jnp.broadcast_to(line[:, 0:face], (8, face))
            note[face + 8 :, :] = pack[half : half + 8, 0:face]


def partner_build_kernel(half, live_elems, ops, pack, high, low, diag, *scratch):
    build_kernel(False, half, live_elems, ops, pack, high, low, diag, None, *scratch)


def apply(value, mats, columns, half):
    oh, ol, ph, plo = mats
    return jnp.concatenate(
        [
            rows_times(value[:half], oh[:, columns], ol[:, columns]),
            rows_times(value[half:], ph[:, columns], plo[:, columns]),
        ],
        axis=0,
    )


def assembled(y, outer, half, face):
    inner = y[:half, face : 2 * face] + y[half:, face : 2 * face]
    first = y[:, :face] if outer is None else y[:, :face] + outer
    return jnp.concatenate([first, jnp.concatenate([inner, inner], axis=0), y[:, 2 * face :]], axis=1)


def planes_kernel(u, tables, slope, out):
    count = slope.shape[1]
    both = table_times(tables[0 : 2 * count, :], tables[2 * count : 4 * count, :], u[...])
    rate = jnp.transpose(jnp.broadcast_to(slope[...], (8, count)))[:, 0:1]
    cross = rate * both[:count] * both[count:]
    out[...] = table_times(tables[4 * count : 5 * count, :], tables[5 * count :, :], cross)


def provisional(r, d, g, inv, cm, mats, alpha, beta, half, face):
    r = r - inv * assembled(g, None, half, face)
    d = alpha * d + beta * r if alpha else beta * r
    y = apply(d, mats, slice(0, face), half) + cm[:, :face] * d[:, :face]
    return r, d, y


def even():
    _, z, x = position()
    return lax.rem(x + z, 2) == 0


def put(one, two, g, y, half, face):
    own = jnp.concatenate([g[:half, :face], y[:half]], axis=0)
    oth = jnp.concatenate([g[half:, :face], y[half:]], axis=0)
    first = even()
    one[...] = picked(first, own, oth)
    two[...] = picked(first, oth, own)


def got(one, two):
    a, b = one[...], two[...]
    first = even()
    return picked(first, a, b), picked(first, b, a)


def received(conv, half):
    _, _, x = position()
    parts = conv.shape[0]
    return jnp.concatenate(
        [
            jnp.concatenate([conv[m, x] for m in range(parts)], axis=1),
            jnp.concatenate([conv[m, 1 - x] for m in range(parts)], axis=1),
        ],
        axis=0,
    )


def masses(own, oth, half):
    count = own.shape[1]
    return jnp.concatenate(
        [jnp.broadcast_to(m[half : half + 1, :], (half, count)) for m in (own, oth)], axis=0
    )


def helmholtz(half, mode_count):
    _, _, x = position()
    mode = lax.axis_index("mode") * (2 * half) + x * half + iota((half, 1), 0)
    number = jnp.where(mode == 1, mode_count // 2, lax.shift_right_arithmetic(mode, 1))
    return mass_weight + (8.0 * number.astype(F32) / mode_count) ** 2


def first_source_kernel(
    half, face, mode_count, conv, own, oth, do, dp, na, nb, oh, ol, ph, plo,
    r_out, d_out, v_out, conv_out, inv_out, cm_out, cmn_out, one, two,
):
    mats = (oh, ol, ph, plo)
    c = helmholtz(half, mode_count)
    c = jnp.concatenate([c, c], axis=0)
    mass = masses(own, oth, half)
    stiff = jnp.concatenate([jnp.broadcast_to(t[0:1, :], (half, t.shape[1])) for t in (do, dp)], axis=0)

    def theirs(row):
        return jnp.concatenate(
            [jnp.broadcast_to(n[row : row + 1, :], (half, face)) for n in (nb, na)], axis=0
        )

    their_mass = theirs(face + 8)
    cmn_out[...] = c * their_mass
    stiff = assembled(stiff, theirs(face), half, face)
    inv = 1.0 / (stiff + c * assembled(mass, their_mass, half, face))
    inv_out[...] = inv
    cm = c * mass
    cm_out[...] = cm
    v = jnp.concatenate([own[0:half, :], oth[0:half, :]], axis=0)
    v_out[...] = v
    new = received(conv, half)
    conv_out[...] = new
    m4 = mass_weight * mass
    g = apply(v, mats, slice(None), half) + (cm - m4) * v - m4 * new
    r, d, y = provisional(0.0, None, g, inv, cm, mats, 0.0, 1.0 / centre, half, face)
    r_out[...] = r
    d_out[...] = d
    put(one, two, g, y, half, face)


def source_kernel(half, face, conv, old, own, oth, r, d, inv, cm, oh, ol, ph, plo, r_out, d_out, conv_out, one, two):
    mats = (oh, ol, ph, plo)
    new = received(conv, half)
    conv_out[...] = new
    cmv, dv = cm[...], d[...]
    g = apply(dv, mats, slice(None), half) + cmv * dv - mass_weight * masses(own, oth, half) * (new - old[...])
    rv, dv, y = provisional(r[...], None, g, inv[...], cmv, mats, 0.0, 1.0 / centre, half, face)
    r_out[...] = rv
    d_out[...] = dv
    put(one, two, g, y, half, face)


def rest_kernel(half, face, d, cm, oh, ol, ph, plo, out):
    dv = d[...]
    out[...] = apply(dv, (oh, ol, ph, plo), slice(face, None), half) + cm[:, face:] * dv[:, face:]


def exact(half, face, beta, alpha_next, beta_next, r, d, y_rest, sent, came, na, nb, inv, cm, cmn, mats):
    oh, ol, ph, plo = mats
    inv_face = inv[:, :face]
    mo, mp = got(*sent)
    fo, fp = got(*came)
    forced = jnp.concatenate([fo[0:half, :], fp[0:half, :]], axis=0)
    other = jnp.concatenate([fo[half:, :], fp[half:, :]], axis=0)
    mine = jnp.concatenate([mo[0:half, :], mp[0:half, :]], axis=0)
    mine_y = jnp.concatenate([mo[half:, :], mp[half:, :]], axis=0)
    dr = -(inv_face * forced)
    dd = beta * dr
    theirs = -beta * (inv_face * mine)
    change = jnp.concatenate(
        [
            rows_times(dd[:half], oh[0:face, :], ol[0:face, :]),
            rows_times(dd[half:], ph[0:face, :], plo[0:face, :]),
        ],
        axis=0,
    )
    their_change = jnp.concatenate(
        [
            rows_times(theirs[:half], *split(nb[0:face, :])),
            rows_times(theirs[half:], *split(na[0:face, :])),
        ],
        axis=0,
    )
    y = jnp.concatenate([mine_y + cm[:, :face] * dd, y_rest], axis=1) + change
    outer = other + their_change + cmn * theirs
    r = jnp.concatenate([r[:, :face] + dr, r[:, face:]], axis=1)
    d = jnp.concatenate([d[:, :face] + dd, d[:, face:]], axis=1)
    r = r - inv * assembled(y, outer, half, face)
    return r, d, alpha_next * d + beta_next * r


def sweep_kernel(
    half, face, before, now, then,
    r, d, y_rest, sol, s1, s2, c1, c2, na, nb, inv, cm, cmn, oh, ol, ph, plo,
    r_out, d_out, sol_out, one, two,
):
    mats = (oh, ol, ph, plo)
    inv_v, cm_v = inv[...], cm[...]
    rv, dv, dn = exact(
        half, face, before[1], now[0], now[1], r[...], d[...], y_rest[...], (s1, s2), (c1, c2), na, nb,
        inv_v, cm_v, cmn[...], mats,
    )
    sol_out[...] = sol[...] + dv + dn
    g = apply(dn, mats, slice(None), half) + cm_v * dn
    rv, dv, y = provisional(rv, dn, g, inv_v, cm_v, mats, then[0], then[1], half, face)
    r_out[...] = rv
    d_out[...] = dv
    put(one, two, g, y, half, face)


def last_kernel(
    half, face, before, now,
    r, d, y_rest, sol, s1, s2, c1, c2, na, nb, inv, cm, cmn, oh, ol, ph, plo,
    r_out, d_out, sol_out, chunks,
):
    rv, dv, dn = exact(
        half, face, before[1], now[0], now[1], r[...], d[...], y_rest[...], (s1, s2), (c1, c2), na, nb,
        inv[...], cm[...], cmn[...], (oh, ol, ph, plo),
    )
    new = sol[...] + dv + dn
    r_out[...] = rv
    d_out[...] = dn
    sol_out[...] = new
    _, _, x = position()
    parts, width = chunks.shape[0], chunks.shape[3]
    for m in range(parts):
        chunks[m, x] = new[:half, m * width : (m + 1) * width]
        chunks[m, 1 - x] = new[half:, m * width : (m + 1) * width]


def end_kernel(
    half, face, before, now,
    r, d, y_rest, sol, s1, s2, c1, c2, na, nb, inv, cm, cmn, oh, ol, ph, plo, own_out, oth_out,
):
    _, dv, dn = exact(
        half, face, before[1], now[0], now[1], r[...], d[...], y_rest[...], (s1, s2), (c1, c2), na, nb,
        inv[...], cm[...], cmn[...], (oh, ol, ph, plo),
    )
    new = sol[...] + dv + dn
    own_out[...] = new[:half]
    oth_out[...] = new[half:]


def restored(value, unit):
    count = value.shape[0]
    high = value.astype(BF16)
    middle, low = split(value - high.astype(F32))
    parts = dot(jnp.concatenate([high, middle, low], axis=0), unit)
    return parts[:count] + parts[count : 2 * count] + parts[2 * count :]


def finish_own_kernel(own, place, out, unit_out):
    count = own.shape[1]
    unit = jnp.where(iota((count, count), 0).astype(F32) == place[0:1, :], 1.0, 0.0).astype(BF16)
    unit_out[...] = unit
    out[...] = restored(own[...], unit)


def finish_kernel(own, other, unit, out):
    _, _, x = position()
    a, b = own[...], restored(other[...], unit[...])
    half = own.shape[0]
    out[0:half, :] = picked(x == 0, a, b)
    out[half:, :] = picked(x == 0, b, a)


def body(n_mode, n_dom, velocity_prev, elem_ops, lumped_mass, span_slope, local_to_global, iface_nodes, live_elems):
    modes, count = velocity_prev.shape
    half = modes // 2
    elems, side = local_to_global.shape
    face = iface_nodes.shape[2]
    mode_count = span_slope.shape[0]
    quarter = count // n_mode
    pairs = n_dom // 2
    slots = elems * ROW
    places = [(z, s) for z in range(pairs) for s in (0, 1)]
    swap = [(i, i ^ 1) for i in range(n_dom)]
    long_swap = [(2 * z + s, 2 * ((z + (1 if z % 2 else -1)) % pairs) + s) for z, s in places]
    short_swap = [(2 * z + s, 2 * ((z + (-1 if z % 2 else 1)) % pairs) + s) for z, s in places]
    straight = [(2 * z + s, 2 * ((z + (1 if s else -1)) % pairs) + s) for z, s in places]
    across = [(2 * z + s, 2 * ((z + (1 if s else -1)) % pairs) + 1 - s) for z, s in places]
    groups = [[m * n_dom + 2 * z + s for m in range(n_mode) for s in (0, 1)] for z in range(pairs)]

    def exchange(one, two):
        return lax.ppermute(one, "dom", long_swap), lax.ppermute(two, "dom", short_swap)

    ops = jnp.transpose(elem_ops, (1, 0, 2))
    ops_other = lax.ppermute(ops, "dom", swap)
    pack = (half + 24, count)
    wide = (2 * half, count)
    keep, send, chunks, place = call(
        order_kernel,
        [(pack, F32), (pack, F32), ((n_mode, modes, quarter), F32), ((8, count), F32)],
        [], [iface_nodes[0], local_to_global, velocity_prev, lumped_mass.reshape(1, count)], 24,
    )
    planes_in = lax.all_to_all(chunks, "mode", 0, 0, tiled=True)
    oth = lax.ppermute(send, "dom", swap)

    def build(own, ops, packed):
        matrix = ((count, count), BF16)
        note = [((face + 16, face), F32)] if own else []
        return call(
            functools.partial(build_kernel, True, half) if own else functools.partial(partner_build_kernel, half),
            [matrix, matrix, ((8, count), F32), *note],
            [live_elems], [ops, packed], 40,
            scratch=[
                pltpu.VMEM((count, slots), BF16),
                pltpu.VMEM((slots + 32, count), BF16),
                pltpu.VMEM((slots, count), BF16),
                pltpu.VMEM((slots, count), BF16),
                pltpu.VMEM((ROW, 128), F32),
            ],
            flops=6 << 30,
        )

    oh, ol, do, note = build(True, ops, keep)
    na = lax.ppermute(note, "dom", straight)
    nb = lax.ppermute(note, "dom", across)
    synthesis, derivative, analysis = wave_tables(mode_count)
    tables = jnp.asarray(np.concatenate(halves(np.concatenate([synthesis, derivative])) + halves(analysis)))
    slope = span_slope.reshape(1, mode_count)

    def convect(value):
        (out,) = call(
            planes_kernel, [((mode_count, quarter), F32)], [],
            [value.reshape(mode_count, quarter), tables, slope], 16, flops=600 << 20,
        )
        back = lax.all_to_all(
            out.reshape(2 * n_mode, half, quarter), ("mode", "dom"), 0, 0, axis_index_groups=groups, tiled=True
        )
        return back.reshape(n_mode, 2, half, quarter)

    conv = convect(planes_in)
    ph, plo, dp = build(False, ops_other, oth)
    mats = [oh, ol, ph, plo]
    coefs = chebyshev()
    message = ((2 * half, face), F32)
    for iteration in range(ITERS):
        if iteration == 0:
            r, d, sol, old, inv, cm, cmn, one, two = call(
                functools.partial(first_source_kernel, half, face, mode_count),
                [(wide, F32)] * 6 + [((2 * half, face), F32), message, message],
                [], [conv, keep, oth, do, dp, na, nb, *mats], 20, flops=500 << 20,
            )
        else:
            r, d, old, one, two = call(
                functools.partial(source_kernel, half, face),
                [(wide, F32), (wide, F32), (wide, F32), message, message],
                [], [conv, old, keep, oth, r, d, inv, cm, *mats], 20, flops=500 << 20,
            )
        for k in (0, 2, 4):
            c1, c2 = exchange(one, two)
            (rest,) = call(
                functools.partial(rest_kernel, half, face), [((2 * half, count - face), F32)],
                [], [d, cm, *mats], 20, flops=400 << 20,
            )
            given = [r, d, rest, sol, one, two, c1, c2, na, nb, inv, cm, cmn, *mats]
            if k < 4:
                r, d, sol, one, two = call(
                    functools.partial(sweep_kernel, half, face, coefs[k], coefs[k + 1], coefs[k + 2]),
                    [(wide, F32), (wide, F32), (wide, F32), message, message], [], given, 20, flops=500 << 20,
                )
            elif iteration < ITERS - 1:
                r, d, sol, chunks = call(
                    functools.partial(last_kernel, half, face, coefs[k], coefs[k + 1]),
                    [(wide, F32), (wide, F32), (wide, F32), ((n_mode, 2, half, quarter), F32)],
                    [], given, 20, flops=100 << 20,
                )
            else:
                own, other = call(
                    functools.partial(end_kernel, half, face, coefs[k], coefs[k + 1]),
                    [((half, count), F32)] * 2, [], given, 20, flops=100 << 20,
                )
        if iteration < ITERS - 1:
            planes_in = lax.all_to_all(
                chunks.reshape(2 * n_mode, half, quarter), ("mode", "dom"), 0, 0, axis_index_groups=groups, tiled=True
            )
            conv = convect(planes_in)
    other = lax.ppermute(other, "dom", swap)
    own, unit = call(
        finish_own_kernel, [((half, count), F32), ((count, count), BF16)], [], [own, place], 16, flops=200 << 20
    )
    (out,) = call(finish_kernel, [((modes, count), F32)], [], [own, other, unit], 16)
    return out


def solution(mesh):
    placed = (
        P("mode", "dom"),
        P("dom", None, None),
        P("dom"),
        P(),
        P("dom", None),
        P("dom", None, None),
        P(),
    )
    return jax.shard_map(
        functools.partial(body, mesh.shape["mode"], mesh.shape["dom"]),
        mesh=mesh, in_specs=placed, out_specs=P("mode", "dom"), check_vma=False,
    )
```

```python
import functools

import jax
import jax.numpy as jnp
import numpy as np
from jax import lax
from jax.experimental import pallas as pl
from jax.experimental.pallas import tpu as pltpu
from jax.sharding import PartitionSpec as P

ITERS = 3
SWEEPS = 6

mass_weight = 4.0
bound_low = 0.1
bound_high = 2.0
centre = (bound_high + bound_low) / 2.0
half_width = (bound_high - bound_low) / 2.0

F32 = jnp.float32
BF16 = jnp.bfloat16
ROW = 96


def chebyshev():
    ratio = centre / half_width
    rho = 1.0 / ratio
    coefs = [(0.0, 1.0 / centre)]
    for _ in range(SWEEPS - 1):
        rho_next = 1.0 / (2.0 * ratio - rho)
        coefs.append((rho_next * rho, 2.0 * rho_next / half_width))
        rho = rho_next
    return coefs


def wave_tables(mode_count):
    column = np.arange(mode_count)
    number = np.where(column == 1, mode_count // 2, column // 2)
    is_sine = (column % 2 == 1) & (column > 1)
    planes = np.arange(mode_count)
    angles = (planes[:, None] * number[None, :] % mode_count) * (2.0 * np.pi / mode_count)
    cosine, sine = np.cos(angles), np.sin(angles)
    synthesis = np.where(is_sine[None, :], sine, cosine)
    factor = number / (mode_count // 2)
    derivative = np.where(is_sine[None, :], cosine, -sine) * factor[None, :]
    derivative = np.where(column[None, :] > 1, derivative, 0.0)
    weights = np.where(column < 2, 1.0 / mode_count, 2.0 / mode_count)
    return synthesis, derivative, synthesis.T * weights[:, None]


def halves(table):
    high = table.astype(np.float32).astype(BF16)
    return [high, (table - high.astype(np.float64)).astype(np.float32).astype(BF16)]


def split(value):
    high = value.astype(BF16)
    return high, (value - high.astype(F32)).astype(BF16)


def dot(a, b):
    return lax.dot_general(a, b, (((1,), (0,)), ((), ())), preferred_element_type=F32)


def rows_times(value, high, low):
    count = value.shape[0]
    h, l = split(value)
    both = dot(jnp.concatenate([h, l], axis=0), high)
    return both[:count] + both[count:] + dot(h, low)


def table_times(high, low, value):
    count = value.shape[1]
    h, l = split(value)
    both = dot(high, jnp.concatenate([h, l], axis=1))
    return both[:, :count] + both[:, count:] + dot(low, h)


def iota(shape, dim):
    return lax.broadcasted_iota(jnp.int32, shape, dim)


def call(kernel, outs, smem, vmem, limit, scratch=(), flops=0, moved=1 << 20, keep=0, place=pltpu.VMEM):
    in_specs = [pl.BlockSpec(memory_space=pltpu.SMEM)] * len(smem)
    in_specs += [pl.BlockSpec(memory_space=place)] * len(vmem)
    vmem = [
        pltpu.with_memory_space_constraint(v, place)
        if place is not pltpu.VMEM or v.dtype == BF16 and v.shape[0] == v.shape[1]
        else v
        for v in vmem
    ]
    return pl.pallas_call(
        kernel,
        out_shape=[pltpu.VMEM(s, t) if i < keep else jax.ShapeDtypeStruct(s, t) for i, (s, t) in enumerate(outs)],
        in_specs=in_specs,
        out_specs=[pl.BlockSpec(memory_space=pltpu.VMEM)] * len(outs),
        scratch_shapes=list(scratch),
        compiler_params=pltpu.CompilerParams(vmem_limit_bytes=limit << 20),
        cost_estimate=pl.CostEstimate(flops=flops, bytes_accessed=moved, transcendentals=0),
    )(*smem, *vmem)


def position():
    q = lax.axis_index("dom")
    z = lax.shift_right_arithmetic(q, 1)
    return q, z, q - 2 * z


def picked(first, a, b):
    return jnp.where(first, a, b)


def order_kernel(iface_in, l2g_in, vel_in, mass_in, keep, send, chunks, place_out, iface, l2g, vel, mass, sems):
    _, _, x = position()
    pairs = ((iface_in, iface), (l2g_in, l2g), (vel_in, vel), (mass_in, mass))
    copies = [pltpu.make_async_copy(a, b, sems.at[i]) for i, (a, b) in enumerate(pairs)]
    for copy in copies:
        copy.start()
    for copy in copies:
        copy.wait()
    count = mass.shape[1]
    face = iface.shape[1]
    lists = jnp.concatenate(
        [picked(x == 0, iface[0:1, :], iface[1:2, :]), picked(x == 0, iface[1:2, :], iface[0:1, :])], axis=1
    ).astype(F32)
    lists = jnp.transpose(jnp.broadcast_to(lists, (8, 2 * face)))[:, 0:1]
    hit = jnp.where(lists == iota((2 * face, count), 1).astype(F32), 1.0, 0.0)
    at = jnp.sum(hit * iota((2 * face, count), 0).astype(F32), axis=0, keepdims=True)
    shared = jnp.sum(hit, axis=0, keepdims=True)
    rest = jnp.broadcast_to(1.0 - shared, (8, count))
    lane = iota((8, count), 1)
    run = rest
    step = 1
    while step < count:
        run = run + jnp.where(lane >= step, pltpu.roll(run, step, 1), 0.0)
        step *= 2
    place = jnp.where(rest > 0.5, run - 1.0 + 2.0 * face, jnp.broadcast_to(at, (8, count)))
    place_out[...] = place
    column = jnp.transpose(place)[:, 0:1]
    elems, side = l2g.shape
    slots = elems * ROW
    blank = jnp.full((1, ROW - side), -1, jnp.int32)
    row = jnp.concatenate([piece for e in range(elems) for piece in (l2g[e : e + 1, :], blank)], axis=1)
    pieces = []
    for first in range(0, slots, 512):
        part = row[:, first : first + 512]
        found = jnp.where(iota((count, 512), 0) == part, column, 0.0)
        pieces.append(jnp.where(part < 0, -1.0, jnp.sum(found, axis=0, keepdims=True)))
    index = jnp.concatenate(pieces, axis=1)
    unit = jnp.where(iota((count, count), 1).astype(F32) == column, 1.0, 0.0).astype(BF16)
    modes = vel.shape[0]
    half = modes // 2
    value = jnp.concatenate([vel[...], jnp.broadcast_to(mass[...], (16, count))], axis=0)
    high = value.astype(BF16)
    middle, low = split(value - high.astype(F32))
    total = modes + 16
    parts = dot(jnp.concatenate([high, middle, low], axis=0), unit)
    moved = parts[:total] + parts[total : 2 * total] + parts[2 * total :]
    a, b = moved[:half], moved[half:modes]
    for ref, rows in ((keep, picked(x == 0, a, b)), (send, picked(x == 0, b, a))):
        ref[0:half, :] = rows
        ref[half : half + 8, :] = moved[modes : modes + 8]
        ref[half + 8 : half + 16, :] = jnp.broadcast_to(index[:, :count], (8, count))
        ref[half + 16 : half + 24, 0 : slots - count] = jnp.broadcast_to(
            index[:, count:], (8, slots - count)
        )
        ref[half + 16 : half + 24, slots - count :] = jnp.zeros((8, 2 * count - slots), F32)
    quarter = count // chunks.shape[0]
    for part in range(chunks.shape[0]):
        chunks[part] = moved[:modes, part * quarter : (part + 1) * quarter]


def build_kernel(own, half, live_elems, ops, pack, high, low, diag, note, flat, tall, qh, ql, pad):
    q, z, x = position()
    live = live_elems[q if own else 2 * z + 1 - x]
    side, elems = ops.shape[0], ops.shape[1]
    count = high.shape[0]
    slots = elems * ROW
    index = jnp.concatenate(
        [pack[half + 8 : half + 16, :], pack[half + 16 : half + 24, 0 : slots - count]], axis=1
    )
    column = jnp.transpose(index)[:, 0:1]
    for first in range(0, slots, 256):
        block = jnp.where(iota((256, count), 1).astype(F32) == column[first : first + 256], 1.0, 0.0)
        tall[first : first + 256, :] = block.astype(BF16)
    tall[slots:, :] = jnp.zeros((tall.shape[0] - slots, count), BF16)
    for first in range(0, count, 256):
        block = jnp.where((iota((256, slots), 0) + first).astype(F32) == index[0:1], 1.0, 0.0)
        flat[first : first + 256, :] = block.astype(BF16)
    pad[...] = jnp.zeros(pad.shape, F32)
    for e in range(elems):
        pad[0:side, 0:side] = ops[:, e, :] * jnp.where(e < live, 1.0, 0.0)
        oh, ol = split(pad[...])
        spread = dot(jnp.concatenate([oh, ol], axis=0), tall[e * ROW : e * ROW + 128, :])
        qh[e * ROW : (e + 1) * ROW, :] = spread[:ROW].astype(BF16)
        ql[e * ROW : (e + 1) * ROW, :] = spread[ROW:].astype(BF16)
    tile = 256
    for j in range(0, count, tile):
        top = j + tile
        block = dot(flat[0:top, :], qh[:, j:top]) + dot(flat[0:top, :], ql[:, j:top])
        h, l = split(block)
        high[0:top, j:top] = h
        low[0:top, j:top] = l
        if j:
            mirror = jnp.transpose(block[:j])
            h, l = split(mirror)
            high[j:top, 0:j] = h
            low[j:top, 0:j] = l
        own_node = iota((tile, tile), 0) == iota((tile, tile), 1)
        line = jnp.sum(jnp.where(own_node, block[j:top], 0.0), axis=0, keepdims=True)
        diag[:, j:top] = jnp.broadcast_to(line, (8, tile))
        if not j:
            face = note.shape[1]
            note[0:face, :] = block[0:face, 0:face]
            note[face : face + 8, :] = jnp.broadcast_to(line[:, 0:face], (8, face))
            note[face + 8 :, :] = pack[half : half + 8, 0:face]


def apply(value, mats, columns, half):
    oh, ol, ph, plo = mats
    return jnp.concatenate(
        [
            rows_times(value[:half], oh[:, columns], ol[:, columns]),
            rows_times(value[half:], ph[:, columns], plo[:, columns]),
        ],
        axis=0,
    )


def assembled(y, outer, half, face):
    inner = y[:half, face : 2 * face] + y[half:, face : 2 * face]
    first = y[:, :face] if outer is None else y[:, :face] + outer
    return jnp.concatenate([first, jnp.concatenate([inner, inner], axis=0), y[:, 2 * face :]], axis=1)


def planes_kernel(u, tables, slope, out):
    count = slope.shape[1]
    both = table_times(tables[0 : 2 * count, :], tables[2 * count : 4 * count, :], u[...])
    rate = jnp.transpose(jnp.broadcast_to(slope[...], (8, count)))[:, 0:1]
    cross = rate * both[:count] * both[count:]
    out[...] = table_times(tables[4 * count : 5 * count, :], tables[5 * count :, :], cross)


def provisional(r, d, g, inv, cm, mats, alpha, beta, half, face):
    r = r - inv * assembled(g, None, half, face)
    d = alpha * d + beta * r if alpha else beta * r
    y = apply(d, mats, slice(0, face), half) + cm[:, :face] * d[:, :face]
    return r, d, y


def even():
    _, z, x = position()
    return lax.rem(x + z, 2) == 0


def put(one, two, g, y, half, face, notes=((), ())):
    own = jnp.concatenate([g[:half, :face], y[:half], *notes[0]], axis=0)
    oth = jnp.concatenate([g[half:, :face], y[half:], *notes[1]], axis=0)
    first = even()
    one[...] = picked(first, own, oth)
    two[...] = picked(first, oth, own)


def got(one, two):
    a, b = one[...], two[...]
    first = even()
    return picked(first, a, b), picked(first, b, a)


def received(conv, half):
    _, _, x = position()
    parts = conv.shape[0]
    return jnp.concatenate(
        [
            jnp.concatenate([conv[m, x] for m in range(parts)], axis=1),
            jnp.concatenate([conv[m, 1 - x] for m in range(parts)], axis=1),
        ],
        axis=0,
    )


def masses(own, oth, half):
    count = own.shape[1]
    return jnp.concatenate(
        [jnp.broadcast_to(m[half : half + 1, :], (half, count)) for m in (own, oth)], axis=0
    )


def helmholtz(half, mode_count):
    _, _, x = position()
    mode = lax.axis_index("mode") * (2 * half) + x * half + iota((half, 1), 0)
    number = jnp.where(mode == 1, mode_count // 2, lax.shift_right_arithmetic(mode, 1))
    return mass_weight + (8.0 * number.astype(F32) / mode_count) ** 2


def first_source_kernel(
    half, face, mode_count, conv, own, oth, do, dp, note_o, note_p, oh, ol, ph, plo,
    r_out, d_out, v_out, conv_out, inv_out, cm_out, one, two,
):
    mats = (oh, ol, ph, plo)
    c = helmholtz(half, mode_count)
    c = jnp.concatenate([c, c], axis=0)
    mass = masses(own, oth, half)
    stiff = jnp.concatenate([jnp.broadcast_to(t[0:1, :], (half, t.shape[1])) for t in (do, dp)], axis=0)
    inv = 1.0 / (assembled(stiff, None, half, face) + c * assembled(mass, None, half, face))
    inv_out[...] = inv
    cm = c * mass
    cm_out[...] = cm
    v = jnp.concatenate([own[0:half, :], oth[0:half, :]], axis=0)
    v_out[...] = v
    new = received(conv, half)
    conv_out[...] = new
    m4 = mass_weight * mass
    g = apply(v, mats, slice(None), half) + (cm - m4) * v - m4 * new
    r = -inv * assembled(g, None, half, face)
    r = jnp.concatenate([jnp.zeros((2 * half, face), F32), r[:, face:]], axis=1)
    d = (1.0 / centre) * r
    r_out[...] = r
    d_out[...] = d
    y = apply(d, mats, slice(0, face), half)
    put(one, two, g, y, half, face, ((note_o[...],), (note_p[...],)))


def source_kernel(half, face, conv, old, own, oth, r, d, inv, cm, oh, ol, ph, plo, r_out, d_out, conv_out, one, two):
    mats = (oh, ol, ph, plo)
    new = received(conv, half)
    conv_out[...] = new
    cmv, dv = cm[...], d[...]
    g = apply(dv, mats, slice(None), half) + cmv * dv - mass_weight * masses(own, oth, half) * (new - old[...])
    rv, dv, y = provisional(r[...], None, g, inv[...], cmv, mats, 0.0, 1.0 / centre, half, face)
    r_out[...] = rv
    d_out[...] = dv
    put(one, two, g, y, half, face)


def rest_kernel(half, face, d, cm, oh, ol, ph, plo, out):
    dv = d[...]
    out[...] = apply(dv, (oh, ol, ph, plo), slice(face, None), half) + cm[:, face:] * dv[:, face:]


def change_of(dd, theirs, mats, na, nb, half, face):
    oh, ol, ph, plo = mats
    change = jnp.concatenate(
        [
            rows_times(dd[:half], oh[0:face, :], ol[0:face, :]),
            rows_times(dd[half:], ph[0:face, :], plo[0:face, :]),
        ],
        axis=0,
    )
    their_change = jnp.concatenate(
        [rows_times(theirs[:half], *split(nb)), rows_times(theirs[half:], *split(na))], axis=0
    )
    return change, their_change


def stacked(pair, first, last):
    return jnp.concatenate([t[first:last, :] for t in pair], axis=0)


def exact(half, face, beta, alpha_next, beta_next, r, d, y_rest, sent, came, na, nb, inv, cm, cmn, mats):
    inv_face = inv[:, :face]
    mine, came = got(*sent), got(*came)
    dr = -(inv_face * stacked(came, 0, half))
    dd = beta * dr
    theirs = -beta * (inv_face * stacked(mine, 0, half))
    change, their_change = change_of(dd, theirs, mats, na[...], nb[...], half, face)
    y = jnp.concatenate([stacked(mine, half, 2 * half) + cm[:, :face] * dd, y_rest], axis=1) + change
    outer = stacked(came, half, 2 * half) + their_change + cmn * theirs
    r = jnp.concatenate([r[:, :face] + dr, r[:, face:]], axis=1)
    d = jnp.concatenate([d[:, :face] + dd, d[:, face:]], axis=1)
    r = r - inv * assembled(y, outer, half, face)
    return r, d, alpha_next * d + beta_next * r


def first_sweep_kernel(
    half, face, mode_count, before, now, then,
    r, d, y_rest, sol, s1, s2, c1, c2, inv, cm, oh, ol, ph, plo,
    r_out, d_out, sol_out, inv_out, cmn_out, na_out, nb_out, one, two,
):
    mats = (oh, ol, ph, plo)
    cm_v = cm[...]
    mine, came = got(s1, s2), got(c1, c2)
    c = helmholtz(half, mode_count)
    c = jnp.concatenate([c, c], axis=0)

    def line(pair, row):
        return jnp.concatenate([jnp.broadcast_to(t[row : row + 1, :], (half, face)) for t in pair], axis=0)

    at = 2 * half + face
    their_mass = line(came, at + 8)
    inv_face = 1.0 / (line(mine, at) + line(came, at) + c * (line(mine, at + 8) + their_mass))
    cmn = c * their_mass
    nb, na = (t[2 * half : at, :] for t in came)
    dr = -inv_face * (stacked(mine, 0, half) + stacked(came, 0, half))
    dd = before[1] * dr
    change, their_change = change_of(dd, dd, mats, na, nb, half, face)
    y = jnp.concatenate([stacked(mine, half, 2 * half) + cm_v[:, :face] * dd, y_rest[...]], axis=1) + change
    outer = stacked(came, half, 2 * half) + their_change + cmn * dd
    inv_v = jnp.concatenate([inv_face, inv[:, face:]], axis=1)
    rv = jnp.concatenate([dr, r[:, face:]], axis=1)
    dv = jnp.concatenate([dd, d[:, face:]], axis=1)
    rv = rv - inv_v * assembled(y, outer, half, face)
    dn = now[0] * dv + now[1] * rv
    inv_out[...] = inv_v
    cmn_out[...] = cmn
    na_out[...] = na
    nb_out[...] = nb
    sol_out[...] = sol[...] + dv + dn
    g = apply(dn, mats, slice(None), half) + cm_v * dn
    rv, dv, y = provisional(rv, dn, g, inv_v, cm_v, mats, then[0], then[1], half, face)
    r_out[...] = rv
    d_out[...] = dv
    put(one, two, g, y, half, face)


def sweep_kernel(
    half, face, before, now, then,
    r, d, y_rest, sol, s1, s2, c1, c2, na, nb, inv, cm, cmn, oh, ol, ph, plo,
    r_out, d_out, sol_out, one, two,
):
    mats = (oh, ol, ph, plo)
    inv_v, cm_v = inv[...], cm[...]
    rv, dv, dn = exact(
        half, face, before[1], now[0], now[1], r[...], d[...], y_rest[...], (s1, s2), (c1, c2), na, nb,
        inv_v, cm_v, cmn[...], mats,
    )
    sol_out[...] = sol[...] + dv + dn
    g = apply(dn, mats, slice(None), half) + cm_v * dn
    rv, dv, y = provisional(rv, dn, g, inv_v, cm_v, mats, then[0], then[1], half, face)
    r_out[...] = rv
    d_out[...] = dv
    put(one, two, g, y, half, face)


def last_kernel(
    half, face, before, now,
    r, d, y_rest, sol, s1, s2, c1, c2, na, nb, inv, cm, cmn, oh, ol, ph, plo,
    r_out, d_out, sol_out, chunks,
):
    rv, dv, dn = exact(
        half, face, before[1], now[0], now[1], r[...], d[...], y_rest[...], (s1, s2), (c1, c2), na, nb,
        inv[...], cm[...], cmn[...], (oh, ol, ph, plo),
    )
    new = sol[...] + dv + dn
    r_out[...] = rv
    d_out[...] = dn
    sol_out[...] = new
    _, _, x = position()
    parts, width = chunks.shape[0], chunks.shape[3]
    for m in range(parts):
        chunks[m, x] = new[:half, m * width : (m + 1) * width]
        chunks[m, 1 - x] = new[half:, m * width : (m + 1) * width]


def end_kernel(
    half, face, before, now,
    r, d, y_rest, sol, s1, s2, c1, c2, na, nb, inv, cm, cmn, oh, ol, ph, plo, own_out, oth_out,
):
    _, dv, dn = exact(
        half, face, before[1], now[0], now[1], r[...], d[...], y_rest[...], (s1, s2), (c1, c2), na, nb,
        inv[...], cm[...], cmn[...], (oh, ol, ph, plo),
    )
    new = sol[...] + dv + dn
    own_out[...] = new[:half]
    oth_out[...] = new[half:]


def restored(value, unit):
    count = value.shape[0]
    high = value.astype(BF16)
    middle, low = split(value - high.astype(F32))
    parts = dot(jnp.concatenate([high, middle, low], axis=0), unit)
    return parts[:count] + parts[count : 2 * count] + parts[2 * count :]


def finish_own_kernel(own, place, out, unit_out):
    count = own.shape[1]
    unit = jnp.where(iota((count, count), 0).astype(F32) == place[0:1, :], 1.0, 0.0).astype(BF16)
    unit_out[...] = unit
    out[...] = restored(own[...], unit)


def finish_kernel(own, other, unit, out):
    _, _, x = position()
    a, b = own[...], restored(other[...], unit[...])
    half = own.shape[0]
    out[0:half, :] = picked(x == 0, a, b)
    out[half:, :] = picked(x == 0, b, a)


def body(n_mode, n_dom, velocity_prev, elem_ops, lumped_mass, span_slope, local_to_global, iface_nodes, live_elems):
    modes, count = velocity_prev.shape
    half = modes // 2
    elems, side = local_to_global.shape
    face = iface_nodes.shape[2]
    mode_count = span_slope.shape[0]
    quarter = count // n_mode
    pairs = n_dom // 2
    slots = elems * ROW
    places = [(z, s) for z in range(pairs) for s in (0, 1)]
    swap = [(i, i ^ 1) for i in range(n_dom)]
    long_swap = [(2 * z + s, 2 * ((z + (1 if z % 2 else -1)) % pairs) + s) for z, s in places]
    short_swap = [(2 * z + s, 2 * ((z + (-1 if z % 2 else 1)) % pairs) + s) for z, s in places]
    groups = [[m * n_dom + 2 * z + s for m in range(n_mode) for s in (0, 1)] for z in range(pairs)]

    def exchange(one, two):
        return lax.ppermute(one, "dom", long_swap), lax.ppermute(two, "dom", short_swap)

    ops = jnp.transpose(elem_ops, (1, 0, 2))
    ops_other = lax.ppermute(ops, "dom", swap)
    pack = (half + 24, count)
    wide = (2 * half, count)
    keep, send, chunks, place = call(
        order_kernel,
        [(pack, F32), (pack, F32), ((n_mode, modes, quarter), F32), ((8, count), F32)],
        [], [iface_nodes[0], local_to_global, velocity_prev, lumped_mass.reshape(1, count)], 24, place=pltpu.HBM,
        scratch=[
            pltpu.VMEM((2, face), jnp.int32), pltpu.VMEM((elems, side), jnp.int32),
            pltpu.VMEM((modes, count), F32), pltpu.VMEM((1, count), F32), pltpu.SemaphoreType.DMA((4,)),
        ],
    )
    planes_in = lax.all_to_all(chunks, "mode", 0, 0, tiled=True)
    oth = lax.ppermute(send, "dom", swap)

    def build(own, ops, packed):
        matrix = ((count, count), BF16)
        return call(
            functools.partial(build_kernel, own, half),
            [matrix, matrix, ((8, count), F32), ((face + 16, face), F32)],
            [live_elems], [ops, packed], 40, keep=2,
            scratch=[
                pltpu.VMEM((count, slots), BF16),
                pltpu.VMEM((slots + 32, count), BF16),
                pltpu.VMEM((slots, count), BF16),
                pltpu.VMEM((slots, count), BF16),
                pltpu.VMEM((ROW, 128), F32),
            ],
            flops=6 << 30,
        )

    oh, ol, do, note_o = build(True, ops, keep)
    synthesis, derivative, analysis = wave_tables(mode_count)
    tables = jnp.asarray(np.concatenate(halves(np.concatenate([synthesis, derivative])) + halves(analysis)))
    slope = span_slope.reshape(1, mode_count)

    def convect(value):
        (out,) = call(
            planes_kernel, [((mode_count, quarter), F32)], [],
            [value.reshape(mode_count, quarter), tables, slope], 16, flops=600 << 20,
        )
        back = lax.all_to_all(
            out.reshape(2 * n_mode, half, quarter), ("mode", "dom"), 0, 0, axis_index_groups=groups, tiled=True
        )
        return back.reshape(n_mode, 2, half, quarter)

    conv = convect(planes_in)
    ph, plo, dp, note_p = build(False, ops_other, oth)
    mats = [oh, ol, ph, plo]
    coefs = chebyshev()
    message = ((2 * half, face), F32)
    for iteration in range(ITERS):
        if iteration == 0:
            long_message = ((2 * half + face + 16, face), F32)
            r, d, sol, old, inv, cm, one, two = call(
                functools.partial(first_source_kernel, half, face, mode_count),
                [(wide, F32)] * 6 + [long_message, long_message],
                [], [conv, keep, oth, do, dp, note_o, note_p, *mats], 20, flops=500 << 20,
            )
        else:
            r, d, old, one, two = call(
                functools.partial(source_kernel, half, face),
                [(wide, F32), (wide, F32), (wide, F32), message, message],
                [], [conv, old, keep, oth, r, d, inv, cm, *mats], 20, flops=500 << 20,
            )
        for k in (0, 2, 4):
            c1, c2 = exchange(one, two)
            (rest,) = call(
                functools.partial(rest_kernel, half, face), [((2 * half, count - face), F32)],
                [], [d, cm, *mats], 20, flops=400 << 20,
            )
            if iteration == 0 and k == 0:
                r, d, sol, inv, cmn, na, nb, one, two = call(
                    functools.partial(first_sweep_kernel, half, face, mode_count, coefs[0], coefs[1], coefs[2]),
                    [(wide, F32)] * 4 + [((2 * half, face), F32)] + [((face, face), F32)] * 2 + [message, message],
                    [], [r, d, rest, sol, one, two, c1, c2, inv, cm, *mats], 20, flops=500 << 20,
                )
                continue
            given = [r, d, rest, sol, one, two, c1, c2, na, nb, inv, cm, cmn, *mats]
            if k < 4:
                r, d, sol, one, two = call(
                    functools.partial(sweep_kernel, half, face, coefs[k], coefs[k + 1], coefs[k + 2]),
                    [(wide, F32), (wide, F32), (wide, F32), message, message], [], given, 20, flops=500 << 20,
                )
            elif iteration < ITERS - 1:
                r, d, sol, chunks = call(
                    functools.partial(last_kernel, half, face, coefs[k], coefs[k + 1]),
                    [(wide, F32), (wide, F32), (wide, F32), ((n_mode, 2, half, quarter), F32)],
                    [], given, 20, flops=100 << 20,
                )
            else:
                own, other = call(
                    functools.partial(end_kernel, half, face, coefs[k], coefs[k + 1]),
                    [((half, count), F32)] * 2, [], given, 20, flops=100 << 20,
                )
        if iteration < ITERS - 1:
            planes_in = lax.all_to_all(
                chunks.reshape(2 * n_mode, half, quarter), ("mode", "dom"), 0, 0, axis_index_groups=groups, tiled=True
            )
            conv = convect(planes_in)
    other = lax.ppermute(other, "dom", swap)
    own, unit = call(
        finish_own_kernel, [((half, count), F32), ((count, count), BF16)], [], [own, place], 16, flops=200 << 20
    )
    (out,) = call(finish_kernel, [((modes, count), F32)], [], [own, other, unit], 16)
    return out


def solution(mesh):
    placed = (
        P("mode", "dom"),
        P("dom", None, None),
        P("dom"),
        P(),
        P("dom", None),
        P("dom", None, None),
        P(),
    )
    return jax.shard_map(
        functools.partial(body, mesh.shape["mode"], mesh.shape["dom"]),
        mesh=mesh, in_specs=placed, out_specs=P("mode", "dom"), check_vma=False,
    )
```

```python
import functools

import jax
import jax.numpy as jnp
import numpy as np
from jax import lax
from jax.experimental import pallas as pl
from jax.experimental.pallas import tpu as pltpu
from jax.sharding import PartitionSpec as P

ITERS = 3
SWEEPS = 6

mass_weight = 4.0
bound_low = 0.1
bound_high = 2.0
centre = (bound_high + bound_low) / 2.0
half_width = (bound_high - bound_low) / 2.0

F32 = jnp.float32
BF16 = jnp.bfloat16
ROW = 96


def chebyshev():
    ratio = centre / half_width
    rho = 1.0 / ratio
    coefs = [(0.0, 1.0 / centre)]
    for _ in range(SWEEPS - 1):
        rho_next = 1.0 / (2.0 * ratio - rho)
        coefs.append((rho_next * rho, 2.0 * rho_next / half_width))
        rho = rho_next
    return coefs


def wave_tables(mode_count):
    column = np.arange(mode_count)
    number = np.where(column == 1, mode_count // 2, column // 2)
    is_sine = (column % 2 == 1) & (column > 1)
    planes = np.arange(mode_count)
    angles = (planes[:, None] * number[None, :] % mode_count) * (2.0 * np.pi / mode_count)
    cosine, sine = np.cos(angles), np.sin(angles)
    synthesis = np.where(is_sine[None, :], sine, cosine)
    factor = number / (mode_count // 2)
    derivative = np.where(is_sine[None, :], cosine, -sine) * factor[None, :]
    derivative = np.where(column[None, :] > 1, derivative, 0.0)
    weights = np.where(column < 2, 1.0 / mode_count, 2.0 / mode_count)
    return synthesis, derivative, synthesis.T * weights[:, None]


def halves(table):
    high = table.astype(np.float32).astype(BF16)
    return [high, (table - high.astype(np.float64)).astype(np.float32).astype(BF16)]


def split(value):
    high = value.astype(BF16)
    return high, (value - high.astype(F32)).astype(BF16)


def dot(a, b):
    return lax.dot_general(a, b, (((1,), (0,)), ((), ())), preferred_element_type=F32)


def rows_times(value, high, low):
    count = value.shape[0]
    h, l = split(value)
    both = dot(jnp.concatenate([h, l], axis=0), high)
    return both[:count] + both[count:] + dot(h, low)


def table_times(high, low, value):
    count = value.shape[1]
    h, l = split(value)
    both = dot(high, jnp.concatenate([h, l], axis=1))
    return both[:, :count] + both[:, count:] + dot(low, h)


def iota(shape, dim):
    return lax.broadcasted_iota(jnp.int32, shape, dim)


def call(kernel, outs, vmem, limit, scratch=(), flops=0, moved=1 << 20, far=(), out_far=(), pinned=()):
    in_specs, given = [], []
    for i, v in enumerate(vmem):
        space = pltpu.HBM if i in far else pltpu.VMEM
        in_specs.append(pl.BlockSpec(memory_space=space))
        fixed = i in far or v.dtype == BF16 and v.shape[0] == v.shape[1]
        given.append(pltpu.with_memory_space_constraint(v, space) if fixed else v)
    shapes, out_specs = [], []
    for i, (s, t) in enumerate(outs):
        space = pltpu.HBM if i in out_far else pltpu.VMEM
        out_specs.append(pl.BlockSpec(memory_space=space))
        shapes.append(space(s, t) if i in out_far or i in pinned else jax.ShapeDtypeStruct(s, t))
    return pl.pallas_call(
        kernel,
        out_shape=shapes,
        in_specs=in_specs,
        out_specs=out_specs,
        scratch_shapes=list(scratch),
        compiler_params=pltpu.CompilerParams(vmem_limit_bytes=limit << 20),
        cost_estimate=pl.CostEstimate(flops=flops, bytes_accessed=moved, transcendentals=0),
    )(*given)


def position():
    q = lax.axis_index("dom")
    z = lax.shift_right_arithmetic(q, 1)
    return q, z, q - 2 * z


def picked(first, a, b):
    return jnp.where(first, a, b)


def order_kernel(
    iface_in, l2g_in, vel_in, mass_in, live_in, keep, send, chunks, place_out, iface, l2g, vel, mass, live, sems
):
    q, _, x = position()
    pairs = ((iface_in, iface), (l2g_in, l2g), (vel_in, vel), (mass_in, mass), (live_in, live))
    copies = [pltpu.make_async_copy(a, b, sems.at[i]) for i, (a, b) in enumerate(pairs)]
    for copy in copies:
        copy.start()
    for copy in copies:
        copy.wait()
    count = mass.shape[1]
    face = iface.shape[1]
    lists = jnp.concatenate(
        [picked(x == 0, iface[0:1, :], iface[1:2, :]), picked(x == 0, iface[1:2, :], iface[0:1, :])], axis=1
    ).astype(F32)
    lists = jnp.transpose(jnp.broadcast_to(lists, (8, 2 * face)))[:, 0:1]
    hit = jnp.where(lists == iota((2 * face, count), 1).astype(F32), 1.0, 0.0)
    at = jnp.sum(hit * iota((2 * face, count), 0).astype(F32), axis=0, keepdims=True)
    shared = jnp.sum(hit, axis=0, keepdims=True)
    rest = jnp.broadcast_to(1.0 - shared, (8, count))
    lane = iota((8, count), 1)
    run = rest
    step = 1
    while step < count:
        run = run + jnp.where(lane >= step, pltpu.roll(run, step, 1), 0.0)
        step *= 2
    place = jnp.where(rest > 0.5, run - 1.0 + 2.0 * face, jnp.broadcast_to(at, (8, count)))
    place_out[...] = place
    column = jnp.transpose(place)[:, 0:1]
    elems, side = l2g.shape
    slots = elems * ROW
    blank = jnp.full((1, ROW - side), -1, jnp.int32)
    row = jnp.concatenate([piece for e in range(elems) for piece in (l2g[e : e + 1, :], blank)], axis=1)
    pieces = []
    for first in range(0, slots, 512):
        part = row[:, first : first + 512]
        found = jnp.where(iota((count, 512), 0) == part, column, 0.0)
        pieces.append(jnp.where(part < 0, -1.0, jnp.sum(found, axis=0, keepdims=True)))
    index = jnp.concatenate(pieces, axis=1)
    unit = jnp.where(iota((count, count), 1).astype(F32) == column, 1.0, 0.0).astype(BF16)
    modes = vel.shape[0]
    half = modes // 2
    value = jnp.concatenate([vel[...], jnp.broadcast_to(mass[...], (16, count))], axis=0)
    high = value.astype(BF16)
    middle, low = split(value - high.astype(F32))
    total = modes + 16
    parts = dot(jnp.concatenate([high, middle, low], axis=0), unit)
    moved = parts[:total] + parts[total : 2 * total] + parts[2 * total :]
    a, b = moved[:half], moved[half:modes]
    lived = jnp.where(iota(live.shape, 1) == q, live[...], 0).astype(F32)
    lived = jnp.sum(lived, axis=1, keepdims=True)
    for ref, rows in ((keep, picked(x == 0, a, b)), (send, picked(x == 0, b, a))):
        ref[0:half, :] = rows
        ref[half : half + 8, :] = moved[modes : modes + 8]
        ref[half + 8 : half + 16, :] = jnp.broadcast_to(index[:, :count], (8, count))
        ref[half + 16 : half + 24, 0 : slots - count] = jnp.broadcast_to(
            index[:, count:], (8, slots - count)
        )
        ref[half + 16 : half + 24, slots - count :] = jnp.broadcast_to(lived, (8, 2 * count - slots))
    quarter = count // chunks.shape[0]
    for part in range(chunks.shape[0]):
        chunks[part] = moved[:modes, part * quarter : (part + 1) * quarter]


def build_kernel(half, ops_in, pack, high_out, low_out, diag, note, ops, high, low, flat, tall, qh, ql, pad, sems):
    fetch = pltpu.make_async_copy(ops_in, ops, sems.at[0])
    fetch.start()
    live = pack[half + 16 : half + 17, pack.shape[1] - 1 :]
    side, elems = ops.shape[0], ops.shape[1]
    count = high.shape[0]
    slots = elems * ROW
    index = jnp.concatenate(
        [pack[half + 8 : half + 16, :], pack[half + 16 : half + 24, 0 : slots - count]], axis=1
    )
    column = jnp.transpose(index)[:, 0:1]
    for first in range(0, slots, 256):
        block = jnp.where(iota((256, count), 1).astype(F32) == column[first : first + 256], 1.0, 0.0)
        tall[first : first + 256, :] = block.astype(BF16)
    tall[slots:, :] = jnp.zeros((tall.shape[0] - slots, count), BF16)
    for first in range(0, count, 256):
        block = jnp.where((iota((256, slots), 0) + first).astype(F32) == index[0:1], 1.0, 0.0)
        flat[first : first + 256, :] = block.astype(BF16)
    pad[...] = jnp.zeros(pad.shape, F32)
    fetch.wait()
    for e in range(elems):
        pad[0:side, 0:side] = ops[:, e, :] * jnp.where(live > e + 0.5, 1.0, 0.0)
        oh, ol = split(pad[...])
        spread = dot(jnp.concatenate([oh, ol], axis=0), tall[e * ROW : e * ROW + 128, :])
        qh[e * ROW : (e + 1) * ROW, :] = spread[:ROW].astype(BF16)
        ql[e * ROW : (e + 1) * ROW, :] = spread[ROW:].astype(BF16)
    tile = 256
    copies = []

    def ship(rows, columns):
        for part, out in ((high, high_out), (low, low_out)):
            at = (pl.ds(*rows), pl.ds(*columns))
            copies.append(pltpu.make_async_copy(part.at[at], out.at[at], sems.at[len(copies) + 1]))
            copies[-1].start()

    for j in range(0, count, tile):
        top = j + tile
        block = dot(flat[0:top, :], qh[:, j:top]) + dot(flat[0:top, :], ql[:, j:top])
        h, l = split(block)
        high[0:top, j:top] = h
        low[0:top, j:top] = l
        ship((0, top), (j, tile))
        if j:
            mirror = jnp.transpose(block[:j])
            h, l = split(mirror)
            high[j:top, 0:j] = h
            low[j:top, 0:j] = l
            ship((j, tile), (0, j))
        own_node = iota((tile, tile), 0) == iota((tile, tile), 1)
        line = jnp.sum(jnp.where(own_node, block[j:top], 0.0), axis=0, keepdims=True)
        diag[:, j:top] = jnp.broadcast_to(line, (8, tile))
        if not j:
            face = note.shape[1]
            note[0:face, :] = block[0:face, 0:face]
            note[face : face + 8, :] = jnp.broadcast_to(line[:, 0:face], (8, face))
            note[face + 8 :, :] = pack[half : half + 8, 0:face]
    for copy in copies:
        copy.wait()


def apply(value, mats, columns, half):
    oh, ol, ph, plo = mats
    return jnp.concatenate(
        [
            rows_times(value[:half], oh[:, columns], ol[:, columns]),
            rows_times(value[half:], ph[:, columns], plo[:, columns]),
        ],
        axis=0,
    )


def assembled(y, outer, half, face):
    inner = y[:half, face : 2 * face] + y[half:, face : 2 * face]
    first = y[:, :face] if outer is None else y[:, :face] + outer
    return jnp.concatenate([first, jnp.concatenate([inner, inner], axis=0), y[:, 2 * face :]], axis=1)


def first_planes_kernel(u, tables_in, slope, out, tables, sems):
    rows = 4 * slope.shape[1]
    parts = [pl.ds(0, rows), pl.ds(rows, tables.shape[0] - rows)]
    copies = [pltpu.make_async_copy(tables_in.at[p], tables.at[p], sems.at[i]) for i, p in enumerate(parts)]
    for copy in copies:
        copy.start()
    copies[0].wait()
    planes_kernel(u, tables, slope, out, copies[1].wait)


def planes_kernel(u, tables, slope, out, ready=None):
    count = slope.shape[1]
    both = table_times(tables[0 : 2 * count, :], tables[2 * count : 4 * count, :], u[...])
    rate = jnp.transpose(jnp.broadcast_to(slope[...], (8, count)))[:, 0:1]
    cross = rate * both[:count] * both[count:]
    if ready is not None:
        ready()
    out[...] = table_times(tables[4 * count : 5 * count, :], tables[5 * count :, :], cross)


def provisional(r, d, g, inv, cm, mats, alpha, beta, half, face):
    r = r - inv * assembled(g, None, half, face)
    d = alpha * d + beta * r if alpha else beta * r
    y = apply(d, mats, slice(0, face), half) + cm[:, :face] * d[:, :face]
    return r, d, y


def even():
    _, z, x = position()
    return lax.rem(x + z, 2) == 0


def put(one, two, g, y, half, face, notes=((), ())):
    own = jnp.concatenate([g[:half, :face], y[:half], *notes[0]], axis=0)
    oth = jnp.concatenate([g[half:, :face], y[half:], *notes[1]], axis=0)
    first = even()
    one[...] = picked(first, own, oth)
    two[...] = picked(first, oth, own)


def got(one, two):
    a, b = one[...], two[...]
    first = even()
    return picked(first, a, b), picked(first, b, a)


def received(conv, half):
    _, _, x = position()
    parts = conv.shape[0]
    return jnp.concatenate(
        [
            jnp.concatenate([conv[m, x] for m in range(parts)], axis=1),
            jnp.concatenate([conv[m, 1 - x] for m in range(parts)], axis=1),
        ],
        axis=0,
    )


def masses(own, oth, half):
    count = own.shape[1]
    return jnp.concatenate(
        [jnp.broadcast_to(m[half : half + 1, :], (half, count)) for m in (own, oth)], axis=0
    )


def helmholtz(half, mode_count):
    _, _, x = position()
    mode = lax.axis_index("mode") * (2 * half) + x * half + iota((half, 1), 0)
    number = jnp.where(mode == 1, mode_count // 2, lax.shift_right_arithmetic(mode, 1))
    return mass_weight + (8.0 * number.astype(F32) / mode_count) ** 2


def first_source_kernel(
    half, face, mode_count, conv, own, oth, do, dp, note_o, note_p, oh_in, ol_in, ph_in, plo_in,
    oh, ol, ph, plo, r_out, d_out, v_out, conv_out, inv_out, cm_out, one, two, sems,
):
    mats = (oh, ol, ph, plo)
    copies = [
        pltpu.make_async_copy(a, b, sems.at[i]) for i, (a, b) in enumerate(zip((oh_in, ol_in, ph_in, plo_in), mats))
    ]
    for copy in copies:
        copy.start()
    c = helmholtz(half, mode_count)
    c = jnp.concatenate([c, c], axis=0)
    mass = masses(own, oth, half)
    stiff = jnp.concatenate([jnp.broadcast_to(t[0:1, :], (half, t.shape[1])) for t in (do, dp)], axis=0)
    inv = 1.0 / (assembled(stiff, None, half, face) + c * assembled(mass, None, half, face))
    inv_out[...] = inv
    cm = c * mass
    cm_out[...] = cm
    v = jnp.concatenate([own[0:half, :], oth[0:half, :]], axis=0)
    v_out[...] = v
    new = received(conv, half)
    conv_out[...] = new
    m4 = mass_weight * mass
    copies[0].wait()
    copies[1].wait()
    e_own = rows_times(v[:half], oh[...], ol[...])
    copies[2].wait()
    copies[3].wait()
    e_oth = rows_times(v[half:], ph[...], plo[...])
    g = jnp.concatenate([e_own, e_oth], axis=0) + (cm - m4) * v - m4 * new
    r = -inv * assembled(g, None, half, face)
    r = jnp.concatenate([jnp.zeros((2 * half, face), F32), r[:, face:]], axis=1)
    d = (1.0 / centre) * r
    r_out[...] = r
    d_out[...] = d
    y = apply(d, mats, slice(0, face), half)
    put(one, two, g, y, half, face, ((note_o[...],), (note_p[...],)))


def source_kernel(half, face, conv, old, own, oth, r, d, inv, cm, oh, ol, ph, plo, r_out, d_out, conv_out, one, two):
    mats = (oh, ol, ph, plo)
    new = received(conv, half)
    conv_out[...] = new
    cmv, dv = cm[...], d[...]
    g = apply(dv, mats, slice(None), half) + cmv * dv - mass_weight * masses(own, oth, half) * (new - old[...])
    rv, dv, y = provisional(r[...], None, g, inv[...], cmv, mats, 0.0, 1.0 / centre, half, face)
    r_out[...] = rv
    d_out[...] = dv
    put(one, two, g, y, half, face)


def rest_kernel(half, face, d, cm, oh, ol, ph, plo, out):
    dv = d[...]
    out[...] = apply(dv, (oh, ol, ph, plo), slice(face, None), half) + cm[:, face:] * dv[:, face:]


def change_of(dd, theirs, mats, na, nb, half, face):
    oh, ol, ph, plo = mats
    change = jnp.concatenate(
        [
            rows_times(dd[:half], oh[0:face, :], ol[0:face, :]),
            rows_times(dd[half:], ph[0:face, :], plo[0:face, :]),
        ],
        axis=0,
    )
    their_change = jnp.concatenate(
        [rows_times(theirs[:half], *split(nb)), rows_times(theirs[half:], *split(na))], axis=0
    )
    return change, their_change


def stacked(pair, first, last):
    return jnp.concatenate([t[first:last, :] for t in pair], axis=0)


def exact(half, face, beta, alpha_next, beta_next, r, d, y_rest, sent, came, na, nb, inv, cm, cmn, mats):
    inv_face = inv[:, :face]
    mine, came = got(*sent), got(*came)
    dr = -(inv_face * stacked(came, 0, half))
    dd = beta * dr
    theirs = -beta * (inv_face * stacked(mine, 0, half))
    change, their_change = change_of(dd, theirs, mats, na[...], nb[...], half, face)
    y = jnp.concatenate([stacked(mine, half, 2 * half) + cm[:, :face] * dd, y_rest], axis=1) + change
    outer = stacked(came, half, 2 * half) + their_change + cmn * theirs
    r = jnp.concatenate([r[:, :face] + dr, r[:, face:]], axis=1)
    d = jnp.concatenate([d[:, :face] + dd, d[:, face:]], axis=1)
    r = r - inv * assembled(y, outer, half, face)
    return r, d, alpha_next * d + beta_next * r


def first_sweep_kernel(
    half, face, mode_count, before, now, then,
    r, d, y_rest, sol, s1, s2, c1, c2, inv, cm, oh, ol, ph, plo,
    r_out, d_out, sol_out, inv_out, cmn_out, na_out, nb_out, one, two,
):
    mats = (oh, ol, ph, plo)
    cm_v = cm[...]
    mine, came = got(s1, s2), got(c1, c2)
    c = helmholtz(half, mode_count)
    c = jnp.concatenate([c, c], axis=0)

    def line(pair, row):
        return jnp.concatenate([jnp.broadcast_to(t[row : row + 1, :], (half, face)) for t in pair], axis=0)

    at = 2 * half + face
    their_mass = line(came, at + 8)
    inv_face = 1.0 / (line(mine, at) + line(came, at) + c * (line(mine, at + 8) + their_mass))
    cmn = c * their_mass
    nb, na = (t[2 * half : at, :] for t in came)
    dr = -inv_face * (stacked(mine, 0, half) + stacked(came, 0, half))
    dd = before[1] * dr
    change, their_change = change_of(dd, dd, mats, na, nb, half, face)
    y = jnp.concatenate([stacked(mine, half, 2 * half) + cm_v[:, :face] * dd, y_rest[...]], axis=1) + change
    outer = stacked(came, half, 2 * half) + their_change + cmn * dd
    inv_v = jnp.concatenate([inv_face, inv[:, face:]], axis=1)
    rv = jnp.concatenate([dr, r[:, face:]], axis=1)
    dv = jnp.concatenate([dd, d[:, face:]], axis=1)
    rv = rv - inv_v * assembled(y, outer, half, face)
    dn = now[0] * dv + now[1] * rv
    inv_out[...] = inv_v
    cmn_out[...] = cmn
    na_out[...] = na
    nb_out[...] = nb
    sol_out[...] = sol[...] + dv + dn
    g = apply(dn, mats, slice(None), half) + cm_v * dn
    rv, dv, y = provisional(rv, dn, g, inv_v, cm_v, mats, then[0], then[1], half, face)
    r_out[...] = rv
    d_out[...] = dv
    put(one, two, g, y, half, face)


def sweep_kernel(
    half, face, before, now, then,
    r, d, y_rest, sol, s1, s2, c1, c2, na, nb, inv, cm, cmn, oh, ol, ph, plo,
    r_out, d_out, sol_out, one, two,
):
    mats = (oh, ol, ph, plo)
    inv_v, cm_v = inv[...], cm[...]
    rv, dv, dn = exact(
        half, face, before[1], now[0], now[1], r[...], d[...], y_rest[...], (s1, s2), (c1, c2), na, nb,
        inv_v, cm_v, cmn[...], mats,
    )
    sol_out[...] = sol[...] + dv + dn
    g = apply(dn, mats, slice(None), half) + cm_v * dn
    rv, dv, y = provisional(rv, dn, g, inv_v, cm_v, mats, then[0], then[1], half, face)
    r_out[...] = rv
    d_out[...] = dv
    put(one, two, g, y, half, face)


def last_kernel(
    half, face, before, now,
    r, d, y_rest, sol, s1, s2, c1, c2, na, nb, inv, cm, cmn, oh, ol, ph, plo,
    r_out, d_out, sol_out, chunks,
):
    rv, dv, dn = exact(
        half, face, before[1], now[0], now[1], r[...], d[...], y_rest[...], (s1, s2), (c1, c2), na, nb,
        inv[...], cm[...], cmn[...], (oh, ol, ph, plo),
    )
    new = sol[...] + dv + dn
    r_out[...] = rv
    d_out[...] = dn
    sol_out[...] = new
    _, _, x = position()
    parts, width = chunks.shape[0], chunks.shape[3]
    for m in range(parts):
        chunks[m, x] = new[:half, m * width : (m + 1) * width]
        chunks[m, 1 - x] = new[half:, m * width : (m + 1) * width]


def end_kernel(
    half, face, before, now,
    r, d, y_rest, sol, s1, s2, c1, c2, na, nb, inv, cm, cmn, oh, ol, ph, plo, own_out, oth_out,
):
    _, dv, dn = exact(
        half, face, before[1], now[0], now[1], r[...], d[...], y_rest[...], (s1, s2), (c1, c2), na, nb,
        inv[...], cm[...], cmn[...], (oh, ol, ph, plo),
    )
    new = sol[...] + dv + dn
    own_out[...] = new[:half]
    oth_out[...] = new[half:]


def restored(value, unit):
    count = value.shape[0]
    high = value.astype(BF16)
    middle, low = split(value - high.astype(F32))
    parts = dot(jnp.concatenate([high, middle, low], axis=0), unit)
    return parts[:count] + parts[count : 2 * count] + parts[2 * count :]


def finish_own_kernel(own, place, out, unit_out):
    count = own.shape[1]
    unit = jnp.where(iota((count, count), 0).astype(F32) == place[0:1, :], 1.0, 0.0).astype(BF16)
    unit_out[...] = unit
    out[...] = restored(own[...], unit)


def finish_kernel(own, other, unit, out):
    _, _, x = position()
    a, b = own[...], restored(other[...], unit[...])
    half = own.shape[0]
    out[0:half, :] = picked(x == 0, a, b)
    out[half:, :] = picked(x == 0, b, a)


def body(n_mode, n_dom, velocity_prev, elem_ops, lumped_mass, span_slope, local_to_global, iface_nodes, live_elems):
    modes, count = velocity_prev.shape
    half = modes // 2
    elems, side = local_to_global.shape
    face = iface_nodes.shape[2]
    mode_count = span_slope.shape[0]
    quarter = count // n_mode
    pairs = n_dom // 2
    slots = elems * ROW
    places = [(z, s) for z in range(pairs) for s in (0, 1)]
    swap = [(i, i ^ 1) for i in range(n_dom)]
    long_swap = [(2 * z + s, 2 * ((z + (1 if z % 2 else -1)) % pairs) + s) for z, s in places]
    short_swap = [(2 * z + s, 2 * ((z + (-1 if z % 2 else 1)) % pairs) + s) for z, s in places]
    groups = [[m * n_dom + 2 * z + s for m in range(n_mode) for s in (0, 1)] for z in range(pairs)]

    def exchange(one, two):
        return lax.ppermute(one, "dom", long_swap), lax.ppermute(two, "dom", short_swap)

    ops = jnp.transpose(elem_ops, (1, 0, 2))
    ops_other = lax.ppermute(ops, "dom", swap)
    pack = (half + 24, count)
    wide = (2 * half, count)
    keep, send, chunks, place = call(
        order_kernel,
        [(pack, F32), (pack, F32), ((n_mode, modes, quarter), F32), ((8, count), F32)],
        [iface_nodes[0], local_to_global, velocity_prev, lumped_mass.reshape(1, count), live_elems.reshape(1, n_dom)],
        24, far=range(5),
        scratch=[
            pltpu.VMEM((2, face), jnp.int32), pltpu.VMEM((elems, side), jnp.int32),
            pltpu.VMEM((modes, count), F32), pltpu.VMEM((1, count), F32), pltpu.VMEM((1, n_dom), jnp.int32),
            pltpu.SemaphoreType.DMA((5,)),
        ],
    )
    planes_in = lax.all_to_all(chunks, "mode", 0, 0, tiled=True)
    oth = lax.ppermute(send, "dom", swap)

    def build(ops, packed):
        matrix = ((count, count), BF16)
        return call(
            functools.partial(build_kernel, half),
            [matrix, matrix, ((8, count), F32), ((face + 16, face), F32)], [ops, packed], 36, far=(0,), out_far=(0, 1),
            scratch=[
                pltpu.VMEM((side, elems, side), F32),
                pltpu.VMEM((count, count), BF16),
                pltpu.VMEM((count, count), BF16),
                pltpu.VMEM((count, slots), BF16),
                pltpu.VMEM((slots + 32, count), BF16),
                pltpu.VMEM((slots, count), BF16),
                pltpu.VMEM((slots, count), BF16),
                pltpu.VMEM((ROW, 128), F32),
                pltpu.SemaphoreType.DMA((4 * count // 256 - 1,)),
            ],
            flops=6 << 30,
        )

    oh, ol, do, note_o = build(ops, keep)
    synthesis, derivative, analysis = wave_tables(mode_count)
    tables = jnp.asarray(np.concatenate(halves(np.concatenate([synthesis, derivative])) + halves(analysis)))
    slope = span_slope.reshape(1, mode_count)

    def convect(value, first):
        (out,) = call(
            first_planes_kernel if first else planes_kernel, [((mode_count, quarter), F32)],
            [value.reshape(mode_count, quarter), tables, slope], 16, flops=600 << 20, far=(1,) if first else (),
            scratch=[pltpu.VMEM(tables.shape, BF16), pltpu.SemaphoreType.DMA((2,))] if first else (),
        )
        back = lax.all_to_all(
            out.reshape(2 * n_mode, half, quarter), ("mode", "dom"), 0, 0, axis_index_groups=groups, tiled=True
        )
        return back.reshape(n_mode, 2, half, quarter)

    conv = convect(planes_in, True)
    ph, plo, dp, note_p = build(ops_other, oth)
    mats = [oh, ol, ph, plo]
    coefs = chebyshev()
    message = ((2 * half, face), F32)
    for iteration in range(ITERS):
        if iteration == 0:
            long_message = ((2 * half + face + 16, face), F32)
            *mats, r, d, sol, old, inv, cm, one, two = call(
                functools.partial(first_source_kernel, half, face, mode_count),
                [((count, count), BF16)] * 4 + [(wide, F32)] * 6 + [long_message, long_message],
                [conv, keep, oth, do, dp, note_o, note_p, *mats], 20, flops=500 << 20,
                far=range(7, 11), pinned=range(4), scratch=[pltpu.SemaphoreType.DMA((4,))],
            )
        else:
            r, d, old, one, two = call(
                functools.partial(source_kernel, half, face),
                [(wide, F32), (wide, F32), (wide, F32), message, message],
                [conv, old, keep, oth, r, d, inv, cm, *mats], 20, flops=500 << 20,
            )
        for k in (0, 2, 4):
            c1, c2 = exchange(one, two)
            (rest,) = call(
                functools.partial(rest_kernel, half, face), [((2 * half, count - face), F32)],
                [d, cm, *mats], 20, flops=400 << 20,
            )
            if iteration == 0 and k == 0:
                r, d, sol, inv, cmn, na, nb, one, two = call(
                    functools.partial(first_sweep_kernel, half, face, mode_count, coefs[0], coefs[1], coefs[2]),
                    [(wide, F32)] * 4 + [((2 * half, face), F32)] + [((face, face), F32)] * 2 + [message, message],
                    [r, d, rest, sol, one, two, c1, c2, inv, cm, *mats], 20, flops=500 << 20,
                )
                continue
            given = [r, d, rest, sol, one, two, c1, c2, na, nb, inv, cm, cmn, *mats]
            if k < 4:
                r, d, sol, one, two = call(
                    functools.partial(sweep_kernel, half, face, coefs[k], coefs[k + 1], coefs[k + 2]),
                    [(wide, F32), (wide, F32), (wide, F32), message, message], given, 20, flops=500 << 20,
                )
            elif iteration < ITERS - 1:
                r, d, sol, chunks = call(
                    functools.partial(last_kernel, half, face, coefs[k], coefs[k + 1]),
                    [(wide, F32), (wide, F32), (wide, F32), ((n_mode, 2, half, quarter), F32)],
                    given, 20, flops=100 << 20,
                )
            else:
                own, other = call(
                    functools.partial(end_kernel, half, face, coefs[k], coefs[k + 1]),
                    [((half, count), F32)] * 2, given, 20, flops=100 << 20,
                )
        if iteration < ITERS - 1:
            planes_in = lax.all_to_all(
                chunks.reshape(2 * n_mode, half, quarter), ("mode", "dom"), 0, 0, axis_index_groups=groups, tiled=True
            )
            conv = convect(planes_in, False)
    other = lax.ppermute(other, "dom", swap)
    own, unit = call(
        finish_own_kernel, [((half, count), F32), ((count, count), BF16)], [own, place], 16, flops=200 << 20
    )
    (out,) = call(finish_kernel, [((modes, count), F32)], [own, other, unit], 16)
    return out


def solution(mesh):
    placed = (
        P("mode", "dom"),
        P("dom", None, None),
        P("dom"),
        P(),
        P("dom", None),
        P("dom", None, None),
        P(),
    )
    return jax.shard_map(
        functools.partial(body, mesh.shape["mode"], mesh.shape["dom"]),
        mesh=mesh, in_specs=placed, out_specs=P("mode", "dom"), check_vma=False,
    )
```

```python
import functools

import jax
import jax.numpy as jnp
import numpy as np
from jax import lax
from jax.experimental import pallas as pl
from jax.experimental.pallas import tpu as pltpu
from jax.sharding import PartitionSpec as P

ITERS = 3
SWEEPS = 6

mass_weight = 4.0
bound_low = 0.1
bound_high = 2.0
centre = (bound_high + bound_low) / 2.0
half_width = (bound_high - bound_low) / 2.0

F32 = jnp.float32
BF16 = jnp.bfloat16
ROW = 96


def chebyshev():
    ratio = centre / half_width
    rho = 1.0 / ratio
    coefs = [(0.0, 1.0 / centre)]
    for _ in range(SWEEPS - 1):
        rho_next = 1.0 / (2.0 * ratio - rho)
        coefs.append((rho_next * rho, 2.0 * rho_next / half_width))
        rho = rho_next
    return coefs


def wave_tables(mode_count):
    column = np.arange(mode_count)
    number = np.where(column == 1, mode_count // 2, column // 2)
    is_sine = (column % 2 == 1) & (column > 1)
    planes = np.arange(mode_count)
    angles = (planes[:, None] * number[None, :] % mode_count) * (2.0 * np.pi / mode_count)
    cosine, sine = np.cos(angles), np.sin(angles)
    synthesis = np.where(is_sine[None, :], sine, cosine)
    factor = number / (mode_count // 2)
    derivative = np.where(is_sine[None, :], cosine, -sine) * factor[None, :]
    derivative = np.where(column[None, :] > 1, derivative, 0.0)
    weights = np.where(column < 2, 1.0 / mode_count, 2.0 / mode_count)
    return synthesis, derivative, synthesis.T * weights[:, None]


def halves(table):
    high = table.astype(np.float32).astype(BF16)
    return [high, (table - high.astype(np.float64)).astype(np.float32).astype(BF16)]


def split(value):
    high = value.astype(BF16)
    return high, (value - high.astype(F32)).astype(BF16)


def dot(a, b):
    return lax.dot_general(a, b, (((1,), (0,)), ((), ())), preferred_element_type=F32)


def rows_times(value, high, low):
    count = value.shape[0]
    h, l = split(value)
    both = dot(jnp.concatenate([h, l], axis=0), high)
    return both[:count] + both[count:] + dot(h, low)


def table_times(high, low, value):
    count = value.shape[1]
    h, l = split(value)
    both = dot(high, jnp.concatenate([h, l], axis=1))
    return both[:, :count] + both[:, count:] + dot(low, h)


def iota(shape, dim):
    return lax.broadcasted_iota(jnp.int32, shape, dim)


def call(kernel, outs, vmem, limit, scratch=(), flops=0, moved=1 << 20, far=(), out_far=(), pinned=()):
    in_specs, given = [], []
    for i, v in enumerate(vmem):
        space = pltpu.HBM if i in far else pltpu.VMEM
        in_specs.append(pl.BlockSpec(memory_space=space))
        fixed = i in far or v.dtype == BF16 and v.shape[0] == v.shape[1]
        given.append(pltpu.with_memory_space_constraint(v, space) if fixed else v)
    shapes, out_specs = [], []
    for i, (s, t) in enumerate(outs):
        space = pltpu.HBM if i in out_far else pltpu.VMEM
        out_specs.append(pl.BlockSpec(memory_space=space))
        shapes.append(space(s, t) if i in out_far or i in pinned else jax.ShapeDtypeStruct(s, t))
    return pl.pallas_call(
        kernel,
        out_shape=shapes,
        in_specs=in_specs,
        out_specs=out_specs,
        scratch_shapes=list(scratch),
        compiler_params=pltpu.CompilerParams(vmem_limit_bytes=limit << 20),
        cost_estimate=pl.CostEstimate(flops=flops, bytes_accessed=moved, transcendentals=0),
    )(*given)


def position():
    q = lax.axis_index("dom")
    z = lax.shift_right_arithmetic(q, 1)
    return q, z, q - 2 * z


def picked(first, a, b):
    return jnp.where(first, a, b)


def order_kernel(
    iface_in, l2g_in, vel_in, mass_in, live_in, keep, send, chunks, place_out, iface, l2g, vel, mass, live, sems
):
    q, _, x = position()
    pairs = ((iface_in, iface), (l2g_in, l2g), (vel_in, vel), (mass_in, mass), (live_in, live))
    copies = [pltpu.make_async_copy(a, b, sems.at[i]) for i, (a, b) in enumerate(pairs)]
    for copy in copies:
        copy.start()
    for copy in copies:
        copy.wait()
    count = mass.shape[1]
    face = iface.shape[1]
    lists = jnp.concatenate(
        [picked(x == 0, iface[0:1, :], iface[1:2, :]), picked(x == 0, iface[1:2, :], iface[0:1, :])], axis=1
    ).astype(F32)
    lists = jnp.transpose(jnp.broadcast_to(lists, (8, 2 * face)))[:, 0:1]
    hit = jnp.where(lists == iota((2 * face, count), 1).astype(F32), 1.0, 0.0)
    at = jnp.sum(hit * iota((2 * face, count), 0).astype(F32), axis=0, keepdims=True)
    shared = jnp.sum(hit, axis=0, keepdims=True)
    rest = jnp.broadcast_to(1.0 - shared, (8, count))
    lane = iota((8, count), 1)
    run = rest
    step = 1
    while step < count:
        run = run + jnp.where(lane >= step, pltpu.roll(run, step, 1), 0.0)
        step *= 2
    place = jnp.where(rest > 0.5, run - 1.0 + 2.0 * face, jnp.broadcast_to(at, (8, count)))
    place_out[...] = place
    column = jnp.transpose(place)[:, 0:1]
    elems, side = l2g.shape
    slots = elems * ROW
    blank = jnp.full((1, ROW - side), -1, jnp.int32)
    row = jnp.concatenate([piece for e in range(elems) for piece in (l2g[e : e + 1, :], blank)], axis=1)
    pieces = []
    for first in range(0, slots, 512):
        part = row[:, first : first + 512]
        found = jnp.where(iota((count, 512), 0) == part, column, 0.0)
        pieces.append(jnp.where(part < 0, -1.0, jnp.sum(found, axis=0, keepdims=True)))
    index = jnp.concatenate(pieces, axis=1)
    unit = jnp.where(iota((count, count), 1).astype(F32) == column, 1.0, 0.0).astype(BF16)
    modes = vel.shape[0]
    half = modes // 2
    value = jnp.concatenate([vel[...], jnp.broadcast_to(mass[...], (16, count))], axis=0)
    high = value.astype(BF16)
    middle, low = split(value - high.astype(F32))
    total = modes + 16
    parts = dot(jnp.concatenate([high, middle, low], axis=0), unit)
    moved = parts[:total] + parts[total : 2 * total] + parts[2 * total :]
    a, b = moved[:half], moved[half:modes]
    lived = jnp.where(iota(live.shape, 1) == q, live[...], 0).astype(F32)
    lived = jnp.sum(lived, axis=1, keepdims=True)
    for ref, rows in ((keep, picked(x == 0, a, b)), (send, picked(x == 0, b, a))):
        ref[0:half, :] = rows
        ref[half : half + 8, :] = moved[modes : modes + 8]
        ref[half + 8 : half + 16, :] = jnp.broadcast_to(index[:, :count], (8, count))
        ref[half + 16 : half + 24, 0 : slots - count] = jnp.broadcast_to(
            index[:, count:], (8, slots - count)
        )
        ref[half + 16 : half + 24, slots - count :] = jnp.broadcast_to(lived, (8, 2 * count - slots))
    quarter = count // chunks.shape[0]
    for part in range(chunks.shape[0]):
        chunks[part] = moved[:modes, part * quarter : (part + 1) * quarter]


def own_build_kernel(half, ops_in, pack, high_out, low_out, diag, note, ops, high, low, *scratch):
    sems = scratch[-1]
    fetch = pltpu.make_async_copy(ops_in, ops, sems.at[0])
    fetch.start()
    build_kernel(half, ops, pack, high_out, low_out, diag, note, high, low, *scratch, ready=fetch.wait)


def build_kernel(
    half, ops, pack, high_out, low_out, diag, note, high, low, flat, tall, qh, ql, pad, sems, ready=None
):
    live = pack[half + 16 : half + 17, pack.shape[1] - 1 :]
    side, elems = ops.shape[0], ops.shape[1]
    count = high.shape[0]
    slots = elems * ROW
    index = jnp.concatenate(
        [pack[half + 8 : half + 16, :], pack[half + 16 : half + 24, 0 : slots - count]], axis=1
    )
    column = jnp.transpose(index)[:, 0:1]
    for first in range(0, slots, 256):
        block = jnp.where(iota((256, count), 1).astype(F32) == column[first : first + 256], 1.0, 0.0)
        tall[first : first + 256, :] = block.astype(BF16)
    tall[slots:, :] = jnp.zeros((tall.shape[0] - slots, count), BF16)
    for first in range(0, count, 256):
        block = jnp.where((iota((256, slots), 0) + first).astype(F32) == index[0:1], 1.0, 0.0)
        flat[first : first + 256, :] = block.astype(BF16)
    pad[...] = jnp.zeros(pad.shape, F32)
    if ready is not None:
        ready()
    for e in range(elems):
        pad[0:side, 0:side] = ops[:, e, :] * jnp.where(live > e + 0.5, 1.0, 0.0)
        oh, ol = split(pad[...])
        spread = dot(jnp.concatenate([oh, ol], axis=0), tall[e * ROW : e * ROW + 128, :])
        qh[e * ROW : (e + 1) * ROW, :] = spread[:ROW].astype(BF16)
        ql[e * ROW : (e + 1) * ROW, :] = spread[ROW:].astype(BF16)
    tile = 256
    face = note.shape[1]
    copies = []
    for j in range(0, count, tile):
        top = j + tile
        block = dot(flat[j:top, :], qh[:, j:]) + dot(flat[j:top, :], ql[:, j:])
        h, l = split(block)
        high[j:top, j:] = h
        low[j:top, j:] = l
        for part, out in ((high, high_out), (low, low_out)):
            rows = pl.ds(j, tile)
            copies.append(pltpu.make_async_copy(part.at[rows], out.at[rows], sems.at[len(copies) + 1]))
            copies[-1].start()
        if top < count:
            mirror = jnp.transpose(block[:, tile:])
            h, l = split(mirror)
            high[top:, j:top] = h
            low[top:, j:top] = l
        own_node = iota((tile, tile), 0) == iota((tile, tile), 1)
        line = jnp.sum(jnp.where(own_node, block[:, :tile], 0.0), axis=0, keepdims=True)
        diag[:, j:top] = jnp.broadcast_to(line, (8, tile))
        if not j:
            note[0:face, :] = block[0:face, 0:face]
            note[face : face + 8, :] = jnp.broadcast_to(line[:, 0:face], (8, face))
            note[face + 8 :, :] = pack[half : half + 8, 0:face]
    for copy in copies:
        copy.wait()


def apply(value, mats, columns, half):
    oh, ol, ph, plo = mats
    return jnp.concatenate(
        [
            rows_times(value[:half], oh[:, columns], ol[:, columns]),
            rows_times(value[half:], ph[:, columns], plo[:, columns]),
        ],
        axis=0,
    )


def assembled(y, outer, half, face):
    inner = y[:half, face : 2 * face] + y[half:, face : 2 * face]
    first = y[:, :face] if outer is None else y[:, :face] + outer
    return jnp.concatenate([first, jnp.concatenate([inner, inner], axis=0), y[:, 2 * face :]], axis=1)


def first_planes_kernel(u_in, tables_in, slope_in, out, u, tables, slope, sems):
    rows = 4 * slope.shape[1]
    parts = [pl.ds(0, rows), pl.ds(rows, tables.shape[0] - rows)]
    pairs = [(u_in, u), (slope_in, slope)] + [(tables_in.at[p], tables.at[p]) for p in parts]
    copies = [pltpu.make_async_copy(a, b, sems.at[i]) for i, (a, b) in enumerate(pairs)]
    for copy in copies:
        copy.start()
    for copy in copies[:3]:
        copy.wait()
    planes_kernel(u, tables, slope, out, copies[3].wait)


def planes_kernel(u, tables, slope, out, ready=None):
    count = slope.shape[1]
    both = table_times(tables[0 : 2 * count, :], tables[2 * count : 4 * count, :], u[...])
    rate = jnp.transpose(jnp.broadcast_to(slope[...], (8, count)))[:, 0:1]
    cross = rate * both[:count] * both[count:]
    if ready is not None:
        ready()
    out[...] = table_times(tables[4 * count : 5 * count, :], tables[5 * count :, :], cross)


def provisional(r, d, g, inv, cm, mats, alpha, beta, half, face):
    r = r - inv * assembled(g, None, half, face)
    d = alpha * d + beta * r if alpha else beta * r
    y = apply(d, mats, slice(0, face), half) + cm[:, :face] * d[:, :face]
    return r, d, y


def even():
    _, z, x = position()
    return lax.rem(x + z, 2) == 0


def put(one, two, g, y, half, face, notes=((), ())):
    own = jnp.concatenate([g[:half, :face], y[:half], *notes[0]], axis=0)
    oth = jnp.concatenate([g[half:, :face], y[half:], *notes[1]], axis=0)
    first = even()
    one[...] = picked(first, own, oth)
    two[...] = picked(first, oth, own)


def got(one, two):
    a, b = one[...], two[...]
    first = even()
    return picked(first, a, b), picked(first, b, a)


def received(conv, half):
    _, _, x = position()
    parts = conv.shape[0]
    return jnp.concatenate(
        [
            jnp.concatenate([conv[m, x] for m in range(parts)], axis=1),
            jnp.concatenate([conv[m, 1 - x] for m in range(parts)], axis=1),
        ],
        axis=0,
    )


def masses(own, oth, half):
    count = own.shape[1]
    return jnp.concatenate(
        [jnp.broadcast_to(m[half : half + 1, :], (half, count)) for m in (own, oth)], axis=0
    )


def helmholtz(half, mode_count):
    _, _, x = position()
    mode = lax.axis_index("mode") * (2 * half) + x * half + iota((half, 1), 0)
    number = jnp.where(mode == 1, mode_count // 2, lax.shift_right_arithmetic(mode, 1))
    return mass_weight + (8.0 * number.astype(F32) / mode_count) ** 2


def first_source_kernel(
    half, face, mode_count, conv, own, oth, do, dp, note_o, note_p, oh_in, ol_in, ph_in, plo_in,
    oh, ol, ph, plo, r_out, d_out, v_out, conv_out, inv_out, cm_out, one, two, sems,
):
    mats = (oh, ol, ph, plo)
    copies = [
        pltpu.make_async_copy(a, b, sems.at[i]) for i, (a, b) in enumerate(zip((oh_in, ol_in, ph_in, plo_in), mats))
    ]
    for copy in copies:
        copy.start()
    c = helmholtz(half, mode_count)
    c = jnp.concatenate([c, c], axis=0)
    mass = masses(own, oth, half)
    stiff = jnp.concatenate([jnp.broadcast_to(t[0:1, :], (half, t.shape[1])) for t in (do, dp)], axis=0)
    inv = 1.0 / (assembled(stiff, None, half, face) + c * assembled(mass, None, half, face))
    inv = jnp.concatenate([jnp.zeros((2 * half, face), F32), inv[:, face:]], axis=1)
    inv_out[...] = inv
    cm = c * mass
    cm_out[...] = cm
    v = jnp.concatenate([own[0:half, :], oth[0:half, :]], axis=0)
    v_out[...] = v
    new = received(conv, half)
    conv_out[...] = new
    m4 = mass_weight * mass
    copies[0].wait()
    copies[1].wait()
    e_own = rows_times(v[:half], oh[...], ol[...])
    copies[2].wait()
    copies[3].wait()
    e_oth = rows_times(v[half:], ph[...], plo[...])
    g = jnp.concatenate([e_own, e_oth], axis=0) + (cm - m4) * v - m4 * new
    r = -inv * assembled(g, None, half, face)
    d = (1.0 / centre) * r
    r_out[...] = r
    d_out[...] = d
    y = apply(d, mats, slice(0, face), half)
    put(one, two, g, y, half, face, ((note_o[...],), (note_p[...],)))


def source_kernel(half, face, conv, old, own, oth, r, d, inv, cm, oh, ol, ph, plo, r_out, d_out, conv_out, one, two):
    mats = (oh, ol, ph, plo)
    new = received(conv, half)
    conv_out[...] = new
    cmv, dv = cm[...], d[...]
    g = apply(dv, mats, slice(None), half) + cmv * dv - mass_weight * masses(own, oth, half) * (new - old[...])
    rv, dv, y = provisional(r[...], None, g, inv[...], cmv, mats, 0.0, 1.0 / centre, half, face)
    r_out[...] = rv
    d_out[...] = dv
    put(one, two, g, y, half, face)


def rest_kernel(half, face, now, r, d, sol, s1, s2, inv, cm, oh, ol, ph, plo, r_out, d_out, sol_out):
    dv = d[...]
    y = apply(dv, (oh, ol, ph, plo), slice(face, None), half) + cm[:, face:] * dv[:, face:]
    y = jnp.concatenate([stacked(got(s1, s2), half, 2 * half), y], axis=1)
    rv = r[...] - inv[...] * assembled(y, None, half, face)
    dn = now[0] * dv + now[1] * rv
    r_out[...] = rv
    d_out[...] = dn
    sol_out[...] = sol[...] + dv + dn


def change_of(dd, theirs, mats, na, nb, half, face):
    oh, ol, ph, plo = mats
    change = jnp.concatenate(
        [
            rows_times(dd[:half], oh[0:face, :], ol[0:face, :]),
            rows_times(dd[half:], ph[0:face, :], plo[0:face, :]),
        ],
        axis=0,
    )
    their_change = jnp.concatenate(
        [rows_times(theirs[:half], *split(nb)), rows_times(theirs[half:], *split(na))], axis=0
    )
    return change, their_change


def stacked(pair, first, last):
    return jnp.concatenate([t[first:last, :] for t in pair], axis=0)


def widened(value, face_part):
    face = face_part.shape[1]
    return jnp.concatenate([value[:, :face] + face_part, value[:, face:]], axis=1)


def corrected(half, face, now, r, d, sol, dr, dd, change, outer, inv):
    back = widened(-inv * assembled(change, outer, half, face), dr)
    step = widened(now[1] * back, now[0] * dd)
    return r + back, d + step, widened(sol + step, dd)


def exact(half, face, beta, now, r, d, sol, sent, came, na, nb, inv, cm, cmn, mats):
    inv_face = inv[:, :face]
    mine, came = got(*sent), got(*came)
    dr = -(inv_face * stacked(came, 0, half))
    dd = beta * dr
    theirs = -beta * (inv_face * stacked(mine, 0, half))
    change, their_change = change_of(dd, theirs, mats, na[...], nb[...], half, face)
    change = widened(change, cm[:, :face] * dd)
    outer = stacked(came, half, 2 * half) + their_change + cmn[...] * theirs
    return corrected(half, face, now, r[...], d[...], sol[...], dr, dd, change, outer, inv[...])


def first_sweep_kernel(
    half, face, mode_count, before, now, then,
    r, d, sol, s1, s2, c1, c2, inv, cm, oh, ol, ph, plo,
    r_out, d_out, sol_out, inv_out, cmn_out, na_out, nb_out, one, two,
):
    mats = (oh, ol, ph, plo)
    cm_v = cm[...]
    mine, came = got(s1, s2), got(c1, c2)
    c = helmholtz(half, mode_count)
    c = jnp.concatenate([c, c], axis=0)

    def line(pair, row):
        return jnp.concatenate([jnp.broadcast_to(t[row : row + 1, :], (half, face)) for t in pair], axis=0)

    at = 2 * half + face
    their_mass = line(came, at + 8)
    inv_face = 1.0 / (line(mine, at) + line(came, at) + c * (line(mine, at + 8) + their_mass))
    cmn = c * their_mass
    nb, na = (t[2 * half : at, :] for t in came)
    dr = -inv_face * (stacked(mine, 0, half) + stacked(came, 0, half))
    dd = before[1] * dr
    change, their_change = change_of(dd, dd, mats, na, nb, half, face)
    change = widened(change, cm_v[:, :face] * dd)
    outer = stacked(mine, half, 2 * half) + stacked(came, half, 2 * half) + their_change + cmn * dd
    inv_v = jnp.concatenate([inv_face, inv[:, face:]], axis=1)
    rv, dn, sol_v = corrected(half, face, now, r[...], d[...], sol[...], dr, dd, change, outer, inv_v)
    inv_out[...] = inv_v
    cmn_out[...] = cmn
    na_out[...] = na
    nb_out[...] = nb
    sol_out[...] = sol_v
    g = apply(dn, mats, slice(None), half) + cm_v * dn
    rv, dv, y = provisional(rv, dn, g, inv_v, cm_v, mats, then[0], then[1], half, face)
    r_out[...] = rv
    d_out[...] = dv
    put(one, two, g, y, half, face)


def sweep_kernel(
    half, face, before, now, then,
    r, d, sol, s1, s2, c1, c2, na, nb, inv, cm, cmn, oh, ol, ph, plo,
    r_out, d_out, sol_out, one, two,
):
    mats = (oh, ol, ph, plo)
    rv, dn, sol_v = exact(half, face, before[1], now, r, d, sol, (s1, s2), (c1, c2), na, nb, inv, cm, cmn, mats)
    sol_out[...] = sol_v
    inv_v, cm_v = inv[...], cm[...]
    g = apply(dn, mats, slice(None), half) + cm_v * dn
    rv, dv, y = provisional(rv, dn, g, inv_v, cm_v, mats, then[0], then[1], half, face)
    r_out[...] = rv
    d_out[...] = dv
    put(one, two, g, y, half, face)


def last_kernel(
    half, face, before, now,
    r, d, sol, s1, s2, c1, c2, na, nb, inv, cm, cmn, oh, ol, ph, plo,
    r_out, d_out, sol_out, chunks,
):
    rv, dn, new = exact(
        half, face, before[1], now, r, d, sol, (s1, s2), (c1, c2), na, nb, inv, cm, cmn, (oh, ol, ph, plo)
    )
    r_out[...] = rv
    d_out[...] = dn
    sol_out[...] = new
    _, _, x = position()
    parts, width = chunks.shape[0], chunks.shape[3]
    for m in range(parts):
        chunks[m, x] = new[:half, m * width : (m + 1) * width]
        chunks[m, 1 - x] = new[half:, m * width : (m + 1) * width]


def end_kernel(
    half, face, before, now,
    r, d, sol, s1, s2, c1, c2, na, nb, inv, cm, cmn, oh, ol, ph, plo, own_out, oth_out,
):
    _, _, new = exact(
        half, face, before[1], now, r, d, sol, (s1, s2), (c1, c2), na, nb, inv, cm, cmn, (oh, ol, ph, plo)
    )
    own_out[...] = new[:half]
    oth_out[...] = new[half:]


def restored(value, unit):
    count = value.shape[0]
    high = value.astype(BF16)
    middle, low = split(value - high.astype(F32))
    parts = dot(jnp.concatenate([high, middle, low], axis=0), unit)
    return parts[:count] + parts[count : 2 * count] + parts[2 * count :]


def finish_own_kernel(own, place, out, unit_out):
    count = own.shape[1]
    unit = jnp.where(iota((count, count), 0).astype(F32) == place[0:1, :], 1.0, 0.0).astype(BF16)
    unit_out[...] = unit
    out[...] = restored(own[...], unit)


def finish_kernel(own, other, unit, out):
    _, _, x = position()
    a, b = own[...], restored(other[...], unit[...])
    half = own.shape[0]
    out[0:half, :] = picked(x == 0, a, b)
    out[half:, :] = picked(x == 0, b, a)


def body(n_mode, n_dom, velocity_prev, elem_ops, lumped_mass, span_slope, local_to_global, iface_nodes, live_elems):
    modes, count = velocity_prev.shape
    half = modes // 2
    elems, side = local_to_global.shape
    face = iface_nodes.shape[2]
    mode_count = span_slope.shape[0]
    quarter = count // n_mode
    pairs = n_dom // 2
    slots = elems * ROW
    places = [(z, s) for z in range(pairs) for s in (0, 1)]
    swap = [(i, i ^ 1) for i in range(n_dom)]
    long_swap = [(2 * z + s, 2 * ((z + (1 if z % 2 else -1)) % pairs) + s) for z, s in places]
    short_swap = [(2 * z + s, 2 * ((z + (-1 if z % 2 else 1)) % pairs) + s) for z, s in places]
    groups = [[m * n_dom + 2 * z + s for m in range(n_mode) for s in (0, 1)] for z in range(pairs)]

    def exchange(one, two):
        return lax.ppermute(one, "dom", long_swap), lax.ppermute(two, "dom", short_swap)

    ops = jnp.transpose(elem_ops, (1, 0, 2))
    ops_other = lax.ppermute(ops, "dom", swap)
    pack = (half + 24, count)
    wide = (2 * half, count)
    keep, send, chunks, place = call(
        order_kernel,
        [(pack, F32), (pack, F32), ((n_mode, modes, quarter), F32), ((8, count), F32)],
        [iface_nodes[0], local_to_global, velocity_prev, lumped_mass.reshape(1, count), live_elems.reshape(1, n_dom)],
        24, far=range(5),
        scratch=[
            pltpu.VMEM((2, face), jnp.int32), pltpu.VMEM((elems, side), jnp.int32),
            pltpu.VMEM((modes, count), F32), pltpu.VMEM((1, count), F32), pltpu.VMEM((1, n_dom), jnp.int32),
            pltpu.SemaphoreType.DMA((5,)),
        ],
    )
    planes_in = lax.all_to_all(chunks, "mode", 0, 0, tiled=True)
    oth = lax.ppermute(send, "dom", swap)

    def build(own, ops, packed):
        matrix = ((count, count), BF16)
        scratch = [
            pltpu.VMEM((count, count), BF16),
            pltpu.VMEM((count, count), BF16),
            pltpu.VMEM((count, slots), BF16),
            pltpu.VMEM((slots + 32, count), BF16),
            pltpu.VMEM((slots, count), BF16),
            pltpu.VMEM((slots, count), BF16),
            pltpu.VMEM((ROW, 128), F32),
            pltpu.SemaphoreType.DMA((2 * count // 256 + 1,)),
        ]
        return call(
            functools.partial(own_build_kernel if own else build_kernel, half),
            [matrix, matrix, ((8, count), F32), ((face + 16, face), F32)], [ops, packed], 36,
            far=(0,) if own else (), out_far=(0, 1), flops=6 << 30,
            scratch=[pltpu.VMEM((side, elems, side), F32), *scratch] if own else scratch,
        )

    oh, ol, do, note_o = build(True, ops, keep)
    synthesis, derivative, analysis = wave_tables(mode_count)
    tables = jnp.asarray(np.concatenate(halves(np.concatenate([synthesis, derivative])) + halves(analysis)))
    slope = span_slope.reshape(1, mode_count)

    def convect(value, first):
        (out,) = call(
            first_planes_kernel if first else planes_kernel, [((mode_count, quarter), F32)],
            [value.reshape(mode_count, quarter), tables, slope], 16, flops=600 << 20, far=range(3) if first else (),
            scratch=[
                pltpu.VMEM((mode_count, quarter), F32), pltpu.VMEM(tables.shape, BF16),
                pltpu.VMEM(slope.shape, F32), pltpu.SemaphoreType.DMA((4,)),
            ] if first else (),
        )
        back = lax.all_to_all(
            out.reshape(2 * n_mode, half, quarter), ("mode", "dom"), 0, 0, axis_index_groups=groups, tiled=True
        )
        return back.reshape(n_mode, 2, half, quarter)

    conv = convect(planes_in, True)
    ph, plo, dp, note_p = build(False, ops_other, oth)
    mats = [oh, ol, ph, plo]
    coefs = chebyshev()
    message = ((2 * half, face), F32)
    for iteration in range(ITERS):
        if iteration == 0:
            long_message = ((2 * half + face + 16, face), F32)
            *mats, r, d, sol, old, inv, cm, one, two = call(
                functools.partial(first_source_kernel, half, face, mode_count),
                [((count, count), BF16)] * 4 + [(wide, F32)] * 6 + [long_message, long_message],
                [conv, keep, oth, do, dp, note_o, note_p, *mats], 20, flops=500 << 20,
                far=range(7, 11), pinned=range(4), scratch=[pltpu.SemaphoreType.DMA((4,))],
            )
        else:
            r, d, old, one, two = call(
                functools.partial(source_kernel, half, face),
                [(wide, F32), (wide, F32), (wide, F32), message, message],
                [conv, old, keep, oth, r, d, inv, cm, *mats], 20, flops=500 << 20,
            )
        for k in (0, 2, 4):
            c1, c2 = exchange(one, two)
            r, d, sol = call(
                functools.partial(rest_kernel, half, face, coefs[k + 1]), [(wide, F32)] * 3,
                [r, d, sol, one, two, inv, cm, *mats], 20, flops=400 << 20,
            )
            if iteration == 0 and k == 0:
                r, d, sol, inv, cmn, na, nb, one, two = call(
                    functools.partial(first_sweep_kernel, half, face, mode_count, coefs[0], coefs[1], coefs[2]),
                    [(wide, F32)] * 4 + [((2 * half, face), F32)] + [((face, face), F32)] * 2 + [message, message],
                    [r, d, sol, one, two, c1, c2, inv, cm, *mats], 20, flops=500 << 20,
                )
                continue
            given = [r, d, sol, one, two, c1, c2, na, nb, inv, cm, cmn, *mats]
            if k < 4:
                r, d, sol, one, two = call(
                    functools.partial(sweep_kernel, half, face, coefs[k], coefs[k + 1], coefs[k + 2]),
                    [(wide, F32), (wide, F32), (wide, F32), message, message], given, 20, flops=500 << 20,
                )
            elif iteration < ITERS - 1:
                r, d, sol, chunks = call(
                    functools.partial(last_kernel, half, face, coefs[k], coefs[k + 1]),
                    [(wide, F32), (wide, F32), (wide, F32), ((n_mode, 2, half, quarter), F32)],
                    given, 20, flops=100 << 20,
                )
            else:
                own, other = call(
                    functools.partial(end_kernel, half, face, coefs[k], coefs[k + 1]),
                    [((half, count), F32)] * 2, given, 20, flops=100 << 20,
                )
        if iteration < ITERS - 1:
            planes_in = lax.all_to_all(
                chunks.reshape(2 * n_mode, half, quarter), ("mode", "dom"), 0, 0, axis_index_groups=groups, tiled=True
            )
            conv = convect(planes_in, False)
    other = lax.ppermute(other, "dom", swap)
    own, unit = call(
        finish_own_kernel, [((half, count), F32), ((count, count), BF16)], [own, place], 16, flops=200 << 20
    )
    (out,) = call(finish_kernel, [((modes, count), F32)], [own, other, unit], 16)
    return out


def solution(mesh):
    placed = (
        P("mode", "dom"),
        P("dom", None, None),
        P("dom"),
        P(),
        P("dom", None),
        P("dom", None, None),
        P(),
    )
    return jax.shard_map(
        functools.partial(body, mesh.shape["mode"], mesh.shape["dom"]),
        mesh=mesh, in_specs=placed, out_specs=P("mode", "dom"), check_vma=False,
    )
```

```python
import functools

import jax
import jax.numpy as jnp
import numpy as np
from jax import lax
from jax.experimental import pallas as pl
from jax.experimental.pallas import tpu as pltpu
from jax.sharding import PartitionSpec as P

ITERS = 3
SWEEPS = 6

mass_weight = 4.0
bound_low = 0.1
bound_high = 2.0
centre = (bound_high + bound_low) / 2.0
half_width = (bound_high - bound_low) / 2.0

F32 = jnp.float32
BF16 = jnp.bfloat16
ROW = 96


def chebyshev():
    ratio = centre / half_width
    rho = 1.0 / ratio
    coefs = [(0.0, 1.0 / centre)]
    for _ in range(SWEEPS - 1):
        rho_next = 1.0 / (2.0 * ratio - rho)
        coefs.append((rho_next * rho, 2.0 * rho_next / half_width))
        rho = rho_next
    return coefs


def wave_tables(mode_count):
    column = np.arange(mode_count)
    number = np.where(column == 1, mode_count // 2, column // 2)
    is_sine = (column % 2 == 1) & (column > 1)
    planes = np.arange(mode_count)
    angles = (planes[:, None] * number[None, :] % mode_count) * (2.0 * np.pi / mode_count)
    cosine, sine = np.cos(angles), np.sin(angles)
    synthesis = np.where(is_sine[None, :], sine, cosine)
    factor = number / (mode_count // 2)
    derivative = np.where(is_sine[None, :], cosine, -sine) * factor[None, :]
    derivative = np.where(column[None, :] > 1, derivative, 0.0)
    weights = np.where(column < 2, 1.0 / mode_count, 2.0 / mode_count)
    return synthesis, derivative, synthesis.T * weights[:, None]


def halves(table):
    high = table.astype(np.float32).astype(BF16)
    return [high, (table - high.astype(np.float64)).astype(np.float32).astype(BF16)]


def split(value):
    high = value.astype(BF16)
    return high, (value - high.astype(F32)).astype(BF16)


def dot(a, b):
    return lax.dot_general(a, b, (((1,), (0,)), ((), ())), preferred_element_type=F32)


def rows_times(value, high, low):
    count = value.shape[0]
    h, l = split(value)
    both = dot(jnp.concatenate([h, l], axis=0), high)
    return both[:count] + both[count:] + dot(h, low)


def table_times(high, low, value):
    count = value.shape[1]
    h, l = split(value)
    both = dot(high, jnp.concatenate([h, l], axis=1))
    return both[:, :count] + both[:, count:] + dot(low, h)


def iota(shape, dim):
    return lax.broadcasted_iota(jnp.int32, shape, dim)


def call(kernel, outs, vmem, limit, scratch=(), flops=0, moved=1 << 20, far=(), out_far=(), pinned=(), free=()):
    in_specs, given = [], []
    for i, v in enumerate(vmem):
        space = pltpu.HBM if i in far else pltpu.VMEM
        in_specs.append(pl.BlockSpec(memory_space=space))
        fixed = i in far or v.dtype == BF16 and v.shape not in free
        given.append(pltpu.with_memory_space_constraint(v, space) if fixed else v)
    shapes, out_specs = [], []
    for i, (s, t) in enumerate(outs):
        space = pltpu.HBM if i in out_far else pltpu.VMEM
        out_specs.append(pl.BlockSpec(memory_space=space))
        shapes.append(space(s, t) if i in out_far or i in pinned else jax.ShapeDtypeStruct(s, t))
    return pl.pallas_call(
        kernel,
        out_shape=shapes,
        in_specs=in_specs,
        out_specs=out_specs,
        scratch_shapes=list(scratch),
        compiler_params=pltpu.CompilerParams(vmem_limit_bytes=limit << 20),
        cost_estimate=pl.CostEstimate(flops=flops, bytes_accessed=moved, transcendentals=0),
    )(*given)


def position():
    q = lax.axis_index("dom")
    z = lax.shift_right_arithmetic(q, 1)
    return q, z, q - 2 * z


def picked(first, a, b):
    return jnp.where(first, a, b)


def order_kernel(
    iface_in, l2g_in, vel_in, mass_in, live_in, keep, send, chunks, place_out, iface, l2g, vel, mass, live, sems
):
    q, _, x = position()
    pairs = ((iface_in, iface), (l2g_in, l2g), (vel_in, vel), (mass_in, mass), (live_in, live))
    copies = [pltpu.make_async_copy(a, b, sems.at[i]) for i, (a, b) in enumerate(pairs)]
    for copy in copies:
        copy.start()
    for copy in copies:
        copy.wait()
    count = mass.shape[1]
    face = iface.shape[1]
    lists = jnp.concatenate(
        [picked(x == 0, iface[0:1, :], iface[1:2, :]), picked(x == 0, iface[1:2, :], iface[0:1, :])], axis=1
    ).astype(F32)
    lists = jnp.transpose(jnp.broadcast_to(lists, (8, 2 * face)))[:, 0:1]
    hit = jnp.where(lists == iota((2 * face, count), 1).astype(F32), 1.0, 0.0)
    at = jnp.sum(hit * iota((2 * face, count), 0).astype(F32), axis=0, keepdims=True)
    shared = jnp.sum(hit, axis=0, keepdims=True)
    rest = jnp.broadcast_to(1.0 - shared, (8, count))
    lane = iota((8, count), 1)
    run = rest
    step = 1
    while step < count:
        run = run + jnp.where(lane >= step, pltpu.roll(run, step, 1), 0.0)
        step *= 2
    place = jnp.where(rest > 0.5, run - 1.0 + 2.0 * face, jnp.broadcast_to(at, (8, count)))
    place_out[...] = place
    column = jnp.transpose(place)[:, 0:1]
    elems, side = l2g.shape
    slots = elems * ROW
    blank = jnp.full((1, ROW - side), -1, jnp.int32)
    row = jnp.concatenate([piece for e in range(elems) for piece in (l2g[e : e + 1, :], blank)], axis=1)
    pieces = []
    for first in range(0, slots, 512):
        part = row[:, first : first + 512]
        found = jnp.where(iota((count, 512), 0) == part, column, 0.0)
        pieces.append(jnp.where(part < 0, -1.0, jnp.sum(found, axis=0, keepdims=True)))
    index = jnp.concatenate(pieces, axis=1)
    unit = jnp.where(iota((count, count), 1).astype(F32) == column, 1.0, 0.0).astype(BF16)
    modes = vel.shape[0]
    half = modes // 2
    value = jnp.concatenate([vel[...], jnp.broadcast_to(mass[...], (16, count))], axis=0)
    high = value.astype(BF16)
    middle, low = split(value - high.astype(F32))
    total = modes + 16
    parts = dot(jnp.concatenate([high, middle, low], axis=0), unit)
    moved = parts[:total] + parts[total : 2 * total] + parts[2 * total :]
    a, b = moved[:half], moved[half:modes]
    lived = jnp.where(iota(live.shape, 1) == q, live[...], 0).astype(F32)
    lived = jnp.sum(lived, axis=1, keepdims=True)
    for ref, rows in ((keep, picked(x == 0, a, b)), (send, picked(x == 0, b, a))):
        ref[0:half, :] = rows
        ref[half : half + 8, :] = moved[modes : modes + 8]
        ref[half + 8 : half + 16, :] = jnp.broadcast_to(index[:, :count], (8, count))
        ref[half + 16 : half + 24, 0 : slots - count] = jnp.broadcast_to(
            index[:, count:], (8, slots - count)
        )
        ref[half + 16 : half + 24, slots - count :] = jnp.broadcast_to(lived, (8, 2 * count - slots))
    quarter = count // chunks.shape[0]
    for part in range(chunks.shape[0]):
        chunks[part] = moved[:modes, part * quarter : (part + 1) * quarter]


def own_build_kernel(half, ops_in, pack, high_out, low_out, diag, note, ops, high, low, *scratch):
    sems = scratch[-1]
    fetch = pltpu.make_async_copy(ops_in, ops, sems.at[0])
    fetch.start()
    copies = []

    def ship(*rows):
        for part, out in ((high, high_out), (low, low_out)):
            at = pl.ds(*rows)
            copies.append(pltpu.make_async_copy(part.at[at], out.at[at], sems.at[len(copies) + 1]))
            copies[-1].start()

    build_kernel(half, ops, pack, high, low, diag, note, *scratch[:-1], ready=fetch.wait, ship=ship)
    for copy in copies:
        copy.wait()


def partner_build_kernel(half, ops, pack, high_in, low_in, high_own, low_own, high, low, diag, note, *scratch):
    sems = scratch[-1]
    pairs = ((high_in, high_own), (low_in, low_own))
    copies = [pltpu.make_async_copy(a, b, sems.at[i]) for i, (a, b) in enumerate(pairs)]
    for copy in copies:
        copy.start()
    build_kernel(half, ops, pack, high, low, diag, note, *scratch[:-1])
    for copy in copies:
        copy.wait()


def build_kernel(half, ops, pack, high, low, diag, note, flat, tall, qh, ql, pad, ready=None, ship=None):
    live = pack[half + 16 : half + 17, pack.shape[1] - 1 :]
    side, elems = ops.shape[0], ops.shape[1]
    count = high.shape[0]
    slots = elems * ROW
    index = jnp.concatenate(
        [pack[half + 8 : half + 16, :], pack[half + 16 : half + 24, 0 : slots - count]], axis=1
    )
    column = jnp.transpose(index)[:, 0:1]
    for first in range(0, slots, 256):
        block = jnp.where(iota((256, count), 1).astype(F32) == column[first : first + 256], 1.0, 0.0)
        tall[first : first + 256, :] = block.astype(BF16)
    tall[slots:, :] = jnp.zeros((tall.shape[0] - slots, count), BF16)
    for first in range(0, count, 256):
        block = jnp.where((iota((256, slots), 0) + first).astype(F32) == index[0:1], 1.0, 0.0)
        flat[first : first + 256, :] = block.astype(BF16)
    pad[...] = jnp.zeros(pad.shape, F32)
    if ready is not None:
        ready()
    for e in range(elems):
        pad[0:side, 0:side] = ops[:, e, :] * jnp.where(live > e + 0.5, 1.0, 0.0)
        oh, ol = split(pad[...])
        spread = dot(jnp.concatenate([oh, ol], axis=0), tall[e * ROW : e * ROW + 128, :])
        qh[e * ROW : (e + 1) * ROW, :] = spread[:ROW].astype(BF16)
        ql[e * ROW : (e + 1) * ROW, :] = spread[ROW:].astype(BF16)
    tile = 256
    face = note.shape[1]
    for j in range(0, count, tile):
        top = j + tile
        block = dot(flat[j:top, :], qh[:, j:]) + dot(flat[j:top, :], ql[:, j:])
        h, l = split(block)
        high[j:top, j:] = h
        low[j:top, j:] = l
        if ship is not None:
            ship(j, tile)
        if top < count:
            mirror = jnp.transpose(block[:, tile:])
            h, l = split(mirror)
            high[top:, j:top] = h
            low[top:, j:top] = l
        own_node = iota((tile, tile), 0) == iota((tile, tile), 1)
        line = jnp.sum(jnp.where(own_node, block[:, :tile], 0.0), axis=0, keepdims=True)
        diag[:, j:top] = jnp.broadcast_to(line, (8, tile))
        if not j:
            note[0:face, :] = block[0:face, 0:face]
            note[face : face + 8, :] = jnp.broadcast_to(line[:, 0:face], (8, face))
            note[face + 8 :, :] = pack[half : half + 8, 0:face]


def apply(value, mats, columns, half):
    oh, ol, ph, plo = mats[:4]
    return jnp.concatenate(
        [
            rows_times(value[:half], oh[:, columns], ol[:, columns]),
            rows_times(value[half:], ph[:, columns], plo[:, columns]),
        ],
        axis=0,
    )


def outer_apply(value, mats, half, face):
    parts = []
    for v, columns in ((value[:half], mats[4]), (value[half:], mats[5])):
        both = dot(jnp.concatenate(split(v), axis=0), columns[...])
        parts.append(both[:half, :face] + both[half:, :face] + both[:half, face:])
    return jnp.concatenate(parts, axis=0)


def face_times(value, rows):
    count = value.shape[0]
    h, l = split(value)
    first, second = jnp.concatenate([h, h], axis=1), jnp.concatenate([l, jnp.zeros_like(l)], axis=1)
    both = dot(jnp.concatenate([first, second], axis=0), rows)
    return both[:count] + both[count:]


def assembled(y, outer, half, face):
    inner = y[:half, face : 2 * face] + y[half:, face : 2 * face]
    first = y[:, :face] if outer is None else y[:, :face] + outer
    return jnp.concatenate([first, jnp.concatenate([inner, inner], axis=0), y[:, 2 * face :]], axis=1)


def planes_kernel(u, tables, slope, out):
    count = slope.shape[1]
    both = table_times(tables[0 : 2 * count, :], tables[2 * count : 4 * count, :], u[...])
    rate = jnp.transpose(jnp.broadcast_to(slope[...], (8, count)))[:, 0:1]
    cross = rate * both[:count] * both[count:]
    out[...] = table_times(tables[4 * count : 5 * count, :], tables[5 * count :, :], cross)


def provisional(r, d, g, inv, cm, mats, alpha, beta, half, face):
    r = r - inv * assembled(g, None, half, face)
    d = alpha * d + beta * r if alpha else beta * r
    y = outer_apply(d, mats, half, face) + cm[:, :face] * d[:, :face]
    return r, d, y


def even():
    _, z, x = position()
    return lax.rem(x + z, 2) == 0


def put(one, two, g, y, half, face, notes=((), ())):
    own = jnp.concatenate([g[:half, :face], y[:half], *notes[0]], axis=0)
    oth = jnp.concatenate([g[half:, :face], y[half:], *notes[1]], axis=0)
    first = even()
    one[...] = picked(first, own, oth)
    two[...] = picked(first, oth, own)


def got(one, two):
    a, b = one[...], two[...]
    first = even()
    return picked(first, a, b), picked(first, b, a)


def received(conv, half):
    _, _, x = position()
    parts = conv.shape[0]
    return jnp.concatenate(
        [
            jnp.concatenate([conv[m, x] for m in range(parts)], axis=1),
            jnp.concatenate([conv[m, 1 - x] for m in range(parts)], axis=1),
        ],
        axis=0,
    )


def masses(own, oth, half):
    count = own.shape[1]
    return jnp.concatenate(
        [jnp.broadcast_to(m[half : half + 1, :], (half, count)) for m in (own, oth)], axis=0
    )


def helmholtz(half, mode_count):
    _, _, x = position()
    mode = lax.axis_index("mode") * (2 * half) + x * half + iota((half, 1), 0)
    number = jnp.where(mode == 1, mode_count // 2, lax.shift_right_arithmetic(mode, 1))
    return mass_weight + (8.0 * number.astype(F32) / mode_count) ** 2


def first_source_kernel(
    half, face, mode_count, conv, own, oth, do, dp, note_o, note_p, oh, ol, ph, plo,
    wo, wp, vo, vp, r_out, d_out, v_out, conv_out, inv_out, cm_out, one, two,
):
    for wide, tall, high, low in ((wo, vo, oh, ol), (wp, vp, ph, plo)):
        wide[:, 0:face] = high[:, 0:face]
        wide[:, face:] = low[:, 0:face]
        tall[0:face, :] = high[0:face, :]
        tall[face:, :] = low[0:face, :]
    mats = (oh, ol, ph, plo, wo, wp, vo, vp)
    c = helmholtz(half, mode_count)
    c = jnp.concatenate([c, c], axis=0)
    mass = masses(own, oth, half)
    stiff = jnp.concatenate([jnp.broadcast_to(t[0:1, :], (half, t.shape[1])) for t in (do, dp)], axis=0)
    inv = 1.0 / (assembled(stiff, None, half, face) + c * assembled(mass, None, half, face))
    inv = jnp.concatenate([jnp.zeros((2 * half, face), F32), inv[:, face:]], axis=1)
    inv_out[...] = inv
    cm = c * mass
    cm_out[...] = cm
    v = jnp.concatenate([own[0:half, :], oth[0:half, :]], axis=0)
    v_out[...] = v
    new = received(conv, half)
    conv_out[...] = new
    m4 = mass_weight * mass
    g = apply(v, mats, slice(None), half) + (cm - m4) * v - m4 * new
    r = -inv * assembled(g, None, half, face)
    d = (1.0 / centre) * r
    r_out[...] = r
    d_out[...] = d
    y = outer_apply(d, mats, half, face)
    put(one, two, g, y, half, face, ((note_o[...],), (note_p[...],)))


def source_kernel(half, face, conv, old, own, oth, r, d, inv, cm, oh, ol, ph, plo, wo, wp, vo, vp, r_out, d_out, conv_out, one, two):
    mats = (oh, ol, ph, plo, wo, wp, vo, vp)
    new = received(conv, half)
    conv_out[...] = new
    cmv, dv = cm[...], d[...]
    g = apply(dv, mats, slice(None), half) + cmv * dv - mass_weight * masses(own, oth, half) * (new - old[...])
    rv, dv, y = provisional(r[...], None, g, inv[...], cmv, mats, 0.0, 1.0 / centre, half, face)
    r_out[...] = rv
    d_out[...] = dv
    put(one, two, g, y, half, face)


def rest_kernel(half, face, now, r, d, sol, s1, s2, inv, cm, oh, ol, ph, plo, wo, wp, vo, vp, r_out, d_out, sol_out):
    dv = d[...]
    y = apply(dv, (oh, ol, ph, plo, wo, wp, vo, vp), slice(face, None), half) + cm[:, face:] * dv[:, face:]
    y = jnp.concatenate([stacked(got(s1, s2), half, 2 * half), y], axis=1)
    rv = r[...] - inv[...] * assembled(y, None, half, face)
    dn = now[0] * dv + now[1] * rv
    r_out[...] = rv
    d_out[...] = dn
    sol_out[...] = sol[...] + dv + dn


def change_of(dd, theirs, mats, na, nb, half):
    change = [face_times(dd[:half], mats[6][...]), face_times(dd[half:], mats[7][...])]
    their_change = [face_times(theirs[:half], nb), face_times(theirs[half:], na)]
    return jnp.concatenate(change, axis=0), jnp.concatenate(their_change, axis=0)


def stacked(pair, first, last):
    return jnp.concatenate([t[first:last, :] for t in pair], axis=0)


def widened(value, face_part):
    face = face_part.shape[1]
    return jnp.concatenate([value[:, :face] + face_part, value[:, face:]], axis=1)


def corrected(half, face, now, r, d, sol, dr, dd, change, outer, inv):
    back = widened(-inv * assembled(change, outer, half, face), dr)
    step = widened(now[1] * back, now[0] * dd)
    return r + back, d + step, widened(sol + step, dd)


def exact(half, face, beta, now, r, d, sol, sent, came, na, nb, inv, cm, cmn, mats):
    inv_face = inv[:, :face]
    mine, came = got(*sent), got(*came)
    dr = -(inv_face * stacked(came, 0, half))
    dd = beta * dr
    theirs = -beta * (inv_face * stacked(mine, 0, half))
    change, their_change = change_of(dd, theirs, mats, na[...], nb[...], half)
    change = widened(change, cm[:, :face] * dd)
    outer = stacked(came, half, 2 * half) + their_change + cmn[...] * theirs
    return corrected(half, face, now, r[...], d[...], sol[...], dr, dd, change, outer, inv[...])


def first_sweep_kernel(
    half, face, mode_count, before, now, then,
    r, d, sol, s1, s2, c1, c2, inv, cm, oh, ol, ph, plo, wo, wp, vo, vp,
    r_out, d_out, sol_out, inv_out, cmn_out, na_out, nb_out, one, two,
):
    mats = (oh, ol, ph, plo, wo, wp, vo, vp)
    cm_v = cm[...]
    mine, came = got(s1, s2), got(c1, c2)
    c = helmholtz(half, mode_count)
    c = jnp.concatenate([c, c], axis=0)

    def line(pair, row):
        return jnp.concatenate([jnp.broadcast_to(t[row : row + 1, :], (half, face)) for t in pair], axis=0)

    at = 2 * half + face
    their_mass = line(came, at + 8)
    inv_face = 1.0 / (line(mine, at) + line(came, at) + c * (line(mine, at + 8) + their_mass))
    cmn = c * their_mass
    nb, na = (jnp.concatenate(split(t[2 * half : at, :]), axis=0) for t in came)
    dr = -inv_face * (stacked(mine, 0, half) + stacked(came, 0, half))
    dd = before[1] * dr
    change, their_change = change_of(dd, dd, mats, na, nb, half)
    change = widened(change, cm_v[:, :face] * dd)
    outer = stacked(mine, half, 2 * half) + stacked(came, half, 2 * half) + their_change + cmn * dd
    inv_v = jnp.concatenate([inv_face, inv[:, face:]], axis=1)
    rv, dn, sol_v = corrected(half, face, now, r[...], d[...], sol[...], dr, dd, change, outer, inv_v)
    inv_out[...] = inv_v
    cmn_out[...] = cmn
    na_out[...] = na
    nb_out[...] = nb
    sol_out[...] = sol_v
    g = apply(dn, mats, slice(None), half) + cm_v * dn
    rv, dv, y = provisional(rv, dn, g, inv_v, cm_v, mats, then[0], then[1], half, face)
    r_out[...] = rv
    d_out[...] = dv
    put(one, two, g, y, half, face)


def sweep_kernel(
    half, face, before, now, then,
    r, d, sol, s1, s2, c1, c2, na, nb, inv, cm, cmn, oh, ol, ph, plo, wo, wp, vo, vp,
    r_out, d_out, sol_out, one, two,
):
    mats = (oh, ol, ph, plo, wo, wp, vo, vp)
    rv, dn, sol_v = exact(half, face, before[1], now, r, d, sol, (s1, s2), (c1, c2), na, nb, inv, cm, cmn, mats)
    sol_out[...] = sol_v
    inv_v, cm_v = inv[...], cm[...]
    g = apply(dn, mats, slice(None), half) + cm_v * dn
    rv, dv, y = provisional(rv, dn, g, inv_v, cm_v, mats, then[0], then[1], half, face)
    r_out[...] = rv
    d_out[...] = dv
    put(one, two, g, y, half, face)


def last_kernel(
    half, face, before, now,
    r, d, sol, s1, s2, c1, c2, na, nb, inv, cm, cmn, oh, ol, ph, plo, wo, wp, vo, vp,
    r_out, d_out, sol_out, chunks,
):
    rv, dn, new = exact(
        half, face, before[1], now, r, d, sol, (s1, s2), (c1, c2), na, nb, inv, cm, cmn, (oh, ol, ph, plo, wo, wp, vo, vp)
    )
    r_out[...] = rv
    d_out[...] = dn
    sol_out[...] = new
    _, _, x = position()
    parts, width = chunks.shape[0], chunks.shape[3]
    for m in range(parts):
        chunks[m, x] = new[:half, m * width : (m + 1) * width]
        chunks[m, 1 - x] = new[half:, m * width : (m + 1) * width]


def end_kernel(
    half, face, before, now,
    r, d, sol, s1, s2, c1, c2, na, nb, inv, cm, cmn, oh, ol, ph, plo, wo, wp, vo, vp, own_out, oth_out,
):
    _, _, new = exact(
        half, face, before[1], now, r, d, sol, (s1, s2), (c1, c2), na, nb, inv, cm, cmn, (oh, ol, ph, plo, wo, wp, vo, vp)
    )
    own_out[...] = new[:half]
    oth_out[...] = new[half:]


def restored(value, unit):
    count = value.shape[0]
    high = value.astype(BF16)
    middle, low = split(value - high.astype(F32))
    parts = dot(jnp.concatenate([high, middle, low], axis=0), unit)
    return parts[:count] + parts[count : 2 * count] + parts[2 * count :]


def finish_own_kernel(own, place, out, unit_out):
    count = own.shape[1]
    unit = jnp.where(iota((count, count), 0).astype(F32) == place[0:1, :], 1.0, 0.0).astype(BF16)
    unit_out[...] = unit
    out[...] = restored(own[...], unit)


def finish_kernel(own, other, unit, out):
    _, _, x = position()
    a, b = own[...], restored(other[...], unit[...])
    half = own.shape[0]
    out[0:half, :] = picked(x == 0, a, b)
    out[half:, :] = picked(x == 0, b, a)


def body(n_mode, n_dom, velocity_prev, elem_ops, lumped_mass, span_slope, local_to_global, iface_nodes, live_elems):
    modes, count = velocity_prev.shape
    half = modes // 2
    elems, side = local_to_global.shape
    face = iface_nodes.shape[2]
    mode_count = span_slope.shape[0]
    quarter = count // n_mode
    pairs = n_dom // 2
    slots = elems * ROW
    places = [(z, s) for z in range(pairs) for s in (0, 1)]
    swap = [(i, i ^ 1) for i in range(n_dom)]
    long_swap = [(2 * z + s, 2 * ((z + (1 if z % 2 else -1)) % pairs) + s) for z, s in places]
    short_swap = [(2 * z + s, 2 * ((z + (-1 if z % 2 else 1)) % pairs) + s) for z, s in places]
    groups = [[m * n_dom + 2 * z + s for m in range(n_mode) for s in (0, 1)] for z in range(pairs)]

    def exchange(one, two):
        return lax.ppermute(one, "dom", long_swap), lax.ppermute(two, "dom", short_swap)

    ops = jnp.transpose(elem_ops, (1, 0, 2))
    ops_other = lax.ppermute(ops, "dom", swap)
    pack = (half + 24, count)
    wide = (2 * half, count)
    keep, send, chunks, place = call(
        order_kernel,
        [(pack, F32), (pack, F32), ((n_mode, modes, quarter), F32), ((8, count), F32)],
        [iface_nodes[0], local_to_global, velocity_prev, lumped_mass.reshape(1, count), live_elems.reshape(1, n_dom)],
        24, far=range(5),
        scratch=[
            pltpu.VMEM((2, face), jnp.int32), pltpu.VMEM((elems, side), jnp.int32),
            pltpu.VMEM((modes, count), F32), pltpu.VMEM((1, count), F32), pltpu.VMEM((1, n_dom), jnp.int32),
            pltpu.SemaphoreType.DMA((5,)),
        ],
    )
    planes_in = lax.all_to_all(chunks, "mode", 0, 0, tiled=True)
    oth = lax.ppermute(send, "dom", swap)

    matrix = ((count, count), BF16)
    small = [((8, count), F32), ((face + 16, face), F32)]
    one_hot = [
        pltpu.VMEM((count, slots), BF16),
        pltpu.VMEM((slots + 32, count), BF16),
        pltpu.VMEM((slots, count), BF16),
        pltpu.VMEM((slots, count), BF16),
        pltpu.VMEM((ROW, 128), F32),
    ]
    synthesis, derivative, analysis = wave_tables(mode_count)
    tables = jnp.asarray(np.concatenate(halves(np.concatenate([synthesis, derivative])) + halves(analysis)))
    slope = span_slope.reshape(1, mode_count)

    def planes(value):
        (out,) = call(
            planes_kernel, [((mode_count, quarter), F32)],
            [value.reshape(mode_count, quarter), tables, slope], 16, flops=600 << 20, free=(tables.shape,),
        )
        return out

    def to_solve(value):
        back = lax.all_to_all(
            value.reshape(2 * n_mode, half, quarter), ("mode", "dom"), 0, 0, axis_index_groups=groups, tiled=True
        )
        return back.reshape(n_mode, 2, half, quarter)

    cross, keep_late = lax.optimization_barrier((planes(planes_in), keep))
    conv = to_solve(cross)
    oh, ol, do, note_o = call(
        functools.partial(own_build_kernel, half), [matrix, matrix, *small], [ops, keep_late], 36,
        far=(0,), out_far=(0, 1), flops=6 << 30,
        scratch=[
            pltpu.VMEM((side, elems, side), F32), pltpu.VMEM((count, count), BF16), pltpu.VMEM((count, count), BF16),
            *one_hot, pltpu.SemaphoreType.DMA((2 * count // 256 + 1,)),
        ],
    )
    conv, oth_late = lax.optimization_barrier((conv, oth))
    oh, ol, ph, plo, dp, note_p = call(
        functools.partial(partner_build_kernel, half), [matrix] * 4 + small, [ops_other, oth_late, oh, ol], 24,
        far=(2, 3), pinned=range(4), flops=6 << 30, scratch=[*one_hot, pltpu.SemaphoreType.DMA((2,))],
    )
    mats = [oh, ol, ph, plo]
    coefs = chebyshev()
    message = ((2 * half, face), F32)
    for iteration in range(ITERS):
        if iteration == 0:
            long_message = ((2 * half + face + 16, face), F32)
            beside = [((count, 2 * face), BF16)] * 2 + [((2 * face, count), BF16)] * 2
            *cats, r, d, sol, old, inv, cm, one, two = call(
                functools.partial(first_source_kernel, half, face, mode_count),
                [*beside, *[(wide, F32)] * 6, long_message, long_message],
                [conv, keep, oth, do, dp, note_o, note_p, *mats], 20, flops=500 << 20, pinned=range(4),
            )
            mats = [*mats, *cats]
        else:
            r, d, old, one, two = call(
                functools.partial(source_kernel, half, face),
                [(wide, F32), (wide, F32), (wide, F32), message, message],
                [conv, old, keep, oth, r, d, inv, cm, *mats], 20, flops=500 << 20,
            )
        for k in (0, 2, 4):
            c1, c2 = exchange(one, two)
            r, d, sol = call(
                functools.partial(rest_kernel, half, face, coefs[k + 1]), [(wide, F32)] * 3,
                [r, d, sol, one, two, inv, cm, *mats], 20, flops=400 << 20,
            )
            if iteration == 0 and k == 0:
                r, d, sol, inv, cmn, na, nb, one, two = call(
                    functools.partial(first_sweep_kernel, half, face, mode_count, coefs[0], coefs[1], coefs[2]),
                    [(wide, F32)] * 4 + [((2 * half, face), F32)] + [((2 * face, face), BF16)] * 2 + [message, message],
                    [r, d, sol, one, two, c1, c2, inv, cm, *mats], 20, flops=500 << 20,
                )
                continue
            given = [r, d, sol, one, two, c1, c2, na, nb, inv, cm, cmn, *mats]
            if k < 4:
                r, d, sol, one, two = call(
                    functools.partial(sweep_kernel, half, face, coefs[k], coefs[k + 1], coefs[k + 2]),
                    [(wide, F32), (wide, F32), (wide, F32), message, message], given, 20, flops=500 << 20,
                )
            elif iteration < ITERS - 1:
                r, d, sol, chunks = call(
                    functools.partial(last_kernel, half, face, coefs[k], coefs[k + 1]),
                    [(wide, F32), (wide, F32), (wide, F32), ((n_mode, 2, half, quarter), F32)],
                    given, 20, flops=100 << 20,
                )
            else:
                own, other = call(
                    functools.partial(end_kernel, half, face, coefs[k], coefs[k + 1]),
                    [((half, count), F32)] * 2, given, 20, flops=100 << 20,
                )
        if iteration < ITERS - 1:
            planes_in = lax.all_to_all(
                chunks.reshape(2 * n_mode, half, quarter), ("mode", "dom"), 0, 0, axis_index_groups=groups, tiled=True
            )
            conv = to_solve(planes(planes_in))
    other = lax.ppermute(other, "dom", swap)
    own, unit = call(
        finish_own_kernel, [((half, count), F32), ((count, count), BF16)], [own, place], 16, flops=200 << 20
    )
    (out,) = call(finish_kernel, [((modes, count), F32)], [own, other, unit], 16)
    return out


def solution(mesh):
    placed = (
        P("mode", "dom"),
        P("dom", None, None),
        P("dom"),
        P(),
        P("dom", None),
        P("dom", None, None),
        P(),
    )
    return jax.shard_map(
        functools.partial(body, mesh.shape["mode"], mesh.shape["dom"]),
        mesh=mesh, in_specs=placed, out_specs=P("mode", "dom"), check_vma=False,
    )
```

```python
import functools

import jax
import jax.numpy as jnp
import numpy as np
from jax import lax
from jax.experimental import pallas as pl
from jax.experimental.pallas import tpu as pltpu
from jax.sharding import PartitionSpec as P

ITERS = 3
SWEEPS = 6

mass_weight = 4.0
bound_low = 0.1
bound_high = 2.0
centre = (bound_high + bound_low) / 2.0
half_width = (bound_high - bound_low) / 2.0

F32 = jnp.float32
BF16 = jnp.bfloat16
ROW = 96


def chebyshev():
    ratio = centre / half_width
    rho = 1.0 / ratio
    coefs = [(0.0, 1.0 / centre)]
    for _ in range(SWEEPS - 1):
        rho_next = 1.0 / (2.0 * ratio - rho)
        coefs.append((rho_next * rho, 2.0 * rho_next / half_width))
        rho = rho_next
    return coefs


def wave_tables(mode_count):
    column = np.arange(mode_count)
    number = np.where(column == 1, mode_count // 2, column // 2)
    is_sine = (column % 2 == 1) & (column > 1)
    planes = np.arange(mode_count)
    angles = (planes[:, None] * number[None, :] % mode_count) * (2.0 * np.pi / mode_count)
    cosine, sine = np.cos(angles), np.sin(angles)
    synthesis = np.where(is_sine[None, :], sine, cosine)
    factor = number / (mode_count // 2)
    derivative = np.where(is_sine[None, :], cosine, -sine) * factor[None, :]
    derivative = np.where(column[None, :] > 1, derivative, 0.0)
    weights = np.where(column < 2, 1.0 / mode_count, 2.0 / mode_count)
    return synthesis, derivative, synthesis.T * weights[:, None]


def halves(table):
    high = table.astype(np.float32).astype(BF16)
    return [high, (table - high.astype(np.float64)).astype(np.float32).astype(BF16)]


def split(value):
    high = value.astype(BF16)
    return high, (value - high.astype(F32)).astype(BF16)


def dot(a, b):
    return lax.dot_general(a, b, (((1,), (0,)), ((), ())), preferred_element_type=F32)


def rows_times(value, high, low):
    count = value.shape[0]
    h, l = split(value)
    both = dot(jnp.concatenate([h, l], axis=0), high)
    return both[:count] + both[count:] + dot(h, low)


def table_times(high, low, value):
    count = value.shape[1]
    h, l = split(value)
    both = dot(high, jnp.concatenate([h, l], axis=1))
    return both[:, :count] + both[:, count:] + dot(low, h)


def iota(shape, dim):
    return lax.broadcasted_iota(jnp.int32, shape, dim)


def call(kernel, outs, vmem, limit, scratch=(), flops=0, moved=1 << 20, far=(), out_far=(), pinned=(), free=()):
    in_specs, given = [], []
    for i, v in enumerate(vmem):
        space = pltpu.HBM if i in far else pltpu.VMEM
        in_specs.append(pl.BlockSpec(memory_space=space))
        fixed = i in far or v.dtype == BF16 and v.shape not in free
        given.append(pltpu.with_memory_space_constraint(v, space) if fixed else v)
    shapes, out_specs = [], []
    for i, (s, t) in enumerate(outs):
        space = pltpu.HBM if i in out_far else pltpu.VMEM
        out_specs.append(pl.BlockSpec(memory_space=space))
        shapes.append(space(s, t) if i in out_far or i in pinned else jax.ShapeDtypeStruct(s, t))
    return pl.pallas_call(
        kernel,
        out_shape=shapes,
        in_specs=in_specs,
        out_specs=out_specs,
        scratch_shapes=list(scratch),
        compiler_params=pltpu.CompilerParams(vmem_limit_bytes=limit << 20),
        cost_estimate=pl.CostEstimate(flops=flops, bytes_accessed=moved, transcendentals=0),
    )(*given)


def position():
    q = lax.axis_index("dom")
    z = lax.shift_right_arithmetic(q, 1)
    return q, z, q - 2 * z


def picked(first, a, b):
    return jnp.where(first, a, b)


def order_kernel(
    iface_in, l2g_in, vel_in, mass_in, live_in, keep, send, chunks, place_out, iface, l2g, vel, mass, live, sems
):
    q, _, x = position()
    pairs = ((iface_in, iface), (l2g_in, l2g), (vel_in, vel), (mass_in, mass), (live_in, live))
    copies = [pltpu.make_async_copy(a, b, sems.at[i]) for i, (a, b) in enumerate(pairs)]
    for copy in copies:
        copy.start()
    for copy in copies:
        copy.wait()
    count = mass.shape[1]
    face = iface.shape[1]
    lists = jnp.concatenate(
        [picked(x == 0, iface[0:1, :], iface[1:2, :]), picked(x == 0, iface[1:2, :], iface[0:1, :])], axis=1
    ).astype(F32)
    lists = jnp.transpose(jnp.broadcast_to(lists, (8, 2 * face)))[:, 0:1]
    hit = jnp.where(lists == iota((1, count), 1).astype(F32), 1.0, 0.0)
    at = jnp.sum(hit * iota((2 * face, 1), 0).astype(F32), axis=0, keepdims=True)
    shared = jnp.sum(hit, axis=0, keepdims=True)
    rest = jnp.broadcast_to(1.0 - shared, (8, count))
    lane = iota((8, count), 1)
    run = rest
    step = 1
    while step < count:
        run = run + jnp.where(lane >= step, pltpu.roll(run, step, 1), 0.0)
        step *= 2
    place = jnp.where(rest > 0.5, run - 1.0 + 2.0 * face, jnp.broadcast_to(at, (8, count)))
    place_out[...] = place
    column = jnp.transpose(place)[:, 0:1]
    elems, side = l2g.shape
    slots = elems * ROW
    blank = jnp.full((1, ROW - side), -1, jnp.int32)
    row = jnp.concatenate([piece for e in range(elems) for piece in (l2g[e : e + 1, :], blank)], axis=1)
    pieces = []
    for first in range(0, slots, 512):
        part = row[:, first : first + 512]
        found = jnp.where(iota((count, 1), 0) == part, column, 0.0)
        pieces.append(jnp.where(part < 0, -1.0, jnp.sum(found, axis=0, keepdims=True)))
    index = jnp.concatenate(pieces, axis=1)
    unit = jnp.where(iota((1, count), 1).astype(F32) == column, 1.0, 0.0).astype(BF16)
    modes = vel.shape[0]
    half = modes // 2
    value = jnp.concatenate([vel[...], jnp.broadcast_to(mass[...], (16, count))], axis=0)
    high = value.astype(BF16)
    middle, low = split(value - high.astype(F32))
    total = modes + 16
    parts = dot(jnp.concatenate([high, middle, low], axis=0), unit)
    moved = parts[:total] + parts[total : 2 * total] + parts[2 * total :]
    a, b = moved[:half], moved[half:modes]
    lived = jnp.where(iota(live.shape, 1) == q, live[...], 0).astype(F32)
    lived = jnp.sum(lived, axis=1, keepdims=True)
    for ref, rows in ((keep, picked(x == 0, a, b)), (send, picked(x == 0, b, a))):
        ref[0:half, :] = rows
        ref[half : half + 8, :] = moved[modes : modes + 8]
        ref[half + 8 : half + 16, :] = jnp.broadcast_to(index[:, :count], (8, count))
        ref[half + 16 : half + 24, 0 : slots - count] = jnp.broadcast_to(
            index[:, count:], (8, slots - count)
        )
        ref[half + 16 : half + 24, slots - count :] = jnp.broadcast_to(lived, (8, 2 * count - slots))
    quarter = count // chunks.shape[0]
    for part in range(chunks.shape[0]):
        chunks[part] = moved[:modes, part * quarter : (part + 1) * quarter]


def own_build_kernel(half, ops_in, pack, high_out, low_out, diag, note, ops, *scratch):
    sems = scratch[-1]
    fetch = pltpu.make_async_copy(ops_in, ops, sems.at[0])
    fetch.start()
    partner_build_kernel(half, ops, pack, high_out, low_out, diag, note, *scratch, ready=fetch.wait)


def partner_build_kernel(half, ops, pack, high_out, low_out, diag, note, high, low, *scratch, ready=None):
    sems = scratch[-1]
    copies = []

    def ship(*rows):
        for part, out in ((high, high_out), (low, low_out)):
            at = pl.ds(*rows)
            copies.append(pltpu.make_async_copy(part.at[at], out.at[at], sems.at[len(copies) + 1]))
            copies[-1].start()

    build_kernel(half, ops, pack, high, low, diag, note, *scratch[:-1], ready=ready, ship=ship)
    for copy in copies:
        copy.wait()


def build_kernel(half, ops, pack, high, low, diag, note, flat, tall, qh, ql, pad, ready=None, ship=None):
    live = pack[half + 16 : half + 17, pack.shape[1] - 1 :]
    side, elems = ops.shape[0], ops.shape[1]
    count = high.shape[0]
    slots = elems * ROW
    index = jnp.concatenate(
        [pack[half + 8 : half + 16, :], pack[half + 16 : half + 24, 0 : slots - count]], axis=1
    )
    column = jnp.transpose(index)[:, 0:1]
    for first in range(0, slots, 256):
        block = jnp.where(iota((1, count), 1).astype(F32) == column[first : first + 256], 1.0, 0.0)
        tall[first : first + 256, :] = block.astype(BF16)
    tall[slots:, :] = jnp.zeros((tall.shape[0] - slots, count), BF16)
    for first in range(0, count, 256):
        block = jnp.where((iota((256, 1), 0) + first).astype(F32) == index[0:1], 1.0, 0.0)
        flat[first : first + 256, :] = block.astype(BF16)
    pad[...] = jnp.zeros(pad.shape, F32)
    if ready is not None:
        ready()
    for e in range(elems):
        pad[0:side, 0:side] = ops[:, e, :] * jnp.where(live > e + 0.5, 1.0, 0.0)
        oh, ol = split(pad[...])
        spread = dot(jnp.concatenate([oh, ol], axis=0), tall[e * ROW : e * ROW + 128, :])
        qh[e * ROW : (e + 1) * ROW, :] = spread[:ROW].astype(BF16)
        ql[e * ROW : (e + 1) * ROW, :] = spread[ROW:].astype(BF16)
    tile = 256
    face = note.shape[1]
    for j in range(0, count, tile):
        top = j + tile
        block = dot(flat[j:top, :], qh[:, j:]) + dot(flat[j:top, :], ql[:, j:])
        h, l = split(block)
        high[j:top, j:] = h
        low[j:top, j:] = l
        if ship is not None:
            ship(j, tile)
        if top < count:
            mirror = jnp.transpose(block[:, tile:])
            h, l = split(mirror)
            high[top:, j:top] = h
            low[top:, j:top] = l
        own_node = iota((tile, tile), 0) == iota((tile, tile), 1)
        line = jnp.sum(jnp.where(own_node, block[:, :tile], 0.0), axis=0, keepdims=True)
        diag[:, j:top] = jnp.broadcast_to(line, (8, tile))
        if not j:
            note[0:face, :] = block[0:face, 0:face]
            note[face : face + 8, :] = jnp.broadcast_to(line[:, 0:face], (8, face))
            note[face + 8 :, :] = pack[half : half + 8, 0:face]


def apply(value, mats, columns, half):
    oh, ol, ph, plo = mats[:4]
    return jnp.concatenate(
        [
            rows_times(value[:half], oh[:, columns], ol[:, columns]),
            rows_times(value[half:], ph[:, columns], plo[:, columns]),
        ],
        axis=0,
    )


def outer_apply(value, mats, half, face):
    parts = []
    for v, columns in ((value[:half], mats[4]), (value[half:], mats[5])):
        both = dot(jnp.concatenate(split(v), axis=0), columns[...])
        parts.append(both[:half, :face] + both[half:, :face] + both[:half, face:])
    return jnp.concatenate(parts, axis=0)


def face_times(value, rows):
    count = value.shape[0]
    h, l = split(value)
    first, second = jnp.concatenate([h, h], axis=1), jnp.concatenate([l, jnp.zeros_like(l)], axis=1)
    both = dot(jnp.concatenate([first, second], axis=0), rows)
    return both[:count] + both[count:]


def assembled(y, outer, half, face):
    inner = y[:half, face : 2 * face] + y[half:, face : 2 * face]
    first = y[:, :face] if outer is None else y[:, :face] + outer
    return jnp.concatenate([first, jnp.concatenate([inner, inner], axis=0), y[:, 2 * face :]], axis=1)


def first_planes_kernel(u_in, tables_in, slope_in, out, u, tables, slope, sems):
    rows = 4 * slope.shape[1]
    parts = [pl.ds(0, rows), pl.ds(rows, tables.shape[0] - rows)]
    pairs = [(u_in, u), (slope_in, slope)] + [(tables_in.at[p], tables.at[p]) for p in parts]
    copies = [pltpu.make_async_copy(a, b, sems.at[i]) for i, (a, b) in enumerate(pairs)]
    for copy in copies:
        copy.start()
    for copy in copies[:3]:
        copy.wait()
    planes_kernel(u, tables, slope, out, copies[3].wait)


def planes_kernel(u, tables, slope, out, ready=None):
    count = slope.shape[1]
    both = table_times(tables[0 : 2 * count, :], tables[2 * count : 4 * count, :], u[...])
    rate = jnp.transpose(jnp.broadcast_to(slope[...], (8, count)))[:, 0:1]
    cross = rate * both[:count] * both[count:]
    if ready is not None:
        ready()
    out[...] = table_times(tables[4 * count : 5 * count, :], tables[5 * count :, :], cross)


def provisional(r, d, g, inv, cm, mats, alpha, beta, half, face):
    r = r - inv * assembled(g, None, half, face)
    d = alpha * d + beta * r if alpha else beta * r
    y = outer_apply(d, mats, half, face) + cm[:, :face] * d[:, :face]
    return r, d, y


def even():
    _, z, x = position()
    return lax.rem(x + z, 2) == 0


def put(one, two, g, y, half, face, notes=((), ())):
    own = jnp.concatenate([g[:half, :face], y[:half], *notes[0]], axis=0)
    oth = jnp.concatenate([g[half:, :face], y[half:], *notes[1]], axis=0)
    first = even()
    one[...] = picked(first, own, oth)
    two[...] = picked(first, oth, own)


def got(one, two):
    a, b = one[...], two[...]
    first = even()
    return picked(first, a, b), picked(first, b, a)


def received(conv, half):
    _, _, x = position()
    parts = conv.shape[0]
    return jnp.concatenate(
        [
            jnp.concatenate([conv[m, x] for m in range(parts)], axis=1),
            jnp.concatenate([conv[m, 1 - x] for m in range(parts)], axis=1),
        ],
        axis=0,
    )


def masses(own, oth, half):
    count = own.shape[1]
    return jnp.concatenate(
        [jnp.broadcast_to(m[half : half + 1, :], (half, count)) for m in (own, oth)], axis=0
    )


def helmholtz(half, mode_count):
    _, _, x = position()
    mode = lax.axis_index("mode") * (2 * half) + x * half + iota((half, 1), 0)
    number = jnp.where(mode == 1, mode_count // 2, lax.shift_right_arithmetic(mode, 1))
    return mass_weight + (8.0 * number.astype(F32) / mode_count) ** 2


def beside(columns, rows, high, low):
    face = rows.shape[0] // 2
    columns[:, 0:face] = high[:, 0:face]
    columns[:, face:] = low[:, 0:face]
    rows[0:face, :] = high[0:face, :]
    rows[face:, :] = low[0:face, :]


def first_source_kernel(
    half, face, mode_count, conv, own, oth, do, dp, note_o, note_p, oh_in, ol_in, ph_in, plo_in,
    oh, ol, ph, plo, wo, wp, vo, vp, r_out, d_out, v_out, conv_out, inv_out, cm_out, one, two, sems,
):
    mats = (oh, ol, ph, plo, wo, wp, vo, vp)
    pairs = zip((oh_in, ol_in, ph_in, plo_in), mats)
    copies = [pltpu.make_async_copy(a, b, sems.at[i]) for i, (a, b) in enumerate(pairs)]
    for copy in copies:
        copy.start()
    c = helmholtz(half, mode_count)
    c = jnp.concatenate([c, c], axis=0)
    mass = masses(own, oth, half)
    stiff = jnp.concatenate([jnp.broadcast_to(t[0:1, :], (half, t.shape[1])) for t in (do, dp)], axis=0)
    inv = 1.0 / (assembled(stiff, None, half, face) + c * assembled(mass, None, half, face))
    inv = jnp.concatenate([jnp.zeros((2 * half, face), F32), inv[:, face:]], axis=1)
    inv_out[...] = inv
    cm = c * mass
    cm_out[...] = cm
    v = jnp.concatenate([own[0:half, :], oth[0:half, :]], axis=0)
    v_out[...] = v
    new = received(conv, half)
    conv_out[...] = new
    m4 = mass_weight * mass
    copies[0].wait()
    copies[1].wait()
    beside(wo, vo, oh, ol)
    e_own = rows_times(v[:half], oh[...], ol[...])
    copies[2].wait()
    copies[3].wait()
    beside(wp, vp, ph, plo)
    e_oth = rows_times(v[half:], ph[...], plo[...])
    g = jnp.concatenate([e_own, e_oth], axis=0) + (cm - m4) * v - m4 * new
    r = -inv * assembled(g, None, half, face)
    d = (1.0 / centre) * r
    r_out[...] = r
    d_out[...] = d
    y = outer_apply(d, mats, half, face)
    put(one, two, g, y, half, face, ((note_o[...],), (note_p[...],)))


def source_kernel(half, face, conv, old, own, oth, r, d, inv, cm, oh, ol, ph, plo, wo, wp, vo, vp, r_out, d_out, conv_out, one, two):
    mats = (oh, ol, ph, plo, wo, wp, vo, vp)
    new = received(conv, half)
    conv_out[...] = new
    cmv, dv = cm[...], d[...]
    g = apply(dv, mats, slice(None), half) + cmv * dv - mass_weight * masses(own, oth, half) * (new - old[...])
    rv, dv, y = provisional(r[...], None, g, inv[...], cmv, mats, 0.0, 1.0 / centre, half, face)
    r_out[...] = rv
    d_out[...] = dv
    put(one, two, g, y, half, face)


def rest_kernel(half, face, now, r, d, sol, s1, s2, inv, cm, oh, ol, ph, plo, wo, wp, vo, vp, r_out, d_out, sol_out):
    dv = d[...]
    y = apply(dv, (oh, ol, ph, plo, wo, wp, vo, vp), slice(face, None), half) + cm[:, face:] * dv[:, face:]
    y = jnp.concatenate([stacked(got(s1, s2), half, 2 * half), y], axis=1)
    rv = r[...] - inv[...] * assembled(y, None, half, face)
    dn = now[0] * dv + now[1] * rv
    r_out[...] = rv
    d_out[...] = dn
    sol_out[...] = sol[...] + dv + dn


def change_of(dd, theirs, mats, na, nb, half):
    change = [face_times(dd[:half], mats[6][...]), face_times(dd[half:], mats[7][...])]
    their_change = [face_times(theirs[:half], nb), face_times(theirs[half:], na)]
    return jnp.concatenate(change, axis=0), jnp.concatenate(their_change, axis=0)


def stacked(pair, first, last):
    return jnp.concatenate([t[first:last, :] for t in pair], axis=0)


def widened(value, face_part):
    face = face_part.shape[1]
    return jnp.concatenate([value[:, :face] + face_part, value[:, face:]], axis=1)


def corrected(half, face, now, r, d, sol, dr, dd, change, outer, inv):
    back = widened(-inv * assembled(change, outer, half, face), dr)
    step = widened(now[1] * back, now[0] * dd)
    return r + back, d + step, widened(sol + step, dd)


def exact(half, face, beta, now, r, d, sol, sent, came, na, nb, inv, cm, cmn, mats):
    inv_face = inv[:, :face]
    mine, came = got(*sent), got(*came)
    dr = -(inv_face * stacked(came, 0, half))
    dd = beta * dr
    theirs = -beta * (inv_face * stacked(mine, 0, half))
    change, their_change = change_of(dd, theirs, mats, na[...], nb[...], half)
    change = widened(change, cm[:, :face] * dd)
    outer = stacked(came, half, 2 * half) + their_change + cmn[...] * theirs
    return corrected(half, face, now, r[...], d[...], sol[...], dr, dd, change, outer, inv[...])


def first_sweep_kernel(
    half, face, mode_count, before, now, then,
    r, d, sol, s1, s2, c1, c2, inv, cm, oh, ol, ph, plo, wo, wp, vo, vp,
    r_out, d_out, sol_out, inv_out, cmn_out, na_out, nb_out, one, two,
):
    mats = (oh, ol, ph, plo, wo, wp, vo, vp)
    cm_v = cm[...]
    mine, came = got(s1, s2), got(c1, c2)
    c = helmholtz(half, mode_count)
    c = jnp.concatenate([c, c], axis=0)

    def line(pair, row):
        return jnp.concatenate([jnp.broadcast_to(t[row : row + 1, :], (half, face)) for t in pair], axis=0)

    at = 2 * half + face
    their_mass = line(came, at + 8)
    inv_face = 1.0 / (line(mine, at) + line(came, at) + c * (line(mine, at + 8) + their_mass))
    cmn = c * their_mass
    nb, na = (jnp.concatenate(split(t[2 * half : at, :]), axis=0) for t in came)
    dr = -inv_face * (stacked(mine, 0, half) + stacked(came, 0, half))
    dd = before[1] * dr
    change, their_change = change_of(dd, dd, mats, na, nb, half)
    change = widened(change, cm_v[:, :face] * dd)
    outer = stacked(mine, half, 2 * half) + stacked(came, half, 2 * half) + their_change + cmn * dd
    inv_v = jnp.concatenate([inv_face, inv[:, face:]], axis=1)
    rv, dn, sol_v = corrected(half, face, now, r[...], d[...], sol[...], dr, dd, change, outer, inv_v)
    inv_out[...] = inv_v
    cmn_out[...] = cmn
    na_out[...] = na
    nb_out[...] = nb
    sol_out[...] = sol_v
    g = apply(dn, mats, slice(None), half) + cm_v * dn
    rv, dv, y = provisional(rv, dn, g, inv_v, cm_v, mats, then[0], then[1], half, face)
    r_out[...] = rv
    d_out[...] = dv
    put(one, two, g, y, half, face)


def sweep_kernel(
    half, face, before, now, then,
    r, d, sol, s1, s2, c1, c2, na, nb, inv, cm, cmn, oh, ol, ph, plo, wo, wp, vo, vp,
    r_out, d_out, sol_out, one, two,
):
    mats = (oh, ol, ph, plo, wo, wp, vo, vp)
    rv, dn, sol_v = exact(half, face, before[1], now, r, d, sol, (s1, s2), (c1, c2), na, nb, inv, cm, cmn, mats)
    sol_out[...] = sol_v
    inv_v, cm_v = inv[...], cm[...]
    g = apply(dn, mats, slice(None), half) + cm_v * dn
    rv, dv, y = provisional(rv, dn, g, inv_v, cm_v, mats, then[0], then[1], half, face)
    r_out[...] = rv
    d_out[...] = dv
    put(one, two, g, y, half, face)


def last_kernel(
    half, face, before, now,
    r, d, sol, s1, s2, c1, c2, na, nb, inv, cm, cmn, oh, ol, ph, plo, wo, wp, vo, vp,
    r_out, d_out, sol_out, chunks,
):
    rv, dn, new = exact(
        half, face, before[1], now, r, d, sol, (s1, s2), (c1, c2), na, nb, inv, cm, cmn, (oh, ol, ph, plo, wo, wp, vo, vp)
    )
    r_out[...] = rv
    d_out[...] = dn
    sol_out[...] = new
    _, _, x = position()
    parts, width = chunks.shape[0], chunks.shape[3]
    for m in range(parts):
        chunks[m, x] = new[:half, m * width : (m + 1) * width]
        chunks[m, 1 - x] = new[half:, m * width : (m + 1) * width]


def end_kernel(
    half, face, before, now,
    r, d, sol, s1, s2, c1, c2, na, nb, inv, cm, cmn, oh, ol, ph, plo, wo, wp, vo, vp, own_out, oth_out,
):
    _, _, new = exact(
        half, face, before[1], now, r, d, sol, (s1, s2), (c1, c2), na, nb, inv, cm, cmn, (oh, ol, ph, plo, wo, wp, vo, vp)
    )
    own_out[...] = new[:half]
    oth_out[...] = new[half:]


def restored(value, unit):
    count = value.shape[0]
    high = value.astype(BF16)
    middle, low = split(value - high.astype(F32))
    parts = dot(jnp.concatenate([high, middle, low], axis=0), unit)
    return parts[:count] + parts[count : 2 * count] + parts[2 * count :]


def finish_own_kernel(own, place, out, unit_out):
    count = own.shape[1]
    unit = jnp.where(iota((count, 1), 0).astype(F32) == place[0:1, :], 1.0, 0.0).astype(BF16)
    unit_out[...] = unit
    out[...] = restored(own[...], unit)


def finish_kernel(own, other, unit, out):
    _, _, x = position()
    a, b = own[...], restored(other[...], unit[...])
    half = own.shape[0]
    out[0:half, :] = picked(x == 0, a, b)
    out[half:, :] = picked(x == 0, b, a)


def body(n_mode, n_dom, velocity_prev, elem_ops, lumped_mass, span_slope, local_to_global, iface_nodes, live_elems):
    modes, count = velocity_prev.shape
    half = modes // 2
    elems, side = local_to_global.shape
    face = iface_nodes.shape[2]
    mode_count = span_slope.shape[0]
    quarter = count // n_mode
    pairs = n_dom // 2
    slots = elems * ROW
    places = [(z, s) for z in range(pairs) for s in (0, 1)]
    swap = [(i, i ^ 1) for i in range(n_dom)]
    long_swap = [(2 * z + s, 2 * ((z + (1 if z % 2 else -1)) % pairs) + s) for z, s in places]
    short_swap = [(2 * z + s, 2 * ((z + (-1 if z % 2 else 1)) % pairs) + s) for z, s in places]
    groups = [[m * n_dom + 2 * z + s for m in range(n_mode) for s in (0, 1)] for z in range(pairs)]

    def exchange(one, two):
        return lax.ppermute(one, "dom", long_swap), lax.ppermute(two, "dom", short_swap)

    ops = jnp.transpose(elem_ops, (1, 0, 2))
    ops_other = lax.ppermute(ops, "dom", swap)
    pack = (half + 24, count)
    wide = (2 * half, count)
    keep, send, chunks, place = call(
        order_kernel,
        [(pack, F32), (pack, F32), ((n_mode, modes, quarter), F32), ((8, count), F32)],
        [iface_nodes[0], local_to_global, velocity_prev, lumped_mass.reshape(1, count), live_elems.reshape(1, n_dom)],
        24, far=range(5),
        scratch=[
            pltpu.VMEM((2, face), jnp.int32), pltpu.VMEM((elems, side), jnp.int32),
            pltpu.VMEM((modes, count), F32), pltpu.VMEM((1, count), F32), pltpu.VMEM((1, n_dom), jnp.int32),
            pltpu.SemaphoreType.DMA((5,)),
        ],
    )
    planes_in = lax.all_to_all(chunks, "mode", 0, 0, tiled=True)
    oth = lax.ppermute(send, "dom", swap)

    synthesis, derivative, analysis = wave_tables(mode_count)
    tables = jnp.asarray(np.concatenate(halves(np.concatenate([synthesis, derivative])) + halves(analysis)))
    slope = span_slope.reshape(1, mode_count)

    def build(own, ops, packed):
        matrix = ((count, count), BF16)
        scratch = [
            pltpu.VMEM((count, count), BF16),
            pltpu.VMEM((count, count), BF16),
            pltpu.VMEM((count, slots), BF16),
            pltpu.VMEM((slots + 32, count), BF16),
            pltpu.VMEM((slots, count), BF16),
            pltpu.VMEM((slots, count), BF16),
            pltpu.VMEM((ROW, 128), F32),
            pltpu.SemaphoreType.DMA((2 * count // 256 + 1,)),
        ]
        return call(
            functools.partial(own_build_kernel if own else partner_build_kernel, half),
            [matrix, matrix, ((8, count), F32), ((face + 16, face), F32)], [ops, packed], 36,
            far=(0,) if own else (), out_far=(0, 1), flops=6 << 30,
            scratch=[pltpu.VMEM((side, elems, side), F32), *scratch] if own else scratch,
        )

    def convect(value, first):
        (out,) = call(
            first_planes_kernel if first else planes_kernel, [((mode_count, quarter), F32)],
            [value.reshape(mode_count, quarter), tables, slope], 16, flops=600 << 20,
            far=range(3) if first else (), free=(tables.shape,),
            scratch=[
                pltpu.VMEM((mode_count, quarter), F32), pltpu.VMEM(tables.shape, BF16),
                pltpu.VMEM(slope.shape, F32), pltpu.SemaphoreType.DMA((4,)),
            ] if first else (),
        )
        back = lax.all_to_all(
            out.reshape(2 * n_mode, half, quarter), ("mode", "dom"), 0, 0, axis_index_groups=groups, tiled=True
        )
        return back.reshape(n_mode, 2, half, quarter)

    oh, ol, do, note_o = build(True, ops, keep)
    conv = convect(planes_in, True)
    ph, plo, dp, note_p = build(False, ops_other, oth)
    mats = [oh, ol, ph, plo]
    coefs = chebyshev()
    message = ((2 * half, face), F32)
    for iteration in range(ITERS):
        if iteration == 0:
            long_message = ((2 * half + face + 16, face), F32)
            strips = [((count, 2 * face), BF16)] * 2 + [((2 * face, count), BF16)] * 2
            *mats, r, d, sol, old, inv, cm, one, two = call(
                functools.partial(first_source_kernel, half, face, mode_count),
                [*[((count, count), BF16)] * 4, *strips, *[(wide, F32)] * 6, long_message, long_message],
                [conv, keep, oth, do, dp, note_o, note_p, *mats], 20, flops=500 << 20,
                far=range(7, 11), pinned=range(8), scratch=[pltpu.SemaphoreType.DMA((4,))],
            )
        else:
            r, d, old, one, two = call(
                functools.partial(source_kernel, half, face),
                [(wide, F32), (wide, F32), (wide, F32), message, message],
                [conv, old, keep, oth, r, d, inv, cm, *mats], 20, flops=500 << 20,
            )
        for k in (0, 2, 4):
            c1, c2 = exchange(one, two)
            r, d, sol = call(
                functools.partial(rest_kernel, half, face, coefs[k + 1]), [(wide, F32)] * 3,
                [r, d, sol, one, two, inv, cm, *mats], 20, flops=400 << 20,
            )
            if iteration == 0 and k == 0:
                r, d, sol, inv, cmn, na, nb, one, two = call(
                    functools.partial(first_sweep_kernel, half, face, mode_count, coefs[0], coefs[1], coefs[2]),
                    [(wide, F32)] * 4 + [((2 * half, face), F32)] + [((2 * face, face), BF16)] * 2 + [message, message],
                    [r, d, sol, one, two, c1, c2, inv, cm, *mats], 20, flops=500 << 20,
                )
                continue
            given = [r, d, sol, one, two, c1, c2, na, nb, inv, cm, cmn, *mats]
            if k < 4:
                r, d, sol, one, two = call(
                    functools.partial(sweep_kernel, half, face, coefs[k], coefs[k + 1], coefs[k + 2]),
                    [(wide, F32), (wide, F32), (wide, F32), message, message], given, 20, flops=500 << 20,
                )
            elif iteration < ITERS - 1:
                r, d, sol, chunks = call(
                    functools.partial(last_kernel, half, face, coefs[k], coefs[k + 1]),
                    [(wide, F32), (wide, F32), (wide, F32), ((n_mode, 2, half, quarter), F32)],
                    given, 20, flops=100 << 20,
                )
            else:
                own, other = call(
                    functools.partial(end_kernel, half, face, coefs[k], coefs[k + 1]),
                    [((half, count), F32)] * 2, given, 20, flops=100 << 20,
                )
        if iteration < ITERS - 1:
            planes_in = lax.all_to_all(
                chunks.reshape(2 * n_mode, half, quarter), ("mode", "dom"), 0, 0, axis_index_groups=groups, tiled=True
            )
            conv = convect(planes_in, False)
    other = lax.ppermute(other, "dom", swap)
    own, unit = call(
        finish_own_kernel, [((half, count), F32), ((count, count), BF16)], [own, place], 16, flops=200 << 20
    )
    (out,) = call(finish_kernel, [((modes, count), F32)], [own, other, unit], 16)
    return out


def solution(mesh):
    placed = (
        P("mode", "dom"),
        P("dom", None, None),
        P("dom"),
        P(),
        P("dom", None),
        P("dom", None, None),
        P(),
    )
    return jax.shard_map(
        functools.partial(body, mesh.shape["mode"], mesh.shape["dom"]),
        mesh=mesh, in_specs=placed, out_specs=P("mode", "dom"), check_vma=False,
    )
```

```python
import functools

import jax
import jax.numpy as jnp
import numpy as np
from jax import lax
from jax.experimental import pallas as pl
from jax.experimental.pallas import tpu as pltpu
from jax.sharding import PartitionSpec as P

ITERS = 3
SWEEPS = 6

mass_weight = 4.0
bound_low = 0.1
bound_high = 2.0
centre = (bound_high + bound_low) / 2.0
half_width = (bound_high - bound_low) / 2.0

F32 = jnp.float32
BF16 = jnp.bfloat16
ROW = 96


def chebyshev():
    ratio = centre / half_width
    rho = 1.0 / ratio
    coefs = [(0.0, 1.0 / centre)]
    for _ in range(SWEEPS - 1):
        rho_next = 1.0 / (2.0 * ratio - rho)
        coefs.append((rho_next * rho, 2.0 * rho_next / half_width))
        rho = rho_next
    return coefs


def synthesis_table(mode_count):
    column = np.arange(mode_count)
    number = np.where(column == 1, mode_count // 2, column // 2)
    is_sine = (column % 2 == 1) & (column > 1)
    planes = np.arange(mode_count)
    angles = (planes[:, None] * number[None, :] % mode_count) * (2.0 * np.pi / mode_count)
    return np.where(is_sine[None, :], np.sin(angles), np.cos(angles))


def halves(table):
    high = table.astype(np.float32).astype(BF16)
    return [high, (table - high.astype(np.float64)).astype(np.float32).astype(BF16)]


def split(value):
    high = value.astype(BF16)
    return high, (value - high.astype(F32)).astype(BF16)


def dot(a, b):
    return lax.dot_general(a, b, (((1,), (0,)), ((), ())), preferred_element_type=F32)


def rows_times(value, high, low):
    count = value.shape[0]
    h, l = split(value)
    both = dot(jnp.concatenate([h, l], axis=0), high)
    return both[:count] + both[count:] + dot(h, low)


def table_times(high, low, value, dim=1):
    dims = (((dim,), (0,)), ((), ()))
    count = value.shape[1]
    h, l = split(value)
    both = lax.dot_general(high, jnp.concatenate([h, l], axis=1), dims, preferred_element_type=F32)
    return both[:, :count] + both[:, count:] + lax.dot_general(low, h, dims, preferred_element_type=F32)


def iota(shape, dim):
    return lax.broadcasted_iota(jnp.int32, shape, dim)


def call(kernel, outs, vmem, limit, scratch=(), flops=0, moved=1 << 20, far=(), out_far=(), pinned=(), free=()):
    in_specs, given = [], []
    for i, v in enumerate(vmem):
        space = pltpu.HBM if i in far else pltpu.VMEM
        in_specs.append(pl.BlockSpec(memory_space=space))
        fixed = i in far or v.dtype == BF16 and v.shape not in free
        given.append(pltpu.with_memory_space_constraint(v, space) if fixed else v)
    shapes, out_specs = [], []
    for i, (s, t) in enumerate(outs):
        space = pltpu.HBM if i in out_far else pltpu.VMEM
        out_specs.append(pl.BlockSpec(memory_space=space))
        shapes.append(space(s, t) if i in out_far or i in pinned else jax.ShapeDtypeStruct(s, t))
    return pl.pallas_call(
        kernel,
        out_shape=shapes,
        in_specs=in_specs,
        out_specs=out_specs,
        scratch_shapes=list(scratch),
        compiler_params=pltpu.CompilerParams(vmem_limit_bytes=limit << 20),
        cost_estimate=pl.CostEstimate(flops=flops, bytes_accessed=moved, transcendentals=0),
    )(*given)


def position():
    q = lax.axis_index("dom")
    z = lax.shift_right_arithmetic(q, 1)
    return q, z, q - 2 * z


def picked(first, a, b):
    return jnp.where(first, a, b)


def order_kernel(
    iface_in, l2g_in, vel_in, mass_in, live_in, keep, send, chunks, place_out, iface, l2g, vel, mass, live, sems
):
    q, _, x = position()
    pairs = ((iface_in, iface), (l2g_in, l2g), (vel_in, vel), (mass_in, mass), (live_in, live))
    copies = [pltpu.make_async_copy(a, b, sems.at[i]) for i, (a, b) in enumerate(pairs)]
    for copy in copies:
        copy.start()
    for copy in copies:
        copy.wait()
    count = mass.shape[1]
    face = iface.shape[1]
    lists = jnp.concatenate(
        [picked(x == 0, iface[0:1, :], iface[1:2, :]), picked(x == 0, iface[1:2, :], iface[0:1, :])], axis=1
    ).astype(F32)
    lists = jnp.transpose(jnp.broadcast_to(lists, (8, 2 * face)))[:, 0:1]
    hit = jnp.where(lists == iota((1, count), 1).astype(F32), 1.0, 0.0)
    at = jnp.sum(hit * iota((2 * face, 1), 0).astype(F32), axis=0, keepdims=True)
    shared = jnp.sum(hit, axis=0, keepdims=True)
    rest = jnp.broadcast_to(1.0 - shared, (8, count))
    lane = iota((8, count), 1)
    run = rest
    step = 1
    while step < count:
        run = run + jnp.where(lane >= step, pltpu.roll(run, step, 1), 0.0)
        step *= 2
    place = jnp.where(rest > 0.5, run - 1.0 + 2.0 * face, jnp.broadcast_to(at, (8, count)))
    place_out[...] = place
    column = jnp.transpose(place)[:, 0:1]
    elems, side = l2g.shape
    slots = elems * ROW
    blank = jnp.full((1, ROW - side), -1, jnp.int32)
    row = jnp.concatenate([piece for e in range(elems) for piece in (l2g[e : e + 1, :], blank)], axis=1)
    pieces = []
    for first in range(0, slots, 512):
        part = row[:, first : first + 512]
        found = jnp.where(iota((count, 1), 0) == part, column, 0.0)
        pieces.append(jnp.where(part < 0, -1.0, jnp.sum(found, axis=0, keepdims=True)))
    index = jnp.concatenate(pieces, axis=1)
    unit = jnp.where(iota((1, count), 1).astype(F32) == column, 1.0, 0.0).astype(BF16)
    modes = vel.shape[0]
    half = modes // 2
    value = jnp.concatenate([vel[...], jnp.broadcast_to(mass[...], (16, count))], axis=0)
    high = value.astype(BF16)
    middle, low = split(value - high.astype(F32))
    total = modes + 16
    parts = dot(jnp.concatenate([high, middle, low], axis=0), unit)
    moved = parts[:total] + parts[total : 2 * total] + parts[2 * total :]
    a, b = moved[:half], moved[half:modes]
    lived = jnp.where(iota(live.shape, 1) == q, live[...], 0).astype(F32)
    lived = jnp.sum(lived, axis=1, keepdims=True)
    for ref, rows in ((keep, picked(x == 0, a, b)), (send, picked(x == 0, b, a))):
        ref[0:half, :] = rows
        ref[half : half + 8, :] = moved[modes : modes + 8]
        ref[half + 8 : half + 16, :] = jnp.broadcast_to(index[:, :count], (8, count))
        ref[half + 16 : half + 24, 0 : slots - count] = jnp.broadcast_to(
            index[:, count:], (8, slots - count)
        )
        ref[half + 16 : half + 24, slots - count :] = jnp.broadcast_to(lived, (8, 2 * count - slots))
    quarter = count // chunks.shape[0]
    for part in range(chunks.shape[0]):
        chunks[part] = moved[:modes, part * quarter : (part + 1) * quarter]


def own_build_kernel(half, ops_in, pack, high_out, low_out, diag, note, ops, *scratch):
    sems = scratch[-1]
    fetch = pltpu.make_async_copy(ops_in, ops, sems.at[0])
    fetch.start()
    partner_build_kernel(half, ops, pack, high_out, low_out, diag, note, *scratch, ready=fetch.wait)


def partner_build_kernel(half, ops, pack, high_out, low_out, diag, note, high, low, *scratch, ready=None):
    sems = scratch[-1]
    copies = []

    def ship(*rows):
        for part, out in ((high, high_out), (low, low_out)):
            at = pl.ds(*rows)
            copies.append(pltpu.make_async_copy(part.at[at], out.at[at], sems.at[len(copies) + 1]))
            copies[-1].start()

    build_kernel(half, ops, pack, high, low, diag, note, *scratch[:-1], ready=ready, ship=ship)
    for copy in copies:
        copy.wait()


def build_kernel(half, ops, pack, high, low, diag, note, flat, tall, qh, ql, pad, ready=None, ship=None):
    live = pack[half + 16 : half + 17, pack.shape[1] - 1 :]
    side, elems = ops.shape[0], ops.shape[1]
    count = high.shape[0]
    slots = elems * ROW
    index = jnp.concatenate(
        [pack[half + 8 : half + 16, :], pack[half + 16 : half + 24, 0 : slots - count]], axis=1
    )
    column = jnp.transpose(index)[:, 0:1]
    for first in range(0, slots, 256):
        block = jnp.where(iota((1, count), 1).astype(F32) == column[first : first + 256], 1.0, 0.0)
        tall[first : first + 256, :] = block.astype(BF16)
    tall[slots:, :] = jnp.zeros((tall.shape[0] - slots, count), BF16)
    for first in range(0, count, 256):
        block = jnp.where((iota((256, 1), 0) + first).astype(F32) == index[0:1], 1.0, 0.0)
        flat[first : first + 256, :] = block.astype(BF16)
    pad[...] = jnp.zeros(pad.shape, F32)
    if ready is not None:
        ready()
    for e in range(elems):
        pad[0:side, 0:side] = ops[:, e, :] * jnp.where(live > e + 0.5, 1.0, 0.0)
        oh, ol = split(pad[...])
        spread = dot(jnp.concatenate([oh, ol], axis=0), tall[e * ROW : e * ROW + 128, :])
        qh[e * ROW : (e + 1) * ROW, :] = spread[:ROW].astype(BF16)
        ql[e * ROW : (e + 1) * ROW, :] = spread[ROW:].astype(BF16)
    tile = 256
    face = note.shape[1]
    for j in range(0, count, tile):
        top = j + tile
        block = dot(flat[j:top, :], qh[:, j:]) + dot(flat[j:top, :], ql[:, j:])
        h, l = split(block)
        high[j:top, j:] = h
        low[j:top, j:] = l
        if ship is not None:
            ship(j, tile)
        if top < count:
            mirror = jnp.transpose(block[:, tile:])
            h, l = split(mirror)
            high[top:, j:top] = h
            low[top:, j:top] = l
        own_node = iota((tile, tile), 0) == iota((tile, tile), 1)
        line = jnp.sum(jnp.where(own_node, block[:, :tile], 0.0), axis=0, keepdims=True)
        diag[:, j:top] = jnp.broadcast_to(line, (8, tile))
        if not j:
            note[0:face, :] = block[0:face, 0:face]
            note[face : face + 8, :] = jnp.broadcast_to(line[:, 0:face], (8, face))
            note[face + 8 :, :] = pack[half : half + 8, 0:face]


def apply(value, mats, columns, half):
    oh, ol, ph, plo = mats[:4]
    return jnp.concatenate(
        [
            rows_times(value[:half], oh[:, columns], ol[:, columns]),
            rows_times(value[half:], ph[:, columns], plo[:, columns]),
        ],
        axis=0,
    )


def outer_apply(value, mats, half, face):
    parts = []
    for v, columns in ((value[:half], mats[4]), (value[half:], mats[5])):
        both = dot(jnp.concatenate(split(v), axis=0), columns[...])
        parts.append(both[:half, :face] + both[half:, :face] + both[:half, face:])
    return jnp.concatenate(parts, axis=0)


def face_times(value, rows):
    count = value.shape[0]
    h, l = split(value)
    first, second = jnp.concatenate([h, h], axis=1), jnp.concatenate([l, jnp.zeros_like(l)], axis=1)
    both = dot(jnp.concatenate([first, second], axis=0), rows)
    return both[:count] + both[count:]


def assembled(y, outer, half, face):
    inner = y[:half, face : 2 * face] + y[half:, face : 2 * face]
    first = y[:, :face] if outer is None else y[:, :face] + outer
    return jnp.concatenate([first, jnp.concatenate([inner, inner], axis=0), y[:, 2 * face :]], axis=1)


def first_planes_kernel(u_in, tables_in, slope_in, out, u, tables, slope, sems):
    pairs = ((u_in, u), (slope_in, slope), (tables_in, tables))
    copies = [pltpu.make_async_copy(a, b, sems.at[i]) for i, (a, b) in enumerate(pairs)]
    for copy in copies:
        copy.start()
    for copy in copies:
        copy.wait()
    planes_kernel(u, tables, slope, out)


def planes_kernel(u, tables, slope, out):
    count = slope.shape[1]
    high, low = tables[0:count, :], tables[count:, :]
    value = u[...]
    mode = iota((count, 1), 0)
    scale = lax.shift_right_arithmetic(mode, 1).astype(F32) * (2.0 / count)
    after, before = pltpu.roll(value, count - 1, 0), pltpu.roll(value, 1, 0)
    paired = jnp.where((mode & 1) == 0, scale * after, -scale * before)
    nodes = value.shape[1]
    both = table_times(high, low, jnp.concatenate([value, paired], axis=1))
    rate = jnp.transpose(jnp.broadcast_to(slope[...], (8, count)))[:, 0:1]
    cross = rate * both[:, :nodes] * both[:, nodes:]
    weight = jnp.where(mode < 2, 1.0 / count, 2.0 / count)
    out[...] = weight * table_times(high, low, cross, 0)


def provisional(r, d, g, inv, cm, mats, alpha, beta, half, face):
    r = r - inv * assembled(g, None, half, face)
    d = alpha * d + beta * r if alpha else beta * r
    y = outer_apply(d, mats, half, face) + cm[:, :face] * d[:, :face]
    return r, d, y


def even():
    _, z, x = position()
    return lax.rem(x + z, 2) == 0


def put(one, two, g, y, half, face, notes=((), ())):
    own = jnp.concatenate([g[:half, :face], y[:half], *notes[0]], axis=0)
    oth = jnp.concatenate([g[half:, :face], y[half:], *notes[1]], axis=0)
    first = even()
    one[...] = picked(first, own, oth)
    two[...] = picked(first, oth, own)


def got(one, two):
    a, b = one[...], two[...]
    first = even()
    return picked(first, a, b), picked(first, b, a)


def received(conv, half):
    _, _, x = position()
    parts = conv.shape[0]
    return jnp.concatenate(
        [
            jnp.concatenate([conv[m, x] for m in range(parts)], axis=1),
            jnp.concatenate([conv[m, 1 - x] for m in range(parts)], axis=1),
        ],
        axis=0,
    )


def masses(own, oth, half):
    count = own.shape[1]
    return jnp.concatenate(
        [jnp.broadcast_to(m[half : half + 1, :], (half, count)) for m in (own, oth)], axis=0
    )


def helmholtz(half, mode_count):
    _, _, x = position()
    mode = lax.axis_index("mode") * (2 * half) + x * half + iota((half, 1), 0)
    number = jnp.where(mode == 1, mode_count // 2, lax.shift_right_arithmetic(mode, 1))
    return mass_weight + (8.0 * number.astype(F32) / mode_count) ** 2


def beside(columns, rows, high, low):
    face = rows.shape[0] // 2
    columns[:, 0:face] = high[:, 0:face]
    columns[:, face:] = low[:, 0:face]
    rows[0:face, :] = high[0:face, :]
    rows[face:, :] = low[0:face, :]


def first_source_kernel(
    half, face, mode_count, conv, own, oth, do, dp, note_o, note_p, oh_in, ol_in, ph_in, plo_in,
    oh, ol, ph, plo, wo, wp, vo, vp, r_out, d_out, v_out, conv_out, inv_out, cm_out, one, two, sems,
):
    mats = (oh, ol, ph, plo, wo, wp, vo, vp)
    pairs = zip((oh_in, ol_in, ph_in, plo_in), mats)
    copies = [pltpu.make_async_copy(a, b, sems.at[i]) for i, (a, b) in enumerate(pairs)]
    for copy in copies:
        copy.start()
    c = helmholtz(half, mode_count)
    c = jnp.concatenate([c, c], axis=0)
    mass = masses(own, oth, half)
    stiff = jnp.concatenate([jnp.broadcast_to(t[0:1, :], (half, t.shape[1])) for t in (do, dp)], axis=0)
    inv = 1.0 / (assembled(stiff, None, half, face) + c * assembled(mass, None, half, face))
    inv = jnp.concatenate([jnp.zeros((2 * half, face), F32), inv[:, face:]], axis=1)
    inv_out[...] = inv
    cm = c * mass
    cm_out[...] = cm
    v = jnp.concatenate([own[0:half, :], oth[0:half, :]], axis=0)
    v_out[...] = v
    new = received(conv, half)
    conv_out[...] = new
    m4 = mass_weight * mass
    copies[0].wait()
    copies[1].wait()
    beside(wo, vo, oh, ol)
    e_own = rows_times(v[:half], oh[...], ol[...])
    copies[2].wait()
    copies[3].wait()
    beside(wp, vp, ph, plo)
    e_oth = rows_times(v[half:], ph[...], plo[...])
    g = jnp.concatenate([e_own, e_oth], axis=0) + (cm - m4) * v - m4 * new
    r = -inv * assembled(g, None, half, face)
    d = (1.0 / centre) * r
    r_out[...] = r
    d_out[...] = d
    y = outer_apply(d, mats, half, face)
    put(one, two, g, y, half, face, ((note_o[...],), (note_p[...],)))


def source_kernel(half, face, conv, old, own, oth, r, d, inv, cm, oh, ol, ph, plo, wo, wp, vo, vp, r_out, d_out, conv_out, one, two):
    mats = (oh, ol, ph, plo, wo, wp, vo, vp)
    new = received(conv, half)
    conv_out[...] = new
    cmv, dv = cm[...], d[...]
    g = apply(dv, mats, slice(None), half) + cmv * dv - mass_weight * masses(own, oth, half) * (new - old[...])
    rv, dv, y = provisional(r[...], None, g, inv[...], cmv, mats, 0.0, 1.0 / centre, half, face)
    r_out[...] = rv
    d_out[...] = dv
    put(one, two, g, y, half, face)


def rest_kernel(half, face, now, r, d, sol, s1, s2, inv, cm, oh, ol, ph, plo, wo, wp, vo, vp, r_out, d_out, sol_out):
    dv = d[...]
    y = apply(dv, (oh, ol, ph, plo, wo, wp, vo, vp), slice(face, None), half) + cm[:, face:] * dv[:, face:]
    y = jnp.concatenate([stacked(got(s1, s2), half, 2 * half), y], axis=1)
    rv = r[...] - inv[...] * assembled(y, None, half, face)
    dn = now[0] * dv + now[1] * rv
    r_out[...] = rv
    d_out[...] = dn
    sol_out[...] = sol[...] + dv + dn


def change_of(dd, theirs, mats, na, nb, half):
    change = [face_times(dd[:half], mats[6][...]), face_times(dd[half:], mats[7][...])]
    their_change = [face_times(theirs[:half], nb), face_times(theirs[half:], na)]
    return jnp.concatenate(change, axis=0), jnp.concatenate(their_change, axis=0)


def stacked(pair, first, last):
    return jnp.concatenate([t[first:last, :] for t in pair], axis=0)


def widened(value, face_part):
    face = face_part.shape[1]
    return jnp.concatenate([value[:, :face] + face_part, value[:, face:]], axis=1)


def corrected(half, face, now, r, d, sol, dr, dd, change, outer, inv):
    back = widened(-inv * assembled(change, outer, half, face), dr)
    step = widened(now[1] * back, now[0] * dd)
    return r + back, d + step, widened(sol + step, dd)


def exact(half, face, beta, now, r, d, sol, sent, came, na, nb, inv, cm, cmn, mats):
    inv_face = inv[:, :face]
    mine, came = got(*sent), got(*came)
    dr = -(inv_face * stacked(came, 0, half))
    dd = beta * dr
    theirs = -beta * (inv_face * stacked(mine, 0, half))
    change, their_change = change_of(dd, theirs, mats, na[...], nb[...], half)
    change = widened(change, cm[:, :face] * dd)
    outer = stacked(came, half, 2 * half) + their_change + cmn[...] * theirs
    return corrected(half, face, now, r[...], d[...], sol[...], dr, dd, change, outer, inv[...])


def first_sweep_kernel(
    half, face, mode_count, before, now, then,
    r, d, sol, s1, s2, c1, c2, inv, cm, oh, ol, ph, plo, wo, wp, vo, vp,
    r_out, d_out, sol_out, inv_out, cmn_out, na_out, nb_out, one, two,
):
    mats = (oh, ol, ph, plo, wo, wp, vo, vp)
    cm_v = cm[...]
    mine, came = got(s1, s2), got(c1, c2)
    c = helmholtz(half, mode_count)
    c = jnp.concatenate([c, c], axis=0)

    def line(pair, row):
        return jnp.concatenate([jnp.broadcast_to(t[row : row + 1, :], (half, face)) for t in pair], axis=0)

    at = 2 * half + face
    their_mass = line(came, at + 8)
    inv_face = 1.0 / (line(mine, at) + line(came, at) + c * (line(mine, at + 8) + their_mass))
    cmn = c * their_mass
    nb, na = (jnp.concatenate(split(t[2 * half : at, :]), axis=0) for t in came)
    dr = -inv_face * (stacked(mine, 0, half) + stacked(came, 0, half))
    dd = before[1] * dr
    change, their_change = change_of(dd, dd, mats, na, nb, half)
    change = widened(change, cm_v[:, :face] * dd)
    outer = stacked(mine, half, 2 * half) + stacked(came, half, 2 * half) + their_change + cmn * dd
    inv_v = jnp.concatenate([inv_face, inv[:, face:]], axis=1)
    rv, dn, sol_v = corrected(half, face, now, r[...], d[...], sol[...], dr, dd, change, outer, inv_v)
    inv_out[...] = inv_v
    cmn_out[...] = cmn
    na_out[...] = na
    nb_out[...] = nb
    sol_out[...] = sol_v
    g = apply(dn, mats, slice(None), half) + cm_v * dn
    rv, dv, y = provisional(rv, dn, g, inv_v, cm_v, mats, then[0], then[1], half, face)
    r_out[...] = rv
    d_out[...] = dv
    put(one, two, g, y, half, face)


def sweep_kernel(
    half, face, before, now, then,
    r, d, sol, s1, s2, c1, c2, na, nb, inv, cm, cmn, oh, ol, ph, plo, wo, wp, vo, vp,
    r_out, d_out, sol_out, one, two,
):
    mats = (oh, ol, ph, plo, wo, wp, vo, vp)
    rv, dn, sol_v = exact(half, face, before[1], now, r, d, sol, (s1, s2), (c1, c2), na, nb, inv, cm, cmn, mats)
    sol_out[...] = sol_v
    inv_v, cm_v = inv[...], cm[...]
    g = apply(dn, mats, slice(None), half) + cm_v * dn
    rv, dv, y = provisional(rv, dn, g, inv_v, cm_v, mats, then[0], then[1], half, face)
    r_out[...] = rv
    d_out[...] = dv
    put(one, two, g, y, half, face)


def last_kernel(
    half, face, before, now,
    r, d, sol, s1, s2, c1, c2, na, nb, inv, cm, cmn, oh, ol, ph, plo, wo, wp, vo, vp,
    r_out, d_out, sol_out, chunks,
):
    rv, dn, new = exact(
        half, face, before[1], now, r, d, sol, (s1, s2), (c1, c2), na, nb, inv, cm, cmn, (oh, ol, ph, plo, wo, wp, vo, vp)
    )
    r_out[...] = rv
    d_out[...] = dn
    sol_out[...] = new
    _, _, x = position()
    parts, width = chunks.shape[0], chunks.shape[3]
    for m in range(parts):
        chunks[m, x] = new[:half, m * width : (m + 1) * width]
        chunks[m, 1 - x] = new[half:, m * width : (m + 1) * width]


def end_kernel(
    half, face, before, now,
    r, d, sol, s1, s2, c1, c2, na, nb, inv, cm, cmn, oh, ol, ph, plo, wo, wp, vo, vp, own_out, oth_out,
):
    _, _, new = exact(
        half, face, before[1], now, r, d, sol, (s1, s2), (c1, c2), na, nb, inv, cm, cmn, (oh, ol, ph, plo, wo, wp, vo, vp)
    )
    own_out[...] = new[:half]
    oth_out[...] = new[half:]


def restored(value, unit):
    count = value.shape[0]
    high = value.astype(BF16)
    middle, low = split(value - high.astype(F32))
    parts = dot(jnp.concatenate([high, middle, low], axis=0), unit)
    return parts[:count] + parts[count : 2 * count] + parts[2 * count :]


def finish_own_kernel(own, place, out, unit_out):
    count = own.shape[1]
    unit = jnp.where(iota((count, 1), 0).astype(F32) == place[0:1, :], 1.0, 0.0).astype(BF16)
    unit_out[...] = unit
    out[...] = restored(own[...], unit)


def finish_kernel(own, other, unit, out):
    _, _, x = position()
    a, b = own[...], restored(other[...], unit[...])
    half = own.shape[0]
    out[0:half, :] = picked(x == 0, a, b)
    out[half:, :] = picked(x == 0, b, a)


def body(n_mode, n_dom, velocity_prev, elem_ops, lumped_mass, span_slope, local_to_global, iface_nodes, live_elems):
    modes, count = velocity_prev.shape
    half = modes // 2
    elems, side = local_to_global.shape
    face = iface_nodes.shape[2]
    mode_count = span_slope.shape[0]
    quarter = count // n_mode
    pairs = n_dom // 2
    slots = elems * ROW
    places = [(z, s) for z in range(pairs) for s in (0, 1)]
    swap = [(i, i ^ 1) for i in range(n_dom)]
    long_swap = [(2 * z + s, 2 * ((z + (1 if z % 2 else -1)) % pairs) + s) for z, s in places]
    short_swap = [(2 * z + s, 2 * ((z + (-1 if z % 2 else 1)) % pairs) + s) for z, s in places]
    groups = [[m * n_dom + 2 * z + s for m in range(n_mode) for s in (0, 1)] for z in range(pairs)]

    def exchange(one, two):
        return lax.ppermute(one, "dom", long_swap), lax.ppermute(two, "dom", short_swap)

    ops = jnp.transpose(elem_ops, (1, 0, 2))
    ops_other = lax.ppermute(ops, "dom", swap)
    pack = (half + 24, count)
    wide = (2 * half, count)
    keep, send, chunks, place = call(
        order_kernel,
        [(pack, F32), (pack, F32), ((n_mode, modes, quarter), F32), ((8, count), F32)],
        [iface_nodes[0], local_to_global, velocity_prev, lumped_mass.reshape(1, count), live_elems.reshape(1, n_dom)],
        24, far=range(5),
        scratch=[
            pltpu.VMEM((2, face), jnp.int32), pltpu.VMEM((elems, side), jnp.int32),
            pltpu.VMEM((modes, count), F32), pltpu.VMEM((1, count), F32), pltpu.VMEM((1, n_dom), jnp.int32),
            pltpu.SemaphoreType.DMA((5,)),
        ],
    )
    planes_in = lax.all_to_all(chunks, "mode", 0, 0, tiled=True)
    oth = lax.ppermute(send, "dom", swap)

    tables = jnp.asarray(np.concatenate(halves(synthesis_table(mode_count))))
    slope = span_slope.reshape(1, mode_count)

    def build(own, ops, packed):
        matrix = ((count, count), BF16)
        scratch = [
            pltpu.VMEM((count, count), BF16),
            pltpu.VMEM((count, count), BF16),
            pltpu.VMEM((count, slots), BF16),
            pltpu.VMEM((slots + 32, count), BF16),
            pltpu.VMEM((slots, count), BF16),
            pltpu.VMEM((slots, count), BF16),
            pltpu.VMEM((ROW, 128), F32),
            pltpu.SemaphoreType.DMA((2 * count // 256 + 1,)),
        ]
        return call(
            functools.partial(own_build_kernel if own else partner_build_kernel, half),
            [matrix, matrix, ((8, count), F32), ((face + 16, face), F32)], [ops, packed], 36,
            far=(0,) if own else (), out_far=(0, 1), flops=6 << 30,
            scratch=[pltpu.VMEM((side, elems, side), F32), *scratch] if own else scratch,
        )

    def convect(value, first):
        (out,) = call(
            first_planes_kernel if first else planes_kernel, [((mode_count, quarter), F32)],
            [value.reshape(mode_count, quarter), tables, slope], 16, flops=600 << 20,
            far=range(3) if first else (), free=(tables.shape,),
            scratch=[
                pltpu.VMEM((mode_count, quarter), F32), pltpu.VMEM(tables.shape, BF16),
                pltpu.VMEM(slope.shape, F32), pltpu.SemaphoreType.DMA((3,)),
            ] if first else (),
        )
        back = lax.all_to_all(
            out.reshape(2 * n_mode, half, quarter), ("mode", "dom"), 0, 0, axis_index_groups=groups, tiled=True
        )
        return back.reshape(n_mode, 2, half, quarter)

    oh, ol, do, note_o = build(True, ops, keep)
    conv = convect(planes_in, True)
    ph, plo, dp, note_p = build(False, ops_other, oth)
    mats = [oh, ol, ph, plo]
    coefs = chebyshev()
    message = ((2 * half, face), F32)
    for iteration in range(ITERS):
        if iteration == 0:
            long_message = ((2 * half + face + 16, face), F32)
            strips = [((count, 2 * face), BF16)] * 2 + [((2 * face, count), BF16)] * 2
            *mats, r, d, sol, old, inv, cm, one, two = call(
                functools.partial(first_source_kernel, half, face, mode_count),
                [*[((count, count), BF16)] * 4, *strips, *[(wide, F32)] * 6, long_message, long_message],
                [conv, keep, oth, do, dp, note_o, note_p, *mats], 20, flops=500 << 20,
                far=range(7, 11), pinned=range(8), scratch=[pltpu.SemaphoreType.DMA((4,))],
            )
        else:
            r, d, old, one, two = call(
                functools.partial(source_kernel, half, face),
                [(wide, F32), (wide, F32), (wide, F32), message, message],
                [conv, old, keep, oth, r, d, inv, cm, *mats], 20, flops=500 << 20,
            )
        for k in (0, 2, 4):
            c1, c2 = exchange(one, two)
            r, d, sol = call(
                functools.partial(rest_kernel, half, face, coefs[k + 1]), [(wide, F32)] * 3,
                [r, d, sol, one, two, inv, cm, *mats], 20, flops=400 << 20,
            )
            if iteration == 0 and k == 0:
                r, d, sol, inv, cmn, na, nb, one, two = call(
                    functools.partial(first_sweep_kernel, half, face, mode_count, coefs[0], coefs[1], coefs[2]),
                    [(wide, F32)] * 4 + [((2 * half, face), F32)] + [((2 * face, face), BF16)] * 2 + [message, message],
                    [r, d, sol, one, two, c1, c2, inv, cm, *mats], 20, flops=500 << 20,
                )
                continue
            given = [r, d, sol, one, two, c1, c2, na, nb, inv, cm, cmn, *mats]
            if k < 4:
                r, d, sol, one, two = call(
                    functools.partial(sweep_kernel, half, face, coefs[k], coefs[k + 1], coefs[k + 2]),
                    [(wide, F32), (wide, F32), (wide, F32), message, message], given, 20, flops=500 << 20,
                )
            elif iteration < ITERS - 1:
                r, d, sol, chunks = call(
                    functools.partial(last_kernel, half, face, coefs[k], coefs[k + 1]),
                    [(wide, F32), (wide, F32), (wide, F32), ((n_mode, 2, half, quarter), F32)],
                    given, 20, flops=100 << 20,
                )
            else:
                own, other = call(
                    functools.partial(end_kernel, half, face, coefs[k], coefs[k + 1]),
                    [((half, count), F32)] * 2, given, 20, flops=100 << 20,
                )
        if iteration < ITERS - 1:
            planes_in = lax.all_to_all(
                chunks.reshape(2 * n_mode, half, quarter), ("mode", "dom"), 0, 0, axis_index_groups=groups, tiled=True
            )
            conv = convect(planes_in, False)
    other = lax.ppermute(other, "dom", swap)
    own, unit = call(
        finish_own_kernel, [((half, count), F32), ((count, count), BF16)], [own, place], 16, flops=200 << 20
    )
    (out,) = call(finish_kernel, [((modes, count), F32)], [own, other, unit], 16)
    return out


def solution(mesh):
    placed = (
        P("mode", "dom"),
        P("dom", None, None),
        P("dom"),
        P(),
        P("dom", None),
        P("dom", None, None),
        P(),
    )
    return jax.shard_map(
        functools.partial(body, mesh.shape["mode"], mesh.shape["dom"]),
        mesh=mesh, in_specs=placed, out_specs=P("mode", "dom"), check_vma=False,
    )
```

```python
import functools

import jax
import jax.numpy as jnp
import numpy as np
from jax import lax
from jax.experimental import pallas as pl
from jax.experimental.pallas import tpu as pltpu
from jax.sharding import PartitionSpec as P

ITERS = 3
SWEEPS = 6

mass_weight = 4.0
bound_low = 0.1
bound_high = 2.0
centre = (bound_high + bound_low) / 2.0
half_width = (bound_high - bound_low) / 2.0

F32 = jnp.float32
BF16 = jnp.bfloat16
ROW = 96


def chebyshev():
    ratio = centre / half_width
    rho = 1.0 / ratio
    coefs = [(0.0, 1.0 / centre)]
    for _ in range(SWEEPS - 1):
        rho_next = 1.0 / (2.0 * ratio - rho)
        coefs.append((rho_next * rho, 2.0 * rho_next / half_width))
        rho = rho_next
    return coefs


def synthesis_table(mode_count):
    column = np.arange(mode_count)
    number = np.where(column == 1, mode_count // 2, column // 2)
    is_sine = (column % 2 == 1) & (column > 1)
    planes = np.arange(mode_count)
    angles = (planes[:, None] * number[None, :] % mode_count) * (2.0 * np.pi / mode_count)
    return np.where(is_sine[None, :], np.sin(angles), np.cos(angles))


def halves(table):
    high = table.astype(np.float32).astype(BF16)
    return [high, (table - high.astype(np.float64)).astype(np.float32).astype(BF16)]


def split(value):
    high = value.astype(BF16)
    return high, (value - high.astype(F32)).astype(BF16)


def dot(a, b):
    return lax.dot_general(a, b, (((1,), (0,)), ((), ())), preferred_element_type=F32)


def rows_times(value, high, low):
    count = value.shape[0]
    h, l = split(value)
    both = dot(jnp.concatenate([h, l], axis=0), high)
    return both[:count] + both[count:] + dot(h, low)


def table_times(high, low, value, dim=1):
    dims = (((dim,), (0,)), ((), ()))
    count = value.shape[1]
    h, l = split(value)
    both = lax.dot_general(high, jnp.concatenate([h, l], axis=1), dims, preferred_element_type=F32)
    return both[:, :count] + both[:, count:] + lax.dot_general(low, h, dims, preferred_element_type=F32)


def iota(shape, dim):
    return lax.broadcasted_iota(jnp.int32, shape, dim)


def call(kernel, outs, vmem, limit, scratch=(), flops=0, moved=1 << 20, far=(), out_far=(), pinned=(), free=()):
    in_specs, given = [], []
    for i, v in enumerate(vmem):
        space = pltpu.HBM if i in far else pltpu.VMEM
        in_specs.append(pl.BlockSpec(memory_space=space))
        fixed = i in far or v.dtype == BF16 and v.shape not in free
        given.append(pltpu.with_memory_space_constraint(v, space) if fixed else v)
    shapes, out_specs = [], []
    for i, (s, t) in enumerate(outs):
        space = pltpu.HBM if i in out_far else pltpu.VMEM
        out_specs.append(pl.BlockSpec(memory_space=space))
        shapes.append(space(s, t) if i in out_far or i in pinned else jax.ShapeDtypeStruct(s, t))
    return pl.pallas_call(
        kernel,
        out_shape=shapes,
        in_specs=in_specs,
        out_specs=out_specs,
        scratch_shapes=list(scratch),
        compiler_params=pltpu.CompilerParams(vmem_limit_bytes=limit << 20),
        cost_estimate=pl.CostEstimate(flops=flops, bytes_accessed=moved, transcendentals=0),
    )(*given)


def position():
    q = lax.axis_index("dom")
    z = lax.shift_right_arithmetic(q, 1)
    return q, z, q - 2 * z


def picked(first, a, b):
    return jnp.where(first, a, b)


def order_kernel(
    iface_in, l2g_in, vel_in, mass_in, live_in, keep, send, chunks, place_out, iface, l2g, vel, mass, live, sems
):
    q, _, x = position()
    pairs = ((iface_in, iface), (l2g_in, l2g), (vel_in, vel), (mass_in, mass), (live_in, live))
    copies = [pltpu.make_async_copy(a, b, sems.at[i]) for i, (a, b) in enumerate(pairs)]
    for copy in copies:
        copy.start()
    for copy in copies:
        copy.wait()
    count = mass.shape[1]
    face = iface.shape[1]
    lists = jnp.concatenate(
        [picked(x == 0, iface[0:1, :], iface[1:2, :]), picked(x == 0, iface[1:2, :], iface[0:1, :])], axis=1
    ).astype(F32)
    lists = jnp.transpose(jnp.broadcast_to(lists, (8, 2 * face)))[:, 0:1]
    hit = jnp.where(lists == iota((1, count), 1).astype(F32), 1.0, 0.0)
    at = jnp.sum(hit * iota((2 * face, 1), 0).astype(F32), axis=0, keepdims=True)
    shared = jnp.sum(hit, axis=0, keepdims=True)
    rest = jnp.broadcast_to(1.0 - shared, (8, count))
    lane = iota((8, count), 1)
    run = rest
    step = 1
    while step < count:
        run = run + jnp.where(lane >= step, pltpu.roll(run, step, 1), 0.0)
        step *= 2
    place = jnp.where(rest > 0.5, run - 1.0 + 2.0 * face, jnp.broadcast_to(at, (8, count)))
    place_out[...] = place
    column = jnp.transpose(place)[:, 0:1]
    elems, side = l2g.shape
    slots = elems * ROW
    blank = jnp.full((1, ROW - side), -1, jnp.int32)
    row = jnp.concatenate([piece for e in range(elems) for piece in (l2g[e : e + 1, :], blank)], axis=1)
    pieces = []
    for first in range(0, slots, 512):
        part = row[:, first : first + 512]
        found = jnp.where(iota((count, 1), 0) == part, column, 0.0)
        pieces.append(jnp.where(part < 0, -1.0, jnp.sum(found, axis=0, keepdims=True)))
    index = jnp.concatenate(pieces, axis=1)
    unit = jnp.where(iota((1, count), 1).astype(F32) == column, 1.0, 0.0).astype(BF16)
    modes = vel.shape[0]
    half = modes // 2
    value = jnp.concatenate([vel[...], jnp.broadcast_to(mass[...], (16, count))], axis=0)
    high = value.astype(BF16)
    middle, low = split(value - high.astype(F32))
    total = modes + 16
    parts = dot(jnp.concatenate([high, middle, low], axis=0), unit)
    moved = parts[:total] + parts[total : 2 * total] + parts[2 * total :]
    a, b = moved[:half], moved[half:modes]
    lived = jnp.where(iota(live.shape, 1) == q, live[...], 0).astype(F32)
    lived = jnp.sum(lived, axis=1, keepdims=True)
    for ref, rows in ((keep, picked(x == 0, a, b)), (send, picked(x == 0, b, a))):
        ref[0:half, :] = rows
        ref[half : half + 8, :] = moved[modes : modes + 8]
        ref[half + 8 : half + 16, :] = jnp.broadcast_to(index[:, :count], (8, count))
        ref[half + 16 : half + 24, 0 : slots - count] = jnp.broadcast_to(
            index[:, count:], (8, slots - count)
        )
        ref[half + 16 : half + 24, slots - count :] = jnp.broadcast_to(lived, (8, 2 * count - slots))
    quarter = count // chunks.shape[0]
    for part in range(chunks.shape[0]):
        chunks[part] = moved[:modes, part * quarter : (part + 1) * quarter]


def own_build_kernel(half, ops_in, pack, high_out, low_out, diag, note, ops, *scratch):
    sems = scratch[-1]
    fetch = pltpu.make_async_copy(ops_in, ops, sems.at[0])
    fetch.start()
    partner_build_kernel(half, ops, pack, high_out, low_out, diag, note, *scratch, ready=fetch.wait)


def partner_build_kernel(half, ops, pack, high_out, low_out, diag, note, high, low, *scratch, ready=None):
    sems = scratch[-1]
    copies = []

    def ship(*rows):
        for part, out in ((high, high_out), (low, low_out)):
            at = pl.ds(*rows)
            copies.append(pltpu.make_async_copy(part.at[at], out.at[at], sems.at[len(copies) + 1]))
            copies[-1].start()

    build_kernel(half, ops, pack, high, low, diag, note, *scratch[:-1], ready=ready, ship=ship)
    for copy in copies:
        copy.wait()


def build_kernel(half, ops, pack, high, low, diag, note, flat, tall, qh, ql, pad, ready=None, ship=None):
    live = pack[half + 16 : half + 17, pack.shape[1] - 1 :]
    side, elems = ops.shape[0], ops.shape[1]
    count = high.shape[0]
    slots = elems * ROW
    index = jnp.concatenate(
        [pack[half + 8 : half + 16, :], pack[half + 16 : half + 24, 0 : slots - count]], axis=1
    )
    column = jnp.transpose(index)[:, 0:1]
    for first in range(0, slots, 256):
        block = jnp.where(iota((1, count), 1).astype(F32) == column[first : first + 256], 1.0, 0.0)
        tall[first : first + 256, :] = block.astype(BF16)
    tall[slots:, :] = jnp.zeros((tall.shape[0] - slots, count), BF16)
    for first in range(0, count, 256):
        block = jnp.where((iota((256, 1), 0) + first).astype(F32) == index[0:1], 1.0, 0.0)
        flat[first : first + 256, :] = block.astype(BF16)
    pad[...] = jnp.zeros(pad.shape, F32)
    if ready is not None:
        ready()
    for e in range(elems):
        pad[0:side, 0:side] = ops[:, e, :] * jnp.where(live > e + 0.5, 1.0, 0.0)
        oh, ol = split(pad[...])
        spread = dot(jnp.concatenate([oh, ol], axis=0), tall[e * ROW : e * ROW + 128, :])
        qh[e * ROW : (e + 1) * ROW, :] = spread[:ROW].astype(BF16)
        ql[e * ROW : (e + 1) * ROW, :] = spread[ROW:].astype(BF16)
    tile = 256
    face = note.shape[1]
    for j in range(0, count, tile):
        top = j + tile
        block = dot(flat[j:top, :], qh[:, j:]) + dot(flat[j:top, :], ql[:, j:])
        h, l = split(block)
        high[j:top, j:] = h
        low[j:top, j:] = l
        if ship is not None:
            ship(j, tile)
        if top < count:
            mirror = jnp.transpose(block[:, tile:])
            h, l = split(mirror)
            high[top:, j:top] = h
            low[top:, j:top] = l
        own_node = iota((tile, tile), 0) == iota((tile, tile), 1)
        line = jnp.sum(jnp.where(own_node, block[:, :tile], 0.0), axis=0, keepdims=True)
        diag[:, j:top] = jnp.broadcast_to(line, (8, tile))
        if not j:
            note[0:face, :] = block[0:face, 0:face]
            note[face : face + 8, :] = jnp.broadcast_to(line[:, 0:face], (8, face))
            note[face + 8 :, :] = pack[half : half + 8, 0:face]


def apply(value, mats, columns, half):
    oh, ol, ph, plo = mats[:4]
    return jnp.concatenate(
        [
            rows_times(value[:half], oh[:, columns], ol[:, columns]),
            rows_times(value[half:], ph[:, columns], plo[:, columns]),
        ],
        axis=0,
    )


def outer_apply(value, mats, half, face):
    parts = []
    for v, columns in ((value[:half], mats[4]), (value[half:], mats[5])):
        both = dot(jnp.concatenate(split(v), axis=0), columns[...])
        parts.append(both[:half, :face] + both[half:, :face] + both[:half, face:])
    return jnp.concatenate(parts, axis=0)


def face_times(value, rows):
    count = value.shape[0]
    h, l = split(value)
    first, second = jnp.concatenate([h, h], axis=1), jnp.concatenate([l, jnp.zeros_like(l)], axis=1)
    both = dot(jnp.concatenate([first, second], axis=0), rows)
    return both[:count] + both[count:]


def assembled(y, outer, half, face):
    inner = y[:half, face : 2 * face] + y[half:, face : 2 * face]
    first = y[:, :face] if outer is None else y[:, :face] + outer
    return jnp.concatenate([first, jnp.concatenate([inner, inner], axis=0), y[:, 2 * face :]], axis=1)


def first_planes_kernel(u, tables_in, slope_in, out, tables, slope, sems):
    pairs = ((slope_in, slope), (tables_in, tables))
    copies = [pltpu.make_async_copy(a, b, sems.at[i]) for i, (a, b) in enumerate(pairs)]
    for copy in copies:
        copy.start()
    for copy in copies:
        copy.wait()
    planes_kernel(u, tables, slope, out)


def planes_kernel(u, tables, slope, out):
    count = slope.shape[1]
    high, low = tables[0:count, :], tables[count:, :]
    value = u[...]
    mode = iota((count, 1), 0)
    scale = lax.shift_right_arithmetic(mode, 1).astype(F32) * (2.0 / count)
    after, before = pltpu.roll(value, count - 1, 0), pltpu.roll(value, 1, 0)
    paired = jnp.where((mode & 1) == 0, scale * after, -scale * before)
    nodes = value.shape[1]
    both = table_times(high, low, jnp.concatenate([value, paired], axis=1))
    rate = jnp.transpose(jnp.broadcast_to(slope[...], (8, count)))[:, 0:1]
    cross = rate * both[:, :nodes] * both[:, nodes:]
    weight = jnp.where(mode < 2, 1.0 / count, 2.0 / count)
    out[...] = weight * table_times(high, low, cross, 0)


def provisional(r, d, g, inv, cm, mats, alpha, beta, half, face):
    r = r - inv * assembled(g, None, half, face)
    d = alpha * d + beta * r if alpha else beta * r
    y = outer_apply(d, mats, half, face) + cm[:, :face] * d[:, :face]
    return r, d, y


def even():
    _, z, x = position()
    return lax.rem(x + z, 2) == 0


def put(one, two, g, y, half, face, notes=((), ())):
    own = jnp.concatenate([g[:half, :face], y[:half], *notes[0]], axis=0)
    oth = jnp.concatenate([g[half:, :face], y[half:], *notes[1]], axis=0)
    first = even()
    one[...] = picked(first, own, oth)
    two[...] = picked(first, oth, own)


def got(one, two):
    a, b = one[...], two[...]
    first = even()
    return picked(first, a, b), picked(first, b, a)


def received(conv, half):
    _, _, x = position()
    parts = conv.shape[0]
    return jnp.concatenate(
        [
            jnp.concatenate([conv[m, x] for m in range(parts)], axis=1),
            jnp.concatenate([conv[m, 1 - x] for m in range(parts)], axis=1),
        ],
        axis=0,
    )


def masses(own, oth, half):
    count = own.shape[1]
    return jnp.concatenate(
        [jnp.broadcast_to(m[half : half + 1, :], (half, count)) for m in (own, oth)], axis=0
    )


def helmholtz(half, mode_count):
    _, _, x = position()
    mode = lax.axis_index("mode") * (2 * half) + x * half + iota((half, 1), 0)
    number = jnp.where(mode == 1, mode_count // 2, lax.shift_right_arithmetic(mode, 1))
    return mass_weight + (8.0 * number.astype(F32) / mode_count) ** 2


def beside(columns, rows, high, low):
    face = rows.shape[0] // 2
    columns[:, 0:face] = high[:, 0:face]
    columns[:, face:] = low[:, 0:face]
    rows[0:face, :] = high[0:face, :]
    rows[face:, :] = low[0:face, :]


def first_source_kernel(
    half, face, mode_count, conv, own, oth, do, dp, note_o, note_p, oh_in, ol_in, ph_in, plo_in,
    oh, ol, ph, plo, wo, wp, vo, vp, r_out, d_out, v_out, conv_out, inv_out, cm_out, one, two, sems,
):
    mats = (oh, ol, ph, plo, wo, wp, vo, vp)
    pairs = zip((oh_in, ol_in, ph_in, plo_in), mats)
    copies = [pltpu.make_async_copy(a, b, sems.at[i]) for i, (a, b) in enumerate(pairs)]
    for copy in copies:
        copy.start()
    c = helmholtz(half, mode_count)
    c = jnp.concatenate([c, c], axis=0)
    mass = masses(own, oth, half)
    stiff = jnp.concatenate([jnp.broadcast_to(t[0:1, :], (half, t.shape[1])) for t in (do, dp)], axis=0)
    inv = 1.0 / (assembled(stiff, None, half, face) + c * assembled(mass, None, half, face))
    inv = jnp.concatenate([jnp.zeros((2 * half, face), F32), inv[:, face:]], axis=1)
    inv_out[...] = inv
    cm = c * mass
    cm_out[...] = cm
    v = jnp.concatenate([own[0:half, :], oth[0:half, :]], axis=0)
    v_out[...] = v
    new = received(conv, half)
    conv_out[...] = new
    m4 = mass_weight * mass
    copies[0].wait()
    copies[1].wait()
    beside(wo, vo, oh, ol)
    e_own = rows_times(v[:half], oh[...], ol[...])
    copies[2].wait()
    copies[3].wait()
    beside(wp, vp, ph, plo)
    e_oth = rows_times(v[half:], ph[...], plo[...])
    g = jnp.concatenate([e_own, e_oth], axis=0) + (cm - m4) * v - m4 * new
    r = -inv * assembled(g, None, half, face)
    d = (1.0 / centre) * r
    r_out[...] = r
    d_out[...] = d
    y = outer_apply(d, mats, half, face)
    put(one, two, g, y, half, face, ((note_o[...],), (note_p[...],)))


def source_kernel(half, face, conv, old, own, oth, r, d, inv, cm, oh, ol, ph, plo, wo, wp, vo, vp, r_out, d_out, conv_out, one, two):
    mats = (oh, ol, ph, plo, wo, wp, vo, vp)
    new = received(conv, half)
    conv_out[...] = new
    cmv, dv = cm[...], d[...]
    g = apply(dv, mats, slice(None), half) + cmv * dv - mass_weight * masses(own, oth, half) * (new - old[...])
    rv, dv, y = provisional(r[...], None, g, inv[...], cmv, mats, 0.0, 1.0 / centre, half, face)
    r_out[...] = rv
    d_out[...] = dv
    put(one, two, g, y, half, face)


def rest_kernel(half, face, now, r, d, sol, s1, s2, inv, cm, oh, ol, ph, plo, wo, wp, vo, vp, r_out, d_out, sol_out):
    dv = d[...]
    y = apply(dv, (oh, ol, ph, plo, wo, wp, vo, vp), slice(face, None), half) + cm[:, face:] * dv[:, face:]
    y = jnp.concatenate([stacked(got(s1, s2), half, 2 * half), y], axis=1)
    rv = r[...] - inv[...] * assembled(y, None, half, face)
    dn = now[0] * dv + now[1] * rv
    r_out[...] = rv
    d_out[...] = dn
    sol_out[...] = sol[...] + dv + dn


def change_of(dd, theirs, mats, na, nb, half):
    change = [face_times(dd[:half], mats[6][...]), face_times(dd[half:], mats[7][...])]
    their_change = [face_times(theirs[:half], nb), face_times(theirs[half:], na)]
    return jnp.concatenate(change, axis=0), jnp.concatenate(their_change, axis=0)


def stacked(pair, first, last):
    return jnp.concatenate([t[first:last, :] for t in pair], axis=0)


def widened(value, face_part):
    face = face_part.shape[1]
    return jnp.concatenate([value[:, :face] + face_part, value[:, face:]], axis=1)


def corrected(half, face, now, r, d, sol, dr, dd, change, outer, inv):
    back = widened(-inv * assembled(change, outer, half, face), dr)
    step = widened(now[1] * back, now[0] * dd)
    return r + back, d + step, widened(sol + step, dd)


def exact(half, face, beta, now, r, d, sol, sent, came, na, nb, inv, cm, cmn, mats):
    inv_face = inv[:, :face]
    mine, came = got(*sent), got(*came)
    dr = -(inv_face * stacked(came, 0, half))
    dd = beta * dr
    theirs = -beta * (inv_face * stacked(mine, 0, half))
    change, their_change = change_of(dd, theirs, mats, na[...], nb[...], half)
    change = widened(change, cm[:, :face] * dd)
    outer = stacked(came, half, 2 * half) + their_change + cmn[...] * theirs
    return corrected(half, face, now, r[...], d[...], sol[...], dr, dd, change, outer, inv[...])


def first_sweep_kernel(
    half, face, mode_count, before, now, then,
    r, d, sol, s1, s2, c1, c2, inv, cm, oh, ol, ph, plo, wo, wp, vo, vp,
    r_out, d_out, sol_out, inv_out, cmn_out, na_out, nb_out, one, two,
):
    mats = (oh, ol, ph, plo, wo, wp, vo, vp)
    cm_v = cm[...]
    mine, came = got(s1, s2), got(c1, c2)
    c = helmholtz(half, mode_count)
    c = jnp.concatenate([c, c], axis=0)

    def line(pair, row):
        return jnp.concatenate([jnp.broadcast_to(t[row : row + 1, :], (half, face)) for t in pair], axis=0)

    at = 2 * half + face
    their_mass = line(came, at + 8)
    inv_face = 1.0 / (line(mine, at) + line(came, at) + c * (line(mine, at + 8) + their_mass))
    cmn = c * their_mass
    nb, na = (jnp.concatenate(split(t[2 * half : at, :]), axis=0) for t in came)
    dr = -inv_face * (stacked(mine, 0, half) + stacked(came, 0, half))
    dd = before[1] * dr
    change, their_change = change_of(dd, dd, mats, na, nb, half)
    change = widened(change, cm_v[:, :face] * dd)
    outer = stacked(mine, half, 2 * half) + stacked(came, half, 2 * half) + their_change + cmn * dd
    inv_v = jnp.concatenate([inv_face, inv[:, face:]], axis=1)
    rv, dn, sol_v = corrected(half, face, now, r[...], d[...], sol[...], dr, dd, change, outer, inv_v)
    inv_out[...] = inv_v
    cmn_out[...] = cmn
    na_out[...] = na
    nb_out[...] = nb
    sol_out[...] = sol_v
    g = apply(dn, mats, slice(None), half) + cm_v * dn
    rv, dv, y = provisional(rv, dn, g, inv_v, cm_v, mats, then[0], then[1], half, face)
    r_out[...] = rv
    d_out[...] = dv
    put(one, two, g, y, half, face)


def sweep_kernel(
    half, face, before, now, then,
    r, d, sol, s1, s2, c1, c2, na, nb, inv, cm, cmn, oh, ol, ph, plo, wo, wp, vo, vp,
    r_out, d_out, sol_out, one, two,
):
    mats = (oh, ol, ph, plo, wo, wp, vo, vp)
    rv, dn, sol_v = exact(half, face, before[1], now, r, d, sol, (s1, s2), (c1, c2), na, nb, inv, cm, cmn, mats)
    sol_out[...] = sol_v
    inv_v, cm_v = inv[...], cm[...]
    g = apply(dn, mats, slice(None), half) + cm_v * dn
    rv, dv, y = provisional(rv, dn, g, inv_v, cm_v, mats, then[0], then[1], half, face)
    r_out[...] = rv
    d_out[...] = dv
    put(one, two, g, y, half, face)


def last_kernel(
    half, face, before, now,
    r, d, sol, s1, s2, c1, c2, na, nb, inv, cm, cmn, oh, ol, ph, plo, wo, wp, vo, vp,
    r_out, d_out, sol_out, chunks,
):
    rv, dn, new = exact(
        half, face, before[1], now, r, d, sol, (s1, s2), (c1, c2), na, nb, inv, cm, cmn, (oh, ol, ph, plo, wo, wp, vo, vp)
    )
    r_out[...] = rv
    d_out[...] = dn
    sol_out[...] = new
    _, _, x = position()
    parts, width = chunks.shape[0], chunks.shape[3]
    for m in range(parts):
        chunks[m, x] = new[:half, m * width : (m + 1) * width]
        chunks[m, 1 - x] = new[half:, m * width : (m + 1) * width]


def end_kernel(
    half, face, before, now,
    r, d, sol, s1, s2, c1, c2, na, nb, inv, cm, cmn, oh, ol, ph, plo, wo, wp, vo, vp, own_out, oth_out,
):
    _, _, new = exact(
        half, face, before[1], now, r, d, sol, (s1, s2), (c1, c2), na, nb, inv, cm, cmn, (oh, ol, ph, plo, wo, wp, vo, vp)
    )
    own_out[...] = new[:half]
    oth_out[...] = new[half:]


def restored(value, unit):
    count = value.shape[0]
    high = value.astype(BF16)
    middle, low = split(value - high.astype(F32))
    parts = dot(jnp.concatenate([high, middle, low], axis=0), unit)
    return parts[:count] + parts[count : 2 * count] + parts[2 * count :]


def finish_own_kernel(own, place, out, unit_out):
    count = own.shape[1]
    unit = jnp.where(iota((count, 1), 0).astype(F32) == place[0:1, :], 1.0, 0.0).astype(BF16)
    unit_out[...] = unit
    out[...] = restored(own[...], unit)


def finish_kernel(own, other, unit, out):
    _, _, x = position()
    a, b = own[...], restored(other[...], unit[...])
    half = own.shape[0]
    out[0:half, :] = picked(x == 0, a, b)
    out[half:, :] = picked(x == 0, b, a)


def body(n_mode, n_dom, velocity_prev, elem_ops, lumped_mass, span_slope, local_to_global, iface_nodes, live_elems):
    modes, count = velocity_prev.shape
    half = modes // 2
    elems, side = local_to_global.shape
    face = iface_nodes.shape[2]
    mode_count = span_slope.shape[0]
    quarter = count // n_mode
    pairs = n_dom // 2
    slots = elems * ROW
    places = [(z, s) for z in range(pairs) for s in (0, 1)]
    swap = [(i, i ^ 1) for i in range(n_dom)]
    long_swap = [(2 * z + s, 2 * ((z + (1 if z % 2 else -1)) % pairs) + s) for z, s in places]
    short_swap = [(2 * z + s, 2 * ((z + (-1 if z % 2 else 1)) % pairs) + s) for z, s in places]
    groups = [[m * n_dom + 2 * z + s for m in range(n_mode) for s in (0, 1)] for z in range(pairs)]

    def exchange(one, two):
        return lax.ppermute(one, "dom", long_swap), lax.ppermute(two, "dom", short_swap)

    ops = jnp.transpose(elem_ops, (1, 0, 2))
    pack = (half + 24, count)
    wide = (2 * half, count)
    keep, send, chunks, place = call(
        order_kernel,
        [(pack, F32), (pack, F32), ((n_mode, modes, quarter), F32), ((8, count), F32)],
        [iface_nodes[0], local_to_global, velocity_prev, lumped_mass.reshape(1, count), live_elems.reshape(1, n_dom)],
        24, far=range(5),
        scratch=[
            pltpu.VMEM((2, face), jnp.int32), pltpu.VMEM((elems, side), jnp.int32),
            pltpu.VMEM((modes, count), F32), pltpu.VMEM((1, count), F32), pltpu.VMEM((1, n_dom), jnp.int32),
            pltpu.SemaphoreType.DMA((5,)),
        ],
    )
    planes_in = lax.all_to_all(chunks, "mode", 0, 0, tiled=True)
    send, ops_late = lax.optimization_barrier((send, ops))
    ops_other = lax.ppermute(ops_late, "dom", swap)
    oth = lax.ppermute(send, "dom", swap)

    tables = jnp.asarray(np.concatenate(halves(synthesis_table(mode_count))))
    slope = span_slope.reshape(1, mode_count)

    def build(own, ops, packed):
        matrix = ((count, count), BF16)
        scratch = [
            pltpu.VMEM((count, count), BF16),
            pltpu.VMEM((count, count), BF16),
            pltpu.VMEM((count, slots), BF16),
            pltpu.VMEM((slots + 32, count), BF16),
            pltpu.VMEM((slots, count), BF16),
            pltpu.VMEM((slots, count), BF16),
            pltpu.VMEM((ROW, 128), F32),
            pltpu.SemaphoreType.DMA((2 * count // 256 + 1,)),
        ]
        return call(
            functools.partial(own_build_kernel if own else partner_build_kernel, half),
            [matrix, matrix, ((8, count), F32), ((face + 16, face), F32)], [ops, packed], 36,
            far=(0,) if own else (), out_far=(0, 1), flops=6 << 30,
            scratch=[pltpu.VMEM((side, elems, side), F32), *scratch] if own else scratch,
        )

    def convect(value, first):
        (out,) = call(
            first_planes_kernel if first else planes_kernel, [((mode_count, quarter), F32)],
            [value.reshape(mode_count, quarter), tables, slope], 16, flops=600 << 20,
            far=(1, 2) if first else (), free=(tables.shape,),
            scratch=[
                pltpu.VMEM(tables.shape, BF16), pltpu.VMEM(slope.shape, F32), pltpu.SemaphoreType.DMA((2,)),
            ] if first else (),
        )
        back = lax.all_to_all(
            out.reshape(2 * n_mode, half, quarter), ("mode", "dom"), 0, 0, axis_index_groups=groups, tiled=True
        )
        return back.reshape(n_mode, 2, half, quarter)

    oh, ol, do, note_o = build(True, ops, keep)
    conv = convect(planes_in, True)
    ph, plo, dp, note_p = build(False, ops_other, oth)
    mats = [oh, ol, ph, plo]
    coefs = chebyshev()
    message = ((2 * half, face), F32)
    for iteration in range(ITERS):
        if iteration == 0:
            long_message = ((2 * half + face + 16, face), F32)
            strips = [((count, 2 * face), BF16)] * 2 + [((2 * face, count), BF16)] * 2
            *mats, r, d, sol, old, inv, cm, one, two = call(
                functools.partial(first_source_kernel, half, face, mode_count),
                [*[((count, count), BF16)] * 4, *strips, *[(wide, F32)] * 6, long_message, long_message],
                [conv, keep, oth, do, dp, note_o, note_p, *mats], 20, flops=500 << 20,
                far=range(7, 11), pinned=range(8), scratch=[pltpu.SemaphoreType.DMA((4,))],
            )
        else:
            r, d, old, one, two = call(
                functools.partial(source_kernel, half, face),
                [(wide, F32), (wide, F32), (wide, F32), message, message],
                [conv, old, keep, oth, r, d, inv, cm, *mats], 20, flops=500 << 20,
            )
        for k in (0, 2, 4):
            c1, c2 = exchange(one, two)
            r, d, sol = call(
                functools.partial(rest_kernel, half, face, coefs[k + 1]), [(wide, F32)] * 3,
                [r, d, sol, one, two, inv, cm, *mats], 20, flops=400 << 20,
            )
            if iteration == 0 and k == 0:
                r, d, sol, inv, cmn, na, nb, one, two = call(
                    functools.partial(first_sweep_kernel, half, face, mode_count, coefs[0], coefs[1], coefs[2]),
                    [(wide, F32)] * 4 + [((2 * half, face), F32)] + [((2 * face, face), BF16)] * 2 + [message, message],
                    [r, d, sol, one, two, c1, c2, inv, cm, *mats], 20, flops=500 << 20,
                )
                continue
            given = [r, d, sol, one, two, c1, c2, na, nb, inv, cm, cmn, *mats]
            if k < 4:
                r, d, sol, one, two = call(
                    functools.partial(sweep_kernel, half, face, coefs[k], coefs[k + 1], coefs[k + 2]),
                    [(wide, F32), (wide, F32), (wide, F32), message, message], given, 20, flops=500 << 20,
                )
            elif iteration < ITERS - 1:
                r, d, sol, chunks = call(
                    functools.partial(last_kernel, half, face, coefs[k], coefs[k + 1]),
                    [(wide, F32), (wide, F32), (wide, F32), ((n_mode, 2, half, quarter), F32)],
                    given, 20, flops=100 << 20,
                )
            else:
                own, other = call(
                    functools.partial(end_kernel, half, face, coefs[k], coefs[k + 1]),
                    [((half, count), F32)] * 2, given, 20, flops=100 << 20,
                )
        if iteration < ITERS - 1:
            planes_in = lax.all_to_all(
                chunks.reshape(2 * n_mode, half, quarter), ("mode", "dom"), 0, 0, axis_index_groups=groups, tiled=True
            )
            conv = convect(planes_in, False)
    other = lax.ppermute(other, "dom", swap)
    own, unit = call(
        finish_own_kernel, [((half, count), F32), ((count, count), BF16)], [own, place], 16, flops=200 << 20
    )
    (out,) = call(finish_kernel, [((modes, count), F32)], [own, other, unit], 16)
    return out


def solution(mesh):
    placed = (
        P("mode", "dom"),
        P("dom", None, None),
        P("dom"),
        P(),
        P("dom", None),
        P("dom", None, None),
        P(),
    )
    return jax.shard_map(
        functools.partial(body, mesh.shape["mode"], mesh.shape["dom"]),
        mesh=mesh, in_specs=placed, out_specs=P("mode", "dom"), check_vma=False,
    )
```

```python
import functools

import jax
import jax.numpy as jnp
import numpy as np
from jax import lax
from jax.experimental import pallas as pl
from jax.experimental.pallas import tpu as pltpu
from jax.sharding import PartitionSpec as P

ITERS = 3
SWEEPS = 6

mass_weight = 4.0
bound_low = 0.1
bound_high = 2.0
centre = (bound_high + bound_low) / 2.0
half_width = (bound_high - bound_low) / 2.0

F32 = jnp.float32
BF16 = jnp.bfloat16
ROW = 96


def chebyshev():
    ratio = centre / half_width
    rho = 1.0 / ratio
    coefs = [(0.0, 1.0 / centre)]
    for _ in range(SWEEPS - 1):
        rho_next = 1.0 / (2.0 * ratio - rho)
        coefs.append((rho_next * rho, 2.0 * rho_next / half_width))
        rho = rho_next
    return coefs


def synthesis_table(mode_count):
    column = np.arange(mode_count)
    number = np.where(column == 1, mode_count // 2, column // 2)
    is_sine = (column % 2 == 1) & (column > 1)
    planes = np.arange(mode_count)
    angles = (planes[:, None] * number[None, :] % mode_count) * (2.0 * np.pi / mode_count)
    return np.where(is_sine[None, :], np.sin(angles), np.cos(angles))


def halves(table):
    high = table.astype(np.float32).astype(BF16)
    return [high, (table - high.astype(np.float64)).astype(np.float32).astype(BF16)]


def split(value):
    high = value.astype(BF16)
    return high, (value - high.astype(F32)).astype(BF16)


def dot(a, b):
    return lax.dot_general(a, b, (((1,), (0,)), ((), ())), preferred_element_type=F32)


def rows_times(value, high, low):
    count = value.shape[0]
    h, l = split(value)
    both = dot(jnp.concatenate([h, l], axis=0), high)
    return both[:count] + both[count:] + dot(h, low)


def table_times(high, low, value, dim=1):
    dims = (((dim,), (0,)), ((), ()))
    count = value.shape[1]
    h, l = split(value)
    both = lax.dot_general(high, jnp.concatenate([h, l], axis=1), dims, preferred_element_type=F32)
    return both[:, :count] + both[:, count:] + lax.dot_general(low, h, dims, preferred_element_type=F32)


def iota(shape, dim):
    return lax.broadcasted_iota(jnp.int32, shape, dim)


def call(kernel, outs, vmem, limit, scratch=(), flops=0, moved=1 << 20, far=(), out_far=(), pinned=(), free=()):
    in_specs, given = [], []
    for i, v in enumerate(vmem):
        space = pltpu.HBM if i in far else pltpu.VMEM
        in_specs.append(pl.BlockSpec(memory_space=space))
        fixed = i in far or v.dtype == BF16 and v.shape not in free
        given.append(pltpu.with_memory_space_constraint(v, space) if fixed else v)
    shapes, out_specs = [], []
    for i, (s, t) in enumerate(outs):
        space = pltpu.HBM if i in out_far else pltpu.VMEM
        out_specs.append(pl.BlockSpec(memory_space=space))
        shapes.append(space(s, t) if i in out_far or i in pinned else jax.ShapeDtypeStruct(s, t))
    return pl.pallas_call(
        kernel,
        out_shape=shapes,
        in_specs=in_specs,
        out_specs=out_specs,
        scratch_shapes=list(scratch),
        compiler_params=pltpu.CompilerParams(vmem_limit_bytes=limit << 20),
        cost_estimate=pl.CostEstimate(flops=flops, bytes_accessed=moved, transcendentals=0),
    )(*given)


def position():
    q = lax.axis_index("dom")
    z = lax.shift_right_arithmetic(q, 1)
    return q, z, q - 2 * z


def picked(first, a, b):
    return jnp.where(first, a, b)


def order_kernel(
    iface_in, l2g_in, vel_in, mass_in, live_in, keep, send, chunks, place_out, iface, l2g, vel, mass, live, sems
):
    q, _, x = position()
    pairs = ((iface_in, iface), (l2g_in, l2g), (vel_in, vel), (mass_in, mass), (live_in, live))
    copies = [pltpu.make_async_copy(a, b, sems.at[i]) for i, (a, b) in enumerate(pairs)]
    for copy in copies:
        copy.start()
    for copy in copies:
        copy.wait()
    count = mass.shape[1]
    face = iface.shape[1]
    lists = jnp.concatenate(
        [picked(x == 0, iface[0:1, :], iface[1:2, :]), picked(x == 0, iface[1:2, :], iface[0:1, :])], axis=1
    ).astype(F32)
    lists = jnp.transpose(jnp.broadcast_to(lists, (8, 2 * face)))[:, 0:1]
    hit = jnp.where(lists == iota((1, count), 1).astype(F32), 1.0, 0.0)
    at = jnp.sum(hit * iota((2 * face, 1), 0).astype(F32), axis=0, keepdims=True)
    shared = jnp.sum(hit, axis=0, keepdims=True)
    rest = jnp.broadcast_to(1.0 - shared, (8, count))
    lane = iota((8, count), 1)
    run = rest
    step = 1
    while step < count:
        run = run + jnp.where(lane >= step, pltpu.roll(run, step, 1), 0.0)
        step *= 2
    place = jnp.where(rest > 0.5, run - 1.0 + 2.0 * face, jnp.broadcast_to(at, (8, count)))
    place_out[...] = place
    column = jnp.transpose(place)[:, 0:1]
    elems, side = l2g.shape
    slots = elems * ROW
    blank = jnp.full((1, ROW - side), -1, jnp.int32)
    row = jnp.concatenate([piece for e in range(elems) for piece in (l2g[e : e + 1, :], blank)], axis=1)
    pieces = []
    for first in range(0, slots, 512):
        part = row[:, first : first + 512]
        found = jnp.where(iota((count, 1), 0) == part, column, 0.0)
        pieces.append(jnp.where(part < 0, -1.0, jnp.sum(found, axis=0, keepdims=True)))
    index = jnp.concatenate(pieces, axis=1)
    unit = jnp.where(iota((1, count), 1).astype(F32) == column, 1.0, 0.0).astype(BF16)
    modes = vel.shape[0]
    half = modes // 2
    value = jnp.concatenate([vel[...], jnp.broadcast_to(mass[...], (16, count))], axis=0)
    high = value.astype(BF16)
    middle, low = split(value - high.astype(F32))
    total = modes + 16
    parts = dot(jnp.concatenate([high, middle, low], axis=0), unit)
    moved = parts[:total] + parts[total : 2 * total] + parts[2 * total :]
    a, b = moved[:half], moved[half:modes]
    lived = jnp.where(iota(live.shape, 1) == q, live[...], 0).astype(F32)
    lived = jnp.sum(lived, axis=1, keepdims=True)
    for ref, rows in ((keep, picked(x == 0, a, b)), (send, picked(x == 0, b, a))):
        ref[0:half, :] = rows
        ref[half : half + 8, :] = moved[modes : modes + 8]
        ref[half + 8 : half + 16, :] = jnp.broadcast_to(index[:, :count], (8, count))
        ref[half + 16 : half + 24, 0 : slots - count] = jnp.broadcast_to(
            index[:, count:], (8, slots - count)
        )
        ref[half + 16 : half + 24, slots - count :] = jnp.broadcast_to(lived, (8, 2 * count - slots))
    quarter = count // chunks.shape[0]
    for part in range(chunks.shape[0]):
        chunks[part] = moved[:modes, part * quarter : (part + 1) * quarter]


def own_build_kernel(half, ops_in, pack, high_out, low_out, diag, note, ops, high, low, *scratch):
    sems = scratch[-1]
    fetch = pltpu.make_async_copy(ops_in, ops, sems.at[0])
    fetch.start()
    copies = []

    def ship(*rows):
        for part, out in ((high, high_out), (low, low_out)):
            at = pl.ds(*rows)
            copies.append(pltpu.make_async_copy(part.at[at], out.at[at], sems.at[len(copies) + 1]))
            copies[-1].start()

    build_kernel(half, ops, pack, high, low, diag, note, *scratch[:-1], ready=fetch.wait, ship=ship)
    for copy in copies:
        copy.wait()


def partner_build_kernel(half, ops, pack, high_in, low_in, high_own, low_own, high, low, diag, note, *scratch):
    sems = scratch[-1]
    pairs = ((high_in, high_own), (low_in, low_own))
    copies = [pltpu.make_async_copy(a, b, sems.at[i]) for i, (a, b) in enumerate(pairs)]
    for copy in copies:
        copy.start()
    build_kernel(half, ops, pack, high, low, diag, note, *scratch[:-1])
    for copy in copies:
        copy.wait()


def build_kernel(half, ops, pack, high, low, diag, note, flat, tall, qh, ql, pad, ready=None, ship=None):
    live = pack[half + 16 : half + 17, pack.shape[1] - 1 :]
    side, elems = ops.shape[0], ops.shape[1]
    count = high.shape[0]
    slots = elems * ROW
    index = jnp.concatenate(
        [pack[half + 8 : half + 16, :], pack[half + 16 : half + 24, 0 : slots - count]], axis=1
    )
    column = jnp.transpose(index)[:, 0:1]
    for first in range(0, slots, 256):
        block = jnp.where(iota((1, count), 1).astype(F32) == column[first : first + 256], 1.0, 0.0)
        tall[first : first + 256, :] = block.astype(BF16)
    tall[slots:, :] = jnp.zeros((tall.shape[0] - slots, count), BF16)
    for first in range(0, count, 256):
        block = jnp.where((iota((256, 1), 0) + first).astype(F32) == index[0:1], 1.0, 0.0)
        flat[first : first + 256, :] = block.astype(BF16)
    pad[...] = jnp.zeros(pad.shape, F32)
    if ready is not None:
        ready()
    for e in range(elems):
        pad[0:side, 0:side] = ops[:, e, :] * jnp.where(live > e + 0.5, 1.0, 0.0)
        oh, ol = split(pad[...])
        spread = dot(jnp.concatenate([oh, ol], axis=0), tall[e * ROW : e * ROW + 128, :])
        qh[e * ROW : (e + 1) * ROW, :] = spread[:ROW].astype(BF16)
        ql[e * ROW : (e + 1) * ROW, :] = spread[ROW:].astype(BF16)
    tile = 256
    face = note.shape[1]
    for j in range(0, count, tile):
        top = j + tile
        block = dot(flat[j:top, :], qh[:, j:]) + dot(flat[j:top, :], ql[:, j:])
        h, l = split(block)
        high[j:top, j:] = h
        low[j:top, j:] = l
        if ship is not None:
            ship(j, tile)
        if top < count:
            mirror = jnp.transpose(block[:, tile:])
            h, l = split(mirror)
            high[top:, j:top] = h
            low[top:, j:top] = l
        own_node = iota((tile, tile), 0) == iota((tile, tile), 1)
        line = jnp.sum(jnp.where(own_node, block[:, :tile], 0.0), axis=0, keepdims=True)
        diag[:, j:top] = jnp.broadcast_to(line, (8, tile))
        if not j:
            note[0:face, :] = block[0:face, 0:face]
            note[face : face + 8, :] = jnp.broadcast_to(line[:, 0:face], (8, face))
            note[face + 8 :, :] = pack[half : half + 8, 0:face]


def apply(value, mats, columns, half):
    oh, ol, ph, plo = mats[:4]
    return jnp.concatenate(
        [
            rows_times(value[:half], oh[:, columns], ol[:, columns]),
            rows_times(value[half:], ph[:, columns], plo[:, columns]),
        ],
        axis=0,
    )


def outer_apply(value, mats, half, face):
    parts = []
    for v, columns in ((value[:half], mats[4]), (value[half:], mats[5])):
        both = dot(jnp.concatenate(split(v), axis=0), columns[...])
        parts.append(both[:half, :face] + both[half:, :face] + both[:half, face:])
    return jnp.concatenate(parts, axis=0)


def face_times(value, rows):
    count = value.shape[0]
    h, l = split(value)
    first, second = jnp.concatenate([h, h], axis=1), jnp.concatenate([l, jnp.zeros_like(l)], axis=1)
    both = dot(jnp.concatenate([first, second], axis=0), rows)
    return both[:count] + both[count:]


def assembled(y, outer, half, face):
    inner = y[:half, face : 2 * face] + y[half:, face : 2 * face]
    first = y[:, :face] if outer is None else y[:, :face] + outer
    return jnp.concatenate([first, jnp.concatenate([inner, inner], axis=0), y[:, 2 * face :]], axis=1)


def first_planes_kernel(u, tables_in, slope_in, out, tables, slope, sems):
    pairs = ((slope_in, slope), (tables_in, tables))
    copies = [pltpu.make_async_copy(a, b, sems.at[i]) for i, (a, b) in enumerate(pairs)]
    for copy in copies:
        copy.start()
    for copy in copies:
        copy.wait()
    planes_kernel(u, tables, slope, out)


def planes_kernel(u, tables, slope, out):
    count = slope.shape[1]
    high, low = tables[0:count, :], tables[count:, :]
    value = u[...]
    mode = iota((count, 1), 0)
    scale = lax.shift_right_arithmetic(mode, 1).astype(F32) * (2.0 / count)
    after, before = pltpu.roll(value, count - 1, 0), pltpu.roll(value, 1, 0)
    paired = jnp.where((mode & 1) == 0, scale * after, -scale * before)
    nodes = value.shape[1]
    both = table_times(high, low, jnp.concatenate([value, paired], axis=1))
    rate = jnp.transpose(jnp.broadcast_to(slope[...], (8, count)))[:, 0:1]
    cross = rate * both[:, :nodes] * both[:, nodes:]
    weight = jnp.where(mode < 2, 1.0 / count, 2.0 / count)
    out[...] = weight * table_times(high, low, cross, 0)


def provisional(r, d, g, inv, cm, mats, alpha, beta, half, face):
    r = r - inv * assembled(g, None, half, face)
    d = alpha * d + beta * r if alpha else beta * r
    y = outer_apply(d, mats, half, face) + cm[:, :face] * d[:, :face]
    return r, d, y


def even():
    _, z, x = position()
    return lax.rem(x + z, 2) == 0


def put(one, two, g, y, half, face, notes=((), ())):
    own = jnp.concatenate([g[:half, :face], y[:half], *notes[0]], axis=0)
    oth = jnp.concatenate([g[half:, :face], y[half:], *notes[1]], axis=0)
    first = even()
    one[...] = picked(first, own, oth)
    two[...] = picked(first, oth, own)


def got(one, two):
    a, b = one[...], two[...]
    first = even()
    return picked(first, a, b), picked(first, b, a)


def received(conv, half):
    _, _, x = position()
    parts = conv.shape[0]
    return jnp.concatenate(
        [
            jnp.concatenate([conv[m, x] for m in range(parts)], axis=1),
            jnp.concatenate([conv[m, 1 - x] for m in range(parts)], axis=1),
        ],
        axis=0,
    )


def masses(own, oth, half):
    count = own.shape[1]
    return jnp.concatenate(
        [jnp.broadcast_to(m[half : half + 1, :], (half, count)) for m in (own, oth)], axis=0
    )


def helmholtz(half, mode_count):
    _, _, x = position()
    mode = lax.axis_index("mode") * (2 * half) + x * half + iota((half, 1), 0)
    number = jnp.where(mode == 1, mode_count // 2, lax.shift_right_arithmetic(mode, 1))
    return mass_weight + (8.0 * number.astype(F32) / mode_count) ** 2


def first_source_kernel(
    half, face, mode_count, conv, own, oth, do, dp, note_o, note_p, oh, ol, ph, plo,
    wo, wp, vo, vp, r_out, d_out, v_out, conv_out, inv_out, cm_out, one, two,
):
    for wide, tall, high, low in ((wo, vo, oh, ol), (wp, vp, ph, plo)):
        wide[:, 0:face] = high[:, 0:face]
        wide[:, face:] = low[:, 0:face]
        tall[0:face, :] = high[0:face, :]
        tall[face:, :] = low[0:face, :]
    mats = (oh, ol, ph, plo, wo, wp, vo, vp)
    c = helmholtz(half, mode_count)
    c = jnp.concatenate([c, c], axis=0)
    mass = masses(own, oth, half)
    stiff = jnp.concatenate([jnp.broadcast_to(t[0:1, :], (half, t.shape[1])) for t in (do, dp)], axis=0)
    inv = 1.0 / (assembled(stiff, None, half, face) + c * assembled(mass, None, half, face))
    inv = jnp.concatenate([jnp.zeros((2 * half, face), F32), inv[:, face:]], axis=1)
    inv_out[...] = inv
    cm = c * mass
    cm_out[...] = cm
    v = jnp.concatenate([own[0:half, :], oth[0:half, :]], axis=0)
    v_out[...] = v
    new = received(conv, half)
    conv_out[...] = new
    m4 = mass_weight * mass
    g = apply(v, mats, slice(None), half) + (cm - m4) * v - m4 * new
    r = -inv * assembled(g, None, half, face)
    d = (1.0 / centre) * r
    r_out[...] = r
    d_out[...] = d
    y = outer_apply(d, mats, half, face)
    put(one, two, g, y, half, face, ((note_o[...],), (note_p[...],)))


def source_kernel(half, face, conv, old, own, oth, r, d, inv, cm, oh, ol, ph, plo, wo, wp, vo, vp, r_out, d_out, conv_out, one, two):
    mats = (oh, ol, ph, plo, wo, wp, vo, vp)
    new = received(conv, half)
    conv_out[...] = new
    cmv, dv = cm[...], d[...]
    g = apply(dv, mats, slice(None), half) + cmv * dv - mass_weight * masses(own, oth, half) * (new - old[...])
    rv, dv, y = provisional(r[...], None, g, inv[...], cmv, mats, 0.0, 1.0 / centre, half, face)
    r_out[...] = rv
    d_out[...] = dv
    put(one, two, g, y, half, face)


def rest_kernel(half, face, now, r, d, sol, s1, s2, inv, cm, oh, ol, ph, plo, wo, wp, vo, vp, r_out, d_out, sol_out):
    dv = d[...]
    y = apply(dv, (oh, ol, ph, plo, wo, wp, vo, vp), slice(face, None), half) + cm[:, face:] * dv[:, face:]
    y = jnp.concatenate([stacked(got(s1, s2), half, 2 * half), y], axis=1)
    rv = r[...] - inv[...] * assembled(y, None, half, face)
    dn = now[0] * dv + now[1] * rv
    r_out[...] = rv
    d_out[...] = dn
    sol_out[...] = sol[...] + dv + dn


def change_of(dd, theirs, mats, na, nb, half):
    change = [face_times(dd[:half], mats[6][...]), face_times(dd[half:], mats[7][...])]
    their_change = [face_times(theirs[:half], nb), face_times(theirs[half:], na)]
    return jnp.concatenate(change, axis=0), jnp.concatenate(their_change, axis=0)


def stacked(pair, first, last):
    return jnp.concatenate([t[first:last, :] for t in pair], axis=0)


def widened(value, face_part):
    face = face_part.shape[1]
    return jnp.concatenate([value[:, :face] + face_part, value[:, face:]], axis=1)


def corrected(half, face, now, r, d, sol, dr, dd, change, outer, inv):
    back = widened(-inv * assembled(change, outer, half, face), dr)
    step = widened(now[1] * back, now[0] * dd)
    return r + back, d + step, widened(sol + step, dd)


def exact(half, face, beta, now, r, d, sol, sent, came, na, nb, inv, cm, cmn, mats):
    inv_face = inv[:, :face]
    mine, came = got(*sent), got(*came)
    dr = -(inv_face * stacked(came, 0, half))
    dd = beta * dr
    theirs = -beta * (inv_face * stacked(mine, 0, half))
    change, their_change = change_of(dd, theirs, mats, na[...], nb[...], half)
    change = widened(change, cm[:, :face] * dd)
    outer = stacked(came, half, 2 * half) + their_change + cmn[...] * theirs
    return corrected(half, face, now, r[...], d[...], sol[...], dr, dd, change, outer, inv[...])


def first_sweep_kernel(
    half, face, mode_count, before, now, then,
    r, d, sol, s1, s2, c1, c2, inv, cm, oh, ol, ph, plo, wo, wp, vo, vp,
    r_out, d_out, sol_out, inv_out, cmn_out, na_out, nb_out, one, two,
):
    mats = (oh, ol, ph, plo, wo, wp, vo, vp)
    cm_v = cm[...]
    mine, came = got(s1, s2), got(c1, c2)
    c = helmholtz(half, mode_count)
    c = jnp.concatenate([c, c], axis=0)

    def line(pair, row):
        return jnp.concatenate([jnp.broadcast_to(t[row : row + 1, :], (half, face)) for t in pair], axis=0)

    at = 2 * half + face
    their_mass = line(came, at + 8)
    inv_face = 1.0 / (line(mine, at) + line(came, at) + c * (line(mine, at + 8) + their_mass))
    cmn = c * their_mass
    nb, na = (jnp.concatenate(split(t[2 * half : at, :]), axis=0) for t in came)
    dr = -inv_face * (stacked(mine, 0, half) + stacked(came, 0, half))
    dd = before[1] * dr
    change, their_change = change_of(dd, dd, mats, na, nb, half)
    change = widened(change, cm_v[:, :face] * dd)
    outer = stacked(mine, half, 2 * half) + stacked(came, half, 2 * half) + their_change + cmn * dd
    inv_v = jnp.concatenate([inv_face, inv[:, face:]], axis=1)
    rv, dn, sol_v = corrected(half, face, now, r[...], d[...], sol[...], dr, dd, change, outer, inv_v)
    inv_out[...] = inv_v
    cmn_out[...] = cmn
    na_out[...] = na
    nb_out[...] = nb
    sol_out[...] = sol_v
    g = apply(dn, mats, slice(None), half) + cm_v * dn
    rv, dv, y = provisional(rv, dn, g, inv_v, cm_v, mats, then[0], then[1], half, face)
    r_out[...] = rv
    d_out[...] = dv
    put(one, two, g, y, half, face)


def sweep_kernel(
    half, face, before, now, then,
    r, d, sol, s1, s2, c1, c2, na, nb, inv, cm, cmn, oh, ol, ph, plo, wo, wp, vo, vp,
    r_out, d_out, sol_out, one, two,
):
    mats = (oh, ol, ph, plo, wo, wp, vo, vp)
    rv, dn, sol_v = exact(half, face, before[1], now, r, d, sol, (s1, s2), (c1, c2), na, nb, inv, cm, cmn, mats)
    sol_out[...] = sol_v
    inv_v, cm_v = inv[...], cm[...]
    g = apply(dn, mats, slice(None), half) + cm_v * dn
    rv, dv, y = provisional(rv, dn, g, inv_v, cm_v, mats, then[0], then[1], half, face)
    r_out[...] = rv
    d_out[...] = dv
    put(one, two, g, y, half, face)


def last_kernel(
    half, face, before, now,
    r, d, sol, s1, s2, c1, c2, na, nb, inv, cm, cmn, oh, ol, ph, plo, wo, wp, vo, vp,
    r_out, d_out, sol_out, chunks,
):
    rv, dn, new = exact(
        half, face, before[1], now, r, d, sol, (s1, s2), (c1, c2), na, nb, inv, cm, cmn, (oh, ol, ph, plo, wo, wp, vo, vp)
    )
    r_out[...] = rv
    d_out[...] = dn
    sol_out[...] = new
    _, _, x = position()
    parts, width = chunks.shape[0], chunks.shape[3]
    for m in range(parts):
        chunks[m, x] = new[:half, m * width : (m + 1) * width]
        chunks[m, 1 - x] = new[half:, m * width : (m + 1) * width]


def end_kernel(
    half, face, before, now,
    r, d, sol, s1, s2, c1, c2, na, nb, inv, cm, cmn, oh, ol, ph, plo, wo, wp, vo, vp, own_out, oth_out,
):
    _, _, new = exact(
        half, face, before[1], now, r, d, sol, (s1, s2), (c1, c2), na, nb, inv, cm, cmn, (oh, ol, ph, plo, wo, wp, vo, vp)
    )
    own_out[...] = new[:half]
    oth_out[...] = new[half:]


def restored(value, unit):
    count = value.shape[0]
    high = value.astype(BF16)
    middle, low = split(value - high.astype(F32))
    parts = dot(jnp.concatenate([high, middle, low], axis=0), unit)
    return parts[:count] + parts[count : 2 * count] + parts[2 * count :]


def finish_own_kernel(own, place, out, unit_out):
    count = own.shape[1]
    unit = jnp.where(iota((count, 1), 0).astype(F32) == place[0:1, :], 1.0, 0.0).astype(BF16)
    unit_out[...] = unit
    out[...] = restored(own[...], unit)


def finish_kernel(own, other, unit, out):
    _, _, x = position()
    a, b = own[...], restored(other[...], unit[...])
    half = own.shape[0]
    out[0:half, :] = picked(x == 0, a, b)
    out[half:, :] = picked(x == 0, b, a)


def body(n_mode, n_dom, velocity_prev, elem_ops, lumped_mass, span_slope, local_to_global, iface_nodes, live_elems):
    modes, count = velocity_prev.shape
    half = modes // 2
    elems, side = local_to_global.shape
    face = iface_nodes.shape[2]
    mode_count = span_slope.shape[0]
    quarter = count // n_mode
    pairs = n_dom // 2
    slots = elems * ROW
    places = [(z, s) for z in range(pairs) for s in (0, 1)]
    swap = [(i, i ^ 1) for i in range(n_dom)]
    long_swap = [(2 * z + s, 2 * ((z + (1 if z % 2 else -1)) % pairs) + s) for z, s in places]
    short_swap = [(2 * z + s, 2 * ((z + (-1 if z % 2 else 1)) % pairs) + s) for z, s in places]
    groups = [[m * n_dom + 2 * z + s for m in range(n_mode) for s in (0, 1)] for z in range(pairs)]

    def exchange(one, two):
        return lax.ppermute(one, "dom", long_swap), lax.ppermute(two, "dom", short_swap)

    ops = jnp.transpose(elem_ops, (1, 0, 2))
    ops_other = lax.ppermute(ops, "dom", swap)
    pack = (half + 24, count)
    wide = (2 * half, count)
    keep, send, chunks, place = call(
        order_kernel,
        [(pack, F32), (pack, F32), ((n_mode, modes, quarter), F32), ((8, count), F32)],
        [iface_nodes[0], local_to_global, velocity_prev, lumped_mass.reshape(1, count), live_elems.reshape(1, n_dom)],
        24, far=range(5),
        scratch=[
            pltpu.VMEM((2, face), jnp.int32), pltpu.VMEM((elems, side), jnp.int32),
            pltpu.VMEM((modes, count), F32), pltpu.VMEM((1, count), F32), pltpu.VMEM((1, n_dom), jnp.int32),
            pltpu.SemaphoreType.DMA((5,)),
        ],
    )
    planes_in = lax.all_to_all(chunks, "mode", 0, 0, tiled=True)
    oth = lax.ppermute(send, "dom", swap)

    tables = jnp.asarray(np.concatenate(halves(synthesis_table(mode_count))))
    slope = span_slope.reshape(1, mode_count)

    matrix = ((count, count), BF16)
    small = [((8, count), F32), ((face + 16, face), F32)]
    one_hot = [
        pltpu.VMEM((count, slots), BF16),
        pltpu.VMEM((slots + 32, count), BF16),
        pltpu.VMEM((slots, count), BF16),
        pltpu.VMEM((slots, count), BF16),
        pltpu.VMEM((ROW, 128), F32),
    ]

    def planes(value, first):
        (out,) = call(
            first_planes_kernel if first else planes_kernel, [((mode_count, quarter), F32)],
            [value.reshape(mode_count, quarter), tables, slope], 16, flops=600 << 20,
            far=(1, 2) if first else (), free=(tables.shape,),
            scratch=[
                pltpu.VMEM(tables.shape, BF16), pltpu.VMEM(slope.shape, F32), pltpu.SemaphoreType.DMA((2,)),
            ] if first else (),
        )
        return out

    def to_solve(value):
        back = lax.all_to_all(
            value.reshape(2 * n_mode, half, quarter), ("mode", "dom"), 0, 0, axis_index_groups=groups, tiled=True
        )
        return back.reshape(n_mode, 2, half, quarter)

    cross, keep_late, ops_other = lax.optimization_barrier((planes(planes_in, True), keep, ops_other))
    conv = to_solve(cross)
    oh, ol, do, note_o = call(
        functools.partial(own_build_kernel, half), [matrix, matrix, *small], [ops, keep_late], 36,
        far=(0,), out_far=(0, 1), flops=6 << 30,
        scratch=[
            pltpu.VMEM((side, elems, side), F32), pltpu.VMEM((count, count), BF16), pltpu.VMEM((count, count), BF16),
            *one_hot, pltpu.SemaphoreType.DMA((2 * count // 256 + 1,)),
        ],
    )
    conv, oth_late = lax.optimization_barrier((conv, oth))
    oh, ol, ph, plo, dp, note_p = call(
        functools.partial(partner_build_kernel, half), [matrix] * 4 + small, [ops_other, oth_late, oh, ol], 24,
        far=(2, 3), pinned=range(4), flops=6 << 30, scratch=[*one_hot, pltpu.SemaphoreType.DMA((2,))],
    )
    mats = [oh, ol, ph, plo]
    coefs = chebyshev()
    message = ((2 * half, face), F32)
    for iteration in range(ITERS):
        if iteration == 0:
            long_message = ((2 * half + face + 16, face), F32)
            beside = [((count, 2 * face), BF16)] * 2 + [((2 * face, count), BF16)] * 2
            *cats, r, d, sol, old, inv, cm, one, two = call(
                functools.partial(first_source_kernel, half, face, mode_count),
                [*beside, *[(wide, F32)] * 6, long_message, long_message],
                [conv, keep, oth, do, dp, note_o, note_p, *mats], 20, flops=500 << 20, pinned=range(4),
            )
            mats = [*mats, *cats]
        else:
            r, d, old, one, two = call(
                functools.partial(source_kernel, half, face),
                [(wide, F32), (wide, F32), (wide, F32), message, message],
                [conv, old, keep, oth, r, d, inv, cm, *mats], 20, flops=500 << 20,
            )
        for k in (0, 2, 4):
            c1, c2 = exchange(one, two)
            r, d, sol = call(
                functools.partial(rest_kernel, half, face, coefs[k + 1]), [(wide, F32)] * 3,
                [r, d, sol, one, two, inv, cm, *mats], 20, flops=400 << 20,
            )
            if iteration == 0 and k == 0:
                r, d, sol, inv, cmn, na, nb, one, two = call(
                    functools.partial(first_sweep_kernel, half, face, mode_count, coefs[0], coefs[1], coefs[2]),
                    [(wide, F32)] * 4 + [((2 * half, face), F32)] + [((2 * face, face), BF16)] * 2 + [message, message],
                    [r, d, sol, one, two, c1, c2, inv, cm, *mats], 20, flops=500 << 20,
                )
                continue
            given = [r, d, sol, one, two, c1, c2, na, nb, inv, cm, cmn, *mats]
            if k < 4:
                r, d, sol, one, two = call(
                    functools.partial(sweep_kernel, half, face, coefs[k], coefs[k + 1], coefs[k + 2]),
                    [(wide, F32), (wide, F32), (wide, F32), message, message], given, 20, flops=500 << 20,
                )
            elif iteration < ITERS - 1:
                r, d, sol, chunks = call(
                    functools.partial(last_kernel, half, face, coefs[k], coefs[k + 1]),
                    [(wide, F32), (wide, F32), (wide, F32), ((n_mode, 2, half, quarter), F32)],
                    given, 20, flops=100 << 20,
                )
            else:
                own, other = call(
                    functools.partial(end_kernel, half, face, coefs[k], coefs[k + 1]),
                    [((half, count), F32)] * 2, given, 20, flops=100 << 20,
                )
        if iteration < ITERS - 1:
            planes_in = lax.all_to_all(
                chunks.reshape(2 * n_mode, half, quarter), ("mode", "dom"), 0, 0, axis_index_groups=groups, tiled=True
            )
            conv = to_solve(planes(planes_in, False))
    other = lax.ppermute(other, "dom", swap)
    own, unit = call(
        finish_own_kernel, [((half, count), F32), ((count, count), BF16)], [own, place], 16, flops=200 << 20
    )
    (out,) = call(finish_kernel, [((modes, count), F32)], [own, other, unit], 16)
    return out


def solution(mesh):
    placed = (
        P("mode", "dom"),
        P("dom", None, None),
        P("dom"),
        P(),
        P("dom", None),
        P("dom", None, None),
        P(),
    )
    return jax.shard_map(
        functools.partial(body, mesh.shape["mode"], mesh.shape["dom"]),
        mesh=mesh, in_specs=placed, out_specs=P("mode", "dom"), check_vma=False,
    )
```

```python
import functools

import jax
import jax.numpy as jnp
import numpy as np
from jax import lax
from jax.experimental import pallas as pl
from jax.experimental.pallas import tpu as pltpu
from jax.sharding import PartitionSpec as P

ITERS = 3
SWEEPS = 6

mass_weight = 4.0
bound_low = 0.1
bound_high = 2.0
centre = (bound_high + bound_low) / 2.0
half_width = (bound_high - bound_low) / 2.0

F32 = jnp.float32
BF16 = jnp.bfloat16
ROW = 96


def chebyshev():
    ratio = centre / half_width
    rho = 1.0 / ratio
    coefs = [(0.0, 1.0 / centre)]
    for _ in range(SWEEPS - 1):
        rho_next = 1.0 / (2.0 * ratio - rho)
        coefs.append((rho_next * rho, 2.0 * rho_next / half_width))
        rho = rho_next
    return coefs


def synthesis_table(mode_count):
    column = np.arange(mode_count)
    number = np.where(column == 1, mode_count // 2, column // 2)
    is_sine = (column % 2 == 1) & (column > 1)
    planes = np.arange(mode_count)
    angles = (planes[:, None] * number[None, :] % mode_count) * (2.0 * np.pi / mode_count)
    return np.where(is_sine[None, :], np.sin(angles), np.cos(angles))


def halves(table):
    high = table.astype(np.float32).astype(BF16)
    return [high, (table - high.astype(np.float64)).astype(np.float32).astype(BF16)]


def split(value):
    high = value.astype(BF16)
    return high, (value - high.astype(F32)).astype(BF16)


def dot(a, b):
    return lax.dot_general(a, b, (((1,), (0,)), ((), ())), preferred_element_type=F32)


def rows_times(value, high, low):
    count = value.shape[0]
    h, l = split(value)
    both = dot(jnp.concatenate([h, l], axis=0), high)
    return both[:count] + both[count:] + dot(h, low)


def table_times(high, low, value, dim=1):
    dims = (((dim,), (0,)), ((), ()))
    count = value.shape[1]
    h, l = split(value)
    both = lax.dot_general(high, jnp.concatenate([h, l], axis=1), dims, preferred_element_type=F32)
    return both[:, :count] + both[:, count:] + lax.dot_general(low, h, dims, preferred_element_type=F32)


def iota(shape, dim):
    return lax.broadcasted_iota(jnp.int32, shape, dim)


def call(kernel, outs, vmem, limit, scratch=(), flops=0, moved=1 << 20, far=(), out_far=(), pinned=(), free=()):
    in_specs, given = [], []
    for i, v in enumerate(vmem):
        space = pltpu.HBM if i in far else pltpu.VMEM
        in_specs.append(pl.BlockSpec(memory_space=space))
        fixed = i in far or v.dtype == BF16 and v.shape not in free
        given.append(pltpu.with_memory_space_constraint(v, space) if fixed else v)
    shapes, out_specs = [], []
    for i, (s, t) in enumerate(outs):
        space = pltpu.HBM if i in out_far else pltpu.VMEM
        out_specs.append(pl.BlockSpec(memory_space=space))
        shapes.append(space(s, t) if i in out_far or i in pinned else jax.ShapeDtypeStruct(s, t))
    return pl.pallas_call(
        kernel,
        out_shape=shapes,
        in_specs=in_specs,
        out_specs=out_specs,
        scratch_shapes=list(scratch),
        compiler_params=pltpu.CompilerParams(vmem_limit_bytes=limit << 20),
        cost_estimate=pl.CostEstimate(flops=flops, bytes_accessed=moved, transcendentals=0),
    )(*given)


def position():
    q = lax.axis_index("dom")
    z = lax.shift_right_arithmetic(q, 1)
    return q, z, q - 2 * z


def picked(first, a, b):
    return jnp.where(first, a, b)


def order_kernel(
    iface_in, l2g_in, vel_in, mass_in, live_in, keep, send, chunks, place_out, iface, l2g, vel, mass, live, sems
):
    q, _, x = position()
    pairs = ((iface_in, iface), (l2g_in, l2g), (vel_in, vel), (mass_in, mass), (live_in, live))
    copies = [pltpu.make_async_copy(a, b, sems.at[i]) for i, (a, b) in enumerate(pairs)]
    for copy in copies:
        copy.start()
    for copy in copies:
        copy.wait()
    count = mass.shape[1]
    face = iface.shape[1]
    lists = jnp.concatenate(
        [picked(x == 0, iface[0:1, :], iface[1:2, :]), picked(x == 0, iface[1:2, :], iface[0:1, :])], axis=1
    ).astype(F32)
    lists = jnp.transpose(jnp.broadcast_to(lists, (8, 2 * face)))[:, 0:1]
    hit = jnp.where(lists == iota((1, count), 1).astype(F32), 1.0, 0.0)
    at = jnp.sum(hit * iota((2 * face, 1), 0).astype(F32), axis=0, keepdims=True)
    shared = jnp.sum(hit, axis=0, keepdims=True)
    rest = jnp.broadcast_to(1.0 - shared, (8, count))
    lane = iota((8, count), 1)
    run = rest
    step = 1
    while step < count:
        run = run + jnp.where(lane >= step, pltpu.roll(run, step, 1), 0.0)
        step *= 2
    place = jnp.where(rest > 0.5, run - 1.0 + 2.0 * face, jnp.broadcast_to(at, (8, count)))
    place_out[...] = place
    column = jnp.transpose(place)[:, 0:1]
    elems, side = l2g.shape
    slots = elems * ROW
    blank = jnp.full((1, ROW - side), -1, jnp.int32)
    row = jnp.concatenate([piece for e in range(elems) for piece in (l2g[e : e + 1, :], blank)], axis=1)
    pieces = []
    for first in range(0, slots, 512):
        part = row[:, first : first + 512]
        found = jnp.where(iota((count, 1), 0) == part, column, 0.0)
        pieces.append(jnp.where(part < 0, -1.0, jnp.sum(found, axis=0, keepdims=True)))
    index = jnp.concatenate(pieces, axis=1)
    unit = jnp.where(iota((1, count), 1).astype(F32) == column, 1.0, 0.0).astype(BF16)
    modes = vel.shape[0]
    half = modes // 2
    value = jnp.concatenate([vel[...], jnp.broadcast_to(mass[...], (16, count))], axis=0)
    high = value.astype(BF16)
    middle, low = split(value - high.astype(F32))
    total = modes + 16
    parts = dot(jnp.concatenate([high, middle, low], axis=0), unit)
    moved = parts[:total] + parts[total : 2 * total] + parts[2 * total :]
    a, b = moved[:half], moved[half:modes]
    lived = jnp.where(iota(live.shape, 1) == q, live[...], 0).astype(F32)
    lived = jnp.sum(lived, axis=1, keepdims=True)
    for ref, rows in ((keep, picked(x == 0, a, b)), (send, picked(x == 0, b, a))):
        ref[0:half, :] = rows
        ref[half : half + 8, :] = moved[modes : modes + 8]
        ref[half + 8 : half + 16, :] = jnp.broadcast_to(index[:, :count], (8, count))
        ref[half + 16 : half + 24, 0 : slots - count] = jnp.broadcast_to(
            index[:, count:], (8, slots - count)
        )
        ref[half + 16 : half + 24, slots - count :] = jnp.broadcast_to(lived, (8, 2 * count - slots))
    quarter = count // chunks.shape[0]
    for part in range(chunks.shape[0]):
        chunks[part] = moved[:modes, part * quarter : (part + 1) * quarter]


def own_build_kernel(half, ops_in, pack, high_out, low_out, diag, note, ops, high, low, *scratch):
    sems = scratch[-1]
    fetch = pltpu.make_async_copy(ops_in, ops, sems.at[0])
    fetch.start()
    copies = []

    def ship(*rows):
        for part, out in ((high, high_out), (low, low_out)):
            at = pl.ds(*rows)
            copies.append(pltpu.make_async_copy(part.at[at], out.at[at], sems.at[len(copies) + 1]))
            copies[-1].start()

    build_kernel(half, ops, pack, high, low, diag, note, *scratch[:-1], ready=fetch.wait, ship=ship)
    for copy in copies:
        copy.wait()


def partner_build_kernel(half, ops, pack, high_in, low_in, high_own, low_own, high, low, diag, note, *scratch):
    sems = scratch[-1]
    pairs = ((high_in, high_own), (low_in, low_own))
    copies = [pltpu.make_async_copy(a, b, sems.at[i]) for i, (a, b) in enumerate(pairs)]
    for copy in copies:
        copy.start()
    build_kernel(half, ops, pack, high, low, diag, note, *scratch[:-1])
    for copy in copies:
        copy.wait()


def build_kernel(half, ops, pack, high, low, diag, note, flat, tall, qh, ql, pad, ready=None, ship=None):
    live = pack[half + 16 : half + 17, pack.shape[1] - 1 :]
    side, elems = ops.shape[0], ops.shape[1]
    count = high.shape[0]
    slots = elems * ROW
    index = jnp.concatenate(
        [pack[half + 8 : half + 16, :], pack[half + 16 : half + 24, 0 : slots - count]], axis=1
    )
    column = jnp.transpose(index)[:, 0:1]
    for first in range(0, slots, 256):
        block = jnp.where(iota((1, count), 1).astype(F32) == column[first : first + 256], 1.0, 0.0)
        tall[first : first + 256, :] = block.astype(BF16)
    tall[slots:, :] = jnp.zeros((tall.shape[0] - slots, count), BF16)
    for first in range(0, count, 256):
        block = jnp.where((iota((256, 1), 0) + first).astype(F32) == index[0:1], 1.0, 0.0)
        flat[first : first + 256, :] = block.astype(BF16)
    pad[...] = jnp.zeros(pad.shape, F32)
    if ready is not None:
        ready()
    for e in range(elems):
        pad[0:side, 0:side] = ops[:, e, :] * jnp.where(live > e + 0.5, 1.0, 0.0)
        oh, ol = split(pad[...])
        spread = dot(jnp.concatenate([oh, ol], axis=0), tall[e * ROW : e * ROW + 128, :])
        qh[e * ROW : (e + 1) * ROW, :] = spread[:ROW].astype(BF16)
        ql[e * ROW : (e + 1) * ROW, :] = spread[ROW:].astype(BF16)
    tile = 256
    face = note.shape[1]
    diag[...] = jnp.zeros(diag.shape, F32)
    for j in range(0, count, tile):
        top = j + tile
        block = dot(flat[j:top, :], qh[:, j:]) + dot(flat[j:top, :], ql[:, j:])
        own_node = iota((tile, 1), 0) == iota((1, tile), 1)
        line = jnp.sum(jnp.where(own_node, block[:, :tile], 0.0), axis=0, keepdims=True)
        kept = jnp.where(own_node, 0.0, block[:, :tile])
        block = jnp.concatenate([kept, block[:, tile:]], axis=1) if top < count else kept
        h, l = split(block)
        diag[0:1, j:top] = line
        diag[1:2, j:] += jnp.sum(l.astype(F32), axis=0, keepdims=True)
        high[j:top, j:] = h
        low[j:top, j:] = l
        if ship is not None:
            ship(j, tile)
        if top < count:
            mirror = jnp.transpose(block[:, tile:])
            h, l = split(mirror)
            high[top:, j:top] = h
            low[top:, j:top] = l
            diag[1:2, j:top] += jnp.sum(l.astype(F32), axis=0, keepdims=True)
        if not j:
            note[0:face, :] = block[0:face, 0:face]
            note[face : face + 8, :] = jnp.broadcast_to(line[:, 0:face], (8, face))
            note[face + 8 :, :] = pack[half : half + 8, 0:face]


def apply(value, mats, half, face):
    oh, ol, ph, plo = mats[:4]
    return jnp.concatenate(
        [
            rows_times(value[:half], oh[:, face:], ol[:, face:]),
            rows_times(value[half:], ph[:, face:], plo[:, face:]),
        ],
        axis=0,
    )


def high_apply(value, mats, half):
    parts = []
    for v, high in ((value[:half], mats[0]), (value[half:], mats[2])):
        both = dot(jnp.concatenate(split(v), axis=0), high[...])
        parts.append(both[:half] + both[half:])
    return jnp.concatenate(parts, axis=0)


def low_apply(value, mats, half):
    v = value.astype(BF16)
    return jnp.concatenate([dot(v[:half], mats[1][...]), dot(v[half:], mats[3][...])], axis=0)


def outer_apply(value, mats, half, face):
    parts = []
    for v, columns in ((value[:half], mats[4]), (value[half:], mats[5])):
        both = dot(jnp.concatenate(split(v), axis=0), columns[...])
        parts.append(both[:half, :face] + both[half:, :face] + both[:half, face:])
    return jnp.concatenate(parts, axis=0)


def face_times(value, rows):
    count = value.shape[0]
    h, l = split(value)
    first, second = jnp.concatenate([h, h], axis=1), jnp.concatenate([l, jnp.zeros_like(l)], axis=1)
    both = dot(jnp.concatenate([first, second], axis=0), rows)
    return both[:count] + both[count:]


def assembled(y, outer, half, face):
    inner = y[:half, face : 2 * face] + y[half:, face : 2 * face]
    first = y[:, :face] if outer is None else y[:, :face] + outer
    return jnp.concatenate([first, jnp.concatenate([inner, inner], axis=0), y[:, 2 * face :]], axis=1)


def first_planes_kernel(u, tables_in, slope_in, out, tables, slope, sems):
    pairs = ((slope_in, slope), (tables_in, tables))
    copies = [pltpu.make_async_copy(a, b, sems.at[i]) for i, (a, b) in enumerate(pairs)]
    for copy in copies:
        copy.start()
    for copy in copies:
        copy.wait()
    planes_kernel(u, tables, slope, out)


def planes_kernel(u, tables, slope, out):
    count = slope.shape[1]
    high, low = tables[0:count, :], tables[count:, :]
    value = u[...]
    mode = iota((count, 1), 0)
    scale = lax.shift_right_arithmetic(mode, 1).astype(F32) * (2.0 / count)
    after, before = pltpu.roll(value, count - 1, 0), pltpu.roll(value, 1, 0)
    paired = jnp.where((mode & 1) == 0, scale * after, -scale * before)
    nodes = value.shape[1]
    both = table_times(high, low, jnp.concatenate([value, paired], axis=1))
    rate = jnp.transpose(jnp.broadcast_to(slope[...], (8, count)))[:, 0:1]
    cross = rate * both[:, :nodes] * both[:, nodes:]
    weight = jnp.where(mode < 2, 1.0 / count, 2.0 / count)
    out[...] = weight * table_times(high, low, cross, 0)


def provisional(r, d, g, inv, cm, mats, alpha, beta, half, face):
    r = r - inv * assembled(g, None, half, face)
    d = alpha * d + beta * r if alpha else beta * r
    y = outer_apply(d, mats, half, face) + cm[:, :face] * d[:, :face]
    return r, d, y


def even():
    _, z, x = position()
    return lax.rem(x + z, 2) == 0


def put(one, two, g, y, half, face, notes=((), ())):
    own = jnp.concatenate([g[:half, :face], y[:half], *notes[0]], axis=0)
    oth = jnp.concatenate([g[half:, :face], y[half:], *notes[1]], axis=0)
    first = even()
    one[...] = picked(first, own, oth)
    two[...] = picked(first, oth, own)


def got(one, two):
    a, b = one[...], two[...]
    first = even()
    return picked(first, a, b), picked(first, b, a)


def received(conv, half):
    _, _, x = position()
    parts = conv.shape[0]
    return jnp.concatenate(
        [
            jnp.concatenate([conv[m, x] for m in range(parts)], axis=1),
            jnp.concatenate([conv[m, 1 - x] for m in range(parts)], axis=1),
        ],
        axis=0,
    )


def masses(own, oth, half):
    count = own.shape[1]
    return jnp.concatenate(
        [jnp.broadcast_to(m[half : half + 1, :], (half, count)) for m in (own, oth)], axis=0
    )


def helmholtz(half, mode_count):
    _, _, x = position()
    mode = lax.axis_index("mode") * (2 * half) + x * half + iota((half, 1), 0)
    number = jnp.where(mode == 1, mode_count // 2, lax.shift_right_arithmetic(mode, 1))
    return mass_weight + (8.0 * number.astype(F32) / mode_count) ** 2


def first_source_kernel(
    half, face, mode_count, conv, own, oth, do, dp, note_o, note_p, oh, ol, ph, plo,
    wo, wp, vo, vp, r_out, d_out, v_out, conv_out, inv_out, cm_out, sums_out, one, two,
):
    for wide, tall, high, low in ((wo, vo, oh, ol), (wp, vp, ph, plo)):
        wide[:, 0:face] = high[:, 0:face]
        wide[:, face:] = low[:, 0:face]
        tall[0:face, :] = high[0:face, :]
        tall[face:, :] = low[0:face, :]
    mats = (oh, ol, ph, plo, wo, wp, vo, vp)
    c = helmholtz(half, mode_count)
    c = jnp.concatenate([c, c], axis=0)
    mass = masses(own, oth, half)
    stiff, sums = (
        jnp.concatenate([jnp.broadcast_to(t[row : row + 1, :], (half, t.shape[1])) for t in (do, dp)], axis=0)
        for row in (0, 1)
    )
    inv = 1.0 / (assembled(stiff, None, half, face) + c * assembled(mass, None, half, face))
    inv = jnp.concatenate([jnp.zeros((2 * half, face), F32), inv[:, face:]], axis=1)
    inv_out[...] = inv
    cm = c * mass + stiff
    cm_out[...] = cm
    sums_out[...] = sums
    v = jnp.concatenate([own[0:half, :], oth[0:half, :]], axis=0)
    v_out[...] = v
    new = received(conv, half)
    conv_out[...] = new
    m4 = mass_weight * mass
    g = high_apply(v, mats, half) + (cm + sums - m4) * v - m4 * new
    r = -inv * assembled(g, None, half, face)
    d = (1.0 / centre) * r
    r_out[...] = r
    d_out[...] = d
    y = outer_apply(d, mats, half, face)
    put(one, two, g, y, half, face, ((note_o[...],), (note_p[...],)))


def source_kernel(
    half, face, conv, old, own, oth, r, d, inv, cm, sums, late, oh, ol, ph, plo, wo, wp, vo, vp,
    r_out, d_out, conv_out, one, two,
):
    mats = (oh, ol, ph, plo, wo, wp, vo, vp)
    new = received(conv, half)
    conv_out[...] = new
    cmv, dv = cm[...], d[...]
    g = high_apply(dv, mats, half) + (cmv + sums[...]) * dv - mass_weight * masses(own, oth, half) * (new - old[...])
    g = widened(g, late[...])
    rv, dv, y = provisional(r[...], None, g, inv[...], cmv, mats, 0.0, 1.0 / centre, half, face)
    r_out[...] = rv
    d_out[...] = dv
    put(one, two, g, y, half, face)


def rest_kernel(
    half, face, now, r, d, sol, source, s1, s2, inv, cm, sums, oh, ol, ph, plo, wo, wp, vo, vp,
    r_out, d_out, sol_out, late_out,
):
    mats = (oh, ol, ph, plo, wo, wp, vo, vp)
    dv, sv = d[...], source[...]
    late = low_apply(sv, mats, half) - sums[...] * sv
    late_out[...] = late[:, :face]
    y = apply(dv, mats, half, face) + cm[:, face:] * dv[:, face:] + late[:, face:]
    y = jnp.concatenate([stacked(got(s1, s2), half, 2 * half), y], axis=1)
    rv = r[...] - inv[...] * assembled(y, None, half, face)
    dn = now[0] * dv + now[1] * rv
    r_out[...] = rv
    d_out[...] = dn
    sol_out[...] = sol[...] + dv + dn


def change_of(dd, theirs, mats, na, nb, half):
    change = [face_times(dd[:half], mats[6][...]), face_times(dd[half:], mats[7][...])]
    their_change = [face_times(theirs[:half], nb), face_times(theirs[half:], na)]
    return jnp.concatenate(change, axis=0), jnp.concatenate(their_change, axis=0)


def stacked(pair, first, last):
    return jnp.concatenate([t[first:last, :] for t in pair], axis=0)


def widened(value, face_part):
    face = face_part.shape[1]
    return jnp.concatenate([value[:, :face] + face_part, value[:, face:]], axis=1)


def corrected(half, face, now, r, d, sol, dr, dd, change, outer, inv):
    back = widened(-inv * assembled(change, outer, half, face), dr)
    step = widened(now[1] * back, now[0] * dd)
    return r + back, d + step, widened(sol + step, dd)


def exact(half, face, beta, now, r, d, sol, sent, came, na, nb, inv, cm, cmn, mats):
    inv_face = inv[:, :face]
    mine, came = got(*sent), got(*came)
    dr = -(inv_face * stacked(came, 0, half))
    dd = beta * dr
    theirs = -beta * (inv_face * stacked(mine, 0, half))
    change, their_change = change_of(dd, theirs, mats, na[...], nb[...], half)
    change = widened(change, cm[:, :face] * dd)
    outer = stacked(came, half, 2 * half) + their_change + cmn[...] * theirs
    return corrected(half, face, now, r[...], d[...], sol[...], dr, dd, change, outer, inv[...])


def first_sweep_kernel(
    half, face, mode_count, before, now, then,
    r, d, sol, late, s1, s2, c1, c2, inv, cm, sums, oh, ol, ph, plo, wo, wp, vo, vp,
    r_out, d_out, sol_out, source_out, inv_out, cmn_out, na_out, nb_out, one, two,
):
    mats = (oh, ol, ph, plo, wo, wp, vo, vp)
    cm_v = cm[...]
    mine, came = got(s1, s2), got(c1, c2)
    c = helmholtz(half, mode_count)
    c = jnp.concatenate([c, c], axis=0)

    def line(pair, row):
        return jnp.concatenate([jnp.broadcast_to(t[row : row + 1, :], (half, face)) for t in pair], axis=0)

    at = 2 * half + face
    their_mass = line(came, at + 8)
    inv_face = 1.0 / (line(mine, at) + line(came, at) + c * (line(mine, at + 8) + their_mass))
    cmn = c * their_mass + line(came, at)
    nb, na = (jnp.concatenate(split(t[2 * half : at, :]), axis=0) for t in came)
    dr = -inv_face * (stacked(mine, 0, half) + stacked(came, 0, half))
    dd = before[1] * dr
    change, their_change = change_of(dd, dd, mats, na, nb, half)
    change = widened(change, cm_v[:, :face] * dd)
    outer = stacked(mine, half, 2 * half) + stacked(came, half, 2 * half) + their_change + cmn * dd
    inv_v = jnp.concatenate([inv_face, inv[:, face:]], axis=1)
    rv, dn, sol_v = corrected(half, face, now, r[...], d[...], sol[...], dr, dd, change, outer, inv_v)
    inv_out[...] = inv_v
    cmn_out[...] = cmn
    na_out[...] = na
    nb_out[...] = nb
    sol_out[...] = sol_v
    source_out[...] = dn
    g = widened(high_apply(dn, mats, half) + (cm_v + sums[...]) * dn, late[...])
    rv, dv, y = provisional(rv, dn, g, inv_v, cm_v, mats, then[0], then[1], half, face)
    r_out[...] = rv
    d_out[...] = dv
    put(one, two, g, y, half, face)


def sweep_kernel(
    half, face, before, now, then,
    r, d, sol, late, s1, s2, c1, c2, na, nb, inv, cm, sums, cmn, oh, ol, ph, plo, wo, wp, vo, vp,
    r_out, d_out, sol_out, source_out, one, two,
):
    mats = (oh, ol, ph, plo, wo, wp, vo, vp)
    rv, dn, sol_v = exact(half, face, before[1], now, r, d, sol, (s1, s2), (c1, c2), na, nb, inv, cm, cmn, mats)
    sol_out[...] = sol_v
    source_out[...] = dn
    inv_v, cm_v = inv[...], cm[...]
    g = widened(high_apply(dn, mats, half) + (cm_v + sums[...]) * dn, late[...])
    rv, dv, y = provisional(rv, dn, g, inv_v, cm_v, mats, then[0], then[1], half, face)
    r_out[...] = rv
    d_out[...] = dv
    put(one, two, g, y, half, face)


def last_kernel(
    half, face, before, now,
    r, d, sol, s1, s2, c1, c2, na, nb, inv, cm, cmn, oh, ol, ph, plo, wo, wp, vo, vp,
    r_out, d_out, sol_out, chunks,
):
    rv, dn, new = exact(
        half, face, before[1], now, r, d, sol, (s1, s2), (c1, c2), na, nb, inv, cm, cmn, (oh, ol, ph, plo, wo, wp, vo, vp)
    )
    r_out[...] = rv
    d_out[...] = dn
    sol_out[...] = new
    _, _, x = position()
    parts, width = chunks.shape[0], chunks.shape[3]
    for m in range(parts):
        chunks[m, x] = new[:half, m * width : (m + 1) * width]
        chunks[m, 1 - x] = new[half:, m * width : (m + 1) * width]


def end_kernel(
    half, face, before, now,
    r, d, sol, s1, s2, c1, c2, na, nb, inv, cm, cmn, oh, ol, ph, plo, wo, wp, vo, vp, own_out, oth_out,
):
    _, _, new = exact(
        half, face, before[1], now, r, d, sol, (s1, s2), (c1, c2), na, nb, inv, cm, cmn, (oh, ol, ph, plo, wo, wp, vo, vp)
    )
    own_out[...] = new[:half]
    oth_out[...] = new[half:]


def restored(value, unit):
    count = value.shape[0]
    high = value.astype(BF16)
    middle, low = split(value - high.astype(F32))
    parts = dot(jnp.concatenate([high, middle, low], axis=0), unit)
    return parts[:count] + parts[count : 2 * count] + parts[2 * count :]


def finish_own_kernel(own, place, out, unit_out):
    count = own.shape[1]
    unit = jnp.where(iota((count, 1), 0).astype(F32) == place[0:1, :], 1.0, 0.0).astype(BF16)
    unit_out[...] = unit
    out[...] = restored(own[...], unit)


def finish_kernel(own, other, unit, out):
    _, _, x = position()
    a, b = own[...], restored(other[...], unit[...])
    half = own.shape[0]
    out[0:half, :] = picked(x == 0, a, b)
    out[half:, :] = picked(x == 0, b, a)


def body(n_mode, n_dom, velocity_prev, elem_ops, lumped_mass, span_slope, local_to_global, iface_nodes, live_elems):
    modes, count = velocity_prev.shape
    half = modes // 2
    elems, side = local_to_global.shape
    face = iface_nodes.shape[2]
    mode_count = span_slope.shape[0]
    quarter = count // n_mode
    pairs = n_dom // 2
    slots = elems * ROW
    places = [(z, s) for z in range(pairs) for s in (0, 1)]
    swap = [(i, i ^ 1) for i in range(n_dom)]
    long_swap = [(2 * z + s, 2 * ((z + (1 if z % 2 else -1)) % pairs) + s) for z, s in places]
    short_swap = [(2 * z + s, 2 * ((z + (-1 if z % 2 else 1)) % pairs) + s) for z, s in places]
    groups = [[m * n_dom + 2 * z + s for m in range(n_mode) for s in (0, 1)] for z in range(pairs)]

    def exchange(one, two):
        return lax.ppermute(one, "dom", long_swap), lax.ppermute(two, "dom", short_swap)

    ops = jnp.transpose(elem_ops, (1, 0, 2))
    ops_other = lax.ppermute(ops, "dom", swap)
    pack = (half + 24, count)
    wide = (2 * half, count)
    keep, send, chunks, place = call(
        order_kernel,
        [(pack, F32), (pack, F32), ((n_mode, modes, quarter), F32), ((8, count), F32)],
        [iface_nodes[0], local_to_global, velocity_prev, lumped_mass.reshape(1, count), live_elems.reshape(1, n_dom)],
        24, far=range(5),
        scratch=[
            pltpu.VMEM((2, face), jnp.int32), pltpu.VMEM((elems, side), jnp.int32),
            pltpu.VMEM((modes, count), F32), pltpu.VMEM((1, count), F32), pltpu.VMEM((1, n_dom), jnp.int32),
            pltpu.SemaphoreType.DMA((5,)),
        ],
    )
    planes_in = lax.all_to_all(chunks, "mode", 0, 0, tiled=True)
    oth = lax.ppermute(send, "dom", swap)

    tables = jnp.asarray(np.concatenate(halves(synthesis_table(mode_count))))
    slope = span_slope.reshape(1, mode_count)

    matrix = ((count, count), BF16)
    small = [((8, count), F32), ((face + 16, face), F32)]
    one_hot = [
        pltpu.VMEM((count, slots), BF16),
        pltpu.VMEM((slots + 32, count), BF16),
        pltpu.VMEM((slots, count), BF16),
        pltpu.VMEM((slots, count), BF16),
        pltpu.VMEM((ROW, 128), F32),
    ]

    def planes(value, first):
        (out,) = call(
            first_planes_kernel if first else planes_kernel, [((mode_count, quarter), F32)],
            [value.reshape(mode_count, quarter), tables, slope], 16, flops=600 << 20,
            far=(1, 2) if first else (), free=(tables.shape,),
            scratch=[
                pltpu.VMEM(tables.shape, BF16), pltpu.VMEM(slope.shape, F32), pltpu.SemaphoreType.DMA((2,)),
            ] if first else (),
        )
        return out

    def to_solve(value):
        back = lax.all_to_all(
            value.reshape(2 * n_mode, half, quarter), ("mode", "dom"), 0, 0, axis_index_groups=groups, tiled=True
        )
        return back.reshape(n_mode, 2, half, quarter)

    cross, keep_late, ops_other = lax.optimization_barrier((planes(planes_in, True), keep, ops_other))
    conv = to_solve(cross)
    oh, ol, do, note_o = call(
        functools.partial(own_build_kernel, half), [matrix, matrix, *small], [ops, keep_late], 36,
        far=(0,), out_far=(0, 1), flops=6 << 30,
        scratch=[
            pltpu.VMEM((side, elems, side), F32), pltpu.VMEM((count, count), BF16), pltpu.VMEM((count, count), BF16),
            *one_hot, pltpu.SemaphoreType.DMA((2 * count // 256 + 1,)),
        ],
    )
    conv, oth_late = lax.optimization_barrier((conv, oth))
    oh, ol, ph, plo, dp, note_p = call(
        functools.partial(partner_build_kernel, half), [matrix] * 4 + small, [ops_other, oth_late, oh, ol], 24,
        far=(2, 3), pinned=range(4), flops=6 << 30, scratch=[*one_hot, pltpu.SemaphoreType.DMA((2,))],
    )
    mats = [oh, ol, ph, plo]
    coefs = chebyshev()
    message = ((2 * half, face), F32)
    for iteration in range(ITERS):
        if iteration == 0:
            long_message = ((2 * half + face + 16, face), F32)
            beside = [((count, 2 * face), BF16)] * 2 + [((2 * face, count), BF16)] * 2
            *cats, r, d, sol, old, inv, cm, sums, one, two = call(
                functools.partial(first_source_kernel, half, face, mode_count),
                [*beside, *[(wide, F32)] * 7, long_message, long_message],
                [conv, keep, oth, do, dp, note_o, note_p, *mats], 20, flops=500 << 20, pinned=range(4),
            )
            mats = [*mats, *cats]
            source = sol
        else:
            source = d
            r, d, old, one, two = call(
                functools.partial(source_kernel, half, face),
                [(wide, F32), (wide, F32), (wide, F32), message, message],
                [conv, old, keep, oth, r, d, inv, cm, sums, late, *mats], 20, flops=500 << 20,
            )
        for k in (0, 2, 4):
            c1, c2 = exchange(one, two)
            r, d, sol, late = call(
                functools.partial(rest_kernel, half, face, coefs[k + 1]), [(wide, F32)] * 3 + [((2 * half, face), F32)],
                [r, d, sol, source, one, two, inv, cm, sums, *mats], 20, flops=400 << 20,
            )
            if iteration == 0 and k == 0:
                r, d, sol, source, inv, cmn, na, nb, one, two = call(
                    functools.partial(first_sweep_kernel, half, face, mode_count, coefs[0], coefs[1], coefs[2]),
                    [(wide, F32)] * 5 + [((2 * half, face), F32)] + [((2 * face, face), BF16)] * 2 + [message, message],
                    [r, d, sol, late, one, two, c1, c2, inv, cm, sums, *mats], 20, flops=500 << 20,
                )
                continue
            given = [r, d, sol, one, two, c1, c2, na, nb, inv, cm, cmn, *mats]
            if k < 4:
                r, d, sol, source, one, two = call(
                    functools.partial(sweep_kernel, half, face, coefs[k], coefs[k + 1], coefs[k + 2]),
                    [*[(wide, F32)] * 4, message, message],
                    [r, d, sol, late, one, two, c1, c2, na, nb, inv, cm, sums, cmn, *mats], 20, flops=500 << 20,
                )
            elif iteration < ITERS - 1:
                r, d, sol, chunks = call(
                    functools.partial(last_kernel, half, face, coefs[k], coefs[k + 1]),
                    [(wide, F32), (wide, F32), (wide, F32), ((n_mode, 2, half, quarter), F32)],
                    given, 20, flops=100 << 20,
                )
            else:
                own, other = call(
                    functools.partial(end_kernel, half, face, coefs[k], coefs[k + 1]),
                    [((half, count), F32)] * 2, given, 20, flops=100 << 20,
                )
        if iteration < ITERS - 1:
            planes_in = lax.all_to_all(
                chunks.reshape(2 * n_mode, half, quarter), ("mode", "dom"), 0, 0, axis_index_groups=groups, tiled=True
            )
            conv = to_solve(planes(planes_in, False))
    other = lax.ppermute(other, "dom", swap)
    own, unit = call(
        finish_own_kernel, [((half, count), F32), ((count, count), BF16)], [own, place], 16, flops=200 << 20
    )
    (out,) = call(finish_kernel, [((modes, count), F32)], [own, other, unit], 16)
    return out


def solution(mesh):
    placed = (
        P("mode", "dom"),
        P("dom", None, None),
        P("dom"),
        P(),
        P("dom", None),
        P("dom", None, None),
        P(),
    )
    return jax.shard_map(
        functools.partial(body, mesh.shape["mode"], mesh.shape["dom"]),
        mesh=mesh, in_specs=placed, out_specs=P("mode", "dom"), check_vma=False,
    )
```

```python
import functools

import jax
import jax.numpy as jnp
import numpy as np
from jax import lax
from jax.experimental import pallas as pl
from jax.experimental.pallas import tpu as pltpu
from jax.sharding import PartitionSpec as P

ITERS = 3
SWEEPS = 6

mass_weight = 4.0
bound_low = 0.1
bound_high = 2.0
centre = (bound_high + bound_low) / 2.0
half_width = (bound_high - bound_low) / 2.0

F32 = jnp.float32
BF16 = jnp.bfloat16
ROW = 96


def chebyshev():
    ratio = centre / half_width
    rho = 1.0 / ratio
    coefs = [(0.0, 1.0 / centre)]
    for _ in range(SWEEPS - 1):
        rho_next = 1.0 / (2.0 * ratio - rho)
        coefs.append((rho_next * rho, 2.0 * rho_next / half_width))
        rho = rho_next
    return coefs


def synthesis_table(mode_count):
    column = np.arange(mode_count)
    number = np.where(column == 1, mode_count // 2, column // 2)
    is_sine = (column % 2 == 1) & (column > 1)
    planes = np.arange(mode_count)
    angles = (planes[:, None] * number[None, :] % mode_count) * (2.0 * np.pi / mode_count)
    return np.where(is_sine[None, :], np.sin(angles), np.cos(angles))


def halves(table):
    high = table.astype(np.float32).astype(BF16)
    return [high, (table - high.astype(np.float64)).astype(np.float32).astype(BF16)]


def split(value):
    high = value.astype(BF16)
    return high, (value - high.astype(F32)).astype(BF16)


def dot(a, b):
    return lax.dot_general(a, b, (((1,), (0,)), ((), ())), preferred_element_type=F32)


def rows_times(value, high, low):
    count = value.shape[0]
    h, l = split(value)
    both = dot(jnp.concatenate([h, l], axis=0), high)
    return both[:count] + both[count:] + dot(h, low)


def table_times(high, low, value, dim=1):
    dims = (((dim,), (0,)), ((), ()))
    count = value.shape[1]
    h, l = split(value)
    both = lax.dot_general(high, jnp.concatenate([h, l], axis=1), dims, preferred_element_type=F32)
    return both[:, :count] + both[:, count:] + lax.dot_general(low, h, dims, preferred_element_type=F32)


def iota(shape, dim):
    return lax.broadcasted_iota(jnp.int32, shape, dim)


def call(kernel, outs, vmem, limit, scratch=(), flops=0, moved=1 << 20, far=(), out_far=(), pinned=(), free=()):
    in_specs, given = [], []
    for i, v in enumerate(vmem):
        space = pltpu.HBM if i in far else pltpu.VMEM
        in_specs.append(pl.BlockSpec(memory_space=space))
        fixed = i in far or v.dtype == BF16 and v.shape not in free
        given.append(pltpu.with_memory_space_constraint(v, space) if fixed else v)
    shapes, out_specs = [], []
    for i, (s, t) in enumerate(outs):
        space = pltpu.HBM if i in out_far else pltpu.VMEM
        out_specs.append(pl.BlockSpec(memory_space=space))
        shapes.append(space(s, t) if i in out_far or i in pinned else jax.ShapeDtypeStruct(s, t))
    return pl.pallas_call(
        kernel,
        out_shape=shapes,
        in_specs=in_specs,
        out_specs=out_specs,
        scratch_shapes=list(scratch),
        compiler_params=pltpu.CompilerParams(vmem_limit_bytes=limit << 20),
        cost_estimate=pl.CostEstimate(flops=flops, bytes_accessed=moved, transcendentals=0),
    )(*given)


def position():
    q = lax.axis_index("dom")
    z = lax.shift_right_arithmetic(q, 1)
    return q, z, q - 2 * z


def picked(first, a, b):
    return jnp.where(first, a, b)


def order_kernel(
    iface_in, l2g_in, vel_in, mass_in, live_in, keep, send, chunks, place_out, iface, l2g, vel, mass, live, sems
):
    q, _, x = position()
    pairs = ((iface_in, iface), (l2g_in, l2g), (vel_in, vel), (mass_in, mass), (live_in, live))
    copies = [pltpu.make_async_copy(a, b, sems.at[i]) for i, (a, b) in enumerate(pairs)]
    for copy in copies:
        copy.start()
    for copy in copies:
        copy.wait()
    count = mass.shape[1]
    face = iface.shape[1]
    lists = jnp.concatenate(
        [picked(x == 0, iface[0:1, :], iface[1:2, :]), picked(x == 0, iface[1:2, :], iface[0:1, :])], axis=1
    ).astype(F32)
    lists = jnp.transpose(jnp.broadcast_to(lists, (8, 2 * face)))[:, 0:1]
    hit = jnp.where(lists == iota((1, count), 1).astype(F32), 1.0, 0.0)
    at = jnp.sum(hit * iota((2 * face, 1), 0).astype(F32), axis=0, keepdims=True)
    shared = jnp.sum(hit, axis=0, keepdims=True)
    rest = jnp.broadcast_to(1.0 - shared, (8, count))
    lane = iota((8, count), 1)
    run = rest
    step = 1
    while step < count:
        run = run + jnp.where(lane >= step, pltpu.roll(run, step, 1), 0.0)
        step *= 2
    place = jnp.where(rest > 0.5, run - 1.0 + 2.0 * face, jnp.broadcast_to(at, (8, count)))
    place_out[...] = place
    column = jnp.transpose(place)[:, 0:1]
    elems, side = l2g.shape
    slots = elems * ROW
    blank = jnp.full((1, ROW - side), -1, jnp.int32)
    row = jnp.concatenate([piece for e in range(elems) for piece in (l2g[e : e + 1, :], blank)], axis=1)
    pieces = []
    for first in range(0, slots, 512):
        part = row[:, first : first + 512]
        found = jnp.where(iota((count, 1), 0) == part, column, 0.0)
        pieces.append(jnp.where(part < 0, -1.0, jnp.sum(found, axis=0, keepdims=True)))
    index = jnp.concatenate(pieces, axis=1)
    unit = jnp.where(iota((1, count), 1).astype(F32) == column, 1.0, 0.0).astype(BF16)
    modes = vel.shape[0]
    half = modes // 2
    value = jnp.concatenate([vel[...], jnp.broadcast_to(mass[...], (16, count))], axis=0)
    high = value.astype(BF16)
    middle, low = split(value - high.astype(F32))
    total = modes + 16
    parts = dot(jnp.concatenate([high, middle, low], axis=0), unit)
    moved = parts[:total] + parts[total : 2 * total] + parts[2 * total :]
    a, b = moved[:half], moved[half:modes]
    lived = jnp.where(iota(live.shape, 1) == q, live[...], 0).astype(F32)
    lived = jnp.sum(lived, axis=1, keepdims=True)
    for ref, rows in ((keep, picked(x == 0, a, b)), (send, picked(x == 0, b, a))):
        ref[0:half, :] = rows
        ref[half : half + 8, :] = moved[modes : modes + 8]
        ref[half + 8 : half + 16, :] = jnp.broadcast_to(index[:, :count], (8, count))
        ref[half + 16 : half + 24, 0 : slots - count] = jnp.broadcast_to(
            index[:, count:], (8, slots - count)
        )
        ref[half + 16 : half + 24, slots - count :] = jnp.broadcast_to(lived, (8, 2 * count - slots))
    quarter = count // chunks.shape[0]
    for part in range(chunks.shape[0]):
        chunks[part] = moved[:modes, part * quarter : (part + 1) * quarter]


def own_build_kernel(half, ops_in, pack, high_out, low_out, diag, note, ops, high, low, *scratch):
    sems = scratch[-1]
    fetch = pltpu.make_async_copy(ops_in, ops, sems.at[0])
    fetch.start()
    copies = []

    def ship(*rows):
        for part, out in ((high, high_out), (low, low_out)):
            at = pl.ds(*rows)
            copies.append(pltpu.make_async_copy(part.at[at], out.at[at], sems.at[len(copies) + 1]))
            copies[-1].start()

    build_kernel(half, ops, pack, high, low, diag, note, *scratch[:-1], ready=fetch.wait, ship=ship)
    for copy in copies:
        copy.wait()


def partner_build_kernel(half, ops, pack, high_in, low_in, high_own, low_own, high, low, diag, note, *scratch):
    sems = scratch[-1]
    pairs = ((high_in, high_own), (low_in, low_own))
    copies = [pltpu.make_async_copy(a, b, sems.at[i]) for i, (a, b) in enumerate(pairs)]
    for copy in copies:
        copy.start()
    build_kernel(half, ops, pack, high, low, diag, note, *scratch[:-1])
    for copy in copies:
        copy.wait()


def packed(block):
    h = block.shape[0] // 2
    row, lane = iota((h, 2 * h), 0), iota((h, 2 * h), 1)
    return jnp.where((lane < h) & (row > lane), pltpu.roll(block[h:], h, 1), block[:h])


def unpacked(rows):
    h = rows.shape[0]
    row, lane = iota((h, 2 * h), 0), iota((h, 2 * h), 1)
    turned = jnp.transpose(jnp.concatenate([rows, jnp.zeros_like(rows)], axis=0))
    top = jnp.where((lane < h) & (row > lane), turned[:h], rows)
    last = jnp.where(row > lane, rows, turned[:h])
    return jnp.concatenate([top, jnp.where(lane < h, turned[h:], pltpu.roll(last, h, 1))], axis=0)


def build_kernel(half, ops, pack, high, low, diag, note, flat, tall, qh, ql, pad, ready=None, ship=None):
    live = pack[half + 16 : half + 17, pack.shape[1] - 1 :]
    side, elems = ops.shape[0], ops.shape[1]
    count = high.shape[0]
    slots = elems * ROW
    index = jnp.concatenate(
        [pack[half + 8 : half + 16, :], pack[half + 16 : half + 24, 0 : slots - count]], axis=1
    )
    column = jnp.transpose(index)[:, 0:1]
    for first in range(0, slots, 256):
        block = jnp.where(iota((1, count), 1).astype(F32) == column[first : first + 256], 1.0, 0.0)
        tall[first : first + 256, :] = block.astype(BF16)
    tall[slots:, :] = jnp.zeros((tall.shape[0] - slots, count), BF16)
    for first in range(0, count, 256):
        block = jnp.where((iota((256, 1), 0) + first).astype(F32) == index[0:1], 1.0, 0.0)
        flat[first : first + 256, :] = block.astype(BF16)
    pad[...] = jnp.zeros(pad.shape, F32)
    if ready is not None:
        ready()
    for e in range(elems):
        pad[0:side, 0:side] = ops[:, e, :] * jnp.where(live > e + 0.5, 1.0, 0.0)
        oh, ol = split(pad[...])
        spread = dot(jnp.concatenate([oh, ol], axis=0), tall[e * ROW : e * ROW + 128, :])
        qh[e * ROW : (e + 1) * ROW, :] = spread[:ROW].astype(BF16)
        ql[e * ROW : (e + 1) * ROW, :] = spread[ROW:].astype(BF16)
    tile = 256
    face = note.shape[1]
    diag[...] = jnp.zeros(diag.shape, F32)
    for j in range(0, count, tile):
        top = j + tile
        block = dot(flat[j:top, :], qh[:, j:]) + dot(flat[j:top, :], ql[:, j:])
        own_node = iota((tile, 1), 0) == iota((1, tile), 1)
        line = jnp.sum(jnp.where(own_node, block[:, :tile], 0.0), axis=0, keepdims=True)
        kept = jnp.where(own_node, 0.0, block[:, :tile])
        block = jnp.concatenate([kept, block[:, tile:]], axis=1) if top < count else kept
        h, l = split(block)
        diag[0:1, j:top] = line
        diag[1:2, j:] += jnp.sum(l.astype(F32), axis=0, keepdims=True)
        high[j:top, j:] = h
        low[j:top, j:] = l
        if ship is not None:
            ship(j, tile)
        if top < count:
            mirror = jnp.transpose(block[:, tile:])
            h, l = split(mirror)
            high[top:, j:top] = h
            low[top:, j:top] = l
            diag[1:2, j:top] += jnp.sum(l.astype(F32), axis=0, keepdims=True)
        if not j:
            note[0 : face // 2, :] = packed(block[0:face, 0:face])
            first = iota((8, 1), 0) == 0
            note[face // 2 :, :] = jnp.where(first, line[:, 0:face], pack[half : half + 8, 0:face])


def apply(value, mats, half, face):
    oh, ol, ph, plo = mats[:4]
    return jnp.concatenate(
        [
            rows_times(value[:half], oh[:, face:], ol[:, face:]),
            rows_times(value[half:], ph[:, face:], plo[:, face:]),
        ],
        axis=0,
    )


def high_apply(value, mats, half):
    parts = []
    for v, high in ((value[:half], mats[0]), (value[half:], mats[2])):
        both = dot(jnp.concatenate(split(v), axis=0), high[...])
        parts.append(both[:half] + both[half:])
    return jnp.concatenate(parts, axis=0)


def low_apply(value, mats, half):
    v = value.astype(BF16)
    return jnp.concatenate([dot(v[:half], mats[1][...]), dot(v[half:], mats[3][...])], axis=0)


def outer_apply(value, mats, half, face):
    parts = []
    for v, columns in ((value[:half], mats[4]), (value[half:], mats[5])):
        both = dot(jnp.concatenate(split(v), axis=0), columns[...])
        parts.append(both[:half, :face] + both[half:, :face] + both[:half, face:])
    return jnp.concatenate(parts, axis=0)


def face_times(value, rows):
    count = value.shape[0]
    h, l = split(value)
    first, second = jnp.concatenate([h, h], axis=1), jnp.concatenate([l, jnp.zeros_like(l)], axis=1)
    both = dot(jnp.concatenate([first, second], axis=0), rows)
    return both[:count] + both[count:]


def assembled(y, outer, half, face):
    inner = y[:half, face : 2 * face] + y[half:, face : 2 * face]
    first = y[:, :face] if outer is None else y[:, :face] + outer
    return jnp.concatenate([first, jnp.concatenate([inner, inner], axis=0), y[:, 2 * face :]], axis=1)


def first_planes_kernel(u, tables_in, slope_in, out, tables, slope, sems):
    pairs = ((slope_in, slope), (tables_in, tables))
    copies = [pltpu.make_async_copy(a, b, sems.at[i]) for i, (a, b) in enumerate(pairs)]
    for copy in copies:
        copy.start()
    for copy in copies:
        copy.wait()
    planes_kernel(u, tables, slope, out)


def planes_kernel(u, tables, slope, out):
    count = slope.shape[1]
    high, low = tables[0:count, :], tables[count:, :]
    value = u[...]
    mode = iota((count, 1), 0)
    scale = lax.shift_right_arithmetic(mode, 1).astype(F32) * (2.0 / count)
    after, before = pltpu.roll(value, count - 1, 0), pltpu.roll(value, 1, 0)
    paired = jnp.where((mode & 1) == 0, scale * after, -scale * before)
    nodes = value.shape[1]
    both = table_times(high, low, jnp.concatenate([value, paired], axis=1))
    rate = jnp.transpose(jnp.broadcast_to(slope[...], (8, count)))[:, 0:1]
    cross = rate * both[:, :nodes] * both[:, nodes:]
    weight = jnp.where(mode < 2, 1.0 / count, 2.0 / count)
    out[...] = weight * table_times(high, low, cross, 0)


def provisional(r, d, g, inv, cm, mats, alpha, beta, half, face):
    r = r - inv * assembled(g, None, half, face)
    d = alpha * d + beta * r if alpha else beta * r
    y = outer_apply(d, mats, half, face) + cm[:, :face] * d[:, :face]
    return r, d, y


def even():
    _, z, x = position()
    return lax.rem(x + z, 2) == 0


def put(one, two, g, y, half, face, notes=((), ())):
    own = jnp.concatenate([g[:half, :face], y[:half], *notes[0]], axis=0)
    oth = jnp.concatenate([g[half:, :face], y[half:], *notes[1]], axis=0)
    first = even()
    one[...] = picked(first, own, oth)
    two[...] = picked(first, oth, own)


def got(one, two):
    a, b = one[...], two[...]
    first = even()
    return picked(first, a, b), picked(first, b, a)


def received(conv, half):
    _, _, x = position()
    parts = conv.shape[0]
    return jnp.concatenate(
        [
            jnp.concatenate([conv[m, x] for m in range(parts)], axis=1),
            jnp.concatenate([conv[m, 1 - x] for m in range(parts)], axis=1),
        ],
        axis=0,
    )


def masses(own, oth, half):
    count = own.shape[1]
    return jnp.concatenate(
        [jnp.broadcast_to(m[half : half + 1, :], (half, count)) for m in (own, oth)], axis=0
    )


def helmholtz(half, mode_count):
    _, _, x = position()
    mode = lax.axis_index("mode") * (2 * half) + x * half + iota((half, 1), 0)
    number = jnp.where(mode == 1, mode_count // 2, lax.shift_right_arithmetic(mode, 1))
    return mass_weight + (8.0 * number.astype(F32) / mode_count) ** 2


def first_source_kernel(
    half, face, mode_count, conv, own, oth, do, dp, note_o, note_p, oh, ol, ph, plo,
    wo, wp, vo, vp, r_out, d_out, v_out, conv_out, inv_out, cm_out, sums_out, one, two,
):
    for wide, tall, high, low in ((wo, vo, oh, ol), (wp, vp, ph, plo)):
        wide[:, 0:face] = high[:, 0:face]
        wide[:, face:] = low[:, 0:face]
        tall[0:face, :] = high[0:face, :]
        tall[face:, :] = low[0:face, :]
    mats = (oh, ol, ph, plo, wo, wp, vo, vp)
    c = helmholtz(half, mode_count)
    c = jnp.concatenate([c, c], axis=0)
    mass = masses(own, oth, half)
    stiff, sums = (
        jnp.concatenate([jnp.broadcast_to(t[row : row + 1, :], (half, t.shape[1])) for t in (do, dp)], axis=0)
        for row in (0, 1)
    )
    inv = 1.0 / (assembled(stiff, None, half, face) + c * assembled(mass, None, half, face))
    inv = jnp.concatenate([jnp.zeros((2 * half, face), F32), inv[:, face:]], axis=1)
    inv_out[...] = inv
    cm = c * mass + stiff
    cm_out[...] = cm
    sums_out[...] = sums
    v = jnp.concatenate([own[0:half, :], oth[0:half, :]], axis=0)
    v_out[...] = v
    new = received(conv, half)
    conv_out[...] = new
    m4 = mass_weight * mass
    g = high_apply(v, mats, half) + (cm + sums - m4) * v - m4 * new
    r = -inv * assembled(g, None, half, face)
    d = (1.0 / centre) * r
    r_out[...] = r
    d_out[...] = d
    y = outer_apply(d, mats, half, face)
    put(one, two, g, y, half, face, ((note_o[...],), (note_p[...],)))


def source_kernel(
    half, face, conv, old, own, oth, r, d, inv, cm, sums, late, oh, ol, ph, plo, wo, wp, vo, vp,
    r_out, d_out, conv_out, one, two,
):
    mats = (oh, ol, ph, plo, wo, wp, vo, vp)
    new = received(conv, half)
    conv_out[...] = new
    cmv, dv = cm[...], d[...]
    g = high_apply(dv, mats, half) + (cmv + sums[...]) * dv - mass_weight * masses(own, oth, half) * (new - old[...])
    g = widened(g, late[...])
    rv, dv, y = provisional(r[...], None, g, inv[...], cmv, mats, 0.0, 1.0 / centre, half, face)
    r_out[...] = rv
    d_out[...] = dv
    put(one, two, g, y, half, face)


def rest_kernel(
    half, face, now, r, d, sol, source, s1, s2, inv, cm, sums, oh, ol, ph, plo, wo, wp, vo, vp,
    r_out, d_out, sol_out, late_out,
):
    mats = (oh, ol, ph, plo, wo, wp, vo, vp)
    dv, sv = d[...], source[...]
    late = low_apply(sv, mats, half) - sums[...] * sv
    late_out[...] = late[:, :face]
    y = apply(dv, mats, half, face) + cm[:, face:] * dv[:, face:] + late[:, face:]
    y = jnp.concatenate([stacked(got(s1, s2), half, 2 * half), y], axis=1)
    rv = r[...] - inv[...] * assembled(y, None, half, face)
    dn = now[0] * dv + now[1] * rv
    r_out[...] = rv
    d_out[...] = dn
    sol_out[...] = sol[...] + dv + dn


def change_of(dd, theirs, mats, na, nb, half):
    change = [face_times(dd[:half], mats[6][...]), face_times(dd[half:], mats[7][...])]
    their_change = [face_times(theirs[:half], nb), face_times(theirs[half:], na)]
    return jnp.concatenate(change, axis=0), jnp.concatenate(their_change, axis=0)


def stacked(pair, first, last):
    return jnp.concatenate([t[first:last, :] for t in pair], axis=0)


def widened(value, face_part):
    face = face_part.shape[1]
    return jnp.concatenate([value[:, :face] + face_part, value[:, face:]], axis=1)


def corrected(half, face, now, r, d, sol, dr, dd, change, outer, inv):
    back = widened(-inv * assembled(change, outer, half, face), dr)
    step = widened(now[1] * back, now[0] * dd)
    return r + back, d + step, widened(sol + step, dd)


def exact(half, face, beta, now, r, d, sol, sent, came, na, nb, inv, cm, cmn, mats):
    inv_face = inv[:, :face]
    mine, came = got(*sent), got(*came)
    dr = -(inv_face * stacked(came, 0, half))
    dd = beta * dr
    theirs = -beta * (inv_face * stacked(mine, 0, half))
    change, their_change = change_of(dd, theirs, mats, na[...], nb[...], half)
    change = widened(change, cm[:, :face] * dd)
    outer = stacked(came, half, 2 * half) + their_change + cmn[...] * theirs
    return corrected(half, face, now, r[...], d[...], sol[...], dr, dd, change, outer, inv[...])


def first_sweep_kernel(
    half, face, mode_count, before, now, then,
    r, d, sol, late, s1, s2, c1, c2, inv, cm, sums, oh, ol, ph, plo, wo, wp, vo, vp,
    r_out, d_out, sol_out, source_out, inv_out, cmn_out, na_out, nb_out, one, two,
):
    mats = (oh, ol, ph, plo, wo, wp, vo, vp)
    cm_v = cm[...]
    mine, came = got(s1, s2), got(c1, c2)
    c = helmholtz(half, mode_count)
    c = jnp.concatenate([c, c], axis=0)

    def line(pair, row):
        return jnp.concatenate([jnp.broadcast_to(t[row : row + 1, :], (half, face)) for t in pair], axis=0)

    at = 2 * half + face // 2
    their_mass = line(came, at + 1)
    inv_face = 1.0 / (line(mine, at) + line(came, at) + c * (line(mine, at + 1) + their_mass))
    cmn = c * their_mass + line(came, at)
    nb, na = (jnp.concatenate(split(unpacked(t[2 * half : at, :])), axis=0) for t in came)
    dr = -inv_face * (stacked(mine, 0, half) + stacked(came, 0, half))
    dd = before[1] * dr
    change, their_change = change_of(dd, dd, mats, na, nb, half)
    change = widened(change, cm_v[:, :face] * dd)
    outer = stacked(mine, half, 2 * half) + stacked(came, half, 2 * half) + their_change + cmn * dd
    inv_v = jnp.concatenate([inv_face, inv[:, face:]], axis=1)
    rv, dn, sol_v = corrected(half, face, now, r[...], d[...], sol[...], dr, dd, change, outer, inv_v)
    inv_out[...] = inv_v
    cmn_out[...] = cmn
    na_out[...] = na
    nb_out[...] = nb
    sol_out[...] = sol_v
    source_out[...] = dn
    g = widened(high_apply(dn, mats, half) + (cm_v + sums[...]) * dn, late[...])
    rv, dv, y = provisional(rv, dn, g, inv_v, cm_v, mats, then[0], then[1], half, face)
    r_out[...] = rv
    d_out[...] = dv
    put(one, two, g, y, half, face)


def sweep_kernel(
    half, face, before, now, then,
    r, d, sol, late, s1, s2, c1, c2, na, nb, inv, cm, sums, cmn, oh, ol, ph, plo, wo, wp, vo, vp,
    r_out, d_out, sol_out, source_out, one, two,
):
    mats = (oh, ol, ph, plo, wo, wp, vo, vp)
    rv, dn, sol_v = exact(half, face, before[1], now, r, d, sol, (s1, s2), (c1, c2), na, nb, inv, cm, cmn, mats)
    sol_out[...] = sol_v
    source_out[...] = dn
    inv_v, cm_v = inv[...], cm[...]
    g = widened(high_apply(dn, mats, half) + (cm_v + sums[...]) * dn, late[...])
    rv, dv, y = provisional(rv, dn, g, inv_v, cm_v, mats, then[0], then[1], half, face)
    r_out[...] = rv
    d_out[...] = dv
    put(one, two, g, y, half, face)


def last_kernel(
    half, face, before, now,
    r, d, sol, s1, s2, c1, c2, na, nb, inv, cm, cmn, oh, ol, ph, plo, wo, wp, vo, vp,
    r_out, d_out, sol_out, chunks,
):
    rv, dn, new = exact(
        half, face, before[1], now, r, d, sol, (s1, s2), (c1, c2), na, nb, inv, cm, cmn, (oh, ol, ph, plo, wo, wp, vo, vp)
    )
    r_out[...] = rv
    d_out[...] = dn
    sol_out[...] = new
    _, _, x = position()
    parts, width = chunks.shape[0], chunks.shape[3]
    for m in range(parts):
        chunks[m, x] = new[:half, m * width : (m + 1) * width]
        chunks[m, 1 - x] = new[half:, m * width : (m + 1) * width]


def end_kernel(
    half, face, before, now,
    r, d, sol, s1, s2, c1, c2, na, nb, inv, cm, cmn, oh, ol, ph, plo, wo, wp, vo, vp, own_out, oth_out,
):
    _, _, new = exact(
        half, face, before[1], now, r, d, sol, (s1, s2), (c1, c2), na, nb, inv, cm, cmn, (oh, ol, ph, plo, wo, wp, vo, vp)
    )
    own_out[...] = new[:half]
    oth_out[...] = new[half:]


def restored(value, unit):
    count = value.shape[0]
    high = value.astype(BF16)
    middle, low = split(value - high.astype(F32))
    parts = dot(jnp.concatenate([high, middle, low], axis=0), unit)
    return parts[:count] + parts[count : 2 * count] + parts[2 * count :]


def finish_own_kernel(own, place, out, unit_out):
    count = own.shape[1]
    unit = jnp.where(iota((count, 1), 0).astype(F32) == place[0:1, :], 1.0, 0.0).astype(BF16)
    unit_out[...] = unit
    out[...] = restored(own[...], unit)


def finish_kernel(own, other, unit, out):
    _, _, x = position()
    a, b = own[...], restored(other[...], unit[...])
    half = own.shape[0]
    out[0:half, :] = picked(x == 0, a, b)
    out[half:, :] = picked(x == 0, b, a)


def body(n_mode, n_dom, velocity_prev, elem_ops, lumped_mass, span_slope, local_to_global, iface_nodes, live_elems):
    modes, count = velocity_prev.shape
    half = modes // 2
    elems, side = local_to_global.shape
    face = iface_nodes.shape[2]
    mode_count = span_slope.shape[0]
    quarter = count // n_mode
    pairs = n_dom // 2
    slots = elems * ROW
    places = [(z, s) for z in range(pairs) for s in (0, 1)]
    swap = [(i, i ^ 1) for i in range(n_dom)]
    long_swap = [(2 * z + s, 2 * ((z + (1 if z % 2 else -1)) % pairs) + s) for z, s in places]
    short_swap = [(2 * z + s, 2 * ((z + (-1 if z % 2 else 1)) % pairs) + s) for z, s in places]
    groups = [[m * n_dom + 2 * z + s for m in range(n_mode) for s in (0, 1)] for z in range(pairs)]

    def exchange(one, two):
        return lax.ppermute(one, "dom", long_swap), lax.ppermute(two, "dom", short_swap)

    ops = jnp.transpose(elem_ops, (1, 0, 2))
    pack = (half + 24, count)
    wide = (2 * half, count)
    keep, send, chunks, place = call(
        order_kernel,
        [(pack, F32), (pack, F32), ((n_mode, modes, quarter), F32), ((8, count), F32)],
        [iface_nodes[0], local_to_global, velocity_prev, lumped_mass.reshape(1, count), live_elems.reshape(1, n_dom)],
        24, far=range(5),
        scratch=[
            pltpu.VMEM((2, face), jnp.int32), pltpu.VMEM((elems, side), jnp.int32),
            pltpu.VMEM((modes, count), F32), pltpu.VMEM((1, count), F32), pltpu.VMEM((1, n_dom), jnp.int32),
            pltpu.SemaphoreType.DMA((5,)),
        ],
    )
    planes_in = lax.all_to_all(chunks, "mode", 0, 0, tiled=True)
    oth = lax.ppermute(send, "dom", swap)

    tables = jnp.asarray(np.concatenate(halves(synthesis_table(mode_count))))
    slope = span_slope.reshape(1, mode_count)

    matrix = ((count, count), BF16)
    small = [((8, count), F32), ((face // 2 + 8, face), F32)]
    one_hot = [
        pltpu.VMEM((count, slots), BF16),
        pltpu.VMEM((slots + 32, count), BF16),
        pltpu.VMEM((slots, count), BF16),
        pltpu.VMEM((slots, count), BF16),
        pltpu.VMEM((ROW, 128), F32),
    ]

    def planes(value, first):
        (out,) = call(
            first_planes_kernel if first else planes_kernel, [((mode_count, quarter), F32)],
            [value.reshape(mode_count, quarter), tables, slope], 16, flops=600 << 20,
            far=(1, 2) if first else (), free=(tables.shape,),
            scratch=[
                pltpu.VMEM(tables.shape, BF16), pltpu.VMEM(slope.shape, F32), pltpu.SemaphoreType.DMA((2,)),
            ] if first else (),
        )
        return out

    def to_solve(value):
        back = lax.all_to_all(
            value.reshape(2 * n_mode, half, quarter), ("mode", "dom"), 0, 0, axis_index_groups=groups, tiled=True
        )
        return back.reshape(n_mode, 2, half, quarter)

    planes_in, ops_late = lax.optimization_barrier((planes_in, ops))
    ops_other = lax.ppermute(ops_late, "dom", swap)
    cross, keep_late = lax.optimization_barrier((planes(planes_in, True), keep))
    conv = to_solve(cross)
    oh, ol, do, note_o = call(
        functools.partial(own_build_kernel, half), [matrix, matrix, *small], [ops, keep_late], 36,
        far=(0,), out_far=(0, 1), flops=6 << 30,
        scratch=[
            pltpu.VMEM((side, elems, side), F32), pltpu.VMEM((count, count), BF16), pltpu.VMEM((count, count), BF16),
            *one_hot, pltpu.SemaphoreType.DMA((2 * count // 256 + 1,)),
        ],
    )
    conv, oth_late = lax.optimization_barrier((conv, oth))
    oh, ol, ph, plo, dp, note_p = call(
        functools.partial(partner_build_kernel, half), [matrix] * 4 + small, [ops_other, oth_late, oh, ol], 24,
        far=(2, 3), pinned=range(4), flops=6 << 30, scratch=[*one_hot, pltpu.SemaphoreType.DMA((2,))],
    )
    mats = [oh, ol, ph, plo]
    coefs = chebyshev()
    message = ((2 * half, face), F32)
    for iteration in range(ITERS):
        if iteration == 0:
            long_message = ((2 * half + face // 2 + 8, face), F32)
            beside = [((count, 2 * face), BF16)] * 2 + [((2 * face, count), BF16)] * 2
            *cats, r, d, sol, old, inv, cm, sums, one, two = call(
                functools.partial(first_source_kernel, half, face, mode_count),
                [*beside, *[(wide, F32)] * 7, long_message, long_message],
                [conv, keep, oth, do, dp, note_o, note_p, *mats], 20, flops=500 << 20, pinned=range(4),
            )
            mats = [*mats, *cats]
            source = sol
        else:
            source = d
            r, d, old, one, two = call(
                functools.partial(source_kernel, half, face),
                [(wide, F32), (wide, F32), (wide, F32), message, message],
                [conv, old, keep, oth, r, d, inv, cm, sums, late, *mats], 20, flops=500 << 20,
            )
        for k in (0, 2, 4):
            c1, c2 = exchange(one, two)
            r, d, sol, late = call(
                functools.partial(rest_kernel, half, face, coefs[k + 1]), [(wide, F32)] * 3 + [((2 * half, face), F32)],
                [r, d, sol, source, one, two, inv, cm, sums, *mats], 20, flops=400 << 20,
            )
            if iteration == 0 and k == 0:
                r, d, sol, source, inv, cmn, na, nb, one, two = call(
                    functools.partial(first_sweep_kernel, half, face, mode_count, coefs[0], coefs[1], coefs[2]),
                    [(wide, F32)] * 5 + [((2 * half, face), F32)] + [((2 * face, face), BF16)] * 2 + [message, message],
                    [r, d, sol, late, one, two, c1, c2, inv, cm, sums, *mats], 20, flops=500 << 20,
                )
                continue
            given = [r, d, sol, one, two, c1, c2, na, nb, inv, cm, cmn, *mats]
            if k < 4:
                r, d, sol, source, one, two = call(
                    functools.partial(sweep_kernel, half, face, coefs[k], coefs[k + 1], coefs[k + 2]),
                    [*[(wide, F32)] * 4, message, message],
                    [r, d, sol, late, one, two, c1, c2, na, nb, inv, cm, sums, cmn, *mats], 20, flops=500 << 20,
                )
            elif iteration < ITERS - 1:
                r, d, sol, chunks = call(
                    functools.partial(last_kernel, half, face, coefs[k], coefs[k + 1]),
                    [(wide, F32), (wide, F32), (wide, F32), ((n_mode, 2, half, quarter), F32)],
                    given, 20, flops=100 << 20,
                )
            else:
                own, other = call(
                    functools.partial(end_kernel, half, face, coefs[k], coefs[k + 1]),
                    [((half, count), F32)] * 2, given, 20, flops=100 << 20,
                )
        if iteration < ITERS - 1:
            planes_in = lax.all_to_all(
                chunks.reshape(2 * n_mode, half, quarter), ("mode", "dom"), 0, 0, axis_index_groups=groups, tiled=True
            )
            conv = to_solve(planes(planes_in, False))
    other = lax.ppermute(other, "dom", swap)
    own, unit = call(
        finish_own_kernel, [((half, count), F32), ((count, count), BF16)], [own, place], 16, flops=200 << 20
    )
    (out,) = call(finish_kernel, [((modes, count), F32)], [own, other, unit], 16)
    return out


def solution(mesh):
    placed = (
        P("mode", "dom"),
        P("dom", None, None),
        P("dom"),
        P(),
        P("dom", None),
        P("dom", None, None),
        P(),
    )
    return jax.shard_map(
        functools.partial(body, mesh.shape["mode"], mesh.shape["dom"]),
        mesh=mesh, in_specs=placed, out_specs=P("mode", "dom"), check_vma=False,
    )
```

```python
import functools

import jax
import jax.numpy as jnp
import numpy as np
from jax import lax
from jax.experimental import pallas as pl
from jax.experimental.pallas import tpu as pltpu
from jax.sharding import PartitionSpec as P

ITERS = 3
SWEEPS = 6

mass_weight = 4.0
bound_low = 0.1
bound_high = 2.0
centre = (bound_high + bound_low) / 2.0
half_width = (bound_high - bound_low) / 2.0

F32 = jnp.float32
BF16 = jnp.bfloat16
ROW = 96


def chebyshev():
    ratio = centre / half_width
    rho = 1.0 / ratio
    coefs = [(0.0, 1.0 / centre)]
    for _ in range(SWEEPS - 1):
        rho_next = 1.0 / (2.0 * ratio - rho)
        coefs.append((rho_next * rho, 2.0 * rho_next / half_width))
        rho = rho_next
    return coefs


def synthesis_table(mode_count):
    column = np.arange(mode_count)
    number = np.where(column == 1, mode_count // 2, column // 2)
    is_sine = (column % 2 == 1) & (column > 1)
    planes = np.arange(mode_count)
    angles = (planes[:, None] * number[None, :] % mode_count) * (2.0 * np.pi / mode_count)
    return np.where(is_sine[None, :], np.sin(angles), np.cos(angles))


def halves(table):
    high = table.astype(np.float32).astype(BF16)
    return [high, (table - high.astype(np.float64)).astype(np.float32).astype(BF16)]


def split(value):
    high = value.astype(BF16)
    return high, (value - high.astype(F32)).astype(BF16)


def dot(a, b):
    return lax.dot_general(a, b, (((1,), (0,)), ((), ())), preferred_element_type=F32)


def rows_times(value, high, low):
    count = value.shape[0]
    h, l = split(value)
    both = dot(jnp.concatenate([h, l], axis=0), high)
    return both[:count] + both[count:] + dot(h, low)


def table_times(high, low, value, dim=1):
    dims = (((dim,), (0,)), ((), ()))
    count = value.shape[1]
    h, l = split(value)
    both = lax.dot_general(high, jnp.concatenate([h, l], axis=1), dims, preferred_element_type=F32)
    return both[:, :count] + both[:, count:] + lax.dot_general(low, h, dims, preferred_element_type=F32)


def iota(shape, dim):
    return lax.broadcasted_iota(jnp.int32, shape, dim)


def call(kernel, outs, vmem, limit, scratch=(), flops=0, moved=1 << 20, far=(), out_far=(), pinned=(), free=()):
    in_specs, given = [], []
    for i, v in enumerate(vmem):
        space = pltpu.HBM if i in far else pltpu.VMEM
        in_specs.append(pl.BlockSpec(memory_space=space))
        fixed = i in far or v.dtype == BF16 and v.shape not in free
        given.append(pltpu.with_memory_space_constraint(v, space) if fixed else v)
    shapes, out_specs = [], []
    for i, (s, t) in enumerate(outs):
        space = pltpu.HBM if i in out_far else pltpu.VMEM
        out_specs.append(pl.BlockSpec(memory_space=space))
        shapes.append(space(s, t) if i in out_far or i in pinned else jax.ShapeDtypeStruct(s, t))
    return pl.pallas_call(
        kernel,
        out_shape=shapes,
        in_specs=in_specs,
        out_specs=out_specs,
        scratch_shapes=list(scratch),
        compiler_params=pltpu.CompilerParams(vmem_limit_bytes=limit << 20),
        cost_estimate=pl.CostEstimate(flops=flops, bytes_accessed=moved, transcendentals=0),
    )(*given)


def position():
    q = lax.axis_index("dom")
    z = lax.shift_right_arithmetic(q, 1)
    return q, z, q - 2 * z


def picked(first, a, b):
    return jnp.where(first, a, b)


def order_kernel(iface_in, vel_in, mass_in, chunks, place_out, mass_out, iface, vel, mass, sems):
    _, _, x = position()
    pairs = ((iface_in, iface), (vel_in, vel), (mass_in, mass))
    copies = [pltpu.make_async_copy(a, b, sems.at[i]) for i, (a, b) in enumerate(pairs)]
    for copy in copies:
        copy.start()
    for copy in copies:
        copy.wait()
    count = mass.shape[1]
    face = iface.shape[1]
    lists = jnp.concatenate(
        [picked(x == 0, iface[0:1, :], iface[1:2, :]), picked(x == 0, iface[1:2, :], iface[0:1, :])], axis=1
    ).astype(F32)
    lists = jnp.transpose(jnp.broadcast_to(lists, (8, 2 * face)))[:, 0:1]
    hit = jnp.where(lists == iota((1, count), 1).astype(F32), 1.0, 0.0)
    at = jnp.sum(hit * iota((2 * face, 1), 0).astype(F32), axis=0, keepdims=True)
    shared = jnp.sum(hit, axis=0, keepdims=True)
    rest = jnp.broadcast_to(1.0 - shared, (8, count))
    lane = iota((8, count), 1)
    run = rest
    step = 1
    while step < count:
        run = run + jnp.where(lane >= step, pltpu.roll(run, step, 1), 0.0)
        step *= 2
    place = jnp.where(rest > 0.5, run - 1.0 + 2.0 * face, jnp.broadcast_to(at, (8, count)))
    place_out[...] = place
    column = jnp.transpose(place)[:, 0:1]
    unit = jnp.where(iota((1, count), 1).astype(F32) == column, 1.0, 0.0).astype(BF16)
    modes = vel.shape[0]
    value = jnp.concatenate([vel[...], jnp.broadcast_to(mass[...], (16, count))], axis=0)
    high = value.astype(BF16)
    middle, low = split(value - high.astype(F32))
    total = modes + 16
    parts = dot(jnp.concatenate([high, middle, low], axis=0), unit)
    moved = parts[:total] + parts[total : 2 * total] + parts[2 * total :]
    mass_out[...] = moved[modes : modes + 8]
    quarter = count // chunks.shape[0]
    for part in range(chunks.shape[0]):
        chunks[part] = moved[:modes, part * quarter : (part + 1) * quarter]


def pack_kernel(l2g_in, live_in, chunks, place, mass, keep, send, l2g, live, sems):
    q, _, x = position()
    copies = [pltpu.make_async_copy(a, b, sems.at[i]) for i, (a, b) in enumerate(((l2g_in, l2g), (live_in, live)))]
    for copy in copies:
        copy.start()
    for copy in copies:
        copy.wait()
    count = place.shape[1]
    column = jnp.transpose(place[...])[:, 0:1]
    elems, side = l2g.shape
    slots = elems * ROW
    blank = jnp.full((1, ROW - side), -1, jnp.int32)
    row = jnp.concatenate([piece for e in range(elems) for piece in (l2g[e : e + 1, :], blank)], axis=1)
    pieces = []
    for first in range(0, slots, 512):
        part = row[:, first : first + 512]
        found = jnp.where(iota((count, 1), 0) == part, column, 0.0)
        pieces.append(jnp.where(part < 0, -1.0, jnp.sum(found, axis=0, keepdims=True)))
    index = jnp.concatenate(pieces, axis=1)
    moved = jnp.concatenate([chunks[part] for part in range(chunks.shape[0])], axis=1)
    half = moved.shape[0] // 2
    a, b = moved[:half], moved[half:]
    lived = jnp.where(iota(live.shape, 1) == q, live[...], 0).astype(F32)
    lived = jnp.sum(lived, axis=1, keepdims=True)
    for ref, rows in ((keep, picked(x == 0, a, b)), (send, picked(x == 0, b, a))):
        ref[0:half, :] = rows
        ref[half : half + 8, :] = mass[...]
        ref[half + 8 : half + 16, :] = jnp.broadcast_to(index[:, :count], (8, count))
        ref[half + 16 : half + 24, 0 : slots - count] = jnp.broadcast_to(
            index[:, count:], (8, slots - count)
        )
        ref[half + 16 : half + 24, slots - count :] = jnp.broadcast_to(lived, (8, 2 * count - slots))


def own_build_kernel(
    half, ops_in, pack, high_out, low_out, diag_out, note_out, ops, diag, note, high, low, *scratch
):
    sems = scratch[-1]
    fetch = pltpu.make_async_copy(ops_in, ops, sems.at[0])
    fetch.start()
    copies = []

    def ship(*rows):
        for part, out in ((high, high_out), (low, low_out)):
            at = pl.ds(*rows)
            copies.append(pltpu.make_async_copy(part.at[at], out.at[at], sems.at[len(copies) + 1]))
            copies[-1].start()

    build_kernel(half, ops, pack, high, low, diag, note, *scratch[:-1], ready=fetch.wait, ship=ship)
    for part, out in ((diag, diag_out), (note, note_out)):
        copies.append(pltpu.make_async_copy(part, out, sems.at[len(copies) + 1]))
        copies[-1].start()
    for copy in copies:
        copy.wait()


def partner_build_kernel(half, ops, pack, high_in, low_in, high_own, low_own, high, low, diag, note, *scratch):
    sems = scratch[-1]
    pairs = ((high_in, high_own), (low_in, low_own))
    copies = [pltpu.make_async_copy(a, b, sems.at[i]) for i, (a, b) in enumerate(pairs)]
    for copy in copies:
        copy.start()
    build_kernel(half, ops, pack, high, low, diag, note, *scratch[:-1])
    for copy in copies:
        copy.wait()


def packed(block):
    h = block.shape[0] // 2
    row, lane = iota((h, 2 * h), 0), iota((h, 2 * h), 1)
    return jnp.where((lane < h) & (row > lane), pltpu.roll(block[h:], h, 1), block[:h])


def unpacked(rows):
    h = rows.shape[0]
    row, lane = iota((h, 2 * h), 0), iota((h, 2 * h), 1)
    turned = jnp.transpose(jnp.concatenate([rows, jnp.zeros_like(rows)], axis=0))
    top = jnp.where((lane < h) & (row > lane), turned[:h], rows)
    last = jnp.where(row > lane, rows, turned[:h])
    return jnp.concatenate([top, jnp.where(lane < h, turned[h:], pltpu.roll(last, h, 1))], axis=0)


def build_kernel(half, ops, pack, high, low, diag, note, flat, tall, qh, ql, pad, ready=None, ship=None):
    live = pack[half + 16 : half + 17, pack.shape[1] - 1 :]
    side, elems = ops.shape[0], ops.shape[1]
    count = high.shape[0]
    slots = elems * ROW
    index = jnp.concatenate(
        [pack[half + 8 : half + 16, :], pack[half + 16 : half + 24, 0 : slots - count]], axis=1
    )
    column = jnp.transpose(index)[:, 0:1]
    for first in range(0, slots, 256):
        block = jnp.where(iota((1, count), 1).astype(F32) == column[first : first + 256], 1.0, 0.0)
        tall[first : first + 256, :] = block.astype(BF16)
    tall[slots:, :] = jnp.zeros((tall.shape[0] - slots, count), BF16)
    for first in range(0, count, 256):
        block = jnp.where((iota((256, 1), 0) + first).astype(F32) == index[0:1], 1.0, 0.0)
        flat[first : first + 256, :] = block.astype(BF16)
    pad[...] = jnp.zeros(pad.shape, F32)
    if ready is not None:
        ready()
    for e in range(elems):
        pad[0:side, 0:side] = ops[:, e, :] * jnp.where(live > e + 0.5, 1.0, 0.0)
        oh, ol = split(pad[...])
        spread = dot(jnp.concatenate([oh, ol], axis=0), tall[e * ROW : e * ROW + 128, :])
        qh[e * ROW : (e + 1) * ROW, :] = spread[:ROW].astype(BF16)
        ql[e * ROW : (e + 1) * ROW, :] = spread[ROW:].astype(BF16)
    tile = 256
    face = note.shape[1]
    diag[...] = jnp.zeros(diag.shape, F32)
    for j in range(0, count, tile):
        top = j + tile
        block = dot(flat[j:top, :], qh[:, j:]) + dot(flat[j:top, :], ql[:, j:])
        own_node = iota((tile, 1), 0) == iota((1, tile), 1)
        line = jnp.sum(jnp.where(own_node, block[:, :tile], 0.0), axis=0, keepdims=True)
        kept = jnp.where(own_node, 0.0, block[:, :tile])
        block = jnp.concatenate([kept, block[:, tile:]], axis=1) if top < count else kept
        h, l = split(block)
        diag[0:1, j:top] = line
        diag[1:2, j:] += jnp.sum(l.astype(F32), axis=0, keepdims=True)
        high[j:top, j:] = h
        low[j:top, j:] = l
        if ship is not None:
            ship(j, tile)
        if top < count:
            mirror = jnp.transpose(block[:, tile:])
            h, l = split(mirror)
            high[top:, j:top] = h
            low[top:, j:top] = l
            diag[1:2, j:top] += jnp.sum(l.astype(F32), axis=0, keepdims=True)
        if not j:
            note[0 : face // 2, :] = packed(block[0:face, 0:face])
            first = iota((8, 1), 0) == 0
            note[face // 2 :, :] = jnp.where(first, line[:, 0:face], pack[half : half + 8, 0:face])


def apply(value, mats, half, face):
    oh, ol, ph, plo = mats[:4]
    return jnp.concatenate(
        [
            rows_times(value[:half], oh[:, face:], ol[:, face:]),
            rows_times(value[half:], ph[:, face:], plo[:, face:]),
        ],
        axis=0,
    )


def high_apply(value, mats, half):
    parts = []
    for v, high in ((value[:half], mats[0]), (value[half:], mats[2])):
        both = dot(jnp.concatenate(split(v), axis=0), high[...])
        parts.append(both[:half] + both[half:])
    return jnp.concatenate(parts, axis=0)


def low_apply(value, mats, half):
    v = value.astype(BF16)
    return jnp.concatenate([dot(v[:half], mats[1][...]), dot(v[half:], mats[3][...])], axis=0)


def outer_apply(value, mats, half, face):
    parts = []
    for v, columns in ((value[:half], mats[4]), (value[half:], mats[5])):
        both = dot(jnp.concatenate(split(v), axis=0), columns[...])
        parts.append(both[:half, :face] + both[half:, :face] + both[:half, face:])
    return jnp.concatenate(parts, axis=0)


def face_times(value, rows):
    count = value.shape[0]
    h, l = split(value)
    first, second = jnp.concatenate([h, h], axis=1), jnp.concatenate([l, jnp.zeros_like(l)], axis=1)
    both = dot(jnp.concatenate([first, second], axis=0), rows)
    return both[:count] + both[count:]


def assembled(y, outer, half, face):
    inner = y[:half, face : 2 * face] + y[half:, face : 2 * face]
    first = y[:, :face] if outer is None else y[:, :face] + outer
    return jnp.concatenate([first, jnp.concatenate([inner, inner], axis=0), y[:, 2 * face :]], axis=1)


def first_planes_kernel(u, tables_in, slope_in, out, tables, slope, sems):
    pairs = ((slope_in, slope), (tables_in, tables))
    copies = [pltpu.make_async_copy(a, b, sems.at[i]) for i, (a, b) in enumerate(pairs)]
    for copy in copies:
        copy.start()
    for copy in copies:
        copy.wait()
    planes_kernel(u, tables, slope, out)


def planes_kernel(u, tables, slope, out):
    count = slope.shape[1]
    high, low = tables[0:count, :], tables[count:, :]
    value = u[...]
    mode = iota((count, 1), 0)
    scale = lax.shift_right_arithmetic(mode, 1).astype(F32) * (2.0 / count)
    after, before = pltpu.roll(value, count - 1, 0), pltpu.roll(value, 1, 0)
    paired = jnp.where((mode & 1) == 0, scale * after, -scale * before)
    nodes = value.shape[1]
    both = table_times(high, low, jnp.concatenate([value, paired], axis=1))
    rate = jnp.transpose(jnp.broadcast_to(slope[...], (8, count)))[:, 0:1]
    cross = rate * both[:, :nodes] * both[:, nodes:]
    weight = jnp.where(mode < 2, 1.0 / count, 2.0 / count)
    out[...] = weight * table_times(high, low, cross, 0)


def provisional(r, d, g, inv, cm, mats, alpha, beta, half, face):
    r = r - inv * assembled(g, None, half, face)
    d = alpha * d + beta * r if alpha else beta * r
    y = outer_apply(d, mats, half, face) + cm[:, :face] * d[:, :face]
    return r, d, y


def even():
    _, z, x = position()
    return lax.rem(x + z, 2) == 0


def put(one, two, g, y, half, face, notes=((), ())):
    own = jnp.concatenate([g[:half, :face], y[:half], *notes[0]], axis=0)
    oth = jnp.concatenate([g[half:, :face], y[half:], *notes[1]], axis=0)
    first = even()
    one[...] = picked(first, own, oth)
    two[...] = picked(first, oth, own)


def got(one, two):
    a, b = one[...], two[...]
    first = even()
    return picked(first, a, b), picked(first, b, a)


def received(conv, half):
    _, _, x = position()
    parts = conv.shape[0]
    return jnp.concatenate(
        [
            jnp.concatenate([conv[m, x] for m in range(parts)], axis=1),
            jnp.concatenate([conv[m, 1 - x] for m in range(parts)], axis=1),
        ],
        axis=0,
    )


def masses(own, oth, half):
    count = own.shape[1]
    return jnp.concatenate(
        [jnp.broadcast_to(m[half : half + 1, :], (half, count)) for m in (own, oth)], axis=0
    )


def helmholtz(half, mode_count):
    _, _, x = position()
    mode = lax.axis_index("mode") * (2 * half) + x * half + iota((half, 1), 0)
    number = jnp.where(mode == 1, mode_count // 2, lax.shift_right_arithmetic(mode, 1))
    return mass_weight + (8.0 * number.astype(F32) / mode_count) ** 2


def first_source_kernel(
    half, face, mode_count, conv, own, oth, do, dp, note_o, note_p, oh, ol, ph, plo,
    wo, wp, vo, vp, r_out, d_out, v_out, conv_out, inv_out, cm_out, sums_out, one, two,
):
    for wide, tall, high, low in ((wo, vo, oh, ol), (wp, vp, ph, plo)):
        wide[:, 0:face] = high[:, 0:face]
        wide[:, face:] = low[:, 0:face]
        tall[0:face, :] = high[0:face, :]
        tall[face:, :] = low[0:face, :]
    mats = (oh, ol, ph, plo, wo, wp, vo, vp)
    c = helmholtz(half, mode_count)
    c = jnp.concatenate([c, c], axis=0)
    mass = masses(own, oth, half)
    stiff, sums = (
        jnp.concatenate([jnp.broadcast_to(t[row : row + 1, :], (half, t.shape[1])) for t in (do, dp)], axis=0)
        for row in (0, 1)
    )
    inv = 1.0 / (assembled(stiff, None, half, face) + c * assembled(mass, None, half, face))
    inv = jnp.concatenate([jnp.zeros((2 * half, face), F32), inv[:, face:]], axis=1)
    inv_out[...] = inv
    cm = c * mass + stiff
    cm_out[...] = cm
    sums_out[...] = sums
    v = jnp.concatenate([own[0:half, :], oth[0:half, :]], axis=0)
    v_out[...] = v
    new = received(conv, half)
    conv_out[...] = new
    m4 = mass_weight * mass
    g = high_apply(v, mats, half) + (cm + sums - m4) * v - m4 * new
    r = -inv * assembled(g, None, half, face)
    d = (1.0 / centre) * r
    r_out[...] = r
    d_out[...] = d
    y = outer_apply(d, mats, half, face)
    put(one, two, g, y, half, face, ((note_o[...],), (note_p[...],)))


def source_kernel(
    half, face, conv, old, own, oth, r, d, inv, cm, sums, late, oh, ol, ph, plo, wo, wp, vo, vp,
    r_out, d_out, conv_out, one, two,
):
    mats = (oh, ol, ph, plo, wo, wp, vo, vp)
    new = received(conv, half)
    conv_out[...] = new
    cmv, dv = cm[...], d[...]
    g = high_apply(dv, mats, half) + (cmv + sums[...]) * dv - mass_weight * masses(own, oth, half) * (new - old[...])
    g = widened(g, late[...])
    rv, dv, y = provisional(r[...], None, g, inv[...], cmv, mats, 0.0, 1.0 / centre, half, face)
    r_out[...] = rv
    d_out[...] = dv
    put(one, two, g, y, half, face)


def rest_kernel(
    half, face, now, r, d, sol, source, s1, s2, inv, cm, sums, oh, ol, ph, plo, wo, wp, vo, vp,
    r_out, d_out, sol_out, late_out,
):
    mats = (oh, ol, ph, plo, wo, wp, vo, vp)
    dv, sv = d[...], source[...]
    late = low_apply(sv, mats, half) - sums[...] * sv
    late_out[...] = late[:, :face]
    y = apply(dv, mats, half, face) + cm[:, face:] * dv[:, face:] + late[:, face:]
    y = jnp.concatenate([stacked(got(s1, s2), half, 2 * half), y], axis=1)
    rv = r[...] - inv[...] * assembled(y, None, half, face)
    dn = now[0] * dv + now[1] * rv
    r_out[...] = rv
    d_out[...] = dn
    sol_out[...] = sol[...] + dv + dn


def change_of(dd, theirs, mats, na, nb, half):
    change = [face_times(dd[:half], mats[6][...]), face_times(dd[half:], mats[7][...])]
    their_change = [face_times(theirs[:half], nb), face_times(theirs[half:], na)]
    return jnp.concatenate(change, axis=0), jnp.concatenate(their_change, axis=0)


def stacked(pair, first, last):
    return jnp.concatenate([t[first:last, :] for t in pair], axis=0)


def widened(value, face_part):
    face = face_part.shape[1]
    return jnp.concatenate([value[:, :face] + face_part, value[:, face:]], axis=1)


def corrected(half, face, now, r, d, sol, dr, dd, change, outer, inv):
    back = widened(-inv * assembled(change, outer, half, face), dr)
    step = widened(now[1] * back, now[0] * dd)
    return r + back, d + step, widened(sol + step, dd)


def exact(half, face, beta, now, r, d, sol, sent, came, na, nb, inv, cm, cmn, mats):
    inv_face = inv[:, :face]
    mine, came = got(*sent), got(*came)
    dr = -(inv_face * stacked(came, 0, half))
    dd = beta * dr
    theirs = -beta * (inv_face * stacked(mine, 0, half))
    change, their_change = change_of(dd, theirs, mats, na[...], nb[...], half)
    change = widened(change, cm[:, :face] * dd)
    outer = stacked(came, half, 2 * half) + their_change + cmn[...] * theirs
    return corrected(half, face, now, r[...], d[...], sol[...], dr, dd, change, outer, inv[...])


def first_sweep_kernel(
    half, face, mode_count, before, now, then,
    r, d, sol, late, s1, s2, c1, c2, inv, cm, sums, oh, ol, ph, plo, wo, wp, vo, vp,
    r_out, d_out, sol_out, source_out, inv_out, cmn_out, na_out, nb_out, one, two,
):
    mats = (oh, ol, ph, plo, wo, wp, vo, vp)
    cm_v = cm[...]
    mine, came = got(s1, s2), got(c1, c2)
    c = helmholtz(half, mode_count)
    c = jnp.concatenate([c, c], axis=0)

    def line(pair, row):
        return jnp.concatenate([jnp.broadcast_to(t[row : row + 1, :], (half, face)) for t in pair], axis=0)

    at = 2 * half + face // 2
    their_mass = line(came, at + 1)
    inv_face = 1.0 / (line(mine, at) + line(came, at) + c * (line(mine, at + 1) + their_mass))
    cmn = c * their_mass + line(came, at)
    nb, na = (jnp.concatenate(split(unpacked(t[2 * half : at, :])), axis=0) for t in came)
    dr = -inv_face * (stacked(mine, 0, half) + stacked(came, 0, half))
    dd = before[1] * dr
    change, their_change = change_of(dd, dd, mats, na, nb, half)
    change = widened(change, cm_v[:, :face] * dd)
    outer = stacked(mine, half, 2 * half) + stacked(came, half, 2 * half) + their_change + cmn * dd
    inv_v = jnp.concatenate([inv_face, inv[:, face:]], axis=1)
    rv, dn, sol_v = corrected(half, face, now, r[...], d[...], sol[...], dr, dd, change, outer, inv_v)
    inv_out[...] = inv_v
    cmn_out[...] = cmn
    na_out[...] = na
    nb_out[...] = nb
    sol_out[...] = sol_v
    source_out[...] = dn
    g = widened(high_apply(dn, mats, half) + (cm_v + sums[...]) * dn, late[...])
    rv, dv, y = provisional(rv, dn, g, inv_v, cm_v, mats, then[0], then[1], half, face)
    r_out[...] = rv
    d_out[...] = dv
    put(one, two, g, y, half, face)


def sweep_kernel(
    half, face, before, now, then,
    r, d, sol, late, s1, s2, c1, c2, na, nb, inv, cm, sums, cmn, oh, ol, ph, plo, wo, wp, vo, vp,
    r_out, d_out, sol_out, source_out, one, two,
):
    mats = (oh, ol, ph, plo, wo, wp, vo, vp)
    rv, dn, sol_v = exact(half, face, before[1], now, r, d, sol, (s1, s2), (c1, c2), na, nb, inv, cm, cmn, mats)
    sol_out[...] = sol_v
    source_out[...] = dn
    inv_v, cm_v = inv[...], cm[...]
    g = widened(high_apply(dn, mats, half) + (cm_v + sums[...]) * dn, late[...])
    rv, dv, y = provisional(rv, dn, g, inv_v, cm_v, mats, then[0], then[1], half, face)
    r_out[...] = rv
    d_out[...] = dv
    put(one, two, g, y, half, face)


def last_kernel(
    half, face, before, now,
    r, d, sol, s1, s2, c1, c2, na, nb, inv, cm, cmn, oh, ol, ph, plo, wo, wp, vo, vp,
    r_out, d_out, sol_out, chunks,
):
    rv, dn, new = exact(
        half, face, before[1], now, r, d, sol, (s1, s2), (c1, c2), na, nb, inv, cm, cmn, (oh, ol, ph, plo, wo, wp, vo, vp)
    )
    r_out[...] = rv
    d_out[...] = dn
    sol_out[...] = new
    _, _, x = position()
    parts, width = chunks.shape[0], chunks.shape[3]
    for m in range(parts):
        chunks[m, x] = new[:half, m * width : (m + 1) * width]
        chunks[m, 1 - x] = new[half:, m * width : (m + 1) * width]


def end_kernel(
    half, face, before, now,
    r, d, sol, s1, s2, c1, c2, na, nb, inv, cm, cmn, oh, ol, ph, plo, wo, wp, vo, vp, own_out, oth_out,
):
    _, _, new = exact(
        half, face, before[1], now, r, d, sol, (s1, s2), (c1, c2), na, nb, inv, cm, cmn, (oh, ol, ph, plo, wo, wp, vo, vp)
    )
    own_out[...] = new[:half]
    oth_out[...] = new[half:]


def restored(value, unit):
    count = value.shape[0]
    high = value.astype(BF16)
    middle, low = split(value - high.astype(F32))
    parts = dot(jnp.concatenate([high, middle, low], axis=0), unit)
    return parts[:count] + parts[count : 2 * count] + parts[2 * count :]


def finish_own_kernel(own, place, out, unit_out):
    count = own.shape[1]
    unit = jnp.where(iota((count, 1), 0).astype(F32) == place[0:1, :], 1.0, 0.0).astype(BF16)
    unit_out[...] = unit
    out[...] = restored(own[...], unit)


def finish_kernel(own, other, unit, out):
    _, _, x = position()
    a, b = own[...], restored(other[...], unit[...])
    half = own.shape[0]
    out[0:half, :] = picked(x == 0, a, b)
    out[half:, :] = picked(x == 0, b, a)


def body(n_mode, n_dom, velocity_prev, elem_ops, lumped_mass, span_slope, local_to_global, iface_nodes, live_elems):
    modes, count = velocity_prev.shape
    half = modes // 2
    elems, side = local_to_global.shape
    face = iface_nodes.shape[2]
    mode_count = span_slope.shape[0]
    quarter = count // n_mode
    pairs = n_dom // 2
    slots = elems * ROW
    places = [(z, s) for z in range(pairs) for s in (0, 1)]
    swap = [(i, i ^ 1) for i in range(n_dom)]
    long_swap = [(2 * z + s, 2 * ((z + (1 if z % 2 else -1)) % pairs) + s) for z, s in places]
    short_swap = [(2 * z + s, 2 * ((z + (-1 if z % 2 else 1)) % pairs) + s) for z, s in places]
    groups = [[m * n_dom + 2 * z + s for m in range(n_mode) for s in (0, 1)] for z in range(pairs)]

    def exchange(one, two):
        return lax.ppermute(one, "dom", long_swap), lax.ppermute(two, "dom", short_swap)

    ops = jnp.transpose(elem_ops, (1, 0, 2))
    ops_other = lax.ppermute(ops, "dom", swap)
    pack = (half + 24, count)
    wide = (2 * half, count)
    chunks, place, weights = call(
        order_kernel, [((n_mode, modes, quarter), F32), ((8, count), F32), ((8, count), F32)],
        [iface_nodes[0], velocity_prev, lumped_mass.reshape(1, count)], 24, far=range(3),
        scratch=[
            pltpu.VMEM((2, face), jnp.int32), pltpu.VMEM((modes, count), F32), pltpu.VMEM((1, count), F32),
            pltpu.SemaphoreType.DMA((3,)),
        ],
    )
    planes_in = lax.all_to_all(chunks, "mode", 0, 0, tiled=True)
    keep, send = call(
        pack_kernel, [(pack, F32), (pack, F32)],
        [local_to_global, live_elems.reshape(1, n_dom), chunks, place, weights], 24, far=(0, 1),
        scratch=[
            pltpu.VMEM((elems, side), jnp.int32), pltpu.VMEM((1, n_dom), jnp.int32), pltpu.SemaphoreType.DMA((2,)),
        ],
    )
    oth = lax.ppermute(send, "dom", swap)

    tables = jnp.asarray(np.concatenate(halves(synthesis_table(mode_count))))
    slope = span_slope.reshape(1, mode_count)

    matrix = ((count, count), BF16)
    small = [((8, count), F32), ((face // 2 + 8, face), F32)]
    one_hot = [
        pltpu.VMEM((count, slots), BF16),
        pltpu.VMEM((slots + 32, count), BF16),
        pltpu.VMEM((slots, count), BF16),
        pltpu.VMEM((slots, count), BF16),
        pltpu.VMEM((ROW, 128), F32),
    ]

    def planes(value, first):
        (out,) = call(
            first_planes_kernel if first else planes_kernel, [((mode_count, quarter), F32)],
            [value.reshape(mode_count, quarter), tables, slope], 16, flops=600 << 20,
            far=(1, 2) if first else (), free=(tables.shape,),
            scratch=[
                pltpu.VMEM(tables.shape, BF16), pltpu.VMEM(slope.shape, F32), pltpu.SemaphoreType.DMA((2,)),
            ] if first else (),
        )
        return out

    def to_solve(value):
        back = lax.all_to_all(
            value.reshape(2 * n_mode, half, quarter), ("mode", "dom"), 0, 0, axis_index_groups=groups, tiled=True
        )
        return back.reshape(n_mode, 2, half, quarter)

    cross, keep_late, ops_other = lax.optimization_barrier((planes(planes_in, True), keep, ops_other))
    conv = to_solve(cross)
    oh, ol, do, note_o = call(
        functools.partial(own_build_kernel, half), [matrix, matrix, *small], [ops, keep_late], 36,
        far=(0,), out_far=range(4), flops=6 << 30,
        scratch=[
            pltpu.VMEM((side, elems, side), F32), *[pltpu.VMEM(*v) for v in small],
            pltpu.VMEM((count, count), BF16), pltpu.VMEM((count, count), BF16),
            *one_hot, pltpu.SemaphoreType.DMA((2 * count // 256 + 3,)),
        ],
    )
    conv, oth_late = lax.optimization_barrier((conv, oth))
    oh, ol, ph, plo, dp, note_p = call(
        functools.partial(partner_build_kernel, half), [matrix] * 4 + small, [ops_other, oth_late, oh, ol], 24,
        far=(2, 3), pinned=range(4), flops=6 << 30, scratch=[*one_hot, pltpu.SemaphoreType.DMA((2,))],
    )
    mats = [oh, ol, ph, plo]
    coefs = chebyshev()
    message = ((2 * half, face), F32)
    for iteration in range(ITERS):
        if iteration == 0:
            long_message = ((2 * half + face // 2 + 8, face), F32)
            beside = [((count, 2 * face), BF16)] * 2 + [((2 * face, count), BF16)] * 2
            *cats, r, d, sol, old, inv, cm, sums, one, two = call(
                functools.partial(first_source_kernel, half, face, mode_count),
                [*beside, *[(wide, F32)] * 7, long_message, long_message],
                [conv, keep, oth, do, dp, note_o, note_p, *mats], 20, flops=500 << 20, pinned=range(4),
            )
            mats = [*mats, *cats]
            source = sol
        else:
            source = d
            r, d, old, one, two = call(
                functools.partial(source_kernel, half, face),
                [(wide, F32), (wide, F32), (wide, F32), message, message],
                [conv, old, keep, oth, r, d, inv, cm, sums, late, *mats], 20, flops=500 << 20,
            )
        for k in (0, 2, 4):
            c1, c2 = exchange(one, two)
            r, d, sol, late = call(
                functools.partial(rest_kernel, half, face, coefs[k + 1]), [(wide, F32)] * 3 + [((2 * half, face), F32)],
                [r, d, sol, source, one, two, inv, cm, sums, *mats], 20, flops=400 << 20,
            )
            if iteration == 0 and k == 0:
                r, d, sol, source, inv, cmn, na, nb, one, two = call(
                    functools.partial(first_sweep_kernel, half, face, mode_count, coefs[0], coefs[1], coefs[2]),
                    [(wide, F32)] * 5 + [((2 * half, face), F32)] + [((2 * face, face), BF16)] * 2 + [message, message],
                    [r, d, sol, late, one, two, c1, c2, inv, cm, sums, *mats], 20, flops=500 << 20,
                )
                continue
            given = [r, d, sol, one, two, c1, c2, na, nb, inv, cm, cmn, *mats]
            if k < 4:
                r, d, sol, source, one, two = call(
                    functools.partial(sweep_kernel, half, face, coefs[k], coefs[k + 1], coefs[k + 2]),
                    [*[(wide, F32)] * 4, message, message],
                    [r, d, sol, late, one, two, c1, c2, na, nb, inv, cm, sums, cmn, *mats], 20, flops=500 << 20,
                )
            elif iteration < ITERS - 1:
                r, d, sol, chunks = call(
                    functools.partial(last_kernel, half, face, coefs[k], coefs[k + 1]),
                    [(wide, F32), (wide, F32), (wide, F32), ((n_mode, 2, half, quarter), F32)],
                    given, 20, flops=100 << 20,
                )
            else:
                own, other = call(
                    functools.partial(end_kernel, half, face, coefs[k], coefs[k + 1]),
                    [((half, count), F32)] * 2, given, 20, flops=100 << 20,
                )
        if iteration < ITERS - 1:
            planes_in = lax.all_to_all(
                chunks.reshape(2 * n_mode, half, quarter), ("mode", "dom"), 0, 0, axis_index_groups=groups, tiled=True
            )
            conv = to_solve(planes(planes_in, False))
    other = lax.ppermute(other, "dom", swap)
    own, unit = call(
        finish_own_kernel, [((half, count), F32), ((count, count), BF16)], [own, place], 16, flops=200 << 20
    )
    (out,) = call(finish_kernel, [((modes, count), F32)], [own, other, unit], 16)
    return out


def solution(mesh):
    placed = (
        P("mode", "dom"),
        P("dom", None, None),
        P("dom"),
        P(),
        P("dom", None),
        P("dom", None, None),
        P(),
    )
    return jax.shard_map(
        functools.partial(body, mesh.shape["mode"], mesh.shape["dom"]),
        mesh=mesh, in_specs=placed, out_specs=P("mode", "dom"), check_vma=False,
    )
```

```python
import functools

import jax
import jax.numpy as jnp
import numpy as np
from jax import lax
from jax.experimental import pallas as pl
from jax.experimental.pallas import tpu as pltpu
from jax.sharding import PartitionSpec as P

ITERS = 3
SWEEPS = 6

mass_weight = 4.0
bound_low = 0.1
bound_high = 2.0
centre = (bound_high + bound_low) / 2.0
half_width = (bound_high - bound_low) / 2.0

F32 = jnp.float32
BF16 = jnp.bfloat16
ROW = 96


def chebyshev():
    ratio = centre / half_width
    rho = 1.0 / ratio
    coefs = [(0.0, 1.0 / centre)]
    for _ in range(SWEEPS - 1):
        rho_next = 1.0 / (2.0 * ratio - rho)
        coefs.append((rho_next * rho, 2.0 * rho_next / half_width))
        rho = rho_next
    return coefs


def synthesis_table(mode_count):
    column = np.arange(mode_count)
    number = np.where(column == 1, mode_count // 2, column // 2)
    is_sine = (column % 2 == 1) & (column > 1)
    planes = np.arange(mode_count)
    angles = (planes[:, None] * number[None, :] % mode_count) * (2.0 * np.pi / mode_count)
    return np.where(is_sine[None, :], np.sin(angles), np.cos(angles))


def halves(table):
    high = table.astype(np.float32).astype(BF16)
    return [high, (table - high.astype(np.float64)).astype(np.float32).astype(BF16)]


def split(value):
    high = value.astype(BF16)
    return high, (value - high.astype(F32)).astype(BF16)


def dot(a, b):
    return lax.dot_general(a, b, (((1,), (0,)), ((), ())), preferred_element_type=F32)


def rows_times(value, high, low):
    count = value.shape[0]
    h, l = split(value)
    both = dot(jnp.concatenate([h, l], axis=0), high)
    return both[:count] + both[count:] + dot(h, low)


def table_times(high, low, value, dim=1):
    dims = (((dim,), (0,)), ((), ()))
    count = value.shape[1]
    h, l = split(value)
    both = lax.dot_general(high, jnp.concatenate([h, l], axis=1), dims, preferred_element_type=F32)
    return both[:, :count] + both[:, count:] + lax.dot_general(low, h, dims, preferred_element_type=F32)


def iota(shape, dim):
    return lax.broadcasted_iota(jnp.int32, shape, dim)


def call(kernel, outs, vmem, limit, scratch=(), flops=0, moved=1 << 20, far=(), out_far=(), pinned=(), free=()):
    in_specs, given = [], []
    for i, v in enumerate(vmem):
        space = pltpu.HBM if i in far else pltpu.VMEM
        in_specs.append(pl.BlockSpec(memory_space=space))
        fixed = i in far or v.dtype == BF16 and v.shape not in free
        given.append(pltpu.with_memory_space_constraint(v, space) if fixed else v)
    shapes, out_specs = [], []
    for i, (s, t) in enumerate(outs):
        space = pltpu.HBM if i in out_far else pltpu.VMEM
        out_specs.append(pl.BlockSpec(memory_space=space))
        shapes.append(space(s, t) if i in out_far or i in pinned else jax.ShapeDtypeStruct(s, t))
    return pl.pallas_call(
        kernel,
        out_shape=shapes,
        in_specs=in_specs,
        out_specs=out_specs,
        scratch_shapes=list(scratch),
        compiler_params=pltpu.CompilerParams(vmem_limit_bytes=limit << 20),
        cost_estimate=pl.CostEstimate(flops=flops, bytes_accessed=moved, transcendentals=0),
    )(*given)


def position():
    q = lax.axis_index("dom")
    z = lax.shift_right_arithmetic(q, 1)
    return q, z, q - 2 * z


def picked(first, a, b):
    return jnp.where(first, a, b)


def order_kernel(iface_in, vel_in, mass_in, chunks, place_out, mass_out, iface, vel, mass, sems):
    _, _, x = position()
    pairs = ((iface_in, iface), (vel_in, vel), (mass_in, mass))
    copies = [pltpu.make_async_copy(a, b, sems.at[i]) for i, (a, b) in enumerate(pairs)]
    for copy in copies:
        copy.start()
    for copy in copies:
        copy.wait()
    count = mass.shape[1]
    face = iface.shape[1]
    lists = jnp.concatenate(
        [picked(x == 0, iface[0:1, :], iface[1:2, :]), picked(x == 0, iface[1:2, :], iface[0:1, :])], axis=1
    ).astype(F32)
    lists = jnp.transpose(jnp.broadcast_to(lists, (8, 2 * face)))[:, 0:1]
    hit = jnp.where(lists == iota((1, count), 1).astype(F32), 1.0, 0.0)
    at = jnp.sum(hit * iota((2 * face, 1), 0).astype(F32), axis=0, keepdims=True)
    shared = jnp.sum(hit, axis=0, keepdims=True)
    rest = jnp.broadcast_to(1.0 - shared, (8, count))
    lane = iota((8, count), 1)
    run = rest
    step = 1
    while step < count:
        run = run + jnp.where(lane >= step, pltpu.roll(run, step, 1), 0.0)
        step *= 2
    place = jnp.where(rest > 0.5, run - 1.0 + 2.0 * face, jnp.broadcast_to(at, (8, count)))
    place_out[...] = place
    column = jnp.transpose(place)[:, 0:1]
    unit = jnp.where(iota((1, count), 1).astype(F32) == column, 1.0, 0.0).astype(BF16)
    modes = vel.shape[0]
    value = jnp.concatenate([vel[...], jnp.broadcast_to(mass[...], (16, count))], axis=0)
    high = value.astype(BF16)
    middle, low = split(value - high.astype(F32))
    total = modes + 16
    parts = dot(jnp.concatenate([high, middle, low], axis=0), unit)
    moved = parts[:total] + parts[total : 2 * total] + parts[2 * total :]
    mass_out[...] = moved[modes : modes + 8]
    quarter = count // chunks.shape[0]
    for part in range(chunks.shape[0]):
        chunks[part] = moved[:modes, part * quarter : (part + 1) * quarter]


def pack_kernel(l2g_in, live_in, chunks, place, mass, keep, send, l2g, live, sems):
    q, _, x = position()
    copies = [pltpu.make_async_copy(a, b, sems.at[i]) for i, (a, b) in enumerate(((l2g_in, l2g), (live_in, live)))]
    for copy in copies:
        copy.start()
    for copy in copies:
        copy.wait()
    count = place.shape[1]
    column = jnp.transpose(place[...])[:, 0:1]
    elems, side = l2g.shape
    slots = elems * ROW
    blank = jnp.full((1, ROW - side), -1, jnp.int32)
    row = jnp.concatenate([piece for e in range(elems) for piece in (l2g[e : e + 1, :], blank)], axis=1)
    pieces = []
    for first in range(0, slots, 512):
        part = row[:, first : first + 512]
        found = jnp.where(iota((count, 1), 0) == part, column, 0.0)
        pieces.append(jnp.where(part < 0, -1.0, jnp.sum(found, axis=0, keepdims=True)))
    index = jnp.concatenate(pieces, axis=1)
    moved = jnp.concatenate([chunks[part] for part in range(chunks.shape[0])], axis=1)
    half = moved.shape[0] // 2
    a, b = moved[:half], moved[half:]
    lived = jnp.where(iota(live.shape, 1) == q, live[...], 0).astype(F32)
    lived = jnp.sum(lived, axis=1, keepdims=True)
    for ref, rows in ((keep, picked(x == 0, a, b)), (send, picked(x == 0, b, a))):
        ref[0:half, :] = rows
        ref[half : half + 8, :] = mass[...]
        ref[half + 8 : half + 16, :] = jnp.broadcast_to(index[:, :count], (8, count))
        ref[half + 16 : half + 24, 0 : slots - count] = jnp.broadcast_to(
            index[:, count:], (8, slots - count)
        )
        ref[half + 16 : half + 24, slots - count :] = jnp.broadcast_to(lived, (8, 2 * count - slots))


def own_build_kernel(
    half, ops_in, pack, high_out, low_out, diag_out, note_out, ops, diag, note, high, low, *scratch
):
    sems = scratch[-1]
    fetch = pltpu.make_async_copy(ops_in, ops, sems.at[0])
    fetch.start()
    copies = []

    def ship(*rows):
        for part, out in ((high, high_out), (low, low_out)):
            at = pl.ds(*rows)
            copies.append(pltpu.make_async_copy(part.at[at], out.at[at], sems.at[len(copies) + 1]))
            copies[-1].start()

    build_kernel(half, ops, pack, high, low, diag, note, *scratch[:-1], ready=fetch.wait, ship=ship)
    for part, out in ((diag, diag_out), (note, note_out)):
        copies.append(pltpu.make_async_copy(part, out, sems.at[len(copies) + 1]))
        copies[-1].start()
    for copy in copies:
        copy.wait()


def partner_build_kernel(half, ops, pack, high_in, low_in, high_own, low_own, high, low, diag, note, *scratch):
    sems = scratch[-1]
    pairs = ((high_in, high_own), (low_in, low_own))
    copies = [pltpu.make_async_copy(a, b, sems.at[i]) for i, (a, b) in enumerate(pairs)]
    for copy in copies:
        copy.start()
    build_kernel(half, ops, pack, high, low, diag, note, *scratch[:-1])
    for copy in copies:
        copy.wait()


def packed(block):
    h = block.shape[0] // 2
    row, lane = iota((h, 2 * h), 0), iota((h, 2 * h), 1)
    return jnp.where((lane < h) & (row > lane), pltpu.roll(block[h:], h, 1), block[:h])


def unpacked(rows):
    h = rows.shape[0]
    row, lane = iota((h, 2 * h), 0), iota((h, 2 * h), 1)
    turned = jnp.transpose(jnp.concatenate([rows, jnp.zeros_like(rows)], axis=0))
    top = jnp.where((lane < h) & (row > lane), turned[:h], rows)
    last = jnp.where(row > lane, rows, turned[:h])
    return jnp.concatenate([top, jnp.where(lane < h, turned[h:], pltpu.roll(last, h, 1))], axis=0)


def build_kernel(half, ops, pack, high, low, diag, note, flat, qh, ql, pad, ready=None, ship=None):
    live = pack[half + 16 : half + 17, pack.shape[1] - 1 :]
    side, elems = ops.shape[0], ops.shape[1]
    count = high.shape[0]
    slots = elems * ROW
    index = jnp.concatenate(
        [pack[half + 8 : half + 16, :], pack[half + 16 : half + 24, 0 : slots - count]], axis=1
    )
    column = jnp.transpose(index)[:, 0:1]
    pad[...] = jnp.zeros(pad.shape, F32)
    lane = iota((1, count), 1).astype(F32)
    share = count // elems
    if ready is not None:
        ready()
    for e in range(elems):
        at = slice(e * ROW, (e + 1) * ROW)
        nodes = jnp.where(lane == column[at], 1.0, 0.0).astype(BF16)
        pad[0:side, 0:side] = ops[:, e, :] * jnp.where(live > e + 0.5, 1.0, 0.0)
        spread = dot(jnp.concatenate(split(pad[...]), axis=0), nodes)
        qh[at, :] = spread[:ROW].astype(BF16)
        ql[at, :] = spread[ROW:].astype(BF16)
        rows = jnp.where((iota((share, 1), 0) + e * share).astype(F32) == index[0:1], 1.0, 0.0)
        flat[e * share : (e + 1) * share, :] = rows.astype(BF16)
    tile = 256
    face = note.shape[1]
    diag[...] = jnp.zeros(diag.shape, F32)
    for j in range(0, count, tile):
        top = j + tile
        block = dot(flat[j:top, :], qh[:, j:]) + dot(flat[j:top, :], ql[:, j:])
        own_node = iota((tile, 1), 0) == iota((1, tile), 1)
        line = jnp.sum(jnp.where(own_node, block[:, :tile], 0.0), axis=0, keepdims=True)
        kept = jnp.where(own_node, 0.0, block[:, :tile])
        block = jnp.concatenate([kept, block[:, tile:]], axis=1) if top < count else kept
        h, l = split(block)
        diag[0:1, j:top] = line
        diag[1:2, j:] += jnp.sum(l.astype(F32), axis=0, keepdims=True)
        high[j:top, j:] = h
        low[j:top, j:] = l
        if ship is not None:
            ship(j, tile)
        if top < count:
            mirror = jnp.transpose(block[:, tile:])
            h, l = split(mirror)
            high[top:, j:top] = h
            low[top:, j:top] = l
            diag[1:2, j:top] += jnp.sum(l.astype(F32), axis=0, keepdims=True)
        if not j:
            note[0 : face // 2, :] = packed(block[0:face, 0:face])
            first = iota((8, 1), 0) == 0
            note[face // 2 :, :] = jnp.where(first, line[:, 0:face], pack[half : half + 8, 0:face])


def apply(value, mats, half, face):
    oh, ol, ph, plo = mats[:4]
    return jnp.concatenate(
        [
            rows_times(value[:half], oh[:, face:], ol[:, face:]),
            rows_times(value[half:], ph[:, face:], plo[:, face:]),
        ],
        axis=0,
    )


def high_apply(value, mats, half):
    parts = []
    for v, high in ((value[:half], mats[0]), (value[half:], mats[2])):
        both = dot(jnp.concatenate(split(v), axis=0), high[...])
        parts.append(both[:half] + both[half:])
    return jnp.concatenate(parts, axis=0)


def low_apply(value, mats, half):
    v = value.astype(BF16)
    return jnp.concatenate([dot(v[:half], mats[1][...]), dot(v[half:], mats[3][...])], axis=0)


def outer_apply(value, mats, half, face):
    parts = []
    for v, columns in ((value[:half], mats[4]), (value[half:], mats[5])):
        both = dot(jnp.concatenate(split(v), axis=0), columns[...])
        parts.append(both[:half, :face] + both[half:, :face] + both[:half, face:])
    return jnp.concatenate(parts, axis=0)


def face_times(value, rows):
    count = value.shape[0]
    h, l = split(value)
    first, second = jnp.concatenate([h, h], axis=1), jnp.concatenate([l, jnp.zeros_like(l)], axis=1)
    both = dot(jnp.concatenate([first, second], axis=0), rows)
    return both[:count] + both[count:]


def assembled(y, outer, half, face):
    inner = y[:half, face : 2 * face] + y[half:, face : 2 * face]
    first = y[:, :face] if outer is None else y[:, :face] + outer
    return jnp.concatenate([first, jnp.concatenate([inner, inner], axis=0), y[:, 2 * face :]], axis=1)


def first_planes_kernel(u, tables_in, slope_in, out, tables, slope, sems):
    pairs = ((slope_in, slope), (tables_in, tables))
    copies = [pltpu.make_async_copy(a, b, sems.at[i]) for i, (a, b) in enumerate(pairs)]
    for copy in copies:
        copy.start()
    for copy in copies:
        copy.wait()
    planes_kernel(u, tables, slope, out)


def planes_kernel(u, tables, slope, out):
    count = slope.shape[1]
    high, low = tables[0:count, :], tables[count:, :]
    value = u[...]
    mode = iota((count, 1), 0)
    scale = lax.shift_right_arithmetic(mode, 1).astype(F32) * (2.0 / count)
    after, before = pltpu.roll(value, count - 1, 0), pltpu.roll(value, 1, 0)
    paired = jnp.where((mode & 1) == 0, scale * after, -scale * before)
    nodes = value.shape[1]
    both = table_times(high, low, jnp.concatenate([value, paired], axis=1))
    rate = jnp.transpose(jnp.broadcast_to(slope[...], (8, count)))[:, 0:1]
    cross = rate * both[:, :nodes] * both[:, nodes:]
    weight = jnp.where(mode < 2, 1.0 / count, 2.0 / count)
    out[...] = weight * table_times(high, low, cross, 0)


def provisional(r, d, g, inv, cm, mats, alpha, beta, half, face):
    r = r - inv * assembled(g, None, half, face)
    d = alpha * d + beta * r if alpha else beta * r
    y = outer_apply(d, mats, half, face) + cm[:, :face] * d[:, :face]
    return r, d, y


def even():
    _, z, x = position()
    return lax.rem(x + z, 2) == 0


def put(one, two, g, y, half, face, notes=((), ())):
    own = jnp.concatenate([g[:half, :face], y[:half], *notes[0]], axis=0)
    oth = jnp.concatenate([g[half:, :face], y[half:], *notes[1]], axis=0)
    first = even()
    one[...] = picked(first, own, oth)
    two[...] = picked(first, oth, own)


def got(one, two):
    a, b = one[...], two[...]
    first = even()
    return picked(first, a, b), picked(first, b, a)


def received(conv, half):
    _, _, x = position()
    parts = conv.shape[0]
    return jnp.concatenate(
        [
            jnp.concatenate([conv[m, x] for m in range(parts)], axis=1),
            jnp.concatenate([conv[m, 1 - x] for m in range(parts)], axis=1),
        ],
        axis=0,
    )


def masses(own, oth, half):
    count = own.shape[1]
    return jnp.concatenate(
        [jnp.broadcast_to(m[half : half + 1, :], (half, count)) for m in (own, oth)], axis=0
    )


def helmholtz(half, mode_count):
    _, _, x = position()
    mode = lax.axis_index("mode") * (2 * half) + x * half + iota((half, 1), 0)
    number = jnp.where(mode == 1, mode_count // 2, lax.shift_right_arithmetic(mode, 1))
    return mass_weight + (8.0 * number.astype(F32) / mode_count) ** 2


def first_source_kernel(
    half, face, mode_count, conv, own, oth, do, dp, note_o, note_p, oh, ol, ph, plo,
    wo, wp, vo, vp, r_out, d_out, v_out, conv_out, inv_out, cm_out, sums_out, one, two,
):
    for wide, tall, high, low in ((wo, vo, oh, ol), (wp, vp, ph, plo)):
        wide[:, 0:face] = high[:, 0:face]
        wide[:, face:] = low[:, 0:face]
        tall[0:face, :] = high[0:face, :]
        tall[face:, :] = low[0:face, :]
    mats = (oh, ol, ph, plo, wo, wp, vo, vp)
    c = helmholtz(half, mode_count)
    c = jnp.concatenate([c, c], axis=0)
    mass = masses(own, oth, half)
    stiff, sums = (
        jnp.concatenate([jnp.broadcast_to(t[row : row + 1, :], (half, t.shape[1])) for t in (do, dp)], axis=0)
        for row in (0, 1)
    )
    inv = 1.0 / (assembled(stiff, None, half, face) + c * assembled(mass, None, half, face))
    inv = jnp.concatenate([jnp.zeros((2 * half, face), F32), inv[:, face:]], axis=1)
    inv_out[...] = inv
    cm = c * mass + stiff
    cm_out[...] = cm
    sums_out[...] = sums
    v = jnp.concatenate([own[0:half, :], oth[0:half, :]], axis=0)
    v_out[...] = v
    new = received(conv, half)
    conv_out[...] = new
    m4 = mass_weight * mass
    g = high_apply(v, mats, half) + (cm + sums - m4) * v - m4 * new
    r = -inv * assembled(g, None, half, face)
    d = (1.0 / centre) * r
    r_out[...] = r
    d_out[...] = d
    y = outer_apply(d, mats, half, face)
    put(one, two, g, y, half, face, ((note_o[...],), (note_p[...],)))


def source_kernel(
    half, face, conv, old, own, oth, r, d, inv, cm, sums, late, oh, ol, ph, plo, wo, wp, vo, vp,
    r_out, d_out, conv_out, one, two,
):
    mats = (oh, ol, ph, plo, wo, wp, vo, vp)
    new = received(conv, half)
    conv_out[...] = new
    cmv, dv = cm[...], d[...]
    g = high_apply(dv, mats, half) + (cmv + sums[...]) * dv - mass_weight * masses(own, oth, half) * (new - old[...])
    g = widened(g, late[...])
    rv, dv, y = provisional(r[...], None, g, inv[...], cmv, mats, 0.0, 1.0 / centre, half, face)
    r_out[...] = rv
    d_out[...] = dv
    put(one, two, g, y, half, face)


def rest_kernel(
    half, face, now, r, d, sol, source, s1, s2, inv, cm, sums, oh, ol, ph, plo, wo, wp, vo, vp,
    r_out, d_out, sol_out, late_out,
):
    mats = (oh, ol, ph, plo, wo, wp, vo, vp)
    dv, sv = d[...], source[...]
    late = low_apply(sv, mats, half) - sums[...] * sv
    late_out[...] = late[:, :face]
    y = apply(dv, mats, half, face) + cm[:, face:] * dv[:, face:] + late[:, face:]
    y = jnp.concatenate([stacked(got(s1, s2), half, 2 * half), y], axis=1)
    rv = r[...] - inv[...] * assembled(y, None, half, face)
    dn = now[0] * dv + now[1] * rv
    r_out[...] = rv
    d_out[...] = dn
    sol_out[...] = sol[...] + dv + dn


def change_of(dd, theirs, mats, na, nb, half):
    change = [face_times(dd[:half], mats[6][...]), face_times(dd[half:], mats[7][...])]
    their_change = [face_times(theirs[:half], nb), face_times(theirs[half:], na)]
    return jnp.concatenate(change, axis=0), jnp.concatenate(their_change, axis=0)


def stacked(pair, first, last):
    return jnp.concatenate([t[first:last, :] for t in pair], axis=0)


def widened(value, face_part):
    face = face_part.shape[1]
    return jnp.concatenate([value[:, :face] + face_part, value[:, face:]], axis=1)


def corrected(half, face, now, r, d, sol, dr, dd, change, outer, inv):
    back = widened(-inv * assembled(change, outer, half, face), dr)
    step = widened(now[1] * back, now[0] * dd)
    return r + back, d + step, widened(sol + step, dd)


def exact(half, face, beta, now, r, d, sol, sent, came, na, nb, inv, cm, cmn, mats):
    inv_face = inv[:, :face]
    mine, came = got(*sent), got(*came)
    dr = -(inv_face * stacked(came, 0, half))
    dd = beta * dr
    theirs = -beta * (inv_face * stacked(mine, 0, half))
    change, their_change = change_of(dd, theirs, mats, na[...], nb[...], half)
    change = widened(change, cm[:, :face] * dd)
    outer = stacked(came, half, 2 * half) + their_change + cmn[...] * theirs
    return corrected(half, face, now, r[...], d[...], sol[...], dr, dd, change, outer, inv[...])


def first_sweep_kernel(
    half, face, mode_count, before, now, then,
    r, d, sol, late, s1, s2, c1, c2, inv, cm, sums, oh, ol, ph, plo, wo, wp, vo, vp,
    r_out, d_out, sol_out, source_out, inv_out, cmn_out, na_out, nb_out, one, two,
):
    mats = (oh, ol, ph, plo, wo, wp, vo, vp)
    cm_v = cm[...]
    mine, came = got(s1, s2), got(c1, c2)
    c = helmholtz(half, mode_count)
    c = jnp.concatenate([c, c], axis=0)

    def line(pair, row):
        return jnp.concatenate([jnp.broadcast_to(t[row : row + 1, :], (half, face)) for t in pair], axis=0)

    at = 2 * half + face // 2
    their_mass = line(came, at + 1)
    inv_face = 1.0 / (line(mine, at) + line(came, at) + c * (line(mine, at + 1) + their_mass))
    cmn = c * their_mass + line(came, at)
    nb, na = (jnp.concatenate(split(unpacked(t[2 * half : at, :])), axis=0) for t in came)
    dr = -inv_face * (stacked(mine, 0, half) + stacked(came, 0, half))
    dd = before[1] * dr
    change, their_change = change_of(dd, dd, mats, na, nb, half)
    change = widened(change, cm_v[:, :face] * dd)
    outer = stacked(mine, half, 2 * half) + stacked(came, half, 2 * half) + their_change + cmn * dd
    inv_v = jnp.concatenate([inv_face, inv[:, face:]], axis=1)
    rv, dn, sol_v = corrected(half, face, now, r[...], d[...], sol[...], dr, dd, change, outer, inv_v)
    inv_out[...] = inv_v
    cmn_out[...] = cmn
    na_out[...] = na
    nb_out[...] = nb
    sol_out[...] = sol_v
    source_out[...] = dn
    g = widened(high_apply(dn, mats, half) + (cm_v + sums[...]) * dn, late[...])
    rv, dv, y = provisional(rv, dn, g, inv_v, cm_v, mats, then[0], then[1], half, face)
    r_out[...] = rv
    d_out[...] = dv
    put(one, two, g, y, half, face)


def sweep_kernel(
    half, face, before, now, then,
    r, d, sol, late, s1, s2, c1, c2, na, nb, inv, cm, sums, cmn, oh, ol, ph, plo, wo, wp, vo, vp,
    r_out, d_out, sol_out, source_out, one, two,
):
    mats = (oh, ol, ph, plo, wo, wp, vo, vp)
    rv, dn, sol_v = exact(half, face, before[1], now, r, d, sol, (s1, s2), (c1, c2), na, nb, inv, cm, cmn, mats)
    sol_out[...] = sol_v
    source_out[...] = dn
    inv_v, cm_v = inv[...], cm[...]
    g = widened(high_apply(dn, mats, half) + (cm_v + sums[...]) * dn, late[...])
    rv, dv, y = provisional(rv, dn, g, inv_v, cm_v, mats, then[0], then[1], half, face)
    r_out[...] = rv
    d_out[...] = dv
    put(one, two, g, y, half, face)


def last_kernel(
    half, face, before, now,
    r, d, sol, s1, s2, c1, c2, na, nb, inv, cm, cmn, oh, ol, ph, plo, wo, wp, vo, vp,
    r_out, d_out, sol_out, chunks,
):
    rv, dn, new = exact(
        half, face, before[1], now, r, d, sol, (s1, s2), (c1, c2), na, nb, inv, cm, cmn, (oh, ol, ph, plo, wo, wp, vo, vp)
    )
    r_out[...] = rv
    d_out[...] = dn
    sol_out[...] = new
    _, _, x = position()
    parts, width = chunks.shape[0], chunks.shape[3]
    for m in range(parts):
        chunks[m, x] = new[:half, m * width : (m + 1) * width]
        chunks[m, 1 - x] = new[half:, m * width : (m + 1) * width]


def end_kernel(
    half, face, before, now,
    r, d, sol, s1, s2, c1, c2, na, nb, inv, cm, cmn, oh, ol, ph, plo, wo, wp, vo, vp, own_out, oth_out,
):
    _, _, new = exact(
        half, face, before[1], now, r, d, sol, (s1, s2), (c1, c2), na, nb, inv, cm, cmn, (oh, ol, ph, plo, wo, wp, vo, vp)
    )
    own_out[...] = new[:half]
    oth_out[...] = new[half:]


def restored(value, unit):
    count = value.shape[0]
    high = value.astype(BF16)
    middle, low = split(value - high.astype(F32))
    parts = dot(jnp.concatenate([high, middle, low], axis=0), unit)
    return parts[:count] + parts[count : 2 * count] + parts[2 * count :]


def finish_own_kernel(own, place, out, unit_out):
    count = own.shape[1]
    unit = jnp.where(iota((count, 1), 0).astype(F32) == place[0:1, :], 1.0, 0.0).astype(BF16)
    unit_out[...] = unit
    out[...] = restored(own[...], unit)


def finish_kernel(own, other, unit, out):
    _, _, x = position()
    a, b = own[...], restored(other[...], unit[...])
    half = own.shape[0]
    out[0:half, :] = picked(x == 0, a, b)
    out[half:, :] = picked(x == 0, b, a)


def body(n_mode, n_dom, velocity_prev, elem_ops, lumped_mass, span_slope, local_to_global, iface_nodes, live_elems):
    modes, count = velocity_prev.shape
    half = modes // 2
    elems, side = local_to_global.shape
    face = iface_nodes.shape[2]
    mode_count = span_slope.shape[0]
    quarter = count // n_mode
    pairs = n_dom // 2
    slots = elems * ROW
    places = [(z, s) for z in range(pairs) for s in (0, 1)]
    swap = [(i, i ^ 1) for i in range(n_dom)]
    long_swap = [(2 * z + s, 2 * ((z + (1 if z % 2 else -1)) % pairs) + s) for z, s in places]
    short_swap = [(2 * z + s, 2 * ((z + (-1 if z % 2 else 1)) % pairs) + s) for z, s in places]
    groups = [[m * n_dom + 2 * z + s for m in range(n_mode) for s in (0, 1)] for z in range(pairs)]

    def exchange(one, two):
        return lax.ppermute(one, "dom", long_swap), lax.ppermute(two, "dom", short_swap)

    ops = jnp.transpose(elem_ops, (1, 0, 2))
    ops_other = lax.ppermute(ops, "dom", swap)
    pack = (half + 24, count)
    wide = (2 * half, count)
    chunks, place, weights = call(
        order_kernel, [((n_mode, modes, quarter), F32), ((8, count), F32), ((8, count), F32)],
        [iface_nodes[0], velocity_prev, lumped_mass.reshape(1, count)], 24, far=range(3),
        scratch=[
            pltpu.VMEM((2, face), jnp.int32), pltpu.VMEM((modes, count), F32), pltpu.VMEM((1, count), F32),
            pltpu.SemaphoreType.DMA((3,)),
        ],
    )
    planes_in = lax.all_to_all(chunks, "mode", 0, 0, tiled=True)
    keep, send = call(
        pack_kernel, [(pack, F32), (pack, F32)],
        [local_to_global, live_elems.reshape(1, n_dom), chunks, place, weights], 24, far=(0, 1),
        scratch=[
            pltpu.VMEM((elems, side), jnp.int32), pltpu.VMEM((1, n_dom), jnp.int32), pltpu.SemaphoreType.DMA((2,)),
        ],
    )
    oth = lax.ppermute(send, "dom", swap)

    tables = jnp.asarray(np.concatenate(halves(synthesis_table(mode_count))))
    slope = span_slope.reshape(1, mode_count)

    matrix = ((count, count), BF16)
    small = [((8, count), F32), ((face // 2 + 8, face), F32)]
    one_hot = [
        pltpu.VMEM((count, slots), BF16),
        pltpu.VMEM((slots, count), BF16),
        pltpu.VMEM((slots, count), BF16),
        pltpu.VMEM((ROW, ROW), F32),
    ]

    def planes(value, first):
        (out,) = call(
            first_planes_kernel if first else planes_kernel, [((mode_count, quarter), F32)],
            [value.reshape(mode_count, quarter), tables, slope], 16, flops=600 << 20,
            far=(1, 2) if first else (), free=(tables.shape,),
            scratch=[
                pltpu.VMEM(tables.shape, BF16), pltpu.VMEM(slope.shape, F32), pltpu.SemaphoreType.DMA((2,)),
            ] if first else (),
        )
        return out

    def to_solve(value):
        back = lax.all_to_all(
            value.reshape(2 * n_mode, half, quarter), ("mode", "dom"), 0, 0, axis_index_groups=groups, tiled=True
        )
        return back.reshape(n_mode, 2, half, quarter)

    cross, keep_late = lax.optimization_barrier((planes(planes_in, True), keep))
    keep_late, ops_other = lax.optimization_barrier((keep_late, ops_other))
    conv = to_solve(cross)
    oh, ol, do, note_o = call(
        functools.partial(own_build_kernel, half), [matrix, matrix, *small], [ops, keep_late], 36,
        far=(0,), out_far=range(4), flops=6 << 30,
        scratch=[
            pltpu.VMEM((side, elems, side), F32), *[pltpu.VMEM(*v) for v in small],
            pltpu.VMEM((count, count), BF16), pltpu.VMEM((count, count), BF16),
            *one_hot, pltpu.SemaphoreType.DMA((2 * count // 256 + 3,)),
        ],
    )
    conv, oth_late = lax.optimization_barrier((conv, oth))
    oh, ol, ph, plo, dp, note_p = call(
        functools.partial(partner_build_kernel, half), [matrix] * 4 + small, [ops_other, oth_late, oh, ol], 24,
        far=(2, 3), pinned=range(4), flops=6 << 30, scratch=[*one_hot, pltpu.SemaphoreType.DMA((2,))],
    )
    mats = [oh, ol, ph, plo]
    coefs = chebyshev()
    message = ((2 * half, face), F32)
    for iteration in range(ITERS):
        if iteration == 0:
            long_message = ((2 * half + face // 2 + 8, face), F32)
            beside = [((count, 2 * face), BF16)] * 2 + [((2 * face, count), BF16)] * 2
            *cats, r, d, sol, old, inv, cm, sums, one, two = call(
                functools.partial(first_source_kernel, half, face, mode_count),
                [*beside, *[(wide, F32)] * 7, long_message, long_message],
                [conv, keep, oth, do, dp, note_o, note_p, *mats], 20, flops=500 << 20, pinned=range(4),
            )
            mats = [*mats, *cats]
            source = sol
        else:
            source = d
            r, d, old, one, two = call(
                functools.partial(source_kernel, half, face),
                [(wide, F32), (wide, F32), (wide, F32), message, message],
                [conv, old, keep, oth, r, d, inv, cm, sums, late, *mats], 20, flops=500 << 20,
            )
        for k in (0, 2, 4):
            c1, c2 = exchange(one, two)
            r, d, sol, late = call(
                functools.partial(rest_kernel, half, face, coefs[k + 1]), [(wide, F32)] * 3 + [((2 * half, face), F32)],
                [r, d, sol, source, one, two, inv, cm, sums, *mats], 20, flops=400 << 20,
            )
            if iteration == 0 and k == 0:
                r, d, sol, source, inv, cmn, na, nb, one, two = call(
                    functools.partial(first_sweep_kernel, half, face, mode_count, coefs[0], coefs[1], coefs[2]),
                    [(wide, F32)] * 5 + [((2 * half, face), F32)] + [((2 * face, face), BF16)] * 2 + [message, message],
                    [r, d, sol, late, one, two, c1, c2, inv, cm, sums, *mats], 20, flops=500 << 20,
                )
                continue
            given = [r, d, sol, one, two, c1, c2, na, nb, inv, cm, cmn, *mats]
            if k < 4:
                r, d, sol, source, one, two = call(
                    functools.partial(sweep_kernel, half, face, coefs[k], coefs[k + 1], coefs[k + 2]),
                    [*[(wide, F32)] * 4, message, message],
                    [r, d, sol, late, one, two, c1, c2, na, nb, inv, cm, sums, cmn, *mats], 20, flops=500 << 20,
                )
            elif iteration < ITERS - 1:
                r, d, sol, chunks = call(
                    functools.partial(last_kernel, half, face, coefs[k], coefs[k + 1]),
                    [(wide, F32), (wide, F32), (wide, F32), ((n_mode, 2, half, quarter), F32)],
                    given, 20, flops=100 << 20,
                )
            else:
                own, other = call(
                    functools.partial(end_kernel, half, face, coefs[k], coefs[k + 1]),
                    [((half, count), F32)] * 2, given, 20, flops=100 << 20,
                )
        if iteration < ITERS - 1:
            planes_in = lax.all_to_all(
                chunks.reshape(2 * n_mode, half, quarter), ("mode", "dom"), 0, 0, axis_index_groups=groups, tiled=True
            )
            conv = to_solve(planes(planes_in, False))
    other = lax.ppermute(other, "dom", swap)
    own, unit = call(
        finish_own_kernel, [((half, count), F32), ((count, count), BF16)], [own, place], 16, flops=200 << 20
    )
    (out,) = call(finish_kernel, [((modes, count), F32)], [own, other, unit], 16)
    return out


def solution(mesh):
    placed = (
        P("mode", "dom"),
        P("dom", None, None),
        P("dom"),
        P(),
        P("dom", None),
        P("dom", None, None),
        P(),
    )
    return jax.shard_map(
        functools.partial(body, mesh.shape["mode"], mesh.shape["dom"]),
        mesh=mesh, in_specs=placed, out_specs=P("mode", "dom"), check_vma=False,
    )
```

```python
import functools

import jax
import jax.numpy as jnp
import numpy as np
from jax import lax
from jax.experimental import pallas as pl
from jax.experimental.pallas import tpu as pltpu
from jax.sharding import PartitionSpec as P

ITERS = 3
SWEEPS = 6

mass_weight = 4.0
bound_low = 0.1
bound_high = 2.0
centre = (bound_high + bound_low) / 2.0
half_width = (bound_high - bound_low) / 2.0

F32 = jnp.float32
BF16 = jnp.bfloat16
ROW = 96


def chebyshev():
    ratio = centre / half_width
    rho = 1.0 / ratio
    coefs = [(0.0, 1.0 / centre)]
    for _ in range(SWEEPS - 1):
        rho_next = 1.0 / (2.0 * ratio - rho)
        coefs.append((rho_next * rho, 2.0 * rho_next / half_width))
        rho = rho_next
    return coefs


def synthesis_table(mode_count):
    column = np.arange(mode_count)
    number = np.where(column == 1, mode_count // 2, column // 2)
    is_sine = (column % 2 == 1) & (column > 1)
    planes = np.arange(mode_count)
    angles = (planes[:, None] * number[None, :] % mode_count) * (2.0 * np.pi / mode_count)
    return np.where(is_sine[None, :], np.sin(angles), np.cos(angles))


def halves(table):
    high = table.astype(np.float32).astype(BF16)
    return [high, (table - high.astype(np.float64)).astype(np.float32).astype(BF16)]


def split(value):
    high = value.astype(BF16)
    return high, (value - high.astype(F32)).astype(BF16)


def dot(a, b):
    return lax.dot_general(a, b, (((1,), (0,)), ((), ())), preferred_element_type=F32)


def rows_times(value, high, low):
    count = value.shape[0]
    h, l = split(value)
    both = dot(jnp.concatenate([h, l], axis=0), high)
    return both[:count] + both[count:] + dot(h, low)


def table_times(high, low, value, dim=1):
    dims = (((dim,), (0,)), ((), ()))
    count = value.shape[1]
    h, l = split(value)
    both = lax.dot_general(high, jnp.concatenate([h, l], axis=1), dims, preferred_element_type=F32)
    return both[:, :count] + both[:, count:] + lax.dot_general(low, h, dims, preferred_element_type=F32)


def iota(shape, dim):
    return lax.broadcasted_iota(jnp.int32, shape, dim)


def call(kernel, outs, vmem, limit, scratch=(), flops=0, moved=1 << 20, far=(), out_far=(), pinned=(), free=()):
    in_specs, given = [], []
    for i, v in enumerate(vmem):
        space = pltpu.HBM if i in far else pltpu.VMEM
        in_specs.append(pl.BlockSpec(memory_space=space))
        fixed = i in far or v.dtype == BF16 and v.shape not in free
        given.append(pltpu.with_memory_space_constraint(v, space) if fixed else v)
    shapes, out_specs = [], []
    for i, (s, t) in enumerate(outs):
        space = pltpu.HBM if i in out_far else pltpu.VMEM
        out_specs.append(pl.BlockSpec(memory_space=space))
        shapes.append(space(s, t) if i in out_far or i in pinned else jax.ShapeDtypeStruct(s, t))
    return pl.pallas_call(
        kernel,
        out_shape=shapes,
        in_specs=in_specs,
        out_specs=out_specs,
        scratch_shapes=list(scratch),
        compiler_params=pltpu.CompilerParams(vmem_limit_bytes=limit << 20),
        cost_estimate=pl.CostEstimate(flops=flops, bytes_accessed=moved, transcendentals=0),
    )(*given)


def position():
    q = lax.axis_index("dom")
    z = lax.shift_right_arithmetic(q, 1)
    return q, z, q - 2 * z


def picked(first, a, b):
    return jnp.where(first, a, b)


def order_kernel(iface_in, vel_in, mass_in, chunks, place_out, mass_out, iface, vel, mass, sems):
    _, _, x = position()
    pairs = ((iface_in, iface), (vel_in, vel), (mass_in, mass))
    copies = [pltpu.make_async_copy(a, b, sems.at[i]) for i, (a, b) in enumerate(pairs)]
    for copy in copies:
        copy.start()
    for copy in copies:
        copy.wait()
    count = mass.shape[1]
    face = iface.shape[1]
    lists = jnp.concatenate(
        [picked(x == 0, iface[0:1, :], iface[1:2, :]), picked(x == 0, iface[1:2, :], iface[0:1, :])], axis=1
    ).astype(F32)
    lists = jnp.transpose(jnp.broadcast_to(lists, (8, 2 * face)))[:, 0:1]
    hit = jnp.where(lists == iota((1, count), 1).astype(F32), 1.0, 0.0)
    at = jnp.sum(hit * iota((2 * face, 1), 0).astype(F32), axis=0, keepdims=True)
    shared = jnp.sum(hit, axis=0, keepdims=True)
    rest = jnp.broadcast_to(1.0 - shared, (8, count))
    lane = iota((8, count), 1)
    run = rest
    step = 1
    while step < count:
        run = run + jnp.where(lane >= step, pltpu.roll(run, step, 1), 0.0)
        step *= 2
    place = jnp.where(rest > 0.5, run - 1.0 + 2.0 * face, jnp.broadcast_to(at, (8, count)))
    place_out[...] = place
    column = jnp.transpose(place)[:, 0:1]
    unit = jnp.where(iota((1, count), 1).astype(F32) == column, 1.0, 0.0).astype(BF16)
    modes = vel.shape[0]
    value = jnp.concatenate([vel[...], jnp.broadcast_to(mass[...], (16, count))], axis=0)
    high = value.astype(BF16)
    middle, low = split(value - high.astype(F32))
    total = modes + 16
    parts = dot(jnp.concatenate([high, middle, low], axis=0), unit)
    moved = parts[:total] + parts[total : 2 * total] + parts[2 * total :]
    mass_out[...] = moved[modes : modes + 8]
    quarter = count // chunks.shape[0]
    for part in range(chunks.shape[0]):
        chunks[part] = moved[:modes, part * quarter : (part + 1) * quarter]


def pack_kernel(l2g_in, live_in, chunks, place, mass, keep, send, l2g, live, sems):
    q, _, x = position()
    copies = [pltpu.make_async_copy(a, b, sems.at[i]) for i, (a, b) in enumerate(((l2g_in, l2g), (live_in, live)))]
    for copy in copies:
        copy.start()
    for copy in copies:
        copy.wait()
    count = place.shape[1]
    column = jnp.transpose(place[...])[:, 0:1]
    elems, side = l2g.shape
    slots = elems * ROW
    blank = jnp.full((1, ROW - side), -1, jnp.int32)
    row = jnp.concatenate([piece for e in range(elems) for piece in (l2g[e : e + 1, :], blank)], axis=1)
    pieces = []
    for first in range(0, slots, 512):
        part = row[:, first : first + 512]
        found = jnp.where(iota((count, 1), 0) == part, column, 0.0)
        pieces.append(jnp.where(part < 0, -1.0, jnp.sum(found, axis=0, keepdims=True)))
    index = jnp.concatenate(pieces, axis=1)
    moved = jnp.concatenate([chunks[part] for part in range(chunks.shape[0])], axis=1)
    half = moved.shape[0] // 2
    a, b = moved[:half], moved[half:]
    lived = jnp.where(iota(live.shape, 1) == q, live[...], 0).astype(F32)
    lived = jnp.sum(lived, axis=1, keepdims=True)
    for ref, rows in ((keep, picked(x == 0, a, b)), (send, picked(x == 0, b, a))):
        ref[0:half, :] = rows
        ref[half : half + 8, :] = mass[...]
        ref[half + 8 : half + 16, :] = jnp.broadcast_to(index[:, :count], (8, count))
        ref[half + 16 : half + 24, 0 : slots - count] = jnp.broadcast_to(
            index[:, count:], (8, slots - count)
        )
        ref[half + 16 : half + 24, slots - count :] = jnp.broadcast_to(lived, (8, 2 * count - slots))


def own_build_kernel(
    half, ops_in, pack_in, high_out, low_out, diag_out, note_out, ops, pack, diag, note, high, low, *scratch
):
    sems = scratch[-1]
    first = pltpu.make_async_copy(pack_in, pack, sems.at[sems.shape[0] - 1])
    fetch = pltpu.make_async_copy(ops_in, ops, sems.at[0])
    first.start()
    fetch.start()
    first.wait()
    copies = []

    def ship(*rows):
        for part, out in ((high, high_out), (low, low_out)):
            at = pl.ds(*rows)
            copies.append(pltpu.make_async_copy(part.at[at], out.at[at], sems.at[len(copies) + 1]))
            copies[-1].start()

    build_kernel(half, ops, pack, high, low, diag, note, *scratch[:-1], ready=fetch.wait, ship=ship)
    for part, out in ((diag, diag_out), (note, note_out)):
        copies.append(pltpu.make_async_copy(part, out, sems.at[len(copies) + 1]))
        copies[-1].start()
    for copy in copies:
        copy.wait()


def partner_build_kernel(half, ops, pack, high_in, low_in, high_own, low_own, high, low, diag, note, *scratch):
    sems = scratch[-1]
    pairs = ((high_in, high_own), (low_in, low_own))
    copies = [pltpu.make_async_copy(a, b, sems.at[i]) for i, (a, b) in enumerate(pairs)]
    for copy in copies:
        copy.start()
    build_kernel(half, ops, pack, high, low, diag, note, *scratch[:-1])
    for copy in copies:
        copy.wait()


def packed(block):
    h = block.shape[0] // 2
    row, lane = iota((h, 2 * h), 0), iota((h, 2 * h), 1)
    return jnp.where((lane < h) & (row > lane), pltpu.roll(block[h:], h, 1), block[:h])


def unpacked(rows):
    h = rows.shape[0]
    row, lane = iota((h, 2 * h), 0), iota((h, 2 * h), 1)
    turned = jnp.transpose(jnp.concatenate([rows, jnp.zeros_like(rows)], axis=0))
    top = jnp.where((lane < h) & (row > lane), turned[:h], rows)
    last = jnp.where(row > lane, rows, turned[:h])
    return jnp.concatenate([top, jnp.where(lane < h, turned[h:], pltpu.roll(last, h, 1))], axis=0)


def build_kernel(half, ops, pack, high, low, diag, note, flat, qh, ql, pad, ready=None, ship=None):
    live = pack[half + 16 : half + 17, pack.shape[1] - 1 :]
    side, elems = ops.shape[0], ops.shape[1]
    count = high.shape[0]
    slots = elems * ROW
    index = jnp.concatenate(
        [pack[half + 8 : half + 16, :], pack[half + 16 : half + 24, 0 : slots - count]], axis=1
    )
    column = jnp.transpose(index)[:, 0:1]
    pad[...] = jnp.zeros(pad.shape, F32)
    lane = iota((1, count), 1).astype(F32)
    share = count // elems

    def table_rows(e):
        rows = jnp.where((iota((share, 1), 0) + e * share).astype(F32) == index[0:1], 1.0, 0.0)
        flat[e * share : (e + 1) * share, :] = rows.astype(BF16)

    if ready is not None:
        for e in range(elems):
            table_rows(e)
        ready()
    for e in range(elems):
        at = slice(e * ROW, (e + 1) * ROW)
        nodes = jnp.where(lane == column[at], 1.0, 0.0).astype(BF16)
        pad[0:side, 0:side] = ops[:, e, :] * jnp.where(live > e + 0.5, 1.0, 0.0)
        spread = dot(jnp.concatenate(split(pad[...]), axis=0), nodes)
        qh[at, :] = spread[:ROW].astype(BF16)
        ql[at, :] = spread[ROW:].astype(BF16)
        if ready is None:
            table_rows(e)
    tile = 256
    face = note.shape[1]
    diag[...] = jnp.zeros(diag.shape, F32)
    for j in range(0, count, tile):
        top = j + tile
        block = dot(flat[j:top, :], qh[:, j:]) + dot(flat[j:top, :], ql[:, j:])
        own_node = iota((tile, 1), 0) == iota((1, tile), 1)
        line = jnp.sum(jnp.where(own_node, block[:, :tile], 0.0), axis=0, keepdims=True)
        kept = jnp.where(own_node, 0.0, block[:, :tile])
        block = jnp.concatenate([kept, block[:, tile:]], axis=1) if top < count else kept
        h, l = split(block)
        diag[0:1, j:top] = line
        diag[1:2, j:] += jnp.sum(l.astype(F32), axis=0, keepdims=True)
        high[j:top, j:] = h
        low[j:top, j:] = l
        if ship is not None:
            ship(j, tile)
        if top < count:
            mirror = jnp.transpose(block[:, tile:])
            h, l = split(mirror)
            high[top:, j:top] = h
            low[top:, j:top] = l
            diag[1:2, j:top] += jnp.sum(l.astype(F32), axis=0, keepdims=True)
        if not j:
            note[0 : face // 2, :] = packed(block[0:face, 0:face])
            first = iota((8, 1), 0) == 0
            note[face // 2 :, :] = jnp.where(first, line[:, 0:face], pack[half : half + 8, 0:face])


def apply(value, mats, half, face):
    oh, ol, ph, plo = mats[:4]
    return jnp.concatenate(
        [
            rows_times(value[:half], oh[:, face:], ol[:, face:]),
            rows_times(value[half:], ph[:, face:], plo[:, face:]),
        ],
        axis=0,
    )


def high_apply(value, mats, half):
    parts = []
    for v, high in ((value[:half], mats[0]), (value[half:], mats[2])):
        both = dot(jnp.concatenate(split(v), axis=0), high[...])
        parts.append(both[:half] + both[half:])
    return jnp.concatenate(parts, axis=0)


def low_apply(value, mats, half):
    v = value.astype(BF16)
    return jnp.concatenate([dot(v[:half], mats[1][...]), dot(v[half:], mats[3][...])], axis=0)


def outer_apply(value, mats, half, face):
    parts = []
    for v, columns in ((value[:half], mats[4]), (value[half:], mats[5])):
        both = dot(jnp.concatenate(split(v), axis=0), columns[...])
        parts.append(both[:half, :face] + both[half:, :face] + both[:half, face:])
    return jnp.concatenate(parts, axis=0)


def face_times(value, rows):
    count = value.shape[0]
    h, l = split(value)
    first, second = jnp.concatenate([h, h], axis=1), jnp.concatenate([l, jnp.zeros_like(l)], axis=1)
    both = dot(jnp.concatenate([first, second], axis=0), rows)
    return both[:count] + both[count:]


def assembled(y, outer, half, face):
    inner = y[:half, face : 2 * face] + y[half:, face : 2 * face]
    first = y[:, :face] if outer is None else y[:, :face] + outer
    return jnp.concatenate([first, jnp.concatenate([inner, inner], axis=0), y[:, 2 * face :]], axis=1)


def first_planes_kernel(u, tables_in, slope_in, out, tables, slope, sems):
    pairs = ((slope_in, slope), (tables_in, tables))
    copies = [pltpu.make_async_copy(a, b, sems.at[i]) for i, (a, b) in enumerate(pairs)]
    for copy in copies:
        copy.start()

    def ready():
        for copy in copies:
            copy.wait()

    planes_kernel(u, tables, slope, out, ready)


def planes_kernel(u, tables, slope, out, ready=None):
    count = slope.shape[1]
    value = u[...]
    mode = iota((count, 1), 0)
    scale = lax.shift_right_arithmetic(mode, 1).astype(F32) * (2.0 / count)
    after, before = pltpu.roll(value, count - 1, 0), pltpu.roll(value, 1, 0)
    paired = jnp.where((mode & 1) == 0, scale * after, -scale * before)
    nodes = value.shape[1]
    if ready is not None:
        ready()
    high, low = tables[0:count, :], tables[count:, :]
    both = table_times(high, low, jnp.concatenate([value, paired], axis=1))
    rate = jnp.transpose(jnp.broadcast_to(slope[...], (8, count)))[:, 0:1]
    cross = rate * both[:, :nodes] * both[:, nodes:]
    weight = jnp.where(mode < 2, 1.0 / count, 2.0 / count)
    out[...] = weight * table_times(high, low, cross, 0)


def provisional(r, d, g, inv, cm, mats, alpha, beta, half, face):
    r = r - inv * assembled(g, None, half, face)
    d = alpha * d + beta * r if alpha else beta * r
    y = outer_apply(d, mats, half, face) + cm[:, :face] * d[:, :face]
    return r, d, y


def even():
    _, z, x = position()
    return lax.rem(x + z, 2) == 0


def put(one, two, g, y, half, face, notes=((), ())):
    own = jnp.concatenate([g[:half, :face], y[:half], *notes[0]], axis=0)
    oth = jnp.concatenate([g[half:, :face], y[half:], *notes[1]], axis=0)
    first = even()
    one[...] = picked(first, own, oth)
    two[...] = picked(first, oth, own)


def got(one, two):
    a, b = one[...], two[...]
    first = even()
    return picked(first, a, b), picked(first, b, a)


def received(conv, half):
    _, _, x = position()
    parts = conv.shape[0]
    return jnp.concatenate(
        [
            jnp.concatenate([conv[m, x] for m in range(parts)], axis=1),
            jnp.concatenate([conv[m, 1 - x] for m in range(parts)], axis=1),
        ],
        axis=0,
    )


def masses(own, oth, half):
    count = own.shape[1]
    return jnp.concatenate(
        [jnp.broadcast_to(m[half : half + 1, :], (half, count)) for m in (own, oth)], axis=0
    )


def helmholtz(half, mode_count):
    _, _, x = position()
    mode = lax.axis_index("mode") * (2 * half) + x * half + iota((half, 1), 0)
    number = jnp.where(mode == 1, mode_count // 2, lax.shift_right_arithmetic(mode, 1))
    return mass_weight + (8.0 * number.astype(F32) / mode_count) ** 2


def first_source_kernel(
    half, face, mode_count, conv, own, oth, do, dp, note_o, note_p, oh, ol, ph, plo,
    wo, wp, vo, vp, r_out, d_out, v_out, conv_out, inv_out, cm_out, sums_out, one, two,
):
    for wide, tall, high, low in ((wo, vo, oh, ol), (wp, vp, ph, plo)):
        wide[:, 0:face] = high[:, 0:face]
        wide[:, face:] = low[:, 0:face]
        tall[0:face, :] = high[0:face, :]
        tall[face:, :] = low[0:face, :]
    mats = (oh, ol, ph, plo, wo, wp, vo, vp)
    c = helmholtz(half, mode_count)
    c = jnp.concatenate([c, c], axis=0)
    mass = masses(own, oth, half)
    stiff, sums = (
        jnp.concatenate([jnp.broadcast_to(t[row : row + 1, :], (half, t.shape[1])) for t in (do, dp)], axis=0)
        for row in (0, 1)
    )
    inv = 1.0 / (assembled(stiff, None, half, face) + c * assembled(mass, None, half, face))
    inv = jnp.concatenate([jnp.zeros((2 * half, face), F32), inv[:, face:]], axis=1)
    inv_out[...] = inv
    cm = c * mass + stiff
    cm_out[...] = cm
    sums_out[...] = sums
    v = jnp.concatenate([own[0:half, :], oth[0:half, :]], axis=0)
    v_out[...] = v
    new = received(conv, half)
    conv_out[...] = new
    m4 = mass_weight * mass
    g = high_apply(v, mats, half) + (cm + sums - m4) * v - m4 * new
    r = -inv * assembled(g, None, half, face)
    d = (1.0 / centre) * r
    r_out[...] = r
    d_out[...] = d
    y = outer_apply(d, mats, half, face)
    put(one, two, g, y, half, face, ((note_o[...],), (note_p[...],)))


def source_kernel(
    half, face, conv, old, own, oth, r, d, inv, cm, sums, late, oh, ol, ph, plo, wo, wp, vo, vp,
    r_out, d_out, conv_out, one, two,
):
    mats = (oh, ol, ph, plo, wo, wp, vo, vp)
    new = received(conv, half)
    conv_out[...] = new
    cmv, dv = cm[...], d[...]
    g = high_apply(dv, mats, half) + (cmv + sums[...]) * dv - mass_weight * masses(own, oth, half) * (new - old[...])
    g = widened(g, late[...])
    rv, dv, y = provisional(r[...], None, g, inv[...], cmv, mats, 0.0, 1.0 / centre, half, face)
    r_out[...] = rv
    d_out[...] = dv
    put(one, two, g, y, half, face)


def rest_kernel(
    half, face, now, r, d, sol, source, s1, s2, inv, cm, sums, oh, ol, ph, plo, wo, wp, vo, vp,
    r_out, d_out, sol_out, late_out,
):
    mats = (oh, ol, ph, plo, wo, wp, vo, vp)
    dv, sv = d[...], source[...]
    late = low_apply(sv, mats, half) - sums[...] * sv
    late_out[...] = late[:, :face]
    y = apply(dv, mats, half, face) + cm[:, face:] * dv[:, face:] + late[:, face:]
    y = jnp.concatenate([stacked(got(s1, s2), half, 2 * half), y], axis=1)
    rv = r[...] - inv[...] * assembled(y, None, half, face)
    dn = now[0] * dv + now[1] * rv
    r_out[...] = rv
    d_out[...] = dn
    sol_out[...] = sol[...] + dv + dn


def change_of(dd, theirs, mats, na, nb, half):
    change = [face_times(dd[:half], mats[6][...]), face_times(dd[half:], mats[7][...])]
    their_change = [face_times(theirs[:half], nb), face_times(theirs[half:], na)]
    return jnp.concatenate(change, axis=0), jnp.concatenate(their_change, axis=0)


def stacked(pair, first, last):
    return jnp.concatenate([t[first:last, :] for t in pair], axis=0)


def widened(value, face_part):
    face = face_part.shape[1]
    return jnp.concatenate([value[:, :face] + face_part, value[:, face:]], axis=1)


def corrected(half, face, now, r, d, sol, dr, dd, change, outer, inv):
    back = widened(-inv * assembled(change, outer, half, face), dr)
    step = widened(now[1] * back, now[0] * dd)
    return r + back, d + step, widened(sol + step, dd)


def exact(half, face, beta, now, r, d, sol, sent, came, na, nb, inv, cm, cmn, mats):
    inv_face = inv[:, :face]
    mine, came = got(*sent), got(*came)
    dr = -(inv_face * stacked(came, 0, half))
    dd = beta * dr
    theirs = -beta * (inv_face * stacked(mine, 0, half))
    change, their_change = change_of(dd, theirs, mats, na[...], nb[...], half)
    change = widened(change, cm[:, :face] * dd)
    outer = stacked(came, half, 2 * half) + their_change + cmn[...] * theirs
    return corrected(half, face, now, r[...], d[...], sol[...], dr, dd, change, outer, inv[...])


def first_sweep_kernel(
    half, face, mode_count, before, now, then,
    r, d, sol, late, s1, s2, c1, c2, inv, cm, sums, oh, ol, ph, plo, wo, wp, vo, vp,
    r_out, d_out, sol_out, source_out, inv_out, cmn_out, na_out, nb_out, one, two,
):
    mats = (oh, ol, ph, plo, wo, wp, vo, vp)
    cm_v = cm[...]
    mine, came = got(s1, s2), got(c1, c2)
    c = helmholtz(half, mode_count)
    c = jnp.concatenate([c, c], axis=0)

    def line(pair, row):
        return jnp.concatenate([jnp.broadcast_to(t[row : row + 1, :], (half, face)) for t in pair], axis=0)

    at = 2 * half + face // 2
    their_mass = line(came, at + 1)
    inv_face = 1.0 / (line(mine, at) + line(came, at) + c * (line(mine, at + 1) + their_mass))
    cmn = c * their_mass + line(came, at)
    nb, na = (jnp.concatenate(split(unpacked(t[2 * half : at, :])), axis=0) for t in came)
    dr = -inv_face * (stacked(mine, 0, half) + stacked(came, 0, half))
    dd = before[1] * dr
    change, their_change = change_of(dd, dd, mats, na, nb, half)
    change = widened(change, cm_v[:, :face] * dd)
    outer = stacked(mine, half, 2 * half) + stacked(came, half, 2 * half) + their_change + cmn * dd
    inv_v = jnp.concatenate([inv_face, inv[:, face:]], axis=1)
    rv, dn, sol_v = corrected(half, face, now, r[...], d[...], sol[...], dr, dd, change, outer, inv_v)
    inv_out[...] = inv_v
    cmn_out[...] = cmn
    na_out[...] = na
    nb_out[...] = nb
    sol_out[...] = sol_v
    source_out[...] = dn
    g = widened(high_apply(dn, mats, half) + (cm_v + sums[...]) * dn, late[...])
    rv, dv, y = provisional(rv, dn, g, inv_v, cm_v, mats, then[0], then[1], half, face)
    r_out[...] = rv
    d_out[...] = dv
    put(one, two, g, y, half, face)


def sweep_kernel(
    half, face, before, now, then,
    r, d, sol, late, s1, s2, c1, c2, na, nb, inv, cm, sums, cmn, oh, ol, ph, plo, wo, wp, vo, vp,
    r_out, d_out, sol_out, source_out, one, two,
):
    mats = (oh, ol, ph, plo, wo, wp, vo, vp)
    rv, dn, sol_v = exact(half, face, before[1], now, r, d, sol, (s1, s2), (c1, c2), na, nb, inv, cm, cmn, mats)
    sol_out[...] = sol_v
    source_out[...] = dn
    inv_v, cm_v = inv[...], cm[...]
    g = widened(high_apply(dn, mats, half) + (cm_v + sums[...]) * dn, late[...])
    rv, dv, y = provisional(rv, dn, g, inv_v, cm_v, mats, then[0], then[1], half, face)
    r_out[...] = rv
    d_out[...] = dv
    put(one, two, g, y, half, face)


def last_kernel(
    half, face, before, now,
    r, d, sol, s1, s2, c1, c2, na, nb, inv, cm, cmn, oh, ol, ph, plo, wo, wp, vo, vp,
    r_out, d_out, sol_out, chunks,
):
    rv, dn, new = exact(
        half, face, before[1], now, r, d, sol, (s1, s2), (c1, c2), na, nb, inv, cm, cmn, (oh, ol, ph, plo, wo, wp, vo, vp)
    )
    r_out[...] = rv
    d_out[...] = dn
    sol_out[...] = new
    _, _, x = position()
    parts, width = chunks.shape[0], chunks.shape[3]
    for m in range(parts):
        chunks[m, x] = new[:half, m * width : (m + 1) * width]
        chunks[m, 1 - x] = new[half:, m * width : (m + 1) * width]


def end_kernel(
    half, face, before, now,
    r, d, sol, s1, s2, c1, c2, na, nb, inv, cm, cmn, oh, ol, ph, plo, wo, wp, vo, vp, own_out, oth_out,
):
    _, _, new = exact(
        half, face, before[1], now, r, d, sol, (s1, s2), (c1, c2), na, nb, inv, cm, cmn, (oh, ol, ph, plo, wo, wp, vo, vp)
    )
    own_out[...] = new[:half]
    oth_out[...] = new[half:]


def restored(value, unit):
    count = value.shape[0]
    high = value.astype(BF16)
    middle, low = split(value - high.astype(F32))
    parts = dot(jnp.concatenate([high, middle, low], axis=0), unit)
    return parts[:count] + parts[count : 2 * count] + parts[2 * count :]


def finish_own_kernel(own, place, out, unit_out):
    count = own.shape[1]
    unit = jnp.where(iota((count, 1), 0).astype(F32) == place[0:1, :], 1.0, 0.0).astype(BF16)
    unit_out[...] = unit
    out[...] = restored(own[...], unit)


def finish_kernel(own, other, unit, out, last, sems):
    _, _, x = position()
    half = own.shape[0]
    mine, theirs = (pl.ds(pl.multiple_of(at * half, half), half) for at in (x, 1 - x))
    first = pltpu.make_async_copy(own, out.at[mine], sems.at[0])
    first.start()
    last[...] = restored(other[...], unit[...])
    second = pltpu.make_async_copy(last, out.at[theirs], sems.at[1])
    second.start()
    first.wait()
    second.wait()


def body(n_mode, n_dom, velocity_prev, elem_ops, lumped_mass, span_slope, local_to_global, iface_nodes, live_elems):
    modes, count = velocity_prev.shape
    half = modes // 2
    elems, side = local_to_global.shape
    face = iface_nodes.shape[2]
    mode_count = span_slope.shape[0]
    quarter = count // n_mode
    pairs = n_dom // 2
    slots = elems * ROW
    places = [(z, s) for z in range(pairs) for s in (0, 1)]
    swap = [(i, i ^ 1) for i in range(n_dom)]
    long_swap = [(2 * z + s, 2 * ((z + (1 if z % 2 else -1)) % pairs) + s) for z, s in places]
    short_swap = [(2 * z + s, 2 * ((z + (-1 if z % 2 else 1)) % pairs) + s) for z, s in places]
    groups = [[m * n_dom + 2 * z + s for m in range(n_mode) for s in (0, 1)] for z in range(pairs)]

    def exchange(one, two):
        return lax.ppermute(one, "dom", long_swap), lax.ppermute(two, "dom", short_swap)

    ops = jnp.transpose(elem_ops, (1, 0, 2))
    ops_other = lax.ppermute(ops, "dom", swap)
    pack = (half + 24, count)
    wide = (2 * half, count)
    chunks, place, weights = call(
        order_kernel, [((n_mode, modes, quarter), F32), ((8, count), F32), ((8, count), F32)],
        [iface_nodes[0], velocity_prev, lumped_mass.reshape(1, count)], 24, far=range(3),
        scratch=[
            pltpu.VMEM((2, face), jnp.int32), pltpu.VMEM((modes, count), F32), pltpu.VMEM((1, count), F32),
            pltpu.SemaphoreType.DMA((3,)),
        ],
    )
    planes_in = lax.all_to_all(chunks, "mode", 0, 0, tiled=True)
    keep, send = call(
        pack_kernel, [(pack, F32), (pack, F32)],
        [local_to_global, live_elems.reshape(1, n_dom), chunks, place, weights], 24, far=(0, 1),
        scratch=[
            pltpu.VMEM((elems, side), jnp.int32), pltpu.VMEM((1, n_dom), jnp.int32), pltpu.SemaphoreType.DMA((2,)),
        ],
    )
    oth = lax.ppermute(send, "dom", swap)

    tables = jnp.asarray(np.concatenate(halves(synthesis_table(mode_count))))
    slope = span_slope.reshape(1, mode_count)

    matrix = ((count, count), BF16)
    small = [((8, count), F32), ((face // 2 + 8, face), F32)]
    one_hot = [
        pltpu.VMEM((count, slots), BF16),
        pltpu.VMEM((slots, count), BF16),
        pltpu.VMEM((slots, count), BF16),
        pltpu.VMEM((ROW, ROW), F32),
    ]

    def planes(value, first):
        (out,) = call(
            first_planes_kernel if first else planes_kernel, [((mode_count, quarter), F32)],
            [value.reshape(mode_count, quarter), tables, slope], 16, flops=600 << 20,
            far=(1, 2) if first else (), free=(tables.shape,),
            scratch=[
                pltpu.VMEM(tables.shape, BF16), pltpu.VMEM(slope.shape, F32), pltpu.SemaphoreType.DMA((2,)),
            ] if first else (),
        )
        return out

    def to_solve(value):
        back = lax.all_to_all(
            value.reshape(2 * n_mode, half, quarter), ("mode", "dom"), 0, 0, axis_index_groups=groups, tiled=True
        )
        return back.reshape(n_mode, 2, half, quarter)

    cross, keep_late = lax.optimization_barrier((planes(planes_in, True), keep))
    keep_late, ops_other = lax.optimization_barrier((keep_late, ops_other))
    conv = to_solve(cross)
    oh, ol, do, note_o = call(
        functools.partial(own_build_kernel, half), [matrix, matrix, *small], [ops, keep_late], 36,
        far=(0, 1), out_far=range(4), flops=6 << 30,
        scratch=[
            pltpu.VMEM((side, elems, side), F32), pltpu.VMEM(pack, F32), *[pltpu.VMEM(*v) for v in small],
            pltpu.VMEM((count, count), BF16), pltpu.VMEM((count, count), BF16),
            *one_hot, pltpu.SemaphoreType.DMA((2 * count // 256 + 4,)),
        ],
    )
    conv, oth_late = lax.optimization_barrier((conv, oth))
    oh, ol, ph, plo, dp, note_p = call(
        functools.partial(partner_build_kernel, half), [matrix] * 4 + small, [ops_other, oth_late, oh, ol], 24,
        far=(2, 3), pinned=range(4), flops=6 << 30, scratch=[*one_hot, pltpu.SemaphoreType.DMA((2,))],
    )
    mats = [oh, ol, ph, plo]
    coefs = chebyshev()
    message = ((2 * half, face), F32)
    for iteration in range(ITERS):
        if iteration == 0:
            long_message = ((2 * half + face // 2 + 8, face), F32)
            beside = [((count, 2 * face), BF16)] * 2 + [((2 * face, count), BF16)] * 2
            *cats, r, d, sol, old, inv, cm, sums, one, two = call(
                functools.partial(first_source_kernel, half, face, mode_count),
                [*beside, *[(wide, F32)] * 7, long_message, long_message],
                [conv, keep, oth, do, dp, note_o, note_p, *mats], 20, flops=500 << 20, pinned=range(4),
            )
            mats = [*mats, *cats]
            source = sol
        else:
            source = d
            r, d, old, one, two = call(
                functools.partial(source_kernel, half, face),
                [(wide, F32), (wide, F32), (wide, F32), message, message],
                [conv, old, keep, oth, r, d, inv, cm, sums, late, *mats], 20, flops=500 << 20,
            )
        for k in (0, 2, 4):
            c1, c2 = exchange(one, two)
            r, d, sol, late = call(
                functools.partial(rest_kernel, half, face, coefs[k + 1]), [(wide, F32)] * 3 + [((2 * half, face), F32)],
                [r, d, sol, source, one, two, inv, cm, sums, *mats], 20, flops=400 << 20,
            )
            if iteration == 0 and k == 0:
                r, d, sol, source, inv, cmn, na, nb, one, two = call(
                    functools.partial(first_sweep_kernel, half, face, mode_count, coefs[0], coefs[1], coefs[2]),
                    [(wide, F32)] * 5 + [((2 * half, face), F32)] + [((2 * face, face), BF16)] * 2 + [message, message],
                    [r, d, sol, late, one, two, c1, c2, inv, cm, sums, *mats], 20, flops=500 << 20,
                )
                continue
            given = [r, d, sol, one, two, c1, c2, na, nb, inv, cm, cmn, *mats]
            if k < 4:
                r, d, sol, source, one, two = call(
                    functools.partial(sweep_kernel, half, face, coefs[k], coefs[k + 1], coefs[k + 2]),
                    [*[(wide, F32)] * 4, message, message],
                    [r, d, sol, late, one, two, c1, c2, na, nb, inv, cm, sums, cmn, *mats], 20, flops=500 << 20,
                )
            elif iteration < ITERS - 1:
                r, d, sol, chunks = call(
                    functools.partial(last_kernel, half, face, coefs[k], coefs[k + 1]),
                    [(wide, F32), (wide, F32), (wide, F32), ((n_mode, 2, half, quarter), F32)],
                    given, 20, flops=100 << 20,
                )
            else:
                own, other = call(
                    functools.partial(end_kernel, half, face, coefs[k], coefs[k + 1]),
                    [((half, count), F32)] * 2, given, 20, flops=100 << 20,
                )
        if iteration < ITERS - 1:
            planes_in = lax.all_to_all(
                chunks.reshape(2 * n_mode, half, quarter), ("mode", "dom"), 0, 0, axis_index_groups=groups, tiled=True
            )
            conv = to_solve(planes(planes_in, False))
    other = lax.ppermute(other, "dom", swap)
    own, unit = call(
        finish_own_kernel, [((half, count), F32), ((count, count), BF16)], [own, place], 16, flops=200 << 20
    )
    (out,) = call(
        finish_kernel, [((modes, count), F32)], [own, other, unit], 16, out_far=(0,),
        scratch=[pltpu.VMEM((half, count), F32), pltpu.SemaphoreType.DMA((2,))],
    )
    return out


def solution(mesh):
    placed = (
        P("mode", "dom"),
        P("dom", None, None),
        P("dom"),
        P(),
        P("dom", None),
        P("dom", None, None),
        P(),
    )
    return jax.shard_map(
        functools.partial(body, mesh.shape["mode"], mesh.shape["dom"]),
        mesh=mesh, in_specs=placed, out_specs=P("mode", "dom"), check_vma=False,
    )
```

```python
import functools

import jax
import jax.numpy as jnp
import numpy as np
from jax import lax
from jax.experimental import pallas as pl
from jax.experimental.pallas import tpu as pltpu
from jax.sharding import PartitionSpec as P

ITERS = 3
SWEEPS = 6

mass_weight = 4.0
bound_low = 0.1
bound_high = 2.0
centre = (bound_high + bound_low) / 2.0
half_width = (bound_high - bound_low) / 2.0

F32 = jnp.float32
BF16 = jnp.bfloat16
ROW = 96


def chebyshev():
    ratio = centre / half_width
    rho = 1.0 / ratio
    coefs = [(0.0, 1.0 / centre)]
    for _ in range(SWEEPS - 1):
        rho_next = 1.0 / (2.0 * ratio - rho)
        coefs.append((rho_next * rho, 2.0 * rho_next / half_width))
        rho = rho_next
    return coefs


def synthesis_table(mode_count):
    column = np.arange(mode_count)
    number = np.where(column == 1, mode_count // 2, column // 2)
    is_sine = (column % 2 == 1) & (column > 1)
    planes = np.arange(mode_count)
    angles = (planes[:, None] * number[None, :] % mode_count) * (2.0 * np.pi / mode_count)
    return np.where(is_sine[None, :], np.sin(angles), np.cos(angles))


def halves(table):
    high = table.astype(np.float32).astype(BF16)
    return [high, (table - high.astype(np.float64)).astype(np.float32).astype(BF16)]


def split(value):
    high = value.astype(BF16)
    return high, (value - high.astype(F32)).astype(BF16)


def dot(a, b):
    return lax.dot_general(a, b, (((1,), (0,)), ((), ())), preferred_element_type=F32)


def rows_times(value, high, low):
    count = value.shape[0]
    h, l = split(value)
    both = dot(jnp.concatenate([h, l], axis=0), high)
    return both[:count] + both[count:] + dot(h, low)


def table_times(high, low, value, dim=1):
    dims = (((dim,), (0,)), ((), ()))
    count = value.shape[1]
    h, l = split(value)
    both = lax.dot_general(high, jnp.concatenate([h, l], axis=1), dims, preferred_element_type=F32)
    return both[:, :count] + both[:, count:] + lax.dot_general(low, h, dims, preferred_element_type=F32)


def iota(shape, dim):
    return lax.broadcasted_iota(jnp.int32, shape, dim)


def call(kernel, outs, vmem, limit, scratch=(), flops=0, moved=1 << 20, far=(), out_far=(), pinned=(), free=()):
    in_specs, given = [], []
    for i, v in enumerate(vmem):
        space = pltpu.HBM if i in far else pltpu.VMEM
        in_specs.append(pl.BlockSpec(memory_space=space))
        fixed = i in far or v.dtype == BF16 and v.shape not in free
        given.append(pltpu.with_memory_space_constraint(v, space) if fixed else v)
    shapes, out_specs = [], []
    for i, (s, t) in enumerate(outs):
        space = pltpu.HBM if i in out_far else pltpu.VMEM
        out_specs.append(pl.BlockSpec(memory_space=space))
        shapes.append(space(s, t) if i in out_far or i in pinned else jax.ShapeDtypeStruct(s, t))
    return pl.pallas_call(
        kernel,
        out_shape=shapes,
        in_specs=in_specs,
        out_specs=out_specs,
        scratch_shapes=list(scratch),
        compiler_params=pltpu.CompilerParams(vmem_limit_bytes=limit << 20),
        cost_estimate=pl.CostEstimate(flops=flops, bytes_accessed=moved, transcendentals=0),
    )(*given)


def position():
    q = lax.axis_index("dom")
    z = lax.shift_right_arithmetic(q, 1)
    return q, z, q - 2 * z


def picked(first, a, b):
    return jnp.where(first, a, b)


def order_kernel(iface_in, vel_in, mass_in, chunks, place_out, mass_out, iface, vel, mass, sems):
    _, _, x = position()
    pairs = ((iface_in, iface), (vel_in, vel), (mass_in, mass))
    copies = [pltpu.make_async_copy(a, b, sems.at[i]) for i, (a, b) in enumerate(pairs)]
    for copy in copies:
        copy.start()
    for copy in copies:
        copy.wait()
    count = mass.shape[1]
    face = iface.shape[1]
    lists = jnp.concatenate(
        [picked(x == 0, iface[0:1, :], iface[1:2, :]), picked(x == 0, iface[1:2, :], iface[0:1, :])], axis=1
    ).astype(F32)
    lists = jnp.transpose(jnp.broadcast_to(lists, (8, 2 * face)))[:, 0:1]
    hit = jnp.where(lists == iota((1, count), 1).astype(F32), 1.0, 0.0)
    at = jnp.sum(hit * iota((2 * face, 1), 0).astype(F32), axis=0, keepdims=True)
    shared = jnp.sum(hit, axis=0, keepdims=True)
    rest = jnp.broadcast_to(1.0 - shared, (8, count))
    lane = iota((8, count), 1)
    run = rest
    step = 1
    while step < count:
        run = run + jnp.where(lane >= step, pltpu.roll(run, step, 1), 0.0)
        step *= 2
    place = jnp.where(rest > 0.5, run - 1.0 + 2.0 * face, jnp.broadcast_to(at, (8, count)))
    place_out[...] = place
    column = jnp.transpose(place)[:, 0:1]
    unit = jnp.where(iota((1, count), 1).astype(F32) == column, 1.0, 0.0).astype(BF16)
    modes = vel.shape[0]
    value = jnp.concatenate([vel[...], jnp.broadcast_to(mass[...], (16, count))], axis=0)
    high = value.astype(BF16)
    middle, low = split(value - high.astype(F32))
    total = modes + 16
    parts = dot(jnp.concatenate([high, middle, low], axis=0), unit)
    moved = parts[:total] + parts[total : 2 * total] + parts[2 * total :]
    mass_out[...] = moved[modes : modes + 8]
    quarter = count // chunks.shape[0]
    for part in range(chunks.shape[0]):
        chunks[part] = moved[:modes, part * quarter : (part + 1) * quarter]


def pack_kernel(l2g_in, live_in, chunks, place, mass, keep, send, l2g, live, sems):
    q, _, x = position()
    copies = [pltpu.make_async_copy(a, b, sems.at[i]) for i, (a, b) in enumerate(((l2g_in, l2g), (live_in, live)))]
    for copy in copies:
        copy.start()
    for copy in copies:
        copy.wait()
    count = place.shape[1]
    column = jnp.transpose(place[...])[:, 0:1]
    elems, side = l2g.shape
    slots = elems * ROW
    blank = jnp.full((1, ROW - side), -1, jnp.int32)
    row = jnp.concatenate([piece for e in range(elems) for piece in (l2g[e : e + 1, :], blank)], axis=1)
    pieces = []
    for first in range(0, slots, 512):
        part = row[:, first : first + 512]
        found = jnp.where(iota((count, 1), 0) == part, column, 0.0)
        pieces.append(jnp.where(part < 0, -1.0, jnp.sum(found, axis=0, keepdims=True)))
    index = jnp.concatenate(pieces, axis=1)
    moved = jnp.concatenate([chunks[part] for part in range(chunks.shape[0])], axis=1)
    half = moved.shape[0] // 2
    a, b = moved[:half], moved[half:]
    lived = jnp.where(iota(live.shape, 1) == q, live[...], 0).astype(F32)
    lived = jnp.sum(lived, axis=1, keepdims=True)
    for ref, rows in ((keep, picked(x == 0, a, b)), (send, picked(x == 0, b, a))):
        ref[0:half, :] = rows
        ref[half : half + 8, :] = mass[...]
        ref[half + 8 : half + 16, :] = jnp.broadcast_to(index[:, :count], (8, count))
        ref[half + 16 : half + 24, 0 : slots - count] = jnp.broadcast_to(
            index[:, count:], (8, slots - count)
        )
        ref[half + 16 : half + 24, slots - count :] = jnp.broadcast_to(lived, (8, 2 * count - slots))


def own_build_kernel(
    half, ops_in, pack, high_out, low_out, diag_out, note_out, ops, diag, note, high, low, *scratch
):
    sems = scratch[-1]
    fetch = pltpu.make_async_copy(ops_in, ops, sems.at[0])
    fetch.start()
    copies = []

    def ship(*rows):
        for part, out in ((high, high_out), (low, low_out)):
            at = pl.ds(*rows)
            copies.append(pltpu.make_async_copy(part.at[at], out.at[at], sems.at[len(copies) + 1]))
            copies[-1].start()

    build_kernel(half, ops, pack, high, low, diag, note, *scratch[:-1], ready=fetch.wait, ship=ship)
    for part, out in ((diag, diag_out), (note, note_out)):
        copies.append(pltpu.make_async_copy(part, out, sems.at[len(copies) + 1]))
        copies[-1].start()
    for copy in copies:
        copy.wait()


def partner_build_kernel(half, ops, pack, high_in, low_in, high_own, low_own, high, low, diag, note, *scratch):
    sems = scratch[-1]
    pairs = ((high_in, high_own), (low_in, low_own))
    copies = [pltpu.make_async_copy(a, b, sems.at[i]) for i, (a, b) in enumerate(pairs)]
    for copy in copies:
        copy.start()
    build_kernel(half, ops, pack, high, low, diag, note, *scratch[:-1])
    for copy in copies:
        copy.wait()


def packed(block):
    h = block.shape[0] // 2
    row, lane = iota((h, 2 * h), 0), iota((h, 2 * h), 1)
    return jnp.where((lane < h) & (row > lane), pltpu.roll(block[h:], h, 1), block[:h])


def unpacked(rows):
    h = rows.shape[0]
    row, lane = iota((h, 2 * h), 0), iota((h, 2 * h), 1)
    turned = jnp.transpose(jnp.concatenate([rows, jnp.zeros_like(rows)], axis=0))
    top = jnp.where((lane < h) & (row > lane), turned[:h], rows)
    last = jnp.where(row > lane, rows, turned[:h])
    return jnp.concatenate([top, jnp.where(lane < h, turned[h:], pltpu.roll(last, h, 1))], axis=0)


def build_kernel(half, ops, pack, high, low, diag, note, flat, qh, ql, pad, ready=None, ship=None):
    live = pack[half + 16 : half + 17, pack.shape[1] - 1 :]
    side, elems = ops.shape[0], ops.shape[1]
    count = high.shape[0]
    slots = elems * ROW
    index = jnp.concatenate(
        [pack[half + 8 : half + 16, :], pack[half + 16 : half + 24, 0 : slots - count]], axis=1
    )
    column = jnp.transpose(index)[:, 0:1]
    pad[...] = jnp.zeros(pad.shape, F32)
    lane = iota((1, count), 1).astype(F32)
    share = count // elems

    def table_rows(e):
        rows = jnp.where((iota((share, 1), 0) + e * share).astype(F32) == index[0:1], 1.0, 0.0)
        flat[e * share : (e + 1) * share, :] = rows.astype(BF16)

    ahead = 0
    if ready is not None:
        ahead = elems // 3
        for e in range(ahead):
            table_rows(e)
        ready()
    for e in range(elems):
        at = slice(e * ROW, (e + 1) * ROW)
        nodes = jnp.where(lane == column[at], 1.0, 0.0).astype(BF16)
        pad[0:side, 0:side] = ops[:, e, :] * jnp.where(live > e + 0.5, 1.0, 0.0)
        spread = dot(jnp.concatenate(split(pad[:, 0:ROW]), axis=0), nodes)
        qh[at, :] = spread[:ROW].astype(BF16)
        ql[at, :] = spread[ROW:].astype(BF16)
        if e >= ahead:
            table_rows(e)
    tile = 256
    face = note.shape[1]
    diag[...] = jnp.zeros(diag.shape, F32)
    for j in range(0, count, tile):
        top = j + tile
        block = dot(flat[j:top, :], qh[:, j:]) + dot(flat[j:top, :], ql[:, j:])
        own_node = iota((tile, 1), 0) == iota((1, tile), 1)
        line = jnp.sum(jnp.where(own_node, block[:, :tile], 0.0), axis=0, keepdims=True)
        kept = jnp.where(own_node, 0.0, block[:, :tile])
        block = jnp.concatenate([kept, block[:, tile:]], axis=1) if top < count else kept
        h, l = split(block)
        diag[0:1, j:top] = line
        diag[1:2, j:] += jnp.sum(l.astype(F32), axis=0, keepdims=True)
        high[j:top, j:] = h
        low[j:top, j:] = l
        if ship is not None:
            ship(j, tile)
        if top < count:
            mirror = jnp.transpose(block[:, tile:])
            h, l = split(mirror)
            high[top:, j:top] = h
            low[top:, j:top] = l
            diag[1:2, j:top] += jnp.sum(l.astype(F32), axis=0, keepdims=True)
        if not j:
            note[0 : face // 2, :] = packed(block[0:face, 0:face])
            first = iota((8, 1), 0) == 0
            note[face // 2 :, :] = jnp.where(first, line[:, 0:face], pack[half : half + 8, 0:face])


def apply(value, mats, half, face):
    oh, ol, ph, plo = mats[:4]
    return jnp.concatenate(
        [
            rows_times(value[:half], oh[:, face:], ol[:, face:]),
            rows_times(value[half:], ph[:, face:], plo[:, face:]),
        ],
        axis=0,
    )


def high_apply(value, mats, half):
    parts = []
    for v, high in ((value[:half], mats[0]), (value[half:], mats[2])):
        both = dot(jnp.concatenate(split(v), axis=0), high[...])
        parts.append(both[:half] + both[half:])
    return jnp.concatenate(parts, axis=0)


def low_apply(value, mats, half):
    v = value.astype(BF16)
    return jnp.concatenate([dot(v[:half], mats[1][...]), dot(v[half:], mats[3][...])], axis=0)


def outer_apply(value, mats, half, face):
    parts = []
    for v, columns in ((value[:half], mats[4]), (value[half:], mats[5])):
        both = dot(jnp.concatenate(split(v), axis=0), columns[...])
        parts.append(both[:half, :face] + both[half:, :face] + both[:half, face:])
    return jnp.concatenate(parts, axis=0)


def face_times(value, rows):
    count = value.shape[0]
    h, l = split(value)
    first, second = jnp.concatenate([h, h], axis=1), jnp.concatenate([l, jnp.zeros_like(l)], axis=1)
    both = dot(jnp.concatenate([first, second], axis=0), rows)
    return both[:count] + both[count:]


def assembled(y, outer, half, face):
    inner = y[:half, face : 2 * face] + y[half:, face : 2 * face]
    first = y[:, :face] if outer is None else y[:, :face] + outer
    return jnp.concatenate([first, jnp.concatenate([inner, inner], axis=0), y[:, 2 * face :]], axis=1)


def first_planes_kernel(u, tables_in, slope_in, out, tables, slope, sems):
    pairs = ((slope_in, slope), (tables_in, tables))
    copies = [pltpu.make_async_copy(a, b, sems.at[i]) for i, (a, b) in enumerate(pairs)]
    for copy in copies:
        copy.start()
    for copy in copies:
        copy.wait()
    planes_kernel(u, tables, slope, out)


def planes_kernel(u, tables, slope, out):
    count = slope.shape[1]
    high, low = tables[0:count, :], tables[count:, :]
    value = u[...]
    mode = iota((count, 1), 0)
    scale = lax.shift_right_arithmetic(mode, 1).astype(F32) * (2.0 / count)
    after, before = pltpu.roll(value, count - 1, 0), pltpu.roll(value, 1, 0)
    paired = jnp.where((mode & 1) == 0, scale * after, -scale * before)
    nodes = value.shape[1]
    both = table_times(high, low, jnp.concatenate([value, paired], axis=1))
    rate = jnp.transpose(jnp.broadcast_to(slope[...], (8, count)))[:, 0:1]
    cross = rate * both[:, :nodes] * both[:, nodes:]
    weight = jnp.where(mode < 2, 1.0 / count, 2.0 / count)
    out[...] = weight * table_times(high, low, cross, 0)


def provisional(r, d, g, inv, cm, mats, alpha, beta, half, face):
    r = r - inv * assembled(g, None, half, face)
    d = alpha * d + beta * r if alpha else beta * r
    y = outer_apply(d, mats, half, face) + cm[:, :face] * d[:, :face]
    return r, d, y


def even():
    _, z, x = position()
    return lax.rem(x + z, 2) == 0


def put(one, two, g, y, half, face, notes=((), ())):
    own = jnp.concatenate([g[:half, :face], y[:half], *notes[0]], axis=0)
    oth = jnp.concatenate([g[half:, :face], y[half:], *notes[1]], axis=0)
    first = even()
    one[...] = picked(first, own, oth)
    two[...] = picked(first, oth, own)


def got(one, two):
    a, b = one[...], two[...]
    first = even()
    return picked(first, a, b), picked(first, b, a)


def received(conv, half):
    _, _, x = position()
    parts = conv.shape[0]
    return jnp.concatenate(
        [
            jnp.concatenate([conv[m, x] for m in range(parts)], axis=1),
            jnp.concatenate([conv[m, 1 - x] for m in range(parts)], axis=1),
        ],
        axis=0,
    )


def masses(own, oth, half):
    count = own.shape[1]
    return jnp.concatenate(
        [jnp.broadcast_to(m[half : half + 1, :], (half, count)) for m in (own, oth)], axis=0
    )


def helmholtz(half, mode_count):
    _, _, x = position()
    mode = lax.axis_index("mode") * (2 * half) + x * half + iota((half, 1), 0)
    number = jnp.where(mode == 1, mode_count // 2, lax.shift_right_arithmetic(mode, 1))
    return mass_weight + (8.0 * number.astype(F32) / mode_count) ** 2


def first_source_kernel(
    half, face, mode_count, conv, own, oth, do, dp, note_o, note_p, oh, ol, ph, plo,
    wo, wp, vo, vp, r_out, d_out, v_out, conv_out, inv_out, cm_out, sums_out, one, two,
):
    for wide, tall, high, low in ((wo, vo, oh, ol), (wp, vp, ph, plo)):
        wide[:, 0:face] = high[:, 0:face]
        wide[:, face:] = low[:, 0:face]
        tall[0:face, :] = high[0:face, :]
        tall[face:, :] = low[0:face, :]
    mats = (oh, ol, ph, plo, wo, wp, vo, vp)
    c = helmholtz(half, mode_count)
    c = jnp.concatenate([c, c], axis=0)
    mass = masses(own, oth, half)
    stiff, sums = (
        jnp.concatenate([jnp.broadcast_to(t[row : row + 1, :], (half, t.shape[1])) for t in (do, dp)], axis=0)
        for row in (0, 1)
    )
    inv = 1.0 / (assembled(stiff, None, half, face) + c * assembled(mass, None, half, face))
    inv = jnp.concatenate([jnp.zeros((2 * half, face), F32), inv[:, face:]], axis=1)
    inv_out[...] = inv
    cm = c * mass + stiff
    cm_out[...] = cm
    sums_out[...] = sums
    v = jnp.concatenate([own[0:half, :], oth[0:half, :]], axis=0)
    v_out[...] = v
    new = received(conv, half)
    conv_out[...] = new
    m4 = mass_weight * mass
    g = high_apply(v, mats, half) + (cm + sums - m4) * v - m4 * new
    r = -inv * assembled(g, None, half, face)
    d = (1.0 / centre) * r
    r_out[...] = r
    d_out[...] = d
    y = outer_apply(d, mats, half, face)
    put(one, two, g, y, half, face, ((note_o[...],), (note_p[...],)))


def source_kernel(
    half, face, conv, old, own, oth, r, d, inv, cm, sums, late, oh, ol, ph, plo, wo, wp, vo, vp,
    r_out, d_out, conv_out, one, two,
):
    mats = (oh, ol, ph, plo, wo, wp, vo, vp)
    new = received(conv, half)
    conv_out[...] = new
    cmv, dv = cm[...], d[...]
    g = high_apply(dv, mats, half) + (cmv + sums[...]) * dv - mass_weight * masses(own, oth, half) * (new - old[...])
    g = widened(g, late[...])
    rv, dv, y = provisional(r[...], None, g, inv[...], cmv, mats, 0.0, 1.0 / centre, half, face)
    r_out[...] = rv
    d_out[...] = dv
    put(one, two, g, y, half, face)


def rest_kernel(
    half, face, now, r, d, sol, source, s1, s2, inv, cm, sums, oh, ol, ph, plo, wo, wp, vo, vp,
    r_out, d_out, sol_out, late_out,
):
    mats = (oh, ol, ph, plo, wo, wp, vo, vp)
    dv, sv = d[...], source[...]
    late = low_apply(sv, mats, half) - sums[...] * sv
    late_out[...] = late[:, :face]
    y = apply(dv, mats, half, face) + cm[:, face:] * dv[:, face:] + late[:, face:]
    y = jnp.concatenate([stacked(got(s1, s2), half, 2 * half), y], axis=1)
    rv = r[...] - inv[...] * assembled(y, None, half, face)
    dn = now[0] * dv + now[1] * rv
    r_out[...] = rv
    d_out[...] = dn
    sol_out[...] = sol[...] + dv + dn


def change_of(dd, theirs, mats, na, nb, half):
    change = [face_times(dd[:half], mats[6][...]), face_times(dd[half:], mats[7][...])]
    their_change = [face_times(theirs[:half], nb), face_times(theirs[half:], na)]
    return jnp.concatenate(change, axis=0), jnp.concatenate(their_change, axis=0)


def stacked(pair, first, last):
    return jnp.concatenate([t[first:last, :] for t in pair], axis=0)


def widened(value, face_part):
    face = face_part.shape[1]
    return jnp.concatenate([value[:, :face] + face_part, value[:, face:]], axis=1)


def corrected(half, face, now, r, d, sol, dr, dd, change, outer, inv):
    back = widened(-inv * assembled(change, outer, half, face), dr)
    step = widened(now[1] * back, now[0] * dd)
    return r + back, d + step, widened(sol + step, dd)


def exact(half, face, beta, now, r, d, sol, sent, came, na, nb, inv, cm, cmn, mats):
    inv_face = inv[:, :face]
    mine, came = got(*sent), got(*came)
    dr = -(inv_face * stacked(came, 0, half))
    dd = beta * dr
    theirs = -beta * (inv_face * stacked(mine, 0, half))
    change, their_change = change_of(dd, theirs, mats, na[...], nb[...], half)
    change = widened(change, cm[:, :face] * dd)
    outer = stacked(came, half, 2 * half) + their_change + cmn[...] * theirs
    return corrected(half, face, now, r[...], d[...], sol[...], dr, dd, change, outer, inv[...])


def first_sweep_kernel(
    half, face, mode_count, before, now, then,
    r, d, sol, late, s1, s2, c1, c2, inv, cm, sums, oh, ol, ph, plo, wo, wp, vo, vp,
    r_out, d_out, sol_out, source_out, inv_out, cmn_out, na_out, nb_out, one, two,
):
    mats = (oh, ol, ph, plo, wo, wp, vo, vp)
    cm_v = cm[...]
    mine, came = got(s1, s2), got(c1, c2)
    c = helmholtz(half, mode_count)
    c = jnp.concatenate([c, c], axis=0)

    def line(pair, row):
        return jnp.concatenate([jnp.broadcast_to(t[row : row + 1, :], (half, face)) for t in pair], axis=0)

    at = 2 * half + face // 2
    their_mass = line(came, at + 1)
    inv_face = 1.0 / (line(mine, at) + line(came, at) + c * (line(mine, at + 1) + their_mass))
    cmn = c * their_mass + line(came, at)
    nb, na = (jnp.concatenate(split(unpacked(t[2 * half : at, :])), axis=0) for t in came)
    dr = -inv_face * (stacked(mine, 0, half) + stacked(came, 0, half))
    dd = before[1] * dr
    change, their_change = change_of(dd, dd, mats, na, nb, half)
    change = widened(change, cm_v[:, :face] * dd)
    outer = stacked(mine, half, 2 * half) + stacked(came, half, 2 * half) + their_change + cmn * dd
    inv_v = jnp.concatenate([inv_face, inv[:, face:]], axis=1)
    rv, dn, sol_v = corrected(half, face, now, r[...], d[...], sol[...], dr, dd, change, outer, inv_v)
    inv_out[...] = inv_v
    cmn_out[...] = cmn
    na_out[...] = na
    nb_out[...] = nb
    sol_out[...] = sol_v
    source_out[...] = dn
    g = widened(high_apply(dn, mats, half) + (cm_v + sums[...]) * dn, late[...])
    rv, dv, y = provisional(rv, dn, g, inv_v, cm_v, mats, then[0], then[1], half, face)
    r_out[...] = rv
    d_out[...] = dv
    put(one, two, g, y, half, face)


def sweep_kernel(
    half, face, before, now, then,
    r, d, sol, late, s1, s2, c1, c2, na, nb, inv, cm, sums, cmn, oh, ol, ph, plo, wo, wp, vo, vp,
    r_out, d_out, sol_out, source_out, one, two,
):
    mats = (oh, ol, ph, plo, wo, wp, vo, vp)
    rv, dn, sol_v = exact(half, face, before[1], now, r, d, sol, (s1, s2), (c1, c2), na, nb, inv, cm, cmn, mats)
    sol_out[...] = sol_v
    source_out[...] = dn
    inv_v, cm_v = inv[...], cm[...]
    g = widened(high_apply(dn, mats, half) + (cm_v + sums[...]) * dn, late[...])
    rv, dv, y = provisional(rv, dn, g, inv_v, cm_v, mats, then[0], then[1], half, face)
    r_out[...] = rv
    d_out[...] = dv
    put(one, two, g, y, half, face)


def last_kernel(
    half, face, before, now,
    r, d, sol, s1, s2, c1, c2, na, nb, inv, cm, cmn, oh, ol, ph, plo, wo, wp, vo, vp,
    r_out, d_out, sol_out, chunks,
):
    rv, dn, new = exact(
        half, face, before[1], now, r, d, sol, (s1, s2), (c1, c2), na, nb, inv, cm, cmn, (oh, ol, ph, plo, wo, wp, vo, vp)
    )
    r_out[...] = rv
    d_out[...] = dn
    sol_out[...] = new
    _, _, x = position()
    parts, width = chunks.shape[0], chunks.shape[3]
    for m in range(parts):
        chunks[m, x] = new[:half, m * width : (m + 1) * width]
        chunks[m, 1 - x] = new[half:, m * width : (m + 1) * width]


def end_kernel(
    half, face, before, now,
    r, d, sol, s1, s2, c1, c2, na, nb, inv, cm, cmn, oh, ol, ph, plo, wo, wp, vo, vp, own_out, oth_out,
):
    _, _, new = exact(
        half, face, before[1], now, r, d, sol, (s1, s2), (c1, c2), na, nb, inv, cm, cmn, (oh, ol, ph, plo, wo, wp, vo, vp)
    )
    own_out[...] = new[:half]
    oth_out[...] = new[half:]


def restored(value, unit):
    count = value.shape[0]
    high = value.astype(BF16)
    middle, low = split(value - high.astype(F32))
    parts = dot(jnp.concatenate([high, middle, low], axis=0), unit)
    return parts[:count] + parts[count : 2 * count] + parts[2 * count :]


def finish_own_kernel(own, place, out, unit_out):
    count = own.shape[1]
    unit = jnp.where(iota((count, 1), 0).astype(F32) == place[0:1, :], 1.0, 0.0).astype(BF16)
    unit_out[...] = unit
    out[...] = restored(own[...], unit)


def finish_kernel(own, other, unit, out):
    _, _, x = position()
    a, b = own[...], restored(other[...], unit[...])
    half = own.shape[0]
    out[0:half, :] = picked(x == 0, a, b)
    out[half:, :] = picked(x == 0, b, a)


def body(n_mode, n_dom, velocity_prev, elem_ops, lumped_mass, span_slope, local_to_global, iface_nodes, live_elems):
    modes, count = velocity_prev.shape
    half = modes // 2
    elems, side = local_to_global.shape
    face = iface_nodes.shape[2]
    mode_count = span_slope.shape[0]
    quarter = count // n_mode
    pairs = n_dom // 2
    slots = elems * ROW
    places = [(z, s) for z in range(pairs) for s in (0, 1)]
    swap = [(i, i ^ 1) for i in range(n_dom)]
    long_swap = [(2 * z + s, 2 * ((z + (1 if z % 2 else -1)) % pairs) + s) for z, s in places]
    short_swap = [(2 * z + s, 2 * ((z + (-1 if z % 2 else 1)) % pairs) + s) for z, s in places]
    groups = [[m * n_dom + 2 * z + s for m in range(n_mode) for s in (0, 1)] for z in range(pairs)]

    def exchange(one, two):
        return lax.ppermute(one, "dom", long_swap), lax.ppermute(two, "dom", short_swap)

    ops = jnp.transpose(elem_ops, (1, 0, 2))
    ops_other = lax.ppermute(ops, "dom", swap)
    pack = (half + 24, count)
    wide = (2 * half, count)
    chunks, place, weights = call(
        order_kernel, [((n_mode, modes, quarter), F32), ((8, count), F32), ((8, count), F32)],
        [iface_nodes[0], velocity_prev, lumped_mass.reshape(1, count)], 24, far=range(3),
        scratch=[
            pltpu.VMEM((2, face), jnp.int32), pltpu.VMEM((modes, count), F32), pltpu.VMEM((1, count), F32),
            pltpu.SemaphoreType.DMA((3,)),
        ],
    )
    planes_in = lax.all_to_all(chunks, "mode", 0, 0, tiled=True)
    keep, send = call(
        pack_kernel, [(pack, F32), (pack, F32)],
        [local_to_global, live_elems.reshape(1, n_dom), chunks, place, weights], 24, far=(0, 1),
        scratch=[
            pltpu.VMEM((elems, side), jnp.int32), pltpu.VMEM((1, n_dom), jnp.int32), pltpu.SemaphoreType.DMA((2,)),
        ],
    )
    oth = lax.ppermute(send, "dom", swap)

    tables = jnp.asarray(np.concatenate(halves(synthesis_table(mode_count))))
    slope = span_slope.reshape(1, mode_count)

    matrix = ((count, count), BF16)
    small = [((8, count), F32), ((face // 2 + 8, face), F32)]
    one_hot = [
        pltpu.VMEM((count, slots), BF16),
        pltpu.VMEM((slots, count), BF16),
        pltpu.VMEM((slots, count), BF16),
        pltpu.VMEM((ROW, 128), F32),
    ]

    def planes(value, first):
        (out,) = call(
            first_planes_kernel if first else planes_kernel, [((mode_count, quarter), F32)],
            [value.reshape(mode_count, quarter), tables, slope], 16, flops=600 << 20,
            far=(1, 2) if first else (), free=(tables.shape,),
            scratch=[
                pltpu.VMEM(tables.shape, BF16), pltpu.VMEM(slope.shape, F32), pltpu.SemaphoreType.DMA((2,)),
            ] if first else (),
        )
        return out

    def to_solve(value):
        back = lax.all_to_all(
            value.reshape(2 * n_mode, half, quarter), ("mode", "dom"), 0, 0, axis_index_groups=groups, tiled=True
        )
        return back.reshape(n_mode, 2, half, quarter)

    cross, keep_late = lax.optimization_barrier((planes(planes_in, True), keep))
    keep_late, ops_other = lax.optimization_barrier((keep_late, ops_other))
    conv = to_solve(cross)
    oh, ol, do, note_o = call(
        functools.partial(own_build_kernel, half), [matrix, matrix, *small], [ops, keep_late], 36,
        far=(0,), out_far=range(4), flops=6 << 30,
        scratch=[
            pltpu.VMEM((side, elems, side), F32), *[pltpu.VMEM(*v) for v in small],
            pltpu.VMEM((count, count), BF16), pltpu.VMEM((count, count), BF16),
            *one_hot, pltpu.SemaphoreType.DMA((2 * count // 256 + 3,)),
        ],
    )
    conv, oth_late = lax.optimization_barrier((conv, oth))
    oh, ol, ph, plo, dp, note_p = call(
        functools.partial(partner_build_kernel, half), [matrix] * 4 + small, [ops_other, oth_late, oh, ol], 24,
        far=(2, 3), pinned=range(4), flops=6 << 30, scratch=[*one_hot, pltpu.SemaphoreType.DMA((2,))],
    )
    mats = [oh, ol, ph, plo]
    coefs = chebyshev()
    message = ((2 * half, face), F32)
    for iteration in range(ITERS):
        if iteration == 0:
            long_message = ((2 * half + face // 2 + 8, face), F32)
            beside = [((count, 2 * face), BF16)] * 2 + [((2 * face, count), BF16)] * 2
            *cats, r, d, sol, old, inv, cm, sums, one, two = call(
                functools.partial(first_source_kernel, half, face, mode_count),
                [*beside, *[(wide, F32)] * 7, long_message, long_message],
                [conv, keep, oth, do, dp, note_o, note_p, *mats], 20, flops=500 << 20, pinned=range(4),
            )
            mats = [*mats, *cats]
            source = sol
        else:
            source = d
            r, d, old, one, two = call(
                functools.partial(source_kernel, half, face),
                [(wide, F32), (wide, F32), (wide, F32), message, message],
                [conv, old, keep, oth, r, d, inv, cm, sums, late, *mats], 20, flops=500 << 20,
            )
        for k in (0, 2, 4):
            c1, c2 = exchange(one, two)
            r, d, sol, late = call(
                functools.partial(rest_kernel, half, face, coefs[k + 1]), [(wide, F32)] * 3 + [((2 * half, face), F32)],
                [r, d, sol, source, one, two, inv, cm, sums, *mats], 20, flops=400 << 20,
            )
            if iteration == 0 and k == 0:
                r, d, sol, source, inv, cmn, na, nb, one, two = call(
                    functools.partial(first_sweep_kernel, half, face, mode_count, coefs[0], coefs[1], coefs[2]),
                    [(wide, F32)] * 5 + [((2 * half, face), F32)] + [((2 * face, face), BF16)] * 2 + [message, message],
                    [r, d, sol, late, one, two, c1, c2, inv, cm, sums, *mats], 20, flops=500 << 20,
                )
                continue
            given = [r, d, sol, one, two, c1, c2, na, nb, inv, cm, cmn, *mats]
            if k < 4:
                r, d, sol, source, one, two = call(
                    functools.partial(sweep_kernel, half, face, coefs[k], coefs[k + 1], coefs[k + 2]),
                    [*[(wide, F32)] * 4, message, message],
                    [r, d, sol, late, one, two, c1, c2, na, nb, inv, cm, sums, cmn, *mats], 20, flops=500 << 20,
                )
            elif iteration < ITERS - 1:
                r, d, sol, chunks = call(
                    functools.partial(last_kernel, half, face, coefs[k], coefs[k + 1]),
                    [(wide, F32), (wide, F32), (wide, F32), ((n_mode, 2, half, quarter), F32)],
                    given, 20, flops=100 << 20,
                )
            else:
                own, other = call(
                    functools.partial(end_kernel, half, face, coefs[k], coefs[k + 1]),
                    [((half, count), F32)] * 2, given, 20, flops=100 << 20,
                )
        if iteration < ITERS - 1:
            planes_in = lax.all_to_all(
                chunks.reshape(2 * n_mode, half, quarter), ("mode", "dom"), 0, 0, axis_index_groups=groups, tiled=True
            )
            conv = to_solve(planes(planes_in, False))
    other = lax.ppermute(other, "dom", swap)
    own, unit = call(
        finish_own_kernel, [((half, count), F32), ((count, count), BF16)], [own, place], 16, flops=200 << 20
    )
    (out,) = call(finish_kernel, [((modes, count), F32)], [own, other, unit], 16)
    return out


def solution(mesh):
    placed = (
        P("mode", "dom"),
        P("dom", None, None),
        P("dom"),
        P(),
        P("dom", None),
        P("dom", None, None),
        P(),
    )
    return jax.shard_map(
        functools.partial(body, mesh.shape["mode"], mesh.shape["dom"]),
        mesh=mesh, in_specs=placed, out_specs=P("mode", "dom"), check_vma=False,
    )
```

```python
import functools

import jax
import jax.numpy as jnp
import numpy as np
from jax import lax
from jax.experimental import pallas as pl
from jax.experimental.pallas import tpu as pltpu
from jax.sharding import PartitionSpec as P

ITERS = 3
SWEEPS = 6

mass_weight = 4.0
bound_low = 0.1
bound_high = 2.0
centre = (bound_high + bound_low) / 2.0
half_width = (bound_high - bound_low) / 2.0

F32 = jnp.float32
BF16 = jnp.bfloat16
ROW = 96


def chebyshev():
    ratio = centre / half_width
    rho = 1.0 / ratio
    coefs = [(0.0, 1.0 / centre)]
    for _ in range(SWEEPS - 1):
        rho_next = 1.0 / (2.0 * ratio - rho)
        coefs.append((rho_next * rho, 2.0 * rho_next / half_width))
        rho = rho_next
    return coefs


def synthesis_table(mode_count):
    column = np.arange(mode_count)
    number = np.where(column == 1, mode_count // 2, column // 2)
    is_sine = (column % 2 == 1) & (column > 1)
    planes = np.arange(mode_count)
    angles = (planes[:, None] * number[None, :] % mode_count) * (2.0 * np.pi / mode_count)
    return np.where(is_sine[None, :], np.sin(angles), np.cos(angles))


def halves(table):
    high = table.astype(np.float32).astype(BF16)
    return [high, (table - high.astype(np.float64)).astype(np.float32).astype(BF16)]


def split(value):
    high = value.astype(BF16)
    return high, (value - high.astype(F32)).astype(BF16)


def dot(a, b):
    return lax.dot_general(a, b, (((1,), (0,)), ((), ())), preferred_element_type=F32)


def rows_times(value, high, low):
    count = value.shape[0]
    h, l = split(value)
    both = dot(jnp.concatenate([h, l], axis=0), high)
    return both[:count] + both[count:] + dot(h, low)


def table_times(high, low, value, dim=1):
    dims = (((dim,), (0,)), ((), ()))
    count = value.shape[1]
    h, l = split(value)
    both = lax.dot_general(high, jnp.concatenate([h, l], axis=1), dims, preferred_element_type=F32)
    return both[:, :count] + both[:, count:] + lax.dot_general(low, h, dims, preferred_element_type=F32)


def iota(shape, dim):
    return lax.broadcasted_iota(jnp.int32, shape, dim)


def call(kernel, outs, vmem, limit, scratch=(), flops=0, moved=1 << 20, far=(), out_far=(), pinned=(), free=()):
    in_specs, given = [], []
    for i, v in enumerate(vmem):
        space = pltpu.HBM if i in far else pltpu.VMEM
        in_specs.append(pl.BlockSpec(memory_space=space))
        fixed = i in far or v.dtype == BF16 and v.shape not in free
        given.append(pltpu.with_memory_space_constraint(v, space) if fixed else v)
    shapes, out_specs = [], []
    for i, (s, t) in enumerate(outs):
        space = pltpu.HBM if i in out_far else pltpu.VMEM
        out_specs.append(pl.BlockSpec(memory_space=space))
        shapes.append(space(s, t) if i in out_far or i in pinned else jax.ShapeDtypeStruct(s, t))
    return pl.pallas_call(
        kernel,
        out_shape=shapes,
        in_specs=in_specs,
        out_specs=out_specs,
        scratch_shapes=list(scratch),
        compiler_params=pltpu.CompilerParams(vmem_limit_bytes=limit << 20),
        cost_estimate=pl.CostEstimate(flops=flops, bytes_accessed=moved, transcendentals=0),
    )(*given)


def position():
    q = lax.axis_index("dom")
    z = lax.shift_right_arithmetic(q, 1)
    return q, z, q - 2 * z


def picked(first, a, b):
    return jnp.where(first, a, b)


def order_kernel(iface_in, vel_in, mass_in, chunks, place_out, mass_out, iface, vel, mass, sems):
    _, _, x = position()
    pairs = ((iface_in, iface), (vel_in, vel), (mass_in, mass))
    copies = [pltpu.make_async_copy(a, b, sems.at[i]) for i, (a, b) in enumerate(pairs)]
    for copy in copies:
        copy.start()
    for copy in copies:
        copy.wait()
    count = mass.shape[1]
    face = iface.shape[1]
    lists = jnp.concatenate(
        [picked(x == 0, iface[0:1, :], iface[1:2, :]), picked(x == 0, iface[1:2, :], iface[0:1, :])], axis=1
    ).astype(F32)
    lists = jnp.transpose(jnp.broadcast_to(lists, (8, 2 * face)))[:, 0:1]
    hit = jnp.where(lists == iota((1, count), 1).astype(F32), 1.0, 0.0)
    at = jnp.sum(hit * iota((2 * face, 1), 0).astype(F32), axis=0, keepdims=True)
    shared = jnp.sum(hit, axis=0, keepdims=True)
    rest = jnp.broadcast_to(1.0 - shared, (8, count))
    lane = iota((8, count), 1)
    run = rest
    step = 1
    while step < count:
        run = run + jnp.where(lane >= step, pltpu.roll(run, step, 1), 0.0)
        step *= 2
    place = jnp.where(rest > 0.5, run - 1.0 + 2.0 * face, jnp.broadcast_to(at, (8, count)))
    place_out[...] = place
    column = jnp.transpose(place)[:, 0:1]
    unit = jnp.where(iota((1, count), 1).astype(F32) == column, 1.0, 0.0).astype(BF16)
    modes = vel.shape[0]
    value = jnp.concatenate([vel[...], jnp.broadcast_to(mass[...], (16, count))], axis=0)
    high = value.astype(BF16)
    middle, low = split(value - high.astype(F32))
    total = modes + 16
    parts = dot(jnp.concatenate([high, middle, low], axis=0), unit)
    moved = parts[:total] + parts[total : 2 * total] + parts[2 * total :]
    mass_out[...] = moved[modes : modes + 8]
    quarter = count // chunks.shape[0]
    for part in range(chunks.shape[0]):
        chunks[part] = moved[:modes, part * quarter : (part + 1) * quarter]


def pack_kernel(l2g_in, live_in, chunks, place, mass, keep, send, l2g, live, sems):
    q, _, x = position()
    copies = [pltpu.make_async_copy(a, b, sems.at[i]) for i, (a, b) in enumerate(((l2g_in, l2g), (live_in, live)))]
    for copy in copies:
        copy.start()
    for copy in copies:
        copy.wait()
    count = place.shape[1]
    column = jnp.transpose(place[...])[:, 0:1]
    elems, side = l2g.shape
    slots = elems * ROW
    blank = jnp.full((1, ROW - side), -1, jnp.int32)
    row = jnp.concatenate([piece for e in range(elems) for piece in (l2g[e : e + 1, :], blank)], axis=1)
    pieces = []
    for first in range(0, slots, 512):
        part = row[:, first : first + 512]
        found = jnp.where(iota((count, 1), 0) == part, column, 0.0)
        pieces.append(jnp.where(part < 0, -1.0, jnp.sum(found, axis=0, keepdims=True)))
    index = jnp.concatenate(pieces, axis=1)
    moved = jnp.concatenate([chunks[part] for part in range(chunks.shape[0])], axis=1)
    half = moved.shape[0] // 2
    a, b = moved[:half], moved[half:]
    lived = jnp.where(iota(live.shape, 1) == q, live[...], 0).astype(F32)
    lived = jnp.sum(lived, axis=1, keepdims=True)
    for ref, rows in ((keep, picked(x == 0, a, b)), (send, picked(x == 0, b, a))):
        ref[0:half, :] = rows
        ref[half : half + 8, :] = mass[...]
        ref[half + 8 : half + 16, :] = jnp.broadcast_to(index[:, :count], (8, count))
        ref[half + 16 : half + 24, 0 : slots - count] = jnp.broadcast_to(
            index[:, count:], (8, slots - count)
        )
        ref[half + 16 : half + 24, slots - count :] = jnp.broadcast_to(lived, (8, 2 * count - slots))


def own_build_kernel(
    half, ops_in, pack, high_out, low_out, diag_out, note_out, ops, diag, note, high, low, *scratch
):
    sems = scratch[-1]
    fetch = pltpu.make_async_copy(ops_in, ops, sems.at[0])
    fetch.start()
    copies = []

    def ship(*rows):
        for part, out in ((high, high_out), (low, low_out)):
            at = pl.ds(*rows)
            copies.append(pltpu.make_async_copy(part.at[at], out.at[at], sems.at[len(copies) + 1]))
            copies[-1].start()

    build_kernel(half, ops, pack, high, low, diag, note, *scratch[:-1], ready=fetch.wait, ship=ship)
    for part, out in ((diag, diag_out), (note, note_out)):
        copies.append(pltpu.make_async_copy(part, out, sems.at[len(copies) + 1]))
        copies[-1].start()
    for copy in copies:
        copy.wait()


def partner_build_kernel(half, ops, pack, high_in, low_in, high_own, low_own, high, low, diag, note, *scratch):
    sems = scratch[-1]
    pairs = ((high_in, high_own), (low_in, low_own))
    copies = [pltpu.make_async_copy(a, b, sems.at[i]) for i, (a, b) in enumerate(pairs)]
    for copy in copies:
        copy.start()
    build_kernel(half, ops, pack, high, low, diag, note, *scratch[:-1])
    for copy in copies:
        copy.wait()


def packed(block):
    h = block.shape[0] // 2
    row, lane = iota((h, 2 * h), 0), iota((h, 2 * h), 1)
    return jnp.where((lane < h) & (row > lane), pltpu.roll(block[h:], h, 1), block[:h])


def unpacked(rows):
    h = rows.shape[0]
    row, lane = iota((h, 2 * h), 0), iota((h, 2 * h), 1)
    turned = jnp.transpose(jnp.concatenate([rows, jnp.zeros_like(rows)], axis=0))
    top = jnp.where((lane < h) & (row > lane), turned[:h], rows)
    last = jnp.where(row > lane, rows, turned[:h])
    return jnp.concatenate([top, jnp.where(lane < h, turned[h:], pltpu.roll(last, h, 1))], axis=0)


def build_kernel(half, ops, pack, high, low, diag, note, flat, qh, ql, pad, ready=None, ship=None):
    live = pack[half + 16 : half + 17, pack.shape[1] - 1 :]
    side, elems = ops.shape[0], ops.shape[1]
    count = high.shape[0]
    slots = elems * ROW
    index = jnp.concatenate(
        [pack[half + 8 : half + 16, :], pack[half + 16 : half + 24, 0 : slots - count]], axis=1
    )
    column = jnp.transpose(index)[:, 0:1]
    pad[...] = jnp.zeros(pad.shape, F32)
    lane = iota((1, count), 1).astype(F32)
    share = count // elems

    def table_rows(e):
        rows = jnp.where((iota((share, 1), 0) + e * share).astype(F32) == index[0:1], 1.0, 0.0)
        flat[e * share : (e + 1) * share, :] = rows.astype(BF16)

    ahead = 0
    if ready is not None:
        ahead = elems // 3
        for e in range(ahead):
            table_rows(e)
        ready()
    for e in range(elems):
        at = slice(e * ROW, (e + 1) * ROW)
        nodes = jnp.where(lane == column[at], 1.0, 0.0).astype(BF16)
        pad[0:side, 0:side] = ops[:, e, :] * jnp.where(live > e + 0.5, 1.0, 0.0)
        spread = dot(jnp.concatenate(split(pad[:, 0:ROW]), axis=0), nodes)
        qh[at, :] = spread[:ROW].astype(BF16)
        ql[at, :] = spread[ROW:].astype(BF16)
        if e >= ahead:
            table_rows(e)
    tile = 256
    face = note.shape[1]
    diag[...] = jnp.zeros(diag.shape, F32)
    for j in range(0, count, tile):
        top = j + tile
        block = dot(flat[j:top, :], qh[:, j:]) + dot(flat[j:top, :], ql[:, j:])
        own_node = iota((tile, 1), 0) == iota((1, tile), 1)
        line = jnp.sum(jnp.where(own_node, block[:, :tile], 0.0), axis=0, keepdims=True)
        kept = jnp.where(own_node, 0.0, block[:, :tile])
        block = jnp.concatenate([kept, block[:, tile:]], axis=1) if top < count else kept
        h, l = split(block)
        diag[0:1, j:top] = line
        diag[1:2, j:] += jnp.sum(l.astype(F32), axis=0, keepdims=True)
        high[j:top, j:] = h
        low[j:top, j:] = l
        if ship is not None:
            ship(j, tile)
        if top < count:
            mirror = jnp.transpose(block[:, tile:])
            h, l = split(mirror)
            high[top:, j:top] = h
            low[top:, j:top] = l
            diag[1:2, j:top] += jnp.sum(l.astype(F32), axis=0, keepdims=True)
        if not j:
            note[0 : face // 2, :] = packed(block[0:face, 0:face])
            first = iota((8, 1), 0) == 0
            note[face // 2 :, :] = jnp.where(first, line[:, 0:face], pack[half : half + 8, 0:face])


def apply(value, mats, half, face):
    oh, ol, ph, plo = mats[:4]
    return jnp.concatenate(
        [
            rows_times(value[:half], oh[:, face:], ol[:, face:]),
            rows_times(value[half:], ph[:, face:], plo[:, face:]),
        ],
        axis=0,
    )


def high_apply(value, mats, half):
    parts = []
    for v, high in ((value[:half], mats[0]), (value[half:], mats[2])):
        both = lax.dot_general(
            jnp.concatenate(split(v), axis=0), high[...], (((1,), (1,)), ((), ())), preferred_element_type=F32
        )
        parts.append(both[:half] + both[half:])
    return jnp.concatenate(parts, axis=0)


def low_apply(value, mats, half):
    v = value.astype(BF16)
    return jnp.concatenate([dot(v[:half], mats[1][...]), dot(v[half:], mats[3][...])], axis=0)


def outer_apply(value, mats, half, face):
    parts = []
    for v, columns in ((value[:half], mats[4]), (value[half:], mats[5])):
        both = dot(jnp.concatenate(split(v), axis=0), columns[...])
        parts.append(both[:half, :face] + both[half:, :face] + both[:half, face:])
    return jnp.concatenate(parts, axis=0)


def face_times(value, rows):
    count = value.shape[0]
    h, l = split(value)
    first, second = jnp.concatenate([h, h], axis=1), jnp.concatenate([l, jnp.zeros_like(l)], axis=1)
    both = dot(jnp.concatenate([first, second], axis=0), rows)
    return both[:count] + both[count:]


def assembled(y, outer, half, face):
    inner = y[:half, face : 2 * face] + y[half:, face : 2 * face]
    first = y[:, :face] if outer is None else y[:, :face] + outer
    return jnp.concatenate([first, jnp.concatenate([inner, inner], axis=0), y[:, 2 * face :]], axis=1)


def first_planes_kernel(u, tables_in, slope_in, out, tables, slope, sems):
    pairs = ((slope_in, slope), (tables_in, tables))
    copies = [pltpu.make_async_copy(a, b, sems.at[i]) for i, (a, b) in enumerate(pairs)]
    for copy in copies:
        copy.start()
    for copy in copies:
        copy.wait()
    planes_kernel(u, tables, slope, out)


def planes_kernel(u, tables, slope, out):
    count = slope.shape[1]
    high, low = tables[0:count, :], tables[count:, :]
    value = u[...]
    mode = iota((count, 1), 0)
    scale = lax.shift_right_arithmetic(mode, 1).astype(F32) * (2.0 / count)
    after, before = pltpu.roll(value, count - 1, 0), pltpu.roll(value, 1, 0)
    paired = jnp.where((mode & 1) == 0, scale * after, -scale * before)
    nodes = value.shape[1]
    both = table_times(high, low, jnp.concatenate([value, paired], axis=1))
    rate = jnp.transpose(jnp.broadcast_to(slope[...], (8, count)))[:, 0:1]
    cross = rate * both[:, :nodes] * both[:, nodes:]
    weight = jnp.where(mode < 2, 1.0 / count, 2.0 / count)
    out[...] = weight * table_times(high, low, cross, 0)


def provisional(r, d, g, inv, cm, mats, alpha, beta, half, face):
    r = r - inv * assembled(g, None, half, face)
    d = alpha * d + beta * r if alpha else beta * r
    y = outer_apply(d, mats, half, face) + cm[:, :face] * d[:, :face]
    return r, d, y


def even():
    _, z, x = position()
    return lax.rem(x + z, 2) == 0


def put(one, two, g, y, half, face, notes=((), ())):
    own = jnp.concatenate([g[:half, :face], y[:half], *notes[0]], axis=0)
    oth = jnp.concatenate([g[half:, :face], y[half:], *notes[1]], axis=0)
    first = even()
    one[...] = picked(first, own, oth)
    two[...] = picked(first, oth, own)


def got(one, two):
    a, b = one[...], two[...]
    first = even()
    return picked(first, a, b), picked(first, b, a)


def received(conv, half):
    _, _, x = position()
    parts = conv.shape[0]
    return jnp.concatenate(
        [
            jnp.concatenate([conv[m, x] for m in range(parts)], axis=1),
            jnp.concatenate([conv[m, 1 - x] for m in range(parts)], axis=1),
        ],
        axis=0,
    )


def masses(own, oth, half):
    count = own.shape[1]
    return jnp.concatenate(
        [jnp.broadcast_to(m[half : half + 1, :], (half, count)) for m in (own, oth)], axis=0
    )


def helmholtz(half, mode_count):
    _, _, x = position()
    mode = lax.axis_index("mode") * (2 * half) + x * half + iota((half, 1), 0)
    number = jnp.where(mode == 1, mode_count // 2, lax.shift_right_arithmetic(mode, 1))
    return mass_weight + (8.0 * number.astype(F32) / mode_count) ** 2


def first_source_kernel(
    half, face, mode_count, conv, own, oth, do, dp, note_o, note_p, oh, ol, ph, plo,
    wo, wp, vo, vp, r_out, d_out, v_out, conv_out, inv_out, cm_out, sums_out, one, two,
):
    for wide, tall, high, low in ((wo, vo, oh, ol), (wp, vp, ph, plo)):
        wide[:, 0:face] = high[:, 0:face]
        wide[:, face:] = low[:, 0:face]
        tall[0:face, :] = high[0:face, :]
        tall[face:, :] = low[0:face, :]
    mats = (oh, ol, ph, plo, wo, wp, vo, vp)
    c = helmholtz(half, mode_count)
    c = jnp.concatenate([c, c], axis=0)
    mass = masses(own, oth, half)
    stiff, sums = (
        jnp.concatenate([jnp.broadcast_to(t[row : row + 1, :], (half, t.shape[1])) for t in (do, dp)], axis=0)
        for row in (0, 1)
    )
    inv = 1.0 / (assembled(stiff, None, half, face) + c * assembled(mass, None, half, face))
    inv = jnp.concatenate([jnp.zeros((2 * half, face), F32), inv[:, face:]], axis=1)
    inv_out[...] = inv
    cm = c * mass + stiff
    cm_out[...] = cm
    sums_out[...] = sums
    v = jnp.concatenate([own[0:half, :], oth[0:half, :]], axis=0)
    v_out[...] = v
    new = received(conv, half)
    conv_out[...] = new
    m4 = mass_weight * mass
    g = high_apply(v, mats, half) + (cm + sums - m4) * v - m4 * new
    r = -inv * assembled(g, None, half, face)
    d = (1.0 / centre) * r
    r_out[...] = r
    d_out[...] = d
    y = outer_apply(d, mats, half, face)
    put(one, two, g, y, half, face, ((note_o[...],), (note_p[...],)))


def source_kernel(
    half, face, conv, old, own, oth, r, d, inv, cm, sums, late, oh, ol, ph, plo, wo, wp, vo, vp,
    r_out, d_out, conv_out, one, two,
):
    mats = (oh, ol, ph, plo, wo, wp, vo, vp)
    new = received(conv, half)
    conv_out[...] = new
    cmv, dv = cm[...], d[...]
    g = high_apply(dv, mats, half) + (cmv + sums[...]) * dv - mass_weight * masses(own, oth, half) * (new - old[...])
    g = widened(g, late[...])
    rv, dv, y = provisional(r[...], None, g, inv[...], cmv, mats, 0.0, 1.0 / centre, half, face)
    r_out[...] = rv
    d_out[...] = dv
    put(one, two, g, y, half, face)


def rest_kernel(
    half, face, now, r, d, sol, source, s1, s2, inv, cm, sums, oh, ol, ph, plo, wo, wp, vo, vp,
    r_out, d_out, sol_out, late_out,
):
    mats = (oh, ol, ph, plo, wo, wp, vo, vp)
    dv, sv = d[...], source[...]
    late = low_apply(sv, mats, half) - sums[...] * sv
    late_out[...] = late[:, :face]
    y = apply(dv, mats, half, face) + cm[:, face:] * dv[:, face:] + late[:, face:]
    y = jnp.concatenate([stacked(got(s1, s2), half, 2 * half), y], axis=1)
    rv = r[...] - inv[...] * assembled(y, None, half, face)
    dn = now[0] * dv + now[1] * rv
    r_out[...] = rv
    d_out[...] = dn
    sol_out[...] = sol[...] + dv + dn


def change_of(dd, theirs, mats, na, nb, half):
    change = [face_times(dd[:half], mats[6][...]), face_times(dd[half:], mats[7][...])]
    their_change = [face_times(theirs[:half], nb), face_times(theirs[half:], na)]
    return jnp.concatenate(change, axis=0), jnp.concatenate(their_change, axis=0)


def stacked(pair, first, last):
    return jnp.concatenate([t[first:last, :] for t in pair], axis=0)


def widened(value, face_part):
    face = face_part.shape[1]
    return jnp.concatenate([value[:, :face] + face_part, value[:, face:]], axis=1)


def corrected(half, face, now, r, d, sol, dr, dd, change, outer, inv):
    back = widened(-inv * assembled(change, outer, half, face), dr)
    step = widened(now[1] * back, now[0] * dd)
    return r + back, d + step, widened(sol + step, dd)


def exact(half, face, beta, now, r, d, sol, sent, came, na, nb, inv, cm, cmn, mats):
    inv_face = inv[:, :face]
    mine, came = got(*sent), got(*came)
    dr = -(inv_face * stacked(came, 0, half))
    dd = beta * dr
    theirs = -beta * (inv_face * stacked(mine, 0, half))
    change, their_change = change_of(dd, theirs, mats, na[...], nb[...], half)
    change = widened(change, cm[:, :face] * dd)
    outer = stacked(came, half, 2 * half) + their_change + cmn[...] * theirs
    return corrected(half, face, now, r[...], d[...], sol[...], dr, dd, change, outer, inv[...])


def first_sweep_kernel(
    half, face, mode_count, before, now, then,
    r, d, sol, late, s1, s2, c1, c2, inv, cm, sums, oh, ol, ph, plo, wo, wp, vo, vp,
    r_out, d_out, sol_out, source_out, inv_out, cmn_out, na_out, nb_out, one, two,
):
    mats = (oh, ol, ph, plo, wo, wp, vo, vp)
    cm_v = cm[...]
    mine, came = got(s1, s2), got(c1, c2)
    c = helmholtz(half, mode_count)
    c = jnp.concatenate([c, c], axis=0)

    def line(pair, row):
        return jnp.concatenate([jnp.broadcast_to(t[row : row + 1, :], (half, face)) for t in pair], axis=0)

    at = 2 * half + face // 2
    their_mass = line(came, at + 1)
    inv_face = 1.0 / (line(mine, at) + line(came, at) + c * (line(mine, at + 1) + their_mass))
    cmn = c * their_mass + line(came, at)
    nb, na = (jnp.concatenate(split(unpacked(t[2 * half : at, :])), axis=0) for t in came)
    dr = -inv_face * (stacked(mine, 0, half) + stacked(came, 0, half))
    dd = before[1] * dr
    change, their_change = change_of(dd, dd, mats, na, nb, half)
    change = widened(change, cm_v[:, :face] * dd)
    outer = stacked(mine, half, 2 * half) + stacked(came, half, 2 * half) + their_change + cmn * dd
    inv_v = jnp.concatenate([inv_face, inv[:, face:]], axis=1)
    rv, dn, sol_v = corrected(half, face, now, r[...], d[...], sol[...], dr, dd, change, outer, inv_v)
    inv_out[...] = inv_v
    cmn_out[...] = cmn
    na_out[...] = na
    nb_out[...] = nb
    sol_out[...] = sol_v
    source_out[...] = dn
    g = widened(high_apply(dn, mats, half) + (cm_v + sums[...]) * dn, late[...])
    rv, dv, y = provisional(rv, dn, g, inv_v, cm_v, mats, then[0], then[1], half, face)
    r_out[...] = rv
    d_out[...] = dv
    put(one, two, g, y, half, face)


def sweep_kernel(
    half, face, before, now, then,
    r, d, sol, late, s1, s2, c1, c2, na, nb, inv, cm, sums, cmn, oh, ol, ph, plo, wo, wp, vo, vp,
    r_out, d_out, sol_out, source_out, one, two,
):
    mats = (oh, ol, ph, plo, wo, wp, vo, vp)
    rv, dn, sol_v = exact(half, face, before[1], now, r, d, sol, (s1, s2), (c1, c2), na, nb, inv, cm, cmn, mats)
    sol_out[...] = sol_v
    source_out[...] = dn
    inv_v, cm_v = inv[...], cm[...]
    g = widened(high_apply(dn, mats, half) + (cm_v + sums[...]) * dn, late[...])
    rv, dv, y = provisional(rv, dn, g, inv_v, cm_v, mats, then[0], then[1], half, face)
    r_out[...] = rv
    d_out[...] = dv
    put(one, two, g, y, half, face)


def last_kernel(
    half, face, before, now,
    r, d, sol, s1, s2, c1, c2, na, nb, inv, cm, cmn, oh, ol, ph, plo, wo, wp, vo, vp,
    r_out, d_out, sol_out, chunks,
):
    rv, dn, new = exact(
        half, face, before[1], now, r, d, sol, (s1, s2), (c1, c2), na, nb, inv, cm, cmn, (oh, ol, ph, plo, wo, wp, vo, vp)
    )
    r_out[...] = rv
    d_out[...] = dn
    sol_out[...] = new
    _, _, x = position()
    parts, width = chunks.shape[0], chunks.shape[3]
    for m in range(parts):
        chunks[m, x] = new[:half, m * width : (m + 1) * width]
        chunks[m, 1 - x] = new[half:, m * width : (m + 1) * width]


def end_kernel(
    half, face, before, now,
    r, d, sol, s1, s2, c1, c2, na, nb, inv, cm, cmn, oh, ol, ph, plo, wo, wp, vo, vp, own_out, oth_out,
):
    _, _, new = exact(
        half, face, before[1], now, r, d, sol, (s1, s2), (c1, c2), na, nb, inv, cm, cmn, (oh, ol, ph, plo, wo, wp, vo, vp)
    )
    own_out[...] = new[:half]
    oth_out[...] = new[half:]


def restored(value, unit):
    count = value.shape[0]
    high = value.astype(BF16)
    middle, low = split(value - high.astype(F32))
    parts = dot(jnp.concatenate([high, middle, low], axis=0), unit)
    return parts[:count] + parts[count : 2 * count] + parts[2 * count :]


def finish_own_kernel(own, place, out, unit_out):
    count = own.shape[1]
    unit = jnp.where(iota((count, 1), 0).astype(F32) == place[0:1, :], 1.0, 0.0).astype(BF16)
    unit_out[...] = unit
    out[...] = restored(own[...], unit)


def finish_kernel(own, other, unit, out):
    _, _, x = position()
    a, b = own[...], restored(other[...], unit[...])
    half = own.shape[0]
    out[0:half, :] = picked(x == 0, a, b)
    out[half:, :] = picked(x == 0, b, a)


def body(n_mode, n_dom, velocity_prev, elem_ops, lumped_mass, span_slope, local_to_global, iface_nodes, live_elems):
    modes, count = velocity_prev.shape
    half = modes // 2
    elems, side = local_to_global.shape
    face = iface_nodes.shape[2]
    mode_count = span_slope.shape[0]
    quarter = count // n_mode
    pairs = n_dom // 2
    slots = elems * ROW
    places = [(z, s) for z in range(pairs) for s in (0, 1)]
    swap = [(i, i ^ 1) for i in range(n_dom)]
    long_swap = [(2 * z + s, 2 * ((z + (1 if z % 2 else -1)) % pairs) + s) for z, s in places]
    short_swap = [(2 * z + s, 2 * ((z + (-1 if z % 2 else 1)) % pairs) + s) for z, s in places]
    groups = [[m * n_dom + 2 * z + s for m in range(n_mode) for s in (0, 1)] for z in range(pairs)]

    def exchange(one, two):
        return lax.ppermute(one, "dom", long_swap), lax.ppermute(two, "dom", short_swap)

    ops = jnp.transpose(elem_ops, (1, 0, 2))
    ops_other = lax.ppermute(ops, "dom", swap)
    pack = (half + 24, count)
    wide = (2 * half, count)
    chunks, place, weights = call(
        order_kernel, [((n_mode, modes, quarter), F32), ((8, count), F32), ((8, count), F32)],
        [iface_nodes[0], velocity_prev, lumped_mass.reshape(1, count)], 24, far=range(3),
        scratch=[
            pltpu.VMEM((2, face), jnp.int32), pltpu.VMEM((modes, count), F32), pltpu.VMEM((1, count), F32),
            pltpu.SemaphoreType.DMA((3,)),
        ],
    )
    planes_in = lax.all_to_all(chunks, "mode", 0, 0, tiled=True)
    keep, send = call(
        pack_kernel, [(pack, F32), (pack, F32)],
        [local_to_global, live_elems.reshape(1, n_dom), chunks, place, weights], 24, far=(0, 1),
        scratch=[
            pltpu.VMEM((elems, side), jnp.int32), pltpu.VMEM((1, n_dom), jnp.int32), pltpu.SemaphoreType.DMA((2,)),
        ],
    )
    oth = lax.ppermute(send, "dom", swap)

    tables = jnp.asarray(np.concatenate(halves(synthesis_table(mode_count))))
    slope = span_slope.reshape(1, mode_count)

    matrix = ((count, count), BF16)
    small = [((8, count), F32), ((face // 2 + 8, face), F32)]
    one_hot = [
        pltpu.VMEM((count, slots), BF16),
        pltpu.VMEM((slots, count), BF16),
        pltpu.VMEM((slots, count), BF16),
        pltpu.VMEM((ROW, 128), F32),
    ]

    def planes(value, first):
        (out,) = call(
            first_planes_kernel if first else planes_kernel, [((mode_count, quarter), F32)],
            [value.reshape(mode_count, quarter), tables, slope], 16, flops=600 << 20,
            far=(1, 2) if first else (), free=(tables.shape,),
            scratch=[
                pltpu.VMEM(tables.shape, BF16), pltpu.VMEM(slope.shape, F32), pltpu.SemaphoreType.DMA((2,)),
            ] if first else (),
        )
        return out

    def to_solve(value):
        back = lax.all_to_all(
            value.reshape(2 * n_mode, half, quarter), ("mode", "dom"), 0, 0, axis_index_groups=groups, tiled=True
        )
        return back.reshape(n_mode, 2, half, quarter)

    cross, keep_late = lax.optimization_barrier((planes(planes_in, True), keep))
    keep_late, ops_other = lax.optimization_barrier((keep_late, ops_other))
    conv = to_solve(cross)
    oh, ol, do, note_o = call(
        functools.partial(own_build_kernel, half), [matrix, matrix, *small], [ops, keep_late], 36,
        far=(0,), out_far=range(4), flops=6 << 30,
        scratch=[
            pltpu.VMEM((side, elems, side), F32), *[pltpu.VMEM(*v) for v in small],
            pltpu.VMEM((count, count), BF16), pltpu.VMEM((count, count), BF16),
            *one_hot, pltpu.SemaphoreType.DMA((2 * count // 256 + 3,)),
        ],
    )
    conv, oth_late = lax.optimization_barrier((conv, oth))
    oh, ol, ph, plo, dp, note_p = call(
        functools.partial(partner_build_kernel, half), [matrix] * 4 + small, [ops_other, oth_late, oh, ol], 24,
        far=(2, 3), pinned=range(4), flops=6 << 30, scratch=[*one_hot, pltpu.SemaphoreType.DMA((2,))],
    )
    mats = [oh, ol, ph, plo]
    coefs = chebyshev()
    message = ((2 * half, face), F32)
    for iteration in range(ITERS):
        if iteration == 0:
            long_message = ((2 * half + face // 2 + 8, face), F32)
            beside = [((count, 2 * face), BF16)] * 2 + [((2 * face, count), BF16)] * 2
            *cats, r, d, sol, old, inv, cm, sums, one, two = call(
                functools.partial(first_source_kernel, half, face, mode_count),
                [*beside, *[(wide, F32)] * 7, long_message, long_message],
                [conv, keep, oth, do, dp, note_o, note_p, *mats], 20, flops=500 << 20, pinned=range(4),
            )
            mats = [*mats, *cats]
            source = sol
        else:
            source = d
            r, d, old, one, two = call(
                functools.partial(source_kernel, half, face),
                [(wide, F32), (wide, F32), (wide, F32), message, message],
                [conv, old, keep, oth, r, d, inv, cm, sums, late, *mats], 20, flops=500 << 20,
            )
        for k in (0, 2, 4):
            c1, c2 = exchange(one, two)
            r, d, sol, late = call(
                functools.partial(rest_kernel, half, face, coefs[k + 1]), [(wide, F32)] * 3 + [((2 * half, face), F32)],
                [r, d, sol, source, one, two, inv, cm, sums, *mats], 20, flops=400 << 20,
            )
            if iteration == 0 and k == 0:
                r, d, sol, source, inv, cmn, na, nb, one, two = call(
                    functools.partial(first_sweep_kernel, half, face, mode_count, coefs[0], coefs[1], coefs[2]),
                    [(wide, F32)] * 5 + [((2 * half, face), F32)] + [((2 * face, face), BF16)] * 2 + [message, message],
                    [r, d, sol, late, one, two, c1, c2, inv, cm, sums, *mats], 20, flops=500 << 20,
                )
                continue
            given = [r, d, sol, one, two, c1, c2, na, nb, inv, cm, cmn, *mats]
            if k < 4:
                r, d, sol, source, one, two = call(
                    functools.partial(sweep_kernel, half, face, coefs[k], coefs[k + 1], coefs[k + 2]),
                    [*[(wide, F32)] * 4, message, message],
                    [r, d, sol, late, one, two, c1, c2, na, nb, inv, cm, sums, cmn, *mats], 20, flops=500 << 20,
                )
            elif iteration < ITERS - 1:
                r, d, sol, chunks = call(
                    functools.partial(last_kernel, half, face, coefs[k], coefs[k + 1]),
                    [(wide, F32), (wide, F32), (wide, F32), ((n_mode, 2, half, quarter), F32)],
                    given, 20, flops=100 << 20,
                )
            else:
                own, other = call(
                    functools.partial(end_kernel, half, face, coefs[k], coefs[k + 1]),
                    [((half, count), F32)] * 2, given, 20, flops=100 << 20,
                )
        if iteration < ITERS - 1:
            planes_in = lax.all_to_all(
                chunks.reshape(2 * n_mode, half, quarter), ("mode", "dom"), 0, 0, axis_index_groups=groups, tiled=True
            )
            conv = to_solve(planes(planes_in, False))
    other = lax.ppermute(other, "dom", swap)
    own, unit = call(
        finish_own_kernel, [((half, count), F32), ((count, count), BF16)], [own, place], 16, flops=200 << 20
    )
    (out,) = call(finish_kernel, [((modes, count), F32)], [own, other, unit], 16)
    return out


def solution(mesh):
    placed = (
        P("mode", "dom"),
        P("dom", None, None),
        P("dom"),
        P(),
        P("dom", None),
        P("dom", None, None),
        P(),
    )
    return jax.shard_map(
        functools.partial(body, mesh.shape["mode"], mesh.shape["dom"]),
        mesh=mesh, in_specs=placed, out_specs=P("mode", "dom"), check_vma=False,
    )
```

```python
import functools

import jax
import jax.numpy as jnp
import numpy as np
from jax import lax
from jax.experimental import pallas as pl
from jax.experimental.pallas import tpu as pltpu
from jax.sharding import PartitionSpec as P

ITERS = 3
SWEEPS = 6

mass_weight = 4.0
bound_low = 0.1
bound_high = 2.0
centre = (bound_high + bound_low) / 2.0
half_width = (bound_high - bound_low) / 2.0

F32 = jnp.float32
BF16 = jnp.bfloat16
ROW = 96


def chebyshev():
    ratio = centre / half_width
    rho = 1.0 / ratio
    coefs = [(0.0, 1.0 / centre)]
    for _ in range(SWEEPS - 1):
        rho_next = 1.0 / (2.0 * ratio - rho)
        coefs.append((rho_next * rho, 2.0 * rho_next / half_width))
        rho = rho_next
    return coefs


def synthesis_table(mode_count):
    column = np.arange(mode_count)
    number = np.where(column == 1, mode_count // 2, column // 2)
    is_sine = (column % 2 == 1) & (column > 1)
    planes = np.arange(mode_count)
    angles = (planes[:, None] * number[None, :] % mode_count) * (2.0 * np.pi / mode_count)
    return np.where(is_sine[None, :], np.sin(angles), np.cos(angles))


def halves(table):
    high = table.astype(np.float32).astype(BF16)
    return [high, (table - high.astype(np.float64)).astype(np.float32).astype(BF16)]


def split(value):
    high = value.astype(BF16)
    return high, (value - high.astype(F32)).astype(BF16)


def dot(a, b):
    return lax.dot_general(a, b, (((1,), (0,)), ((), ())), preferred_element_type=F32)


def rows_times(value, high, low):
    count = value.shape[0]
    h, l = split(value)
    both = dot(jnp.concatenate([h, l], axis=0), high)
    return both[:count] + both[count:] + dot(h, low)


def table_times(high, low, value, dim=1):
    dims = (((dim,), (0,)), ((), ()))
    count = value.shape[1]
    h, l = split(value)
    both = lax.dot_general(high, jnp.concatenate([h, l], axis=1), dims, preferred_element_type=F32)
    return both[:, :count] + both[:, count:] + lax.dot_general(low, h, dims, preferred_element_type=F32)


def iota(shape, dim):
    return lax.broadcasted_iota(jnp.int32, shape, dim)


def call(kernel, outs, vmem, limit, scratch=(), flops=0, moved=1 << 20, far=(), out_far=(), pinned=(), free=()):
    in_specs, given = [], []
    for i, v in enumerate(vmem):
        space = pltpu.HBM if i in far else pltpu.VMEM
        in_specs.append(pl.BlockSpec(memory_space=space))
        fixed = i in far or v.dtype == BF16 and v.shape not in free
        given.append(pltpu.with_memory_space_constraint(v, space) if fixed else v)
    shapes, out_specs = [], []
    for i, (s, t) in enumerate(outs):
        space = pltpu.HBM if i in out_far else pltpu.VMEM
        out_specs.append(pl.BlockSpec(memory_space=space))
        shapes.append(space(s, t) if i in out_far or i in pinned else jax.ShapeDtypeStruct(s, t))
    return pl.pallas_call(
        kernel,
        out_shape=shapes,
        in_specs=in_specs,
        out_specs=out_specs,
        scratch_shapes=list(scratch),
        compiler_params=pltpu.CompilerParams(vmem_limit_bytes=limit << 20),
        cost_estimate=pl.CostEstimate(flops=flops, bytes_accessed=moved, transcendentals=0),
    )(*given)


def position():
    q = lax.axis_index("dom")
    z = lax.shift_right_arithmetic(q, 1)
    return q, z, q - 2 * z


def picked(first, a, b):
    return jnp.where(first, a, b)


def order_kernel(iface_in, vel_in, mass_in, chunks, place_out, mass_out, iface, vel, mass, sems):
    _, _, x = position()
    pairs = ((iface_in, iface), (vel_in, vel), (mass_in, mass))
    copies = [pltpu.make_async_copy(a, b, sems.at[i]) for i, (a, b) in enumerate(pairs)]
    for copy in copies:
        copy.start()
    for copy in copies:
        copy.wait()
    count = mass.shape[1]
    face = iface.shape[1]
    lists = jnp.concatenate(
        [picked(x == 0, iface[0:1, :], iface[1:2, :]), picked(x == 0, iface[1:2, :], iface[0:1, :])], axis=1
    ).astype(F32)
    lists = jnp.transpose(jnp.broadcast_to(lists, (8, 2 * face)))[:, 0:1]
    hit = jnp.where(lists == iota((1, count), 1).astype(F32), 1.0, 0.0)
    at = jnp.sum(hit * iota((2 * face, 1), 0).astype(F32), axis=0, keepdims=True)
    shared = jnp.sum(hit, axis=0, keepdims=True)
    rest = jnp.broadcast_to(1.0 - shared, (8, count))
    lane = iota((8, count), 1)
    run = rest
    step = 1
    while step < count:
        run = run + jnp.where(lane >= step, pltpu.roll(run, step, 1), 0.0)
        step *= 2
    place = jnp.where(rest > 0.5, run - 1.0 + 2.0 * face, jnp.broadcast_to(at, (8, count)))
    place_out[...] = place
    column = jnp.transpose(place)[:, 0:1]
    unit = jnp.where(iota((1, count), 1).astype(F32) == column, 1.0, 0.0).astype(BF16)
    modes = vel.shape[0]
    value = jnp.concatenate([vel[...], jnp.broadcast_to(mass[...], (16, count))], axis=0)
    high = value.astype(BF16)
    middle, low = split(value - high.astype(F32))
    total = modes + 16
    parts = dot(jnp.concatenate([high, middle, low], axis=0), unit)
    moved = parts[:total] + parts[total : 2 * total] + parts[2 * total :]
    mass_out[...] = moved[modes : modes + 8]
    quarter = count // chunks.shape[0]
    for part in range(chunks.shape[0]):
        chunks[part] = moved[:modes, part * quarter : (part + 1) * quarter]


def pack_kernel(l2g_in, live_in, chunks, place, mass, keep, send, l2g, live, sems):
    q, _, x = position()
    copies = [pltpu.make_async_copy(a, b, sems.at[i]) for i, (a, b) in enumerate(((l2g_in, l2g), (live_in, live)))]
    for copy in copies:
        copy.start()
    for copy in copies:
        copy.wait()
    count = place.shape[1]
    column = jnp.transpose(place[...])[:, 0:1]
    elems, side = l2g.shape
    slots = elems * ROW
    blank = jnp.full((1, ROW - side), -1, jnp.int32)
    row = jnp.concatenate([piece for e in range(elems) for piece in (l2g[e : e + 1, :], blank)], axis=1)
    pieces = []
    for first in range(0, slots, 512):
        part = row[:, first : first + 512]
        found = jnp.where(iota((count, 1), 0) == part, column, 0.0)
        pieces.append(jnp.where(part < 0, -1.0, jnp.sum(found, axis=0, keepdims=True)))
    index = jnp.concatenate(pieces, axis=1)
    moved = jnp.concatenate([chunks[part] for part in range(chunks.shape[0])], axis=1)
    half = moved.shape[0] // 2
    a, b = moved[:half], moved[half:]
    lived = jnp.where(iota(live.shape, 1) == q, live[...], 0).astype(F32)
    lived = jnp.sum(lived, axis=1, keepdims=True)
    for ref, rows in ((keep, picked(x == 0, a, b)), (send, picked(x == 0, b, a))):
        ref[0:half, :] = rows
        ref[half : half + 8, :] = mass[...]
        ref[half + 8 : half + 16, :] = jnp.broadcast_to(index[:, :count], (8, count))
        ref[half + 16 : half + 24, 0 : slots - count] = jnp.broadcast_to(
            index[:, count:], (8, slots - count)
        )
        ref[half + 16 : half + 24, slots - count :] = jnp.broadcast_to(lived, (8, 2 * count - slots))


def own_build_kernel(
    half, ops_in, pack, high_out, low_out, diag_out, note_out, ops, diag, note, high, low, *scratch
):
    sems = scratch[-1]
    fetch = pltpu.make_async_copy(ops_in, ops, sems.at[0])
    fetch.start()
    copies = []

    def ship(*rows):
        for part, out in ((high, high_out), (low, low_out)):
            at = pl.ds(*rows)
            copies.append(pltpu.make_async_copy(part.at[at], out.at[at], sems.at[len(copies) + 1]))
            copies[-1].start()

    build_kernel(half, ops, pack, high, low, diag, note, *scratch[:-1], ready=fetch.wait, ship=ship)
    for part, out in ((diag, diag_out), (note, note_out)):
        copies.append(pltpu.make_async_copy(part, out, sems.at[len(copies) + 1]))
        copies[-1].start()
    for copy in copies:
        copy.wait()


def partner_build_kernel(
    half, ops, pack, high_in, low_in, high_own, low_own, high, low, wo, wp, vo, vp, diag, note, *scratch
):
    sems = scratch[-1]
    pairs = ((high_in, high_own), (low_in, low_own))
    copies = [pltpu.make_async_copy(a, b, sems.at[i]) for i, (a, b) in enumerate(pairs)]
    for copy in copies:
        copy.start()
    face = note.shape[1]

    def strips(first, tile):
        if first != tile:
            return
        for copy in copies:
            copy.wait()
        for wide, tall, h, l in ((wo, vo, high_own, low_own), (wp, vp, high, low)):
            wide[:, 0:face] = h[:, 0:face]
            wide[:, face:] = l[:, 0:face]
            tall[0:face, :] = h[0:face, :]
            tall[face:, :] = l[0:face, :]

    build_kernel(half, ops, pack, high, low, diag, note, *scratch[:-1], ship=strips)


def packed(block):
    h = block.shape[0] // 2
    row, lane = iota((h, 2 * h), 0), iota((h, 2 * h), 1)
    return jnp.where((lane < h) & (row > lane), pltpu.roll(block[h:], h, 1), block[:h])


def unpacked(rows):
    h = rows.shape[0]
    row, lane = iota((h, 2 * h), 0), iota((h, 2 * h), 1)
    turned = jnp.transpose(jnp.concatenate([rows, jnp.zeros_like(rows)], axis=0))
    top = jnp.where((lane < h) & (row > lane), turned[:h], rows)
    last = jnp.where(row > lane, rows, turned[:h])
    return jnp.concatenate([top, jnp.where(lane < h, turned[h:], pltpu.roll(last, h, 1))], axis=0)


def build_kernel(half, ops, pack, high, low, diag, note, flat, qh, ql, pad, ready=None, ship=None):
    live = pack[half + 16 : half + 17, pack.shape[1] - 1 :]
    side, elems = ops.shape[0], ops.shape[1]
    count = high.shape[0]
    slots = elems * ROW
    index = jnp.concatenate(
        [pack[half + 8 : half + 16, :], pack[half + 16 : half + 24, 0 : slots - count]], axis=1
    )
    column = jnp.transpose(index)[:, 0:1]
    pad[...] = jnp.zeros(pad.shape, F32)
    lane = iota((1, count), 1).astype(F32)
    share = count // elems

    def table_rows(e):
        rows = jnp.where((iota((share, 1), 0) + e * share).astype(F32) == index[0:1], 1.0, 0.0)
        flat[e * share : (e + 1) * share, :] = rows.astype(BF16)

    ahead = 0
    if ready is not None:
        ahead = elems // 3
        for e in range(ahead):
            table_rows(e)
        ready()
    for e in range(elems):
        at = slice(e * ROW, (e + 1) * ROW)
        nodes = jnp.where(lane == column[at], 1.0, 0.0).astype(BF16)
        pad[0:side, 0:side] = ops[:, e, :] * jnp.where(live > e + 0.5, 1.0, 0.0)
        spread = dot(jnp.concatenate(split(pad[:, 0:ROW]), axis=0), nodes)
        qh[at, :] = spread[:ROW].astype(BF16)
        ql[at, :] = spread[ROW:].astype(BF16)
        if e >= ahead:
            table_rows(e)
    tile = 256
    face = note.shape[1]
    diag[...] = jnp.zeros(diag.shape, F32)
    for j in range(0, count, tile):
        top = j + tile
        block = dot(flat[j:top, :], qh[:, j:]) + dot(flat[j:top, :], ql[:, j:])
        own_node = iota((tile, 1), 0) == iota((1, tile), 1)
        line = jnp.sum(jnp.where(own_node, block[:, :tile], 0.0), axis=0, keepdims=True)
        kept = jnp.where(own_node, 0.0, block[:, :tile])
        block = jnp.concatenate([kept, block[:, tile:]], axis=1) if top < count else kept
        h, l = split(block)
        diag[0:1, j:top] = line
        diag[1:2, j:] += jnp.sum(l.astype(F32), axis=0, keepdims=True)
        high[j:top, j:] = h
        low[j:top, j:] = l
        if ship is not None:
            ship(j, tile)
        if top < count:
            mirror = jnp.transpose(block[:, tile:])
            h, l = split(mirror)
            high[top:, j:top] = h
            low[top:, j:top] = l
            diag[1:2, j:top] += jnp.sum(l.astype(F32), axis=0, keepdims=True)
        if not j:
            note[0 : face // 2, :] = packed(block[0:face, 0:face])
            first = iota((8, 1), 0) == 0
            note[face // 2 :, :] = jnp.where(first, line[:, 0:face], pack[half : half + 8, 0:face])


def apply(value, mats, half, face):
    oh, ol, ph, plo = mats[:4]
    return jnp.concatenate(
        [
            rows_times(value[:half], oh[:, face:], ol[:, face:]),
            rows_times(value[half:], ph[:, face:], plo[:, face:]),
        ],
        axis=0,
    )


def high_apply(value, mats, half):
    parts = []
    for v, high in ((value[:half], mats[0]), (value[half:], mats[2])):
        both = dot(jnp.concatenate(split(v), axis=0), high[...])
        parts.append(both[:half] + both[half:])
    return jnp.concatenate(parts, axis=0)


def low_apply(value, mats, half):
    v = value.astype(BF16)
    return jnp.concatenate([dot(v[:half], mats[1][...]), dot(v[half:], mats[3][...])], axis=0)


def outer_apply(value, mats, half, face):
    parts = []
    for v, columns in ((value[:half], mats[4]), (value[half:], mats[5])):
        both = dot(jnp.concatenate(split(v), axis=0), columns[...])
        parts.append(both[:half, :face] + both[half:, :face] + both[:half, face:])
    return jnp.concatenate(parts, axis=0)


def face_times(value, rows):
    count = value.shape[0]
    h, l = split(value)
    first, second = jnp.concatenate([h, h], axis=1), jnp.concatenate([l, jnp.zeros_like(l)], axis=1)
    both = dot(jnp.concatenate([first, second], axis=0), rows)
    return both[:count] + both[count:]


def assembled(y, outer, half, face):
    inner = y[:half, face : 2 * face] + y[half:, face : 2 * face]
    first = y[:, :face] if outer is None else y[:, :face] + outer
    return jnp.concatenate([first, jnp.concatenate([inner, inner], axis=0), y[:, 2 * face :]], axis=1)


def first_planes_kernel(u, tables_in, slope_in, out, tables, slope, sems):
    pairs = ((slope_in, slope), (tables_in, tables))
    copies = [pltpu.make_async_copy(a, b, sems.at[i]) for i, (a, b) in enumerate(pairs)]
    for copy in copies:
        copy.start()
    for copy in copies:
        copy.wait()
    planes_kernel(u, tables, slope, out)


def planes_kernel(u, tables, slope, out):
    count = slope.shape[1]
    high, low = tables[0:count, :], tables[count:, :]
    value = u[...]
    mode = iota((count, 1), 0)
    scale = lax.shift_right_arithmetic(mode, 1).astype(F32) * (2.0 / count)
    after, before = pltpu.roll(value, count - 1, 0), pltpu.roll(value, 1, 0)
    paired = jnp.where((mode & 1) == 0, scale * after, -scale * before)
    nodes = value.shape[1]
    both = table_times(high, low, jnp.concatenate([value, paired], axis=1))
    rate = jnp.transpose(jnp.broadcast_to(slope[...], (8, count)))[:, 0:1]
    cross = rate * both[:, :nodes] * both[:, nodes:]
    weight = jnp.where(mode < 2, 1.0 / count, 2.0 / count)
    out[...] = weight * table_times(high, low, cross, 0)


def provisional(r, d, g, inv, cm, mats, alpha, beta, half, face):
    r = r - inv * assembled(g, None, half, face)
    d = alpha * d + beta * r if alpha else beta * r
    y = outer_apply(d, mats, half, face) + cm[:, :face] * d[:, :face]
    return r, d, y


def even():
    _, z, x = position()
    return lax.rem(x + z, 2) == 0


def put(one, two, g, y, half, face, notes=((), ())):
    own = jnp.concatenate([g[:half, :face], y[:half], *notes[0]], axis=0)
    oth = jnp.concatenate([g[half:, :face], y[half:], *notes[1]], axis=0)
    first = even()
    one[...] = picked(first, own, oth)
    two[...] = picked(first, oth, own)


def got(one, two):
    a, b = one[...], two[...]
    first = even()
    return picked(first, a, b), picked(first, b, a)


def received(conv, half):
    _, _, x = position()
    parts = conv.shape[0]
    return jnp.concatenate(
        [
            jnp.concatenate([conv[m, x] for m in range(parts)], axis=1),
            jnp.concatenate([conv[m, 1 - x] for m in range(parts)], axis=1),
        ],
        axis=0,
    )


def masses(own, oth, half):
    count = own.shape[1]
    return jnp.concatenate(
        [jnp.broadcast_to(m[half : half + 1, :], (half, count)) for m in (own, oth)], axis=0
    )


def helmholtz(half, mode_count):
    _, _, x = position()
    mode = lax.axis_index("mode") * (2 * half) + x * half + iota((half, 1), 0)
    number = jnp.where(mode == 1, mode_count // 2, lax.shift_right_arithmetic(mode, 1))
    return mass_weight + (8.0 * number.astype(F32) / mode_count) ** 2


def first_source_kernel(
    half, face, mode_count, conv, own, oth, do, dp, note_o, note_p, oh, ol, ph, plo,
    wo, wp, vo, vp, r_out, d_out, v_out, conv_out, inv_out, cm_out, sums_out, one, two,
):
    mats = (oh, ol, ph, plo, wo, wp, vo, vp)
    c = helmholtz(half, mode_count)
    c = jnp.concatenate([c, c], axis=0)
    mass = masses(own, oth, half)
    stiff, sums = (
        jnp.concatenate([jnp.broadcast_to(t[row : row + 1, :], (half, t.shape[1])) for t in (do, dp)], axis=0)
        for row in (0, 1)
    )
    inv = 1.0 / (assembled(stiff, None, half, face) + c * assembled(mass, None, half, face))
    inv = jnp.concatenate([jnp.zeros((2 * half, face), F32), inv[:, face:]], axis=1)
    inv_out[...] = inv
    cm = c * mass + stiff
    cm_out[...] = cm
    sums_out[...] = sums
    v = jnp.concatenate([own[0:half, :], oth[0:half, :]], axis=0)
    v_out[...] = v
    new = received(conv, half)
    conv_out[...] = new
    m4 = mass_weight * mass
    g = high_apply(v, mats, half) + (cm + sums - m4) * v - m4 * new
    r = -inv * assembled(g, None, half, face)
    d = (1.0 / centre) * r
    r_out[...] = r
    d_out[...] = d
    y = outer_apply(d, mats, half, face)
    put(one, two, g, y, half, face, ((note_o[...],), (note_p[...],)))


def source_kernel(
    half, face, conv, old, own, oth, r, d, inv, cm, sums, late, oh, ol, ph, plo, wo, wp, vo, vp,
    r_out, d_out, conv_out, one, two,
):
    mats = (oh, ol, ph, plo, wo, wp, vo, vp)
    new = received(conv, half)
    conv_out[...] = new
    cmv, dv = cm[...], d[...]
    g = high_apply(dv, mats, half) + (cmv + sums[...]) * dv - mass_weight * masses(own, oth, half) * (new - old[...])
    g = widened(g, late[...])
    rv, dv, y = provisional(r[...], None, g, inv[...], cmv, mats, 0.0, 1.0 / centre, half, face)
    r_out[...] = rv
    d_out[...] = dv
    put(one, two, g, y, half, face)


def rest_kernel(
    half, face, now, r, d, sol, source, s1, s2, inv, cm, sums, oh, ol, ph, plo, wo, wp, vo, vp,
    r_out, d_out, sol_out, late_out,
):
    mats = (oh, ol, ph, plo, wo, wp, vo, vp)
    dv, sv = d[...], source[...]
    late = low_apply(sv, mats, half) - sums[...] * sv
    late_out[...] = late[:, :face]
    y = apply(dv, mats, half, face) + cm[:, face:] * dv[:, face:] + late[:, face:]
    y = jnp.concatenate([stacked(got(s1, s2), half, 2 * half), y], axis=1)
    rv = r[...] - inv[...] * assembled(y, None, half, face)
    dn = now[0] * dv + now[1] * rv
    r_out[...] = rv
    d_out[...] = dn
    sol_out[...] = sol[...] + dv + dn


def change_of(dd, theirs, mats, na, nb, half):
    change = [face_times(dd[:half], mats[6][...]), face_times(dd[half:], mats[7][...])]
    their_change = [face_times(theirs[:half], nb), face_times(theirs[half:], na)]
    return jnp.concatenate(change, axis=0), jnp.concatenate(their_change, axis=0)


def stacked(pair, first, last):
    return jnp.concatenate([t[first:last, :] for t in pair], axis=0)


def widened(value, face_part):
    face = face_part.shape[1]
    return jnp.concatenate([value[:, :face] + face_part, value[:, face:]], axis=1)


def corrected(half, face, now, r, d, sol, dr, dd, change, outer, inv):
    back = widened(-inv * assembled(change, outer, half, face), dr)
    step = widened(now[1] * back, now[0] * dd)
    return r + back, d + step, widened(sol + step, dd)


def exact(half, face, beta, now, r, d, sol, sent, came, na, nb, inv, cm, cmn, mats):
    inv_face = inv[:, :face]
    mine, came = got(*sent), got(*came)
    dr = -(inv_face * stacked(came, 0, half))
    dd = beta * dr
    theirs = -beta * (inv_face * stacked(mine, 0, half))
    change, their_change = change_of(dd, theirs, mats, na[...], nb[...], half)
    change = widened(change, cm[:, :face] * dd)
    outer = stacked(came, half, 2 * half) + their_change + cmn[...] * theirs
    return corrected(half, face, now, r[...], d[...], sol[...], dr, dd, change, outer, inv[...])


def first_sweep_kernel(
    half, face, mode_count, before, now, then,
    r, d, sol, late, s1, s2, c1, c2, inv, cm, sums, oh, ol, ph, plo, wo, wp, vo, vp,
    r_out, d_out, sol_out, source_out, inv_out, cmn_out, na_out, nb_out, one, two,
):
    mats = (oh, ol, ph, plo, wo, wp, vo, vp)
    cm_v = cm[...]
    mine, came = got(s1, s2), got(c1, c2)
    c = helmholtz(half, mode_count)
    c = jnp.concatenate([c, c], axis=0)

    def line(pair, row):
        return jnp.concatenate([jnp.broadcast_to(t[row : row + 1, :], (half, face)) for t in pair], axis=0)

    at = 2 * half + face // 2
    their_mass = line(came, at + 1)
    inv_face = 1.0 / (line(mine, at) + line(came, at) + c * (line(mine, at + 1) + their_mass))
    cmn = c * their_mass + line(came, at)
    nb, na = (jnp.concatenate(split(unpacked(t[2 * half : at, :])), axis=0) for t in came)
    dr = -inv_face * (stacked(mine, 0, half) + stacked(came, 0, half))
    dd = before[1] * dr
    change, their_change = change_of(dd, dd, mats, na, nb, half)
    change = widened(change, cm_v[:, :face] * dd)
    outer = stacked(mine, half, 2 * half) + stacked(came, half, 2 * half) + their_change + cmn * dd
    inv_v = jnp.concatenate([inv_face, inv[:, face:]], axis=1)
    rv, dn, sol_v = corrected(half, face, now, r[...], d[...], sol[...], dr, dd, change, outer, inv_v)
    inv_out[...] = inv_v
    cmn_out[...] = cmn
    na_out[...] = na
    nb_out[...] = nb
    sol_out[...] = sol_v
    source_out[...] = dn
    g = widened(high_apply(dn, mats, half) + (cm_v + sums[...]) * dn, late[...])
    rv, dv, y = provisional(rv, dn, g, inv_v, cm_v, mats, then[0], then[1], half, face)
    r_out[...] = rv
    d_out[...] = dv
    put(one, two, g, y, half, face)


def sweep_kernel(
    half, face, before, now, then,
    r, d, sol, late, s1, s2, c1, c2, na, nb, inv, cm, sums, cmn, oh, ol, ph, plo, wo, wp, vo, vp,
    r_out, d_out, sol_out, source_out, one, two,
):
    mats = (oh, ol, ph, plo, wo, wp, vo, vp)
    rv, dn, sol_v = exact(half, face, before[1], now, r, d, sol, (s1, s2), (c1, c2), na, nb, inv, cm, cmn, mats)
    sol_out[...] = sol_v
    source_out[...] = dn
    inv_v, cm_v = inv[...], cm[...]
    g = widened(high_apply(dn, mats, half) + (cm_v + sums[...]) * dn, late[...])
    rv, dv, y = provisional(rv, dn, g, inv_v, cm_v, mats, then[0], then[1], half, face)
    r_out[...] = rv
    d_out[...] = dv
    put(one, two, g, y, half, face)


def last_kernel(
    half, face, before, now,
    r, d, sol, s1, s2, c1, c2, na, nb, inv, cm, cmn, oh, ol, ph, plo, wo, wp, vo, vp,
    r_out, d_out, sol_out, chunks,
):
    rv, dn, new = exact(
        half, face, before[1], now, r, d, sol, (s1, s2), (c1, c2), na, nb, inv, cm, cmn, (oh, ol, ph, plo, wo, wp, vo, vp)
    )
    r_out[...] = rv
    d_out[...] = dn
    sol_out[...] = new
    _, _, x = position()
    parts, width = chunks.shape[0], chunks.shape[3]
    for m in range(parts):
        chunks[m, x] = new[:half, m * width : (m + 1) * width]
        chunks[m, 1 - x] = new[half:, m * width : (m + 1) * width]


def end_kernel(
    half, face, before, now,
    r, d, sol, s1, s2, c1, c2, na, nb, inv, cm, cmn, oh, ol, ph, plo, wo, wp, vo, vp, own_out, oth_out,
):
    _, _, new = exact(
        half, face, before[1], now, r, d, sol, (s1, s2), (c1, c2), na, nb, inv, cm, cmn, (oh, ol, ph, plo, wo, wp, vo, vp)
    )
    own_out[...] = new[:half]
    oth_out[...] = new[half:]


def restored(value, unit):
    count = value.shape[0]
    high = value.astype(BF16)
    middle, low = split(value - high.astype(F32))
    parts = dot(jnp.concatenate([high, middle, low], axis=0), unit)
    return parts[:count] + parts[count : 2 * count] + parts[2 * count :]


def finish_own_kernel(own, place, out, unit_out):
    count = own.shape[1]
    unit = jnp.where(iota((count, 1), 0).astype(F32) == place[0:1, :], 1.0, 0.0).astype(BF16)
    unit_out[...] = unit
    out[...] = restored(own[...], unit)


def finish_kernel(own, other, unit, out):
    _, _, x = position()
    a, b = own[...], restored(other[...], unit[...])
    half = own.shape[0]
    out[0:half, :] = picked(x == 0, a, b)
    out[half:, :] = picked(x == 0, b, a)


def body(n_mode, n_dom, velocity_prev, elem_ops, lumped_mass, span_slope, local_to_global, iface_nodes, live_elems):
    modes, count = velocity_prev.shape
    half = modes // 2
    elems, side = local_to_global.shape
    face = iface_nodes.shape[2]
    mode_count = span_slope.shape[0]
    quarter = count // n_mode
    pairs = n_dom // 2
    slots = elems * ROW
    places = [(z, s) for z in range(pairs) for s in (0, 1)]
    swap = [(i, i ^ 1) for i in range(n_dom)]
    long_swap = [(2 * z + s, 2 * ((z + (1 if z % 2 else -1)) % pairs) + s) for z, s in places]
    short_swap = [(2 * z + s, 2 * ((z + (-1 if z % 2 else 1)) % pairs) + s) for z, s in places]
    groups = [[m * n_dom + 2 * z + s for m in range(n_mode) for s in (0, 1)] for z in range(pairs)]

    def exchange(one, two):
        return lax.ppermute(one, "dom", long_swap), lax.ppermute(two, "dom", short_swap)

    ops = jnp.transpose(elem_ops, (1, 0, 2))
    ops_other = lax.ppermute(ops, "dom", swap)
    pack = (half + 24, count)
    wide = (2 * half, count)
    chunks, place, weights = call(
        order_kernel, [((n_mode, modes, quarter), F32), ((8, count), F32), ((8, count), F32)],
        [iface_nodes[0], velocity_prev, lumped_mass.reshape(1, count)], 24, far=range(3),
        scratch=[
            pltpu.VMEM((2, face), jnp.int32), pltpu.VMEM((modes, count), F32), pltpu.VMEM((1, count), F32),
            pltpu.SemaphoreType.DMA((3,)),
        ],
    )
    planes_in = lax.all_to_all(chunks, "mode", 0, 0, tiled=True)
    keep, send = call(
        pack_kernel, [(pack, F32), (pack, F32)],
        [local_to_global, live_elems.reshape(1, n_dom), chunks, place, weights], 24, far=(0, 1),
        scratch=[
            pltpu.VMEM((elems, side), jnp.int32), pltpu.VMEM((1, n_dom), jnp.int32), pltpu.SemaphoreType.DMA((2,)),
        ],
    )
    oth = lax.ppermute(send, "dom", swap)

    tables = jnp.asarray(np.concatenate(halves(synthesis_table(mode_count))))
    slope = span_slope.reshape(1, mode_count)

    matrix = ((count, count), BF16)
    small = [((8, count), F32), ((face // 2 + 8, face), F32)]
    one_hot = [
        pltpu.VMEM((count, slots), BF16),
        pltpu.VMEM((slots, count), BF16),
        pltpu.VMEM((slots, count), BF16),
        pltpu.VMEM((ROW, 128), F32),
    ]

    def planes(value, first):
        (out,) = call(
            first_planes_kernel if first else planes_kernel, [((mode_count, quarter), F32)],
            [value.reshape(mode_count, quarter), tables, slope], 16, flops=600 << 20,
            far=(1, 2) if first else (), free=(tables.shape,),
            scratch=[
                pltpu.VMEM(tables.shape, BF16), pltpu.VMEM(slope.shape, F32), pltpu.SemaphoreType.DMA((2,)),
            ] if first else (),
        )
        return out

    def to_solve(value):
        back = lax.all_to_all(
            value.reshape(2 * n_mode, half, quarter), ("mode", "dom"), 0, 0, axis_index_groups=groups, tiled=True
        )
        return back.reshape(n_mode, 2, half, quarter)

    cross, keep_late = lax.optimization_barrier((planes(planes_in, True), keep))
    keep_late, ops_other = lax.optimization_barrier((keep_late, ops_other))
    conv = to_solve(cross)
    oh, ol, do, note_o = call(
        functools.partial(own_build_kernel, half), [matrix, matrix, *small], [ops, keep_late], 36,
        far=(0,), out_far=range(4), flops=6 << 30,
        scratch=[
            pltpu.VMEM((side, elems, side), F32), *[pltpu.VMEM(*v) for v in small],
            pltpu.VMEM((count, count), BF16), pltpu.VMEM((count, count), BF16),
            *one_hot, pltpu.SemaphoreType.DMA((2 * count // 256 + 3,)),
        ],
    )
    conv, oth_late = lax.optimization_barrier((conv, oth))
    strips = [((count, 2 * face), BF16)] * 2 + [((2 * face, count), BF16)] * 2
    *mats, dp, note_p = call(
        functools.partial(partner_build_kernel, half), [*[matrix] * 4, *strips, *small],
        [ops_other, oth_late, oh, ol], 24, far=(2, 3), pinned=range(8), flops=6 << 30, scratch=[*one_hot, pltpu.SemaphoreType.DMA((2,))],
    )
    coefs = chebyshev()
    message = ((2 * half, face), F32)
    for iteration in range(ITERS):
        if iteration == 0:
            long_message = ((2 * half + face // 2 + 8, face), F32)
            r, d, sol, old, inv, cm, sums, one, two = call(
                functools.partial(first_source_kernel, half, face, mode_count),
                [*[(wide, F32)] * 7, long_message, long_message],
                [conv, keep, oth, do, dp, note_o, note_p, *mats], 20, flops=500 << 20,
            )
            source = sol
        else:
            source = d
            r, d, old, one, two = call(
                functools.partial(source_kernel, half, face),
                [(wide, F32), (wide, F32), (wide, F32), message, message],
                [conv, old, keep, oth, r, d, inv, cm, sums, late, *mats], 20, flops=500 << 20,
            )
        for k in (0, 2, 4):
            c1, c2 = exchange(one, two)
            r, d, sol, late = call(
                functools.partial(rest_kernel, half, face, coefs[k + 1]), [(wide, F32)] * 3 + [((2 * half, face), F32)],
                [r, d, sol, source, one, two, inv, cm, sums, *mats], 20, flops=400 << 20,
            )
            if iteration == 0 and k == 0:
                r, d, sol, source, inv, cmn, na, nb, one, two = call(
                    functools.partial(first_sweep_kernel, half, face, mode_count, coefs[0], coefs[1], coefs[2]),
                    [(wide, F32)] * 5 + [((2 * half, face), F32)] + [((2 * face, face), BF16)] * 2 + [message, message],
                    [r, d, sol, late, one, two, c1, c2, inv, cm, sums, *mats], 20, flops=500 << 20,
                )
                continue
            given = [r, d, sol, one, two, c1, c2, na, nb, inv, cm, cmn, *mats]
            if k < 4:
                r, d, sol, source, one, two = call(
                    functools.partial(sweep_kernel, half, face, coefs[k], coefs[k + 1], coefs[k + 2]),
                    [*[(wide, F32)] * 4, message, message],
                    [r, d, sol, late, one, two, c1, c2, na, nb, inv, cm, sums, cmn, *mats], 20, flops=500 << 20,
                )
            elif iteration < ITERS - 1:
                r, d, sol, chunks = call(
                    functools.partial(last_kernel, half, face, coefs[k], coefs[k + 1]),
                    [(wide, F32), (wide, F32), (wide, F32), ((n_mode, 2, half, quarter), F32)],
                    given, 20, flops=100 << 20,
                )
            else:
                own, other = call(
                    functools.partial(end_kernel, half, face, coefs[k], coefs[k + 1]),
                    [((half, count), F32)] * 2, given, 20, flops=100 << 20,
                )
        if iteration < ITERS - 1:
            planes_in = lax.all_to_all(
                chunks.reshape(2 * n_mode, half, quarter), ("mode", "dom"), 0, 0, axis_index_groups=groups, tiled=True
            )
            conv = to_solve(planes(planes_in, False))
    other = lax.ppermute(other, "dom", swap)
    own, unit = call(
        finish_own_kernel, [((half, count), F32), ((count, count), BF16)], [own, place], 16, flops=200 << 20
    )
    (out,) = call(finish_kernel, [((modes, count), F32)], [own, other, unit], 16)
    return out


def solution(mesh):
    placed = (
        P("mode", "dom"),
        P("dom", None, None),
        P("dom"),
        P(),
        P("dom", None),
        P("dom", None, None),
        P(),
    )
    return jax.shard_map(
        functools.partial(body, mesh.shape["mode"], mesh.shape["dom"]),
        mesh=mesh, in_specs=placed, out_specs=P("mode", "dom"), check_vma=False,
    )
```
